32 devices in a mesh: scan: 2 (over x), coil: 4 (over z), pencil: 4 (over y, core).
Axes of the slice: x: 2, y: 2, z: 4, core: 2. Of those that a mesh axis runs over, the one named last changes fastest.
Arguments:
- kspace: bfloat16 [4, 16, 2, 4096], P('coil', 'scan', None, 'pencil'), parts along dimension 1, may hold values from -6 to 6
- sens_maps: bfloat16 [4, 16, 2, 512, 512], P('coil', 'scan', None, 'pencil'), parts along dimension 1, may hold values from -5 to 5
- weights: bfloat16 [128, 128, 128], P('pencil'), may hold values from -0.25 to 0.25
- tile_slot: int32 [128], P('pencil'), may hold values from 0 to 31, as said below
- tile_block: int32 [128], P('pencil'), may hold values from 0 to 7
- send_list: int32 [4, 4, 8], P('pencil'), may hold values from 0 to 511
Outputs:
- solution: float32 [16, 2, 512, 512], P('scan', None, 'pencil'), parts along dimension 0
- residual: float32 [16, 2, 512, 512], P('scan', None, 'pencil'), parts along dimension 0
The draws below stay inside these ranges and needn't reach their ends.
There are 2 independent parts, one for each index of `scan`. The reference program is written for one: setup_inputs(seed, part) draws one part's arguments, and reference() takes and returns one part's arrays. A program takes and returns all parts, laid end to end along the dimension named above; an argument that names none is the same for every part. Nothing has to cross between parts.
Inputs may be any that keep to these rules, and one draw needn't show every extreme that they name: For the tiles of one device, tile_slot // 8 is the device that owns the tile's brick and tile_slot % 8 the place of that brick in the owner's list for this device; every place up to the largest used one for an owner has a tile, and every device uses all 8 places of some owners.
All inputs are finite; a program needn't handle non-finite values.
Results may differ from the reference program's by a relative error of at most 0.0075.
Values may be sent and summed in bfloat16 or wider, within the bound.
No kernel may reach another device: no remote copies, remote signals or barrier semaphores. Data moves between devices by JAX's collectives and lax.ppermute only.
A program may use at most 192 MiB of HBM per device.

```python
import math
import jax
import jax.numpy as jnp
from jax import lax

NX = 512
NY = 512
TILE = 128
P_SIZE = 8
BLOCKS_DEV = 8
ITERS = 2
COILS = 4
TILE_DEV = 32
TILES = 128
CAP = 8
SLOTS = 32
BRICK_DEV = 512
SAMPLES = 4096
N_PENCIL = 4


def draw_sens_maps(key, part):
    key = jax.random.fold_in(key, 5)
    first_key = jax.random.fold_in(key, 0)
    rows_pos = jnp.arange(NX, dtype=jnp.float32) / NX
    envelope = jnp.exp(math.log(10.0) * rows_pos)[:, None]
    shape_all = (COILS, P_SIZE, 2, NX, NY)
    values = jnp.clip(jax.random.normal(first_key, shape_all, jnp.float32), -4.0, 4.0) * envelope
    scaled = values / (3.0 * math.sqrt(COILS))
    return jnp.clip(scaled, -5.0, 5.0).astype(jnp.bfloat16)


def draw_tile_slot(key, part):
    key = jax.random.fold_in(key, 11)
    count_key, pick_key, order_key = jax.random.split(key, 3)
    peer_ids = jnp.arange(N_PENCIL, dtype=jnp.int32)
    central = (peer_ids >= N_PENCIL // 4) & (peer_ids < N_PENCIL - N_PENCIL // 4)
    mirror = peer_ids[None, :] == (N_PENCIL - 1 - peer_ids)[:, None]
    drawn_used = jax.random.randint(count_key, (N_PENCIL, N_PENCIL), 1, CAP + 1)
    used_slots = jnp.where(central[None, :] | mirror, CAP, drawn_used)
    slot_ids = jnp.arange(SLOTS, dtype=jnp.int32)
    live_slots = (slot_ids % CAP)[None, :] < jnp.repeat(used_slots, CAP, axis=1)
    live_count = jnp.sum(live_slots.astype(jnp.int32), axis=1)
    slot_ranks = jnp.cumsum(live_slots.astype(jnp.int32), axis=1) - 1
    positions = jnp.arange(TILE_DEV, dtype=jnp.int32)
    extra = jax.random.randint(pick_key, (N_PENCIL, TILE_DEV), 0, 1 << 20) % live_count[:, None]
    wanted = jnp.where(positions[None, :] < live_count[:, None], positions[None, :], extra)
    matches = live_slots[:, None, :] & (slot_ranks[:, None, :] == wanted[:, :, None])
    chosen = jnp.sum(jnp.where(matches, slot_ids[None, None, :], 0), axis=-1)
    orders = jax.vmap(lambda row_key: jax.random.permutation(row_key, TILE_DEV))(jax.random.split(order_key, N_PENCIL))
    return jnp.take_along_axis(chosen, orders, axis=1).reshape(-1).astype(jnp.int32)


def touch_ends(drawn, own_key, smallest, high):
    place = [jax.random.randint(jax.random.fold_in(own_key, axis), (), 0, length) for axis, length in enumerate(drawn.shape)]
    widest = drawn.shape.index(max(drawn.shape))
    neighbour = place[:widest] + [(place[widest] + 1) % drawn.shape[widest]] + place[widest + 1:]
    return drawn.at[tuple(place)].set(smallest).at[tuple(neighbour)].set(high)


def shard_levels(rng, extent, cuts, low, high):
    def one(dim, parts):
        heights = jax.random.uniform(jax.random.fold_in(jax.random.fold_in(rng, 6), dim), (parts,), jnp.float32, low / len(cuts), high / len(cuts))
        return jnp.repeat(jnp.exp(heights), extent[dim] // parts).reshape((-1,) + (1,) * (len(extent) - dim - 1))

    level = one(*cuts[0])
    for cut in cuts[1:]:
        level = level * one(*cut)
    return level


def gaussian(rng, dims, width, bound, cuts=(), kind=jnp.bfloat16):
    values = jax.random.normal(rng, dims, jnp.float32) * width
    if len(cuts) > 0:
        values = shard_levels(rng, dims, cuts, -0.22, 0.18) * values
    return jnp.clip(values, min=-bound, max=bound).astype(kind)


def setup_inputs(seed: int = 0, part: int = 0) -> dict:
    arg_keys = jax.random.split(jax.random.key(seed), 7)
    part_splits = jax.random.split(jax.random.fold_in(arg_keys[6], part), 7)
    kspace = gaussian(part_splits[0], (COILS, P_SIZE, 2, SAMPLES), 1.0, 6.0, ((0, 4), (3, 4)))
    sens_maps = draw_sens_maps(jax.random.fold_in(jax.random.fold_in(arg_keys[6], part), 71), part)
    weights = gaussian(arg_keys[2], (TILES, TILE, TILE), (4 * TILE) ** -0.5, 0.25, ((0, 4),))
    tile_slot = draw_tile_slot(jax.random.fold_in(arg_keys[6], 71), part)
    tile_block = touch_ends(jax.random.randint(arg_keys[4], (TILES,), 0, BLOCKS_DEV), jax.random.fold_in(arg_keys[4], 1), 0, BLOCKS_DEV - 1).astype(jnp.int32)
    send_list = touch_ends(jax.random.randint(arg_keys[5], (N_PENCIL, N_PENCIL, CAP), 0, BRICK_DEV), jax.random.fold_in(arg_keys[5], 1), 0, BRICK_DEV - 1).astype(jnp.int32)
    return {"kspace": kspace, "sens_maps": sens_maps, "weights": weights, "tile_slot": tile_slot, "tile_block": tile_block, "send_list": send_list}


damping = 0.5
highest_precision = lax.Precision.HIGHEST


def centred_forward(values):
    shifted = jnp.fft.ifftshift(values, axes=(1, 2))
    return jnp.fft.fftshift(jnp.fft.fft2(shifted, axes=(1, 2), norm="ortho"), axes=(1, 2))


def centred_inverse(values):
    shifted = jnp.fft.ifftshift(values, axes=(1, 2))
    return jnp.fft.fftshift(jnp.fft.ifft2(shifted, axes=(1, 2), norm="ortho"), axes=(1, 2))


def tile_targets(tile_slot, tile_block, send_list):
    tile_ids = jnp.arange(TILES, dtype=jnp.int32)
    holder = tile_ids // TILE_DEV
    source = tile_slot // CAP
    within = tile_slot % CAP
    bricks = source * BRICK_DEV + send_list[source, holder, within]
    blocks = holder * BLOCKS_DEV + tile_block
    return bricks.astype(jnp.int32), blocks.astype(jnp.int32)


def to_kspace(picture, sens_map):
    sensitivity = sens_map[:, 0].astype(jnp.float32) + 1j * sens_map[:, 1].astype(jnp.float32)
    coil_image = sensitivity * (picture[:, 0] + 1j * picture[:, 1])
    spectrum = centred_forward(coil_image)
    k_grid = jnp.stack([jnp.real(spectrum), jnp.imag(spectrum)], 1)
    return jnp.transpose(k_grid, (0, 1, 3, 2))


def to_image(k_grid, sens_map):
    spectrum = jnp.transpose(k_grid[:, 0] + 1j * k_grid[:, 1], (0, 2, 1))
    coil_image = centred_inverse(spectrum)
    sensitivity = sens_map[:, 0].astype(jnp.float32) + 1j * sens_map[:, 1].astype(jnp.float32)
    combined = jnp.conj(sensitivity) * coil_image
    return jnp.stack([jnp.real(combined), jnp.imag(combined)], 1)


def sample_grid(k_grid, weights_float, bricks, blocks):
    rounded = lax.optimization_barrier(k_grid.astype(jnp.bfloat16)).astype(jnp.float32)
    rounded = rounded.reshape(2 * P_SIZE, NY * NX // TILE, TILE)
    selected_entries = jnp.take(rounded, bricks, axis=1)
    operator_product = jnp.einsum("gem,emk->egk", selected_entries, weights_float, precision=highest_precision)
    summed = jax.ops.segment_sum(operator_product, blocks, num_segments=N_PENCIL * BLOCKS_DEV)
    return lax.optimization_barrier(summed.astype(jnp.bfloat16))


def spread_samples(samples, weights_float, bricks, blocks):
    selected_entries = jnp.take(samples.astype(jnp.float32), blocks, axis=0)
    spread_onto_grid = jnp.einsum("oeu,oku->oek", selected_entries, weights_float, precision=highest_precision)
    summed = jax.ops.segment_sum(spread_onto_grid, bricks, num_segments=NY * NX // TILE)
    return jnp.transpose(summed, (1, 0, 2)).reshape(P_SIZE, 2, NY, NX)


def reference(kspace, sens_maps, weights, tile_slot, tile_block, send_list):
    bricks, blocks = tile_targets(tile_slot, tile_block, send_list)
    weights_float = weights.astype(jnp.float32)

    def normal(direction):
        summed_image = damping * direction
        for coil_index in range(COILS):
            k_grid = to_kspace(direction, sens_maps[coil_index])
            samples = sample_grid(k_grid, weights_float, bricks, blocks)
            spread_onto_grid = spread_samples(samples, weights_float, bricks, blocks)
            summed_image = summed_image + to_image(spread_onto_grid, sens_maps[coil_index])
        return summed_image

    right_side = jnp.zeros((P_SIZE, 2, NX, NY), jnp.float32)
    for coil_index in range(COILS):
        measured = jnp.transpose(kspace[coil_index].reshape(2 * P_SIZE, N_PENCIL * BLOCKS_DEV, TILE), (1, 0, 2))
        spread_onto_grid = spread_samples(measured, weights_float, bricks, blocks)
        right_side = right_side + to_image(spread_onto_grid, sens_maps[coil_index])

    solution = jnp.zeros_like(right_side)
    residual = right_side
    direction = right_side
    norm_now = jnp.sum(residual * residual)
    for step_index in range(ITERS):
        applied = normal(direction)
        step_size = norm_now / jnp.sum(direction * applied)
        solution = solution + step_size * direction
        residual = residual - step_size * applied
        norm_next = jnp.sum(residual * residual)
        direction = residual + (norm_next / norm_now) * direction
        norm_now = norm_next
    return solution, residual
```

```python
import math

import jax
import jax.numpy as jnp
from jax import lax
from jax.sharding import PartitionSpec as P

ITERS = 2


damping = 0.5
pass_precision = lax.Precision.HIGH


def wave(left, right, length):
    phases = left[:, None] * right[None, :] % length
    angles = phases.astype(jnp.float32) * (2.0 * math.pi / length)
    return jnp.cos(angles) / math.sqrt(length), jnp.sin(angles) / math.sqrt(length)


def einsum(form, left, right):
    return jnp.einsum(form, left, right, precision=pass_precision)


def on_device(kspace, sens_maps, weights, tile_slot, tile_block, send_list):
    coil_count = lax.axis_size("coil")
    peers = lax.axis_size("pencil")
    planes = sens_maps.shape[1]
    own_planes = planes // coil_count
    rows = sens_maps.shape[3]
    columns = sens_maps.shape[4]
    rows_total = rows * peers
    tile_size = weights.shape[1]
    tile_count = tile_slot.shape[0]
    tiles = tile_count * peers
    blocks_dev = kspace.shape[3] // tile_size
    blocks = blocks_dev * peers
    cap = send_list.shape[2]
    runs = rows_total // tile_size
    brick_dev = columns // peers * runs

    packed = jnp.concatenate([tile_slot, tile_block, send_list.reshape(-1)])
    places = lax.all_gather(packed, "pencil")
    slots = places[:, :tile_count]
    block_of = (
        places[:, tile_count : 2 * tile_count]
        + blocks_dev * jnp.arange(peers, dtype=jnp.int32)[:, None]
    ).reshape(-1)
    lists = places[:, 2 * tile_count :].reshape(peers, peers, cap)
    owner = slots // cap
    holder = jnp.arange(peers, dtype=jnp.int32)[:, None]
    brick = (owner * brick_dev + lists[owner, holder, slots % cap]).reshape(-1)
    line = brick // runs
    run = brick % runs

    sens = lax.all_to_all(sens_maps[0], "coil", split_axis=0, concat_axis=0, tiled=True)
    sens = sens.reshape(coil_count, own_planes, 2, rows, columns)
    measured = lax.all_to_all(kspace[0], "coil", split_axis=0, concat_axis=0, tiled=True)
    measured = lax.all_gather(
        measured.reshape(coil_count, own_planes, 2, blocks_dev, tile_size),
        "pencil",
        axis=3,
        tiled=True,
    )
    all_weights = lax.all_gather(weights, "pencil", axis=0, tiled=True)

    cos_y, sin_y = wave(
        line - columns // 2, jnp.arange(columns, dtype=jnp.int32) - columns // 2, columns
    )
    row_ids = jnp.arange(rows, dtype=jnp.int32) + lax.axis_index("pencil") * rows - rows_total // 2
    cos_x, sin_x = wave(
        row_ids, jnp.arange(tile_size, dtype=jnp.int32) - rows_total // 2, rows_total
    )
    fine = run[:, None] * row_ids[None, :] * tile_size % rows_total
    angles = fine.astype(jnp.float32) * (2.0 * math.pi / rows_total)
    turn_cos, turn_sin = jnp.cos(angles), jnp.sin(angles)
    block_map = (block_of[:, None] == jnp.arange(blocks, dtype=jnp.int32)[None, :]).astype(
        jnp.bfloat16
    )
    sens_real = sens[:, :, 0].astype(jnp.float32)
    sens_imag = sens[:, :, 1].astype(jnp.float32)

    def forward(picture):
        coil_real = sens_real * picture[None, :, 0] - sens_imag * picture[None, :, 1]
        coil_imag = sens_real * picture[None, :, 1] + sens_imag * picture[None, :, 0]
        half_real = einsum("ty,cpxy->tcpx", cos_y, coil_real) + einsum(
            "ty,cpxy->tcpx", sin_y, coil_imag
        )
        half_imag = einsum("ty,cpxy->tcpx", cos_y, coil_imag) - einsum(
            "ty,cpxy->tcpx", sin_y, coil_real
        )
        tc, ts = turn_cos[:, None, None], turn_sin[:, None, None]
        turned_real = half_real * tc + half_imag * ts
        turned_imag = half_imag * tc - half_real * ts
        grid_real = einsum("tcpx,xi->tcpi", turned_real, cos_x) + einsum(
            "tcpx,xi->tcpi", turned_imag, sin_x
        )
        grid_imag = einsum("tcpx,xi->tcpi", turned_imag, cos_x) - einsum(
            "tcpx,xi->tcpi", turned_real, sin_x
        )
        grid = jnp.stack([grid_real, grid_imag], 3).astype(jnp.bfloat16)
        product = jnp.einsum(
            "tcpqi,tis->tcpqs", grid, all_weights, preferred_element_type=jnp.float32
        )
        partial = einsum("tb,tcpqs->cpqbs", block_map.astype(jnp.float32), product)
        return lax.psum(partial, "pencil").astype(jnp.bfloat16)

    def adjoint(samples):
        selected = jnp.einsum("tb,cpqbs->tcpqs", block_map, samples).astype(jnp.bfloat16)
        spread = jnp.einsum(
            "tcpqs,tis->tcpqi", selected, all_weights, preferred_element_type=jnp.float32
        )
        back_real = einsum("tcpi,xi->tcpx", spread[:, :, :, 0], cos_x) - einsum(
            "tcpi,xi->tcpx", spread[:, :, :, 1], sin_x
        )
        back_imag = einsum("tcpi,xi->tcpx", spread[:, :, :, 1], cos_x) + einsum(
            "tcpi,xi->tcpx", spread[:, :, :, 0], sin_x
        )
        tc, ts = turn_cos[:, None, None], turn_sin[:, None, None]
        turned_real = back_real * tc - back_imag * ts
        turned_imag = back_imag * tc + back_real * ts
        image_real = einsum("tcpx,ty->cpxy", turned_real, cos_y) - einsum(
            "tcpx,ty->cpxy", turned_imag, sin_y
        )
        image_imag = einsum("tcpx,ty->cpxy", turned_imag, cos_y) + einsum(
            "tcpx,ty->cpxy", turned_real, sin_y
        )
        return jnp.stack(
            [
                jnp.sum(sens_real * image_real + sens_imag * image_imag, 0),
                jnp.sum(sens_real * image_imag - sens_imag * image_real, 0),
            ],
            1,
        )

    def total(value):
        return lax.psum(value, ("coil", "pencil"))

    right_side = adjoint(measured)
    picture = jnp.zeros_like(right_side)
    residual = right_side
    direction = right_side
    norm_now = total(jnp.sum(residual * residual))
    for _ in range(ITERS):
        applied = adjoint(forward(direction)) + damping * direction
        step_size = norm_now / total(jnp.sum(direction * applied))
        picture = picture + step_size * direction
        residual = residual - step_size * applied
        norm_next = total(jnp.sum(residual * residual))
        direction = residual + norm_next / norm_now * direction
        norm_now = norm_next

    def to_all(own):
        return lax.all_gather(own.astype(jnp.bfloat16), "coil", axis=0, tiled=True).astype(
            jnp.float32
        )

    return to_all(picture), to_all(residual)


def solution(mesh):
    in_specs = (
        P("coil", "scan", None, "pencil"),
        P("coil", "scan", None, "pencil", None),
        P("pencil", None, None),
        P("pencil"),
        P("pencil"),
        P("pencil", None, None),
    )
    out_specs = (P("scan", None, "pencil", None), P("scan", None, "pencil", None))
    return jax.shard_map(
        on_device, mesh=mesh, in_specs=in_specs, out_specs=out_specs, check_vma=False
    )
```

```python
import functools
import math

import jax
import jax.numpy as jnp
from jax import lax
from jax.experimental import pallas as pl
from jax.experimental.pallas import tpu as pltpu
from jax.sharding import PartitionSpec as P


damping = 0.5
f32, bf16 = jnp.float32, jnp.bfloat16
vmem_limit = 56 * 1024 * 1024


def wave(left, right, length):
    phases = left[:, None] * right[None, :] % length
    angles = phases.astype(f32) * (2.0 * math.pi / length)
    return jnp.cos(angles) / math.sqrt(length), jnp.sin(angles) / math.sqrt(length)


def quarter_turns(left, right, count):
    turns = left[:, None] * right[None, :] % count
    if count == 4:
        cosine = jnp.where(turns == 0, 1.0, 0.0) - jnp.where(turns == 2, 1.0, 0.0)
        sine = jnp.where(turns == 1, 1.0, 0.0) - jnp.where(turns == 3, 1.0, 0.0)
        return cosine.astype(f32), sine.astype(f32)
    angles = turns.astype(f32) * (2.0 * math.pi / count)
    return jnp.cos(angles), jnp.sin(angles)


def split(value):
    high = value.astype(bf16)
    return high, (value - high.astype(f32)).astype(bf16)


def split_table(table):
    high = lax.reduce_precision(table, 8, 7)
    return high.astype(bf16), (table - high).astype(bf16)


def nt(left, right):
    return lax.dot_general(left, right, (((1,), (1,)), ((), ())), preferred_element_type=f32)


def nn(left, right):
    return jnp.dot(left, right, preferred_element_type=f32)


def three(product, left, right):
    return (
        product(left[0], right[0]) + product(left[0], right[1]) + product(left[1], right[0])
    )


def tree_sum(values):
    while len(values) > 1:
        values = [left + right for left, right in zip(values[::2], values[1::2])]
    return values[0]


def forward_image(step, real, imag, sens_ref, ey, mx, turn_ref, grid_ref):
    tiles = turn_ref.shape[1]
    rows = turn_ref.shape[2]
    channels = grid_ref.shape[0] // tiles
    sens_real = sens_ref[0].astype(f32)
    sens_imag = sens_ref[1].astype(f32)
    coil = jnp.concatenate(
        [sens_real * real - sens_imag * imag, sens_real * imag + sens_imag * real], 0
    )
    both = three(nt, (ey[0][...], ey[1][...]), split(coil))
    half_real = both[:tiles, :rows] + both[tiles:, rows:]
    half_imag = both[:tiles, rows:] - both[tiles:, :rows]
    turned = jnp.concatenate(
        [
            half_real * turn_ref[0] + half_imag * turn_ref[1],
            half_imag * turn_ref[0] - half_real * turn_ref[1],
        ],
        1,
    )
    grid = three(nn, split(turned), (mx[0][...], mx[1][...]))
    size = grid.shape[1] // 2
    grid_ref[pl.ds(2 * step, tiles, stride=channels), :] = grid[:, :size]
    grid_ref[pl.ds(2 * step + 1, tiles, stride=channels), :] = grid[:, size:]


def sample_tiles(block_ref, weights_ref, grid_ref, sums_ref, out_ref):
    tiles = weights_ref.shape[0]
    channels = grid_ref.shape[0] // tiles
    sums_ref[...] = jnp.zeros_like(sums_ref)

    def one(tile, carry):
        start = pl.multiple_of(tile * channels, channels)
        high, low = split(grid_ref[pl.ds(start, channels), :])
        product = nn(jnp.concatenate([high, low], 0), weights_ref[tile])
        sums_ref[block_ref[tile]] += product[:channels] + product[channels:]
        return carry

    lax.fori_loop(0, tiles, one, 0, unroll=8)
    out_ref[...] = sums_ref[...].astype(bf16)


def spread_tiles(block_ref, weights_ref, parts_ref, grid_ref):
    tiles = weights_ref.shape[0]
    channels = grid_ref.shape[0] // tiles

    def one(tile, carry):
        start = pl.multiple_of(tile * channels, channels)
        product = nt(parts_ref[block_ref[tile]], weights_ref[tile])
        if product.shape[0] > channels:
            product = product[:channels] + product[channels:]
        grid_ref[pl.ds(start, channels), :] = product
        return carry

    lax.fori_loop(0, tiles, one, 0, unroll=8)


def adjoint_image(step, tiles, ey_back, mx, turn_ref, grid_ref):
    channels = grid_ref.shape[0] // tiles
    rows = turn_ref.shape[1]
    grid = jnp.concatenate(
        [
            grid_ref[pl.ds(2 * step, tiles, stride=channels), :],
            grid_ref[pl.ds(2 * step + 1, tiles, stride=channels), :],
        ],
        1,
    )
    back = three(nt, (mx[0][...], mx[1][...]), split(grid))
    turned = jnp.concatenate(
        [
            back[:rows] * turn_ref[0] - back[rows:] * turn_ref[1],
            back[rows:] * turn_ref[0] + back[:rows] * turn_ref[1],
        ],
        1,
    )
    image = three(nn, split(turned), (ey_back[0][...], ey_back[1][...]))
    columns = image.shape[1] // 2
    return image[:, :columns], image[:, columns:]


def add_dots(dots_ref, products):
    rows = lax.broadcasted_iota(jnp.int32, dots_ref.shape, 0)
    total = dots_ref[...]
    for place, (left, right) in enumerate(products):
        total += jnp.where(rows == place, jnp.sum(left * right), 0.0)
    dots_ref[...] = total


def measured_kernel(block, samples, weights, mx0, mx1, eb0, eb1, turn, images, grid):
    step = pl.program_id(0)

    @pl.when(step == 0)
    def _():
        spread_tiles(block, weights, samples, grid)

    real, imag = adjoint_image(step, weights.shape[0], (eb0, eb1), (mx0, mx1), turn, grid)
    images[0, 0] = real
    images[0, 1] = imag


def start_kernel(
    block,
    images,
    sens,
    weights,
    ey0,
    ey1,
    mx0,
    mx1,
    turn,
    right_side,
    samples,
    rounded,
    dots,
    grid,
    sums,
):
    plane, coil = pl.program_id(0), pl.program_id(1)
    coils = pl.num_programs(1)

    @pl.when(coil == 0)
    def _():
        total_real = jnp.zeros(right_side.shape[2:], f32)
        total_imag = jnp.zeros(right_side.shape[2:], f32)
        for other in range(images.shape[0]):
            sens_real = sens[other, 0, 0].astype(f32)
            sens_imag = sens[other, 0, 1].astype(f32)
            total_real += sens_real * images[other, 0, 0] + sens_imag * images[other, 0, 1]
            total_imag += sens_real * images[other, 0, 1] - sens_imag * images[other, 0, 0]
        right_side[0, 0] = total_real
        right_side[0, 1] = total_imag
        rounded[0, 0] = total_real.astype(bf16)
        rounded[0, 1] = total_imag.astype(bf16)

        @pl.when(plane == 0)
        def _():
            dots[...] = jnp.zeros_like(dots)

        add_dots(dots, [(right_side[0], right_side[0])])

    forward_image(
        coil * pl.num_programs(0) + plane,
        right_side[0, 0],
        right_side[0, 1],
        sens.at[coil, 0],
        (ey0, ey1),
        (mx0, mx1),
        turn,
        grid,
    )

    @pl.when((plane == pl.num_programs(0) - 1) & (coil == coils - 1))
    def _():
        sample_tiles(block, weights, grid, sums, samples)


def forward_kernel(
    block,
    totals,
    right_side,
    applied,
    sens,
    weights,
    ey0,
    ey1,
    mx0,
    mx1,
    turn,
    residual,
    samples,
    rounded,
    grid,
    sums,
):
    plane, coil = pl.program_id(0), pl.program_id(1)

    @pl.when(coil == 0)
    def _():
        scale = first_step_of(totals).reshape(1, 1, 1)
        value = right_side[0] - scale * applied[0]
        residual[0] = value
        rounded[0] = value.astype(bf16)

    forward_image(
        coil * pl.num_programs(0) + plane,
        residual[0, 0],
        residual[0, 1],
        sens.at[0, 0],
        (ey0, ey1),
        (mx0, mx1),
        turn,
        grid,
    )

    @pl.when((plane == pl.num_programs(0) - 1) & (coil == pl.num_programs(1) - 1))
    def _():
        sample_tiles(block, weights, grid, sums, samples)


def first_step_of(totals):
    return totals[0:1, 0:1] / (totals[1:2, 0:1] + damping * totals[0:1, 0:1])


def combine(coil, image, sens, out):
    sens_real = sens[0, 0, 0].astype(f32)
    sens_imag = sens[0, 0, 1].astype(f32)
    real = sens_real * image[0] + sens_imag * image[1]
    imag = sens_real * image[1] - sens_imag * image[0]

    @pl.when(coil == 0)
    def _():
        out[0, 0] = real
        out[0, 1] = imag

    @pl.when(coil > 0)
    def _():
        out[0, 0] += real
        out[0, 1] += imag


def first_kernel(peers, block, *refs):
    samples = refs[:peers]
    right_side, sens, weights, mx0, mx1, eb0, eb1, turn, applied, grid, parts = refs[peers:]
    plane, coil = pl.program_id(0), pl.program_id(1)

    @pl.when((plane == 0) & (coil == 0))
    def _():
        summed = tree_sum([part[...].astype(f32) for part in samples])
        channels = summed.shape[1]
        high, low = split(summed)
        parts[:, :channels] = high
        parts[:, channels:] = low
        spread_tiles(block, weights, parts, grid)

    image = adjoint_image(
        coil * pl.num_programs(0) + plane, weights.shape[0], (eb0, eb1), (mx0, mx1), turn, grid
    )
    combine(coil, image, sens, applied)

    @pl.when(coil == pl.num_programs(1) - 1)
    def _():
        applied[...] += damping * right_side[...]


def second_kernel(peers, block, *refs):
    samples = refs[:peers]
    (
        totals,
        right_side,
        first_applied,
        residual,
        sens,
        weights,
        mx0,
        mx1,
        eb0,
        eb1,
        turn,
        rounded,
        dots,
        grid,
        parts,
        applied,
    ) = refs[peers:]
    plane, coil = pl.program_id(0), pl.program_id(1)

    @pl.when((plane == 0) & (coil == 0))
    def _():
        summed = tree_sum([part[...].astype(f32) for part in samples])
        channels = summed.shape[1]
        high, low = split(summed)
        parts[:, :channels] = high
        parts[:, channels:] = low
        dots[...] = jnp.zeros_like(dots)
        spread_tiles(block, weights, parts, grid)

    image = adjoint_image(
        coil * pl.num_programs(0) + plane, weights.shape[0], (eb0, eb1), (mx0, mx1), turn, grid
    )
    combine(coil, image, sens, applied)

    @pl.when(coil == pl.num_programs(1) - 1)
    def _():
        vector = residual[0]
        again = applied[0] + damping * vector
        rounded[0] = (vector - first_step_of(totals).reshape(1, 1, 1) * again).astype(bf16)
        add_dots(
            dots,
            [
                (vector, vector),
                (vector, again),
                (vector, first_applied[0]),
                (right_side[0], again),
            ],
        )


def whole_block(array):
    rank = len(array.shape)
    return pl.BlockSpec(array.shape, lambda *_: (0,) * rank)


def on_device(kspace, sens_maps, weights, tile_slot, tile_block, send_list):
    coil_count = lax.axis_size("coil")
    peers = lax.axis_size("pencil")
    planes = sens_maps.shape[1]
    own_planes = planes // coil_count
    rows = sens_maps.shape[3]
    columns = sens_maps.shape[4]
    rows_total = rows * peers
    size = weights.shape[1]
    tile_count = tile_slot.shape[0]
    tiles = tile_count * peers
    blocks_dev = kspace.shape[3] // size
    blocks = blocks_dev * peers
    cap = send_list.shape[2]
    runs = rows_total // size
    brick_dev = columns // peers * runs
    images_count = coil_count * own_planes
    channels = 2 * images_count

    sens = lax.all_to_all(sens_maps[0], "coil", split_axis=0, concat_axis=0, tiled=True)
    sens = sens.reshape(coil_count, own_planes, 2, rows, columns)

    packed = jnp.concatenate([tile_slot, tile_block, send_list.reshape(-1)])
    places = lax.all_gather(packed, "pencil")
    slots = places[:, :tile_count]
    block_of = (
        places[:, tile_count : 2 * tile_count]
        + blocks_dev * jnp.arange(peers, dtype=jnp.int32)[:, None]
    ).reshape(-1)
    lists = places[:, 2 * tile_count :].reshape(peers, peers, cap)
    holder = jnp.arange(peers, dtype=jnp.int32)[:, None]
    brick = (slots // cap * brick_dev + lists[slots // cap, holder, slots % cap]).reshape(-1)
    line = brick // runs
    run = brick % runs

    measured = lax.all_to_all(kspace[0], "coil", split_axis=0, concat_axis=0, tiled=True)
    measured = lax.all_gather(
        measured.reshape(channels, blocks_dev, size), "pencil", axis=1, tiled=True
    )
    measured = jnp.swapaxes(measured, 0, 1)
    all_weights = lax.all_gather(weights, "pencil", axis=0, tiled=True)

    cos_y, sin_y = wave(
        line - columns // 2, jnp.arange(columns, dtype=jnp.int32) - columns // 2, columns
    )
    row_ids = jnp.arange(rows, dtype=jnp.int32) + lax.axis_index("pencil") * rows - rows_total // 2
    cos_x, sin_x = wave(
        row_ids, jnp.arange(size, dtype=jnp.int32) - rows_total // 2, rows_total
    )
    turn = jnp.stack(quarter_turns(run, row_ids, runs))
    turn_back = jnp.stack(quarter_turns(row_ids, run, runs))

    def exchanged(partial, axis="pencil"):
        count = lax.axis_size(axis)
        return [partial] + [
            lax.ppermute(partial, axis, [(i, i ^ k) for i in range(count)])
            for k in range(1, count)
        ]

    def summed_over(axes, dots):
        for axis in axes:
            dots = tree_sum(exchanged(dots, axis))
        return dots

    def added(samples):
        return tree_sum([part.astype(f32) for part in samples])

    def gathered(own):
        return lax.all_gather(own, "coil", axis=0, tiled=True)

    picture_shape = (own_planes, 2, rows, columns)

    if rows % 128 == 0 and columns % 128 == 0 and size % 128 == 0 and channels % 16 == 0:
        ey = split_table(jnp.concatenate([cos_y, sin_y], 0))
        eb = split_table(
            jnp.concatenate(
                [jnp.concatenate([cos_y, sin_y], 1), jnp.concatenate([-sin_y, cos_y], 1)], 0
            )
        )
        mx = split_table(
            jnp.concatenate(
                [jnp.concatenate([cos_x, -sin_x], 1), jnp.concatenate([sin_x, cos_x], 1)], 0
            )
        )
        places_spec = pl.BlockSpec(memory_space=pltpu.SMEM)
        plane_spec = pl.BlockSpec((1, 2, rows, columns), lambda p, c: (p, 0, 0, 0))
        sens_spec = pl.BlockSpec((1, 1, 2, rows, columns), lambda p, c: (c, p, 0, 0, 0))
        grid_scratch = pltpu.VMEM((tiles * channels, size), f32)
        sums_shape = (blocks, channels, size)
        params = pltpu.CompilerParams(vmem_limit_bytes=vmem_limit)

        def call(kernel, grid, inputs, specs, outs, out_specs, scratch, flops):
            read = sum(math.prod(i.shape) * i.dtype.itemsize for i in inputs)
            return pl.pallas_call(
                kernel,
                grid=grid,
                in_specs=specs,
                out_specs=out_specs,
                out_shape=outs,
                scratch_shapes=scratch,
                compiler_params=params,
                cost_estimate=pl.CostEstimate(
                    flops=flops, bytes_accessed=read, transcendentals=0
                ),
            )(*inputs)

        def shaped(shape, dtype=f32):
            return jax.ShapeDtypeStruct(shape, dtype)

        image_flops = 3 * images_count * 8 * tiles * rows * (columns + size)
        tile_flops = 4 * tiles * channels * size * size
        grid = (own_planes, coil_count)

        def measured_images():
            inputs = [block_of, measured, all_weights, *mx, *eb, turn_back]
            return call(
                measured_kernel,
                (images_count,),
                inputs,
                [places_spec] + [whole_block(i) for i in inputs[1:]],
                shaped((images_count, 2, rows, columns)),
                pl.BlockSpec((1, 2, rows, columns), lambda i: (i, 0, 0, 0)),
                [grid_scratch],
                image_flops + tile_flops,
            )

        def start(images):
            images = images.reshape(coil_count, own_planes, 2, rows, columns)
            inputs = [block_of, images, sens, all_weights, *ey, *mx, turn]
            all_coils = pl.BlockSpec(
                (coil_count, 1, 2, rows, columns), lambda p, c: (0, p, 0, 0, 0)
            )
            return call(
                start_kernel,
                grid,
                inputs,
                [places_spec, all_coils, all_coils] + [whole_block(i) for i in inputs[3:]],
                [
                    shaped(picture_shape),
                    shaped(sums_shape, bf16),
                    shaped(picture_shape, bf16),
                    shaped((8, 128)),
                ],
                [
                    plane_spec,
                    whole_block(shaped(sums_shape)),
                    plane_spec,
                    whole_block(shaped((8, 128))),
                ],
                [grid_scratch, pltpu.VMEM(sums_shape, f32)],
                image_flops + tile_flops,
            )

        def forward(totals, right_side, applied):
            tail = [all_weights, *ey, *mx, turn]
            inputs = [block_of, totals, right_side, applied, sens, *tail]
            return call(
                forward_kernel,
                grid,
                inputs,
                [places_spec, whole_block(totals), plane_spec, plane_spec, sens_spec]
                + [whole_block(i) for i in tail],
                [shaped(picture_shape), shaped(sums_shape, bf16), shaped(picture_shape, bf16)],
                [plane_spec, whole_block(shaped(sums_shape)), plane_spec],
                [grid_scratch, pltpu.VMEM(sums_shape, f32)],
                image_flops + tile_flops,
            )

        parts_scratch = pltpu.VMEM((blocks, 2 * channels, size), bf16)

        def first(samples, right_side):
            tail = [all_weights, *mx, *eb, turn_back]
            inputs = [block_of, *samples, right_side, sens, *tail]
            return call(
                functools.partial(first_kernel, peers),
                grid,
                inputs,
                [places_spec]
                + [whole_block(i) for i in samples]
                + [plane_spec, sens_spec]
                + [whole_block(i) for i in tail],
                shaped(picture_shape),
                plane_spec,
                [grid_scratch, parts_scratch],
                image_flops + tile_flops,
            )

        def second(samples, totals, right_side, applied, residual):
            tail = [all_weights, *mx, *eb, turn_back]
            inputs = [
                block_of,
                *samples,
                totals,
                right_side,
                applied,
                residual,
                sens,
                *tail,
            ]
            return call(
                functools.partial(second_kernel, peers),
                grid,
                inputs,
                [places_spec]
                + [whole_block(i) for i in samples]
                + [whole_block(totals), plane_spec, plane_spec, plane_spec, sens_spec]
                + [whole_block(i) for i in tail],
                [shaped(picture_shape, bf16), shaped((8, 128))],
                [plane_spec, whole_block(shaped((8, 128)))],
                [grid_scratch, parts_scratch, pltpu.VMEM((1, 2, rows, columns), f32)],
                image_flops + tile_flops,
            )

    else:
        ein = functools.partial(jnp.einsum, precision=lax.Precision.HIGH)
        map_real = sens[:, :, 0].astype(f32)
        map_imag = sens[:, :, 1].astype(f32)
        shape = (coil_count, own_planes)
        block_map = (block_of[:, None] == jnp.arange(blocks, dtype=jnp.int32)).astype(f32)
        tc, ts = turn[0][:, None, None], turn[1][:, None, None]
        wide_weights = all_weights.astype(f32)

        def sampled(picture):
            coil_real = map_real * picture[None, :, 0] - map_imag * picture[None, :, 1]
            coil_imag = map_real * picture[None, :, 1] + map_imag * picture[None, :, 0]
            half_real = ein("ty,cpxy->tcpx", cos_y, coil_real) + ein(
                "ty,cpxy->tcpx", sin_y, coil_imag
            )
            half_imag = ein("ty,cpxy->tcpx", cos_y, coil_imag) - ein(
                "ty,cpxy->tcpx", sin_y, coil_real
            )
            real = half_real * tc + half_imag * ts
            imag = half_imag * tc - half_real * ts
            grid = jnp.stack(
                [
                    ein("tcpx,xi->tcpi", real, cos_x) + ein("tcpx,xi->tcpi", imag, sin_x),
                    ein("tcpx,xi->tcpi", imag, cos_x) - ein("tcpx,xi->tcpi", real, sin_x),
                ],
                3,
            ).reshape(tiles, channels, size)
            product = ein("tgi,tis->tgs", grid, wide_weights)
            return ein("tb,tgs->bgs", block_map, product).astype(bf16)

        def images_of(samples):
            spread = ein("tgs,tis->tgi", jnp.take(samples, block_of, axis=0), wide_weights)
            spread = spread.reshape(tiles, *shape, 2, size)
            back_real = ein("tcpi,xi->tcpx", spread[:, :, :, 0], cos_x) - ein(
                "tcpi,xi->tcpx", spread[:, :, :, 1], sin_x
            )
            back_imag = ein("tcpi,xi->tcpx", spread[:, :, :, 1], cos_x) + ein(
                "tcpi,xi->tcpx", spread[:, :, :, 0], sin_x
            )
            real = back_real * tc - back_imag * ts
            imag = back_imag * tc + back_real * ts
            return (
                ein("tcpx,ty->cpxy", real, cos_y) - ein("tcpx,ty->cpxy", imag, sin_y),
                ein("tcpx,ty->cpxy", imag, cos_y) + ein("tcpx,ty->cpxy", real, sin_y),
            )

        def combined(images):
            real, imag = images
            return jnp.stack(
                [
                    jnp.sum(map_real * real + map_imag * imag, 0),
                    jnp.sum(map_real * imag - map_imag * real, 0),
                ],
                1,
            )

        def stacked_dots(products):
            values = [jnp.sum(left * right) for left, right in products]
            values += [jnp.zeros((), f32)] * (8 - len(values))
            return jnp.broadcast_to(jnp.stack(values)[:, None], (8, 128))

        def measured_images():
            return images_of(measured.astype(f32))

        def start(images):
            right_side = combined(images)
            dots = stacked_dots([(right_side, right_side)])
            return right_side, sampled(right_side), right_side.astype(bf16), dots

        def forward(totals, right_side, applied):
            scale = totals[0, 0] / (totals[1, 0] + damping * totals[0, 0])
            residual = right_side - scale * applied
            return residual, sampled(residual), residual.astype(bf16)

        def first(samples, right_side):
            return combined(images_of(added(samples))) + damping * right_side

        def second(samples, totals, right_side, applied, residual):
            scale = totals[0, 0] / (totals[1, 0] + damping * totals[0, 0])
            again = combined(images_of(added(samples))) + damping * residual
            dots = stacked_dots(
                [
                    (residual, residual),
                    (residual, again),
                    (residual, applied),
                    (right_side, again),
                ]
            )
            return (residual - scale * again).astype(bf16), dots

    right_side, start_samples, start_rounded, dots = start(measured_images())
    start_everywhere = gathered(start_rounded)
    samples = exchanged(start_samples)
    dots = summed_over(["pencil"], dots)
    energy = jnp.sum(jnp.square(added(samples)))
    place = lax.broadcasted_iota(jnp.int32, dots.shape, 0)
    first_totals = summed_over(["coil"], jnp.where(place == 1, energy, dots))
    applied = first(samples, right_side)
    residual, samples, residual_rounded = forward(first_totals, right_side, applied)
    residual_everywhere = gathered(residual_rounded)
    mixed_rounded, dots = second(
        exchanged(samples), first_totals, right_side, applied, residual
    )
    mixed_everywhere = gathered(mixed_rounded)
    totals = summed_over(["coil", "pencil"], dots)
    start_norm = first_totals[0, 0]
    start_curve = first_totals[1, 0] + damping * start_norm
    first_step = start_norm / start_curve
    ratio = totals[0, 0] / start_norm
    curve = totals[1, 0] + ratio * (totals[2, 0] + totals[3, 0]) + ratio * ratio * start_curve
    second_step = totals[0, 0] / curve
    start_all = start_everywhere.astype(f32)
    residual_all = residual_everywhere.astype(f32)
    mixed_all = mixed_everywhere.astype(f32)
    picture = (first_step + second_step * ratio) * start_all + second_step * residual_all
    share = second_step / first_step
    residual = (
        (1.0 - share + share * ratio) * residual_all
        + share * mixed_all
        - share * ratio * start_all
    )
    return picture, residual


def solution(mesh):
    in_specs = (
        P("coil", "scan", None, "pencil"),
        P("coil", "scan", None, "pencil", None),
        P("pencil", None, None),
        P("pencil"),
        P("pencil"),
        P("pencil", None, None),
    )
    out_specs = (P("scan", None, "pencil", None), P("scan", None, "pencil", None))
    return jax.shard_map(
        on_device, mesh=mesh, in_specs=in_specs, out_specs=out_specs, check_vma=False
    )
```

```python
import functools
import math

import jax
import jax.numpy as jnp
from jax import lax
from jax.experimental import pallas as pl
from jax.experimental.pallas import tpu as pltpu
from jax.sharding import PartitionSpec as P


damping = 0.5
f32, bf16 = jnp.float32, jnp.bfloat16
vmem_limit = 56 * 1024 * 1024


def wave(left, right, length):
    phases = left[:, None] * right[None, :] % length
    angles = phases.astype(f32) * (2.0 * math.pi / length)
    return jnp.cos(angles) / math.sqrt(length), jnp.sin(angles) / math.sqrt(length)


def quarter_turns(left, right, count):
    turns = left[:, None] * right[None, :] % count
    if count == 4:
        cosine = jnp.where(turns == 0, 1.0, 0.0) - jnp.where(turns == 2, 1.0, 0.0)
        sine = jnp.where(turns == 1, 1.0, 0.0) - jnp.where(turns == 3, 1.0, 0.0)
        return cosine.astype(f32), sine.astype(f32)
    angles = turns.astype(f32) * (2.0 * math.pi / count)
    return jnp.cos(angles), jnp.sin(angles)


def split(value):
    high = value.astype(bf16)
    return high, (value - high.astype(f32)).astype(bf16)


def table_parts(table, axis):
    high = lax.reduce_precision(table, 8, 7)
    low = (table - high).astype(bf16)
    high = high.astype(bf16)
    return jnp.concatenate([high, high, low], axis)


def data_parts(value):
    high, low = split(value)
    return jnp.concatenate([high, low, high], 1)


def nt(left, right):
    return lax.dot_general(left, right, (((1,), (1,)), ((), ())), preferred_element_type=f32)


def nn(left, right):
    return jnp.dot(left, right, preferred_element_type=f32)


def tree_sum(values):
    while len(values) > 1:
        values = [left + right for left, right in zip(values[::2], values[1::2])]
    return values[0]


def forward_image(step, real, imag, sens_ref, ey, mx, turn_ref, grid_ref):
    tiles = turn_ref.shape[1]
    rows = turn_ref.shape[2]
    channels = grid_ref.shape[0] // tiles
    sens_real = sens_ref[0, 0].astype(f32)
    sens_imag = sens_ref[0, 1].astype(f32)
    coil = jnp.concatenate(
        [sens_real * real - sens_imag * imag, sens_real * imag + sens_imag * real], 0
    )
    both = nt(ey[...], data_parts(coil))
    half_real = both[:tiles, :rows] + both[tiles:, rows:]
    half_imag = both[:tiles, rows:] - both[tiles:, :rows]
    turned = jnp.concatenate(
        [
            half_real * turn_ref[0] + half_imag * turn_ref[1],
            half_imag * turn_ref[0] - half_real * turn_ref[1],
        ],
        1,
    )
    grid = nn(data_parts(turned), mx[...])
    size = grid.shape[1] // 2
    grid_ref[pl.ds(2 * step, tiles, stride=channels), :] = grid[:, :size]
    grid_ref[pl.ds(2 * step + 1, tiles, stride=channels), :] = grid[:, size:]


def sample_tiles(block_ref, weights_ref, grid_ref, sums_ref, out_ref):
    tiles = weights_ref.shape[0]
    channels = grid_ref.shape[0] // tiles
    sums_ref[...] = jnp.zeros_like(sums_ref)

    def one(tile, carry):
        start = pl.multiple_of(tile * channels, channels)
        high, low = split(grid_ref[pl.ds(start, channels), :])
        product = nn(jnp.concatenate([high, low], 0), weights_ref[tile])
        sums_ref[block_ref[tile]] += product[:channels] + product[channels:]
        return carry

    lax.fori_loop(0, tiles, one, 0, unroll=32)
    out_ref[...] = sums_ref[...].astype(bf16)


def spread_tiles(block_ref, weights_ref, parts_ref, grid_ref):
    tiles = weights_ref.shape[0]
    channels = grid_ref.shape[0] // tiles

    def one(tile, carry):
        start = pl.multiple_of(tile * channels, channels)
        product = nt(parts_ref[block_ref[tile]], weights_ref[tile])
        if product.shape[0] > channels:
            product = product[:channels] + product[channels:]
        grid_ref[pl.ds(start, channels), :] = product
        return carry

    lax.fori_loop(0, tiles, one, 0, unroll=32)


def adjoint_image(step, tiles, ey_back, mx_back, turn_ref, grid_ref):
    channels = grid_ref.shape[0] // tiles
    rows = turn_ref.shape[1]
    grid = jnp.concatenate(
        [
            grid_ref[pl.ds(2 * step, tiles, stride=channels), :],
            grid_ref[pl.ds(2 * step + 1, tiles, stride=channels), :],
        ],
        1,
    )
    back = nt(mx_back[...], data_parts(grid))
    turned = jnp.concatenate(
        [
            back[:rows] * turn_ref[0] - back[rows:] * turn_ref[1],
            back[rows:] * turn_ref[0] + back[:rows] * turn_ref[1],
        ],
        1,
    )
    image = nn(data_parts(turned), ey_back[...])
    columns = image.shape[1] // 2
    return image[:, :columns], image[:, columns:]


def add_dots(dots_ref, products):
    rows = lax.broadcasted_iota(jnp.int32, dots_ref.shape, 0)
    total = dots_ref[...]
    for place, (left, right) in enumerate(products):
        total += jnp.where(rows == place, jnp.sum(left * right), 0.0)
    dots_ref[...] = total


def measured_kernel(block, samples, weights, mx, eb, turn, images, grid):
    plane = pl.program_id(0)
    coils = images.shape[0]

    @pl.when(plane == 0)
    def _():
        spread_tiles(block, weights, samples, grid)

    for coil in range(coils):
        real, imag = adjoint_image(
            coil * pl.num_programs(0) + plane, weights.shape[0], eb, mx, turn, grid
        )
        images[coil, 0, 0] = real
        images[coil, 0, 1] = imag


def combine(images, sens):
    total_real = total_imag = 0.0
    for (real, imag), sens_ref in zip(images, sens):
        sens_real = sens_ref[0, 0].astype(f32)
        sens_imag = sens_ref[0, 1].astype(f32)
        total_real += sens_real * real + sens_imag * imag
        total_imag += sens_real * imag - sens_imag * real
    return total_real, total_imag


def start_kernel(images, *refs):
    *sens, right_side, rounded, dots = refs
    total = combine([(images[c, 0, 0], images[c, 0, 1]) for c in range(len(sens))], sens)
    for part in range(2):
        right_side[0, part] = total[part]
        rounded[0, part] = total[part].astype(bf16)

    @pl.when((pl.program_id(0) == 0) & (pl.program_id(1) == 0))
    def _():
        dots[...] = jnp.zeros_like(dots)

    add_dots(dots, [(right_side[0], right_side[0])])


def forward_kernel(block, picture, *refs):
    *sens, weights, ey, mx, turn, samples, grid, sums = refs
    plane = pl.program_id(0)
    for coil, sens_ref in enumerate(sens):
        forward_image(
            coil * pl.num_programs(0) + plane,
            picture[0, 0],
            picture[0, 1],
            sens_ref,
            ey,
            mx,
            turn,
            grid,
        )

    @pl.when(plane == pl.num_programs(0) - 1)
    def _():
        sample_tiles(block, weights, grid, sums, samples)


def spread_sum(block, samples, weights, grid, parts):
    summed = tree_sum([part[...].astype(f32) for part in samples])
    channels = summed.shape[1]
    high, low = split(summed)
    parts[:, :channels] = high
    parts[:, channels:] = low
    spread_tiles(block, weights, parts, grid)


def back_images(coils, plane, tiles, eb, mx, turn, grid):
    return [
        adjoint_image(coil * pl.num_programs(0) + plane, tiles, eb, mx, turn, grid)
        for coil in range(coils)
    ]


def first_kernel(peers, block, *refs):
    samples = refs[:peers]
    right_side, *sens, weights, mx, eb, turn, applied, grid, parts = refs[peers:]
    plane = pl.program_id(0)

    @pl.when(plane == 0)
    def _():
        spread_sum(block, samples, weights, grid, parts)

    images = back_images(len(sens), plane, weights.shape[0], eb, mx, turn, grid)
    total = combine(images, sens)
    for part in range(2):
        applied[0, part] = total[part] + damping * right_side[0, part]


def first_step_of(totals):
    return totals[0:1, 0:1] / (totals[1:2, 0:1] + damping * totals[0:1, 0:1])


def second_kernel(peers, block, *refs):
    samples = refs[:peers]
    totals, right_side, applied, residual, *sens = refs[peers:-8]
    weights, mx, eb, turn, rounded, dots, grid, parts = refs[-8:]
    plane = pl.program_id(0)

    @pl.when(plane == 0)
    def _():
        dots[...] = jnp.zeros_like(dots)
        spread_sum(block, samples, weights, grid, parts)

    images = back_images(len(sens), plane, weights.shape[0], eb, mx, turn, grid)
    total = combine(images, sens)
    for part in range(2):
        vector = residual[0, part]
        again = total[part] + damping * vector
        rounded[0, part] = (vector - first_step_of(totals) * again).astype(bf16)
        add_dots(
            dots,
            [
                (vector, vector),
                (vector, again),
                (vector, applied[0, part]),
                (right_side[0, part], again),
            ],
        )


def whole_block(array):
    rank = len(array.shape)
    return pl.BlockSpec(array.shape, lambda *_: (0,) * rank)


def on_device(kspace, sens_maps, weights, tile_slot, tile_block, send_list):
    coil_count = lax.axis_size("coil")
    peers = lax.axis_size("pencil")
    planes = sens_maps.shape[1]
    own_planes = planes // coil_count
    rows = sens_maps.shape[3]
    columns = sens_maps.shape[4]
    rows_total = rows * peers
    size = weights.shape[1]
    tile_count = tile_slot.shape[0]
    tiles = tile_count * peers
    blocks_dev = kspace.shape[3] // size
    blocks = blocks_dev * peers
    cap = send_list.shape[2]
    runs = rows_total // size
    brick_dev = columns // peers * runs
    images_count = coil_count * own_planes
    channels = 2 * images_count

    coil_index = lax.axis_index("coil")

    def to_planes(array):
        pieces = []
        for k in range(coil_count):
            part = lax.dynamic_slice_in_dim(array, (coil_index ^ k) * own_planes, own_planes, 0)
            if k > 0:
                part = lax.ppermute(part, "coil", [(i, i ^ k) for i in range(coil_count)])
            pieces.append(part)
        return pieces

    sens = to_planes(sens_maps[0])

    packed = jnp.concatenate([tile_slot, tile_block, send_list.reshape(-1)])
    places = lax.all_gather(packed, "pencil")
    slots = places[:, :tile_count]
    block_of = (
        places[:, tile_count : 2 * tile_count]
        + blocks_dev * jnp.arange(peers, dtype=jnp.int32)[:, None]
    ).reshape(-1)
    lists = places[:, 2 * tile_count :].reshape(peers, peers, cap)
    holder = jnp.arange(peers, dtype=jnp.int32)[:, None]
    brick = (slots // cap * brick_dev + lists[slots // cap, holder, slots % cap]).reshape(-1)
    line = brick // runs
    run = brick % runs

    measured = jnp.stack(to_planes(kspace[0]))
    measured = lax.all_gather(
        measured.reshape(channels, blocks_dev, size), "pencil", axis=1, tiled=True
    )
    measured = jnp.swapaxes(measured, 0, 1)
    all_weights = lax.all_gather(weights, "pencil", axis=0, tiled=True)

    cos_y, sin_y = wave(
        line - columns // 2, jnp.arange(columns, dtype=jnp.int32) - columns // 2, columns
    )
    row_ids = jnp.arange(rows, dtype=jnp.int32) + lax.axis_index("pencil") * rows - rows_total // 2
    cos_x, sin_x = wave(
        row_ids, jnp.arange(size, dtype=jnp.int32) - rows_total // 2, rows_total
    )
    turn = jnp.stack(quarter_turns(run, row_ids, runs))
    turn_back = jnp.stack(quarter_turns(row_ids, run, runs))

    def exchanged(partial, axis="pencil"):
        count = lax.axis_size(axis)
        return [partial] + [
            lax.ppermute(partial, axis, [(i, i ^ k) for i in range(count)])
            for k in range(1, count)
        ]

    def summed_over(axes, dots):
        for axis in axes:
            dots = tree_sum(exchanged(dots, axis))
        return dots

    def added(samples):
        return tree_sum([part.astype(f32) for part in samples])

    def gathered(own):
        ahead = [(i, i + 1) for i in range(coil_count - 1)]
        behind = [(i + 1, i) for i in range(coil_count - 1)]
        lines = []
        for plane in range(own_planes):
            piece = own[plane : plane + 1]
            lower, upper = [piece], [piece]
            for _ in range(1, coil_count):
                lower.append(lax.ppermute(lower[-1], "coil", ahead))
                upper.append(lax.ppermute(upper[-1], "coil", behind))
            lines.append([(lower[k], upper[-k]) for k in range(coil_count)])
        return [[line[k] for line in lines] for k in range(coil_count)]

    def chosen(k, pair):
        return (pair[0] if k == 0 else jnp.where(coil_index >= k, *pair)).astype(f32)

    def assembled(value_of):
        out = jnp.zeros((planes, 2, rows, columns), f32)
        for k in range(coil_count):
            for plane in range(own_planes):
                place = (coil_index + coil_count - k) % coil_count * own_planes + plane
                out = lax.dynamic_update_slice(out, value_of(k, plane), (place, 0, 0, 0))
        return out

    picture_shape = (own_planes, 2, rows, columns)

    if rows % 128 == 0 and columns % 128 == 0 and size % 128 == 0 and channels % 16 == 0:
        ey = table_parts(jnp.concatenate([cos_y, sin_y], 0), 1)
        eb = jnp.concatenate(
            [jnp.concatenate([cos_y, sin_y], 1), jnp.concatenate([-sin_y, cos_y], 1)], 0
        )
        eb = table_parts(eb, 0)
        mx = jnp.concatenate(
            [jnp.concatenate([cos_x, -sin_x], 1), jnp.concatenate([sin_x, cos_x], 1)], 0
        )
        mx, mx_back = table_parts(mx, 0), table_parts(mx, 1)
        places_spec = pl.BlockSpec(memory_space=pltpu.SMEM)
        plane_spec = pl.BlockSpec((1, 2, rows, columns), lambda p: (p, 0, 0, 0))
        all_coils = pl.BlockSpec(
            (coil_count, 1, 2, rows, columns), lambda p: (0, p, 0, 0, 0)
        )
        grid_scratch = pltpu.VMEM((tiles * channels, size), f32)
        sums_shape = (blocks, channels, size)
        params = pltpu.CompilerParams(vmem_limit_bytes=vmem_limit)

        def call(kernel, grid, inputs, specs, outs, out_specs, scratch, flops):
            read = sum(math.prod(i.shape) * i.dtype.itemsize for i in inputs)
            return pl.pallas_call(
                kernel,
                grid=grid,
                in_specs=specs,
                out_specs=out_specs,
                out_shape=outs,
                scratch_shapes=scratch,
                compiler_params=params,
                cost_estimate=pl.CostEstimate(
                    flops=flops, bytes_accessed=read, transcendentals=0
                ),
            )(*inputs)

        def shaped(shape, dtype=f32):
            return jax.ShapeDtypeStruct(shape, dtype)

        image_flops = 3 * images_count * 8 * tiles * rows * (columns + size)
        tile_flops = 4 * tiles * channels * size * size
        grid = (own_planes,)

        def measured_images():
            inputs = [block_of, measured, all_weights, mx_back, eb, turn_back]
            return call(
                measured_kernel,
                grid,
                inputs,
                [places_spec] + [whole_block(i) for i in inputs[1:]],
                shaped((coil_count,) + picture_shape),
                all_coils,
                [grid_scratch],
                image_flops + tile_flops,
            )

        def start(images):
            chunk = 64
            spec = pl.BlockSpec((1, 2, chunk, columns), lambda p, r: (p, 0, r, 0))
            coils_spec = pl.BlockSpec(
                (coil_count, 1, 2, chunk, columns), lambda p, r: (0, p, 0, r, 0)
            )
            return call(
                start_kernel,
                (own_planes, rows // chunk),
                [images, *sens],
                [coils_spec] + [spec] * coil_count,
                [shaped(picture_shape), shaped(picture_shape, bf16), shaped((8, 128))],
                [spec, spec, whole_block(shaped((8, 128)))],
                [],
                8 * images_count * rows * columns,
            )

        def forward(picture):
            tail = [all_weights, ey, mx, turn]
            return call(
                forward_kernel,
                grid,
                [block_of, picture, *sens, *tail],
                [places_spec] + [plane_spec] * (1 + coil_count) + [whole_block(i) for i in tail],
                shaped(sums_shape, bf16),
                whole_block(shaped(sums_shape)),
                [grid_scratch, pltpu.VMEM(sums_shape, f32)],
                image_flops + tile_flops,
            )

        parts_scratch = pltpu.VMEM((blocks, 2 * channels, size), bf16)

        def first(samples, right_side):
            tail = [all_weights, mx_back, eb, turn_back]
            inputs = [block_of, *samples, right_side, *sens, *tail]
            return call(
                functools.partial(first_kernel, peers),
                grid,
                inputs,
                [places_spec]
                + [whole_block(i) for i in samples]
                + [plane_spec] * (1 + coil_count)
                + [whole_block(i) for i in tail],
                shaped(picture_shape),
                plane_spec,
                [grid_scratch, parts_scratch],
                image_flops + tile_flops,
            )

        def second(samples, totals, right_side, applied, residual):
            tail = [all_weights, mx_back, eb, turn_back]
            inputs = [block_of, *samples, totals, right_side, applied, residual, *sens, *tail]
            return call(
                functools.partial(second_kernel, peers),
                grid,
                inputs,
                [places_spec]
                + [whole_block(i) for i in samples]
                + [whole_block(totals)]
                + [plane_spec] * (3 + coil_count)
                + [whole_block(i) for i in tail],
                [shaped(picture_shape, bf16), shaped((8, 128))],
                [plane_spec, whole_block(shaped((8, 128)))],
                [grid_scratch, parts_scratch],
                image_flops + tile_flops,
            )

    else:
        ein = functools.partial(jnp.einsum, precision=lax.Precision.HIGH)
        all_sens = jnp.stack(sens).astype(f32)
        map_real, map_imag = all_sens[:, :, 0], all_sens[:, :, 1]
        shape = (coil_count, own_planes)
        block_map = (block_of[:, None] == jnp.arange(blocks, dtype=jnp.int32)).astype(f32)
        tc, ts = turn[0][:, None, None], turn[1][:, None, None]
        wide_weights = all_weights.astype(f32)

        def forward(picture):
            coil_real = map_real * picture[None, :, 0] - map_imag * picture[None, :, 1]
            coil_imag = map_real * picture[None, :, 1] + map_imag * picture[None, :, 0]
            half_real = ein("ty,cpxy->tcpx", cos_y, coil_real) + ein(
                "ty,cpxy->tcpx", sin_y, coil_imag
            )
            half_imag = ein("ty,cpxy->tcpx", cos_y, coil_imag) - ein(
                "ty,cpxy->tcpx", sin_y, coil_real
            )
            real = half_real * tc + half_imag * ts
            imag = half_imag * tc - half_real * ts
            grid = jnp.stack(
                [
                    ein("tcpx,xi->tcpi", real, cos_x) + ein("tcpx,xi->tcpi", imag, sin_x),
                    ein("tcpx,xi->tcpi", imag, cos_x) - ein("tcpx,xi->tcpi", real, sin_x),
                ],
                3,
            ).reshape(tiles, channels, size)
            product = ein("tgi,tis->tgs", grid, wide_weights)
            return ein("tb,tgs->bgs", block_map, product).astype(bf16)

        def images_of(samples):
            spread = ein("tgs,tis->tgi", jnp.take(samples, block_of, axis=0), wide_weights)
            spread = spread.reshape(tiles, *shape, 2, size)
            back_real = ein("tcpi,xi->tcpx", spread[:, :, :, 0], cos_x) - ein(
                "tcpi,xi->tcpx", spread[:, :, :, 1], sin_x
            )
            back_imag = ein("tcpi,xi->tcpx", spread[:, :, :, 1], cos_x) + ein(
                "tcpi,xi->tcpx", spread[:, :, :, 0], sin_x
            )
            real = back_real * tc - back_imag * ts
            imag = back_imag * tc + back_real * ts
            return (
                ein("tcpx,ty->cpxy", real, cos_y) - ein("tcpx,ty->cpxy", imag, sin_y),
                ein("tcpx,ty->cpxy", imag, cos_y) + ein("tcpx,ty->cpxy", real, sin_y),
            )

        def combined(images):
            real, imag = images
            return jnp.stack(
                [
                    jnp.sum(map_real * real + map_imag * imag, 0),
                    jnp.sum(map_real * imag - map_imag * real, 0),
                ],
                1,
            )

        def stacked_dots(products):
            values = [jnp.sum(left * right) for left, right in products]
            values += [jnp.zeros((), f32)] * (8 - len(values))
            return jnp.broadcast_to(jnp.stack(values)[:, None], (8, 128))

        def measured_images():
            return images_of(measured.astype(f32))

        def start(images):
            right_side = combined(images)
            dots = stacked_dots([(right_side, right_side)])
            return right_side, right_side.astype(bf16), dots

        def first(samples, right_side):
            return combined(images_of(added(samples))) + damping * right_side

        def second(samples, totals, right_side, applied, residual):
            scale = totals[0, 0] / (totals[1, 0] + damping * totals[0, 0])
            again = combined(images_of(added(samples))) + damping * residual
            dots = stacked_dots(
                [
                    (residual, residual),
                    (residual, again),
                    (residual, applied),
                    (right_side, again),
                ]
            )
            return (residual - scale * again).astype(bf16), dots

    right_side, rounded, dots = start(measured_images())
    start_everywhere = gathered(rounded)
    samples = exchanged(forward(right_side))
    dots = summed_over(["pencil"], dots)
    energy = jnp.sum(jnp.square(added(samples)))
    place = lax.broadcasted_iota(jnp.int32, dots.shape, 0)
    first_totals = summed_over(["coil"], jnp.where(place == 1, energy, dots))
    start_norm = first_totals[0, 0]
    start_curve = first_totals[1, 0] + damping * start_norm
    first_step = start_norm / start_curve
    applied = first(samples, right_side)
    residual = right_side - first_step * applied
    residual_everywhere = gathered(residual.astype(bf16))
    samples = exchanged(forward(residual))
    rounded, dots = second(samples, first_totals, right_side, applied, residual)
    mixed_everywhere = gathered(rounded)
    totals = summed_over(["coil", "pencil"], dots)
    ratio = totals[0, 0] / start_norm
    curve = totals[1, 0] + ratio * (totals[2, 0] + totals[3, 0]) + ratio * ratio * start_curve
    second_step = totals[0, 0] / curve
    share = second_step / first_step

    def picture_of(k, plane):
        return (first_step + second_step * ratio) * chosen(
            k, start_everywhere[k][plane]
        ) + second_step * chosen(k, residual_everywhere[k][plane])

    def residual_of(k, plane):
        return (
            (1.0 - share + share * ratio) * chosen(k, residual_everywhere[k][plane])
            + share * chosen(k, mixed_everywhere[k][plane])
            - share * ratio * chosen(k, start_everywhere[k][plane])
        )

    return assembled(picture_of), assembled(residual_of)


def solution(mesh):
    in_specs = (
        P("coil", "scan", None, "pencil"),
        P("coil", "scan", None, "pencil", None),
        P("pencil", None, None),
        P("pencil"),
        P("pencil"),
        P("pencil", None, None),
    )
    out_specs = (P("scan", None, "pencil", None), P("scan", None, "pencil", None))
    return jax.shard_map(
        on_device, mesh=mesh, in_specs=in_specs, out_specs=out_specs, check_vma=False
    )
```

```python
import functools
import math

import jax
import jax.numpy as jnp
from jax import lax
from jax.experimental import pallas as pl
from jax.experimental.pallas import tpu as pltpu
from jax.sharding import PartitionSpec as P


damping = 0.5
f32, bf16 = jnp.float32, jnp.bfloat16
vmem_limit = 56 * 1024 * 1024


def wave(left, right, length):
    phases = left[:, None] * right[None, :] % length
    angles = phases.astype(f32) * (2.0 * math.pi / length)
    return jnp.cos(angles) / math.sqrt(length), jnp.sin(angles) / math.sqrt(length)


def quarter_turns(left, right, count):
    turns = left[:, None] * right[None, :] % count
    if count == 4:
        cosine = jnp.where(turns == 0, 1.0, 0.0) - jnp.where(turns == 2, 1.0, 0.0)
        sine = jnp.where(turns == 1, 1.0, 0.0) - jnp.where(turns == 3, 1.0, 0.0)
        return cosine.astype(f32), sine.astype(f32)
    angles = turns.astype(f32) * (2.0 * math.pi / count)
    return jnp.cos(angles), jnp.sin(angles)


def split(value):
    high = value.astype(bf16)
    return high, (value - high.astype(f32)).astype(bf16)


def table_parts(table, axis):
    high = lax.reduce_precision(table, 8, 7)
    low = (table - high).astype(bf16)
    high = high.astype(bf16)
    return jnp.concatenate([high, high, low], axis)


def data_parts(value):
    high, low = split(value)
    return jnp.concatenate([high, low, high], 1)


def nt(left, right):
    return lax.dot_general(left, right, (((1,), (1,)), ((), ())), preferred_element_type=f32)


def nn(left, right):
    return jnp.dot(left, right, preferred_element_type=f32)


def tree_sum(values):
    while len(values) > 1:
        values = [left + right for left, right in zip(values[::2], values[1::2])]
    return values[0]


def forward_image(step, real, imag, sens_ref, ey, mx, turn_ref, grid_ref):
    tiles = turn_ref.shape[1]
    rows = turn_ref.shape[2]
    channels = grid_ref.shape[0] // tiles
    sens_real = sens_ref[0, 0].astype(f32)
    sens_imag = sens_ref[0, 1].astype(f32)
    coil = jnp.concatenate(
        [sens_real * real - sens_imag * imag, sens_real * imag + sens_imag * real], 0
    )
    both = nt(ey[...], coil.astype(bf16))
    half_real = both[:tiles, :rows] + both[tiles:, rows:]
    half_imag = both[:tiles, rows:] - both[tiles:, :rows]
    turned = jnp.concatenate(
        [
            half_real * turn_ref[0] + half_imag * turn_ref[1],
            half_imag * turn_ref[0] - half_real * turn_ref[1],
        ],
        1,
    )
    grid = nn(turned.astype(bf16), mx[...])
    size = grid.shape[1] // 2
    grid_ref[pl.ds(2 * step, tiles, stride=channels), :] = grid[:, :size]
    grid_ref[pl.ds(2 * step + 1, tiles, stride=channels), :] = grid[:, size:]


def sample_tiles(block_ref, weights, grid_ref, sums_ref, out_ref):
    count = weights[0].shape[0]
    channels = sums_ref.shape[1]
    sums_ref[...] = jnp.zeros_like(sums_ref)

    for group, weights_ref in enumerate(weights):

        def one(place, carry):
            tile = group * count + place
            start = pl.multiple_of(tile * channels, channels)
            high, low = split(grid_ref[pl.ds(start, channels), :])
            product = nn(jnp.concatenate([high, low], 0), weights_ref[place])
            sums_ref[block_ref[tile]] += product[:channels] + product[channels:]
            return carry

        lax.fori_loop(0, count, one, 0, unroll=True)
    out_ref[...] = sums_ref[...].astype(bf16)


def spread_tiles(block_ref, weights, parts_ref, grid_ref):
    count = weights[0].shape[0]
    channels = grid_ref.shape[0] // (count * len(weights))

    for group, weights_ref in enumerate(weights):

        def one(place, carry):
            tile = group * count + place
            start = pl.multiple_of(tile * channels, channels)
            product = nt(parts_ref[block_ref[tile]], weights_ref[place])
            if product.shape[0] > channels:
                product = product[:channels] + product[channels:]
            grid_ref[pl.ds(start, channels), :] = product
            return carry

        lax.fori_loop(0, count, one, 0, unroll=True)


def adjoint_image(step, tiles, ey_back, mx_back, turn_ref, grid_ref):
    channels = grid_ref.shape[0] // tiles
    rows = turn_ref.shape[1]
    grid = jnp.concatenate(
        [
            grid_ref[pl.ds(2 * step, tiles, stride=channels), :],
            grid_ref[pl.ds(2 * step + 1, tiles, stride=channels), :],
        ],
        1,
    )
    back = nt(mx_back[...], data_parts(grid))
    turned = jnp.concatenate(
        [
            back[:rows] * turn_ref[0] - back[rows:] * turn_ref[1],
            back[rows:] * turn_ref[0] + back[:rows] * turn_ref[1],
        ],
        1,
    )
    image = nn(data_parts(turned), ey_back[...])
    columns = image.shape[1] // 2
    return image[:, :columns], image[:, columns:]


def add_dots(dots_ref, products):
    rows = lax.broadcasted_iota(jnp.int32, dots_ref.shape, 0)
    total = dots_ref[...]
    for place, (left, right) in enumerate(products):
        total += jnp.where(rows == place, jnp.sum(left * right), 0.0)
    dots_ref[...] = total


def measured_kernel(block, samples, *refs):
    *weights, mx, eb, turn, images, grid = refs
    plane = pl.program_id(0)
    coils = images.shape[0]

    @pl.when(plane == 0)
    def _():
        spread_tiles(block, weights, samples, grid)

    for coil in range(coils):
        real, imag = adjoint_image(
            coil * pl.num_programs(0) + plane, turn.shape[2], eb, mx, turn, grid
        )
        images[coil, 0, 0] = real
        images[coil, 0, 1] = imag


def combine(images, sens):
    total_real = total_imag = 0.0
    for (real, imag), sens_ref in zip(images, sens):
        sens_real = sens_ref[0, 0].astype(f32)
        sens_imag = sens_ref[0, 1].astype(f32)
        total_real += sens_real * real + sens_imag * imag
        total_imag += sens_real * imag - sens_imag * real
    return total_real, total_imag


def start_kernel(images, *refs):
    *sens, right_side, rounded, dots = refs
    total = combine([(images[c, 0, 0], images[c, 0, 1]) for c in range(len(sens))], sens)
    for part in range(2):
        right_side[0, part] = total[part]
        rounded[0, part] = total[part].astype(bf16)

    @pl.when((pl.program_id(0) == 0) & (pl.program_id(1) == 0))
    def _():
        dots[...] = jnp.zeros_like(dots)

    add_dots(dots, [(right_side[0], right_side[0])])


def forward_kernel(coils, block, picture, *refs):
    sens = refs[:coils]
    *weights, ey, mx, turn, samples, grid, sums = refs[coils:]
    plane = pl.program_id(0)
    for coil, sens_ref in enumerate(sens):
        forward_image(
            coil * pl.num_programs(0) + plane,
            picture[0, 0],
            picture[0, 1],
            sens_ref,
            ey,
            mx,
            turn,
            grid,
        )

    @pl.when(plane == pl.num_programs(0) - 1)
    def _():
        sample_tiles(block, weights, grid, sums, samples)


def spread_sum(block, samples, weights, grid, parts):
    summed = tree_sum([part[...].astype(f32) for part in samples])
    channels = summed.shape[1]
    high, low = split(summed)
    parts[:, :channels] = high
    parts[:, channels:] = low
    spread_tiles(block, weights, parts, grid)


def back_images(coils, plane, tiles, eb, mx, turn, grid):
    return [
        adjoint_image(coil * pl.num_programs(0) + plane, tiles, eb, mx, turn, grid)
        for coil in range(coils)
    ]


def first_kernel(peers, coils, block, *refs):
    samples, weights, sens = refs[:peers], refs[peers : 2 * peers], refs[2 * peers :][:coils]
    mx, eb, turn, right_side, applied, grid, parts = refs[2 * peers + coils :]
    plane = pl.program_id(0)

    @pl.when(plane == 0)
    def _():
        spread_sum(block, samples, weights, grid, parts)

    images = back_images(len(sens), plane, turn.shape[2], eb, mx, turn, grid)
    total = combine(images, sens)
    for part in range(2):
        applied[0, part] = total[part] + damping * right_side[0, part]


def first_step_of(totals):
    return totals[0:1, 0:1] / (totals[1:2, 0:1] + damping * totals[0:1, 0:1])


def second_kernel(peers, coils, block, *refs):
    samples, weights, sens = refs[:peers], refs[peers : 2 * peers], refs[2 * peers :][:coils]
    mx, eb, turn, totals, right_side, applied, residual = refs[2 * peers + coils :][:7]
    rounded, dots, grid, parts = refs[-4:]
    plane = pl.program_id(0)

    @pl.when(plane == 0)
    def _():
        dots[...] = jnp.zeros_like(dots)
        spread_sum(block, samples, weights, grid, parts)

    images = back_images(len(sens), plane, turn.shape[2], eb, mx, turn, grid)
    total = combine(images, sens)
    for part in range(2):
        vector = residual[0, part]
        again = total[part] + damping * vector
        rounded[0, part] = (vector - first_step_of(totals) * again).astype(bf16)
        add_dots(
            dots,
            [
                (vector, vector),
                (vector, again),
                (vector, applied[0, part]),
                (right_side[0, part], again),
            ],
        )


def whole_block(array):
    rank = len(array.shape)
    return pl.BlockSpec(array.shape, lambda *_: (0,) * rank)


def on_device(kspace, sens_maps, weights, tile_slot, tile_block, send_list):
    coil_count = lax.axis_size("coil")
    peers = lax.axis_size("pencil")
    planes = sens_maps.shape[1]
    own_planes = planes // coil_count
    rows = sens_maps.shape[3]
    columns = sens_maps.shape[4]
    rows_total = rows * peers
    size = weights.shape[1]
    tile_count = tile_slot.shape[0]
    tiles = tile_count * peers
    blocks_dev = kspace.shape[3] // size
    blocks = blocks_dev * peers
    cap = send_list.shape[2]
    runs = rows_total // size
    brick_dev = columns // peers * runs
    images_count = coil_count * own_planes
    channels = 2 * images_count

    coil_index = lax.axis_index("coil")

    def swapped(array, axis, k):
        return lax.ppermute(array, axis, [(i, i ^ k) for i in range(lax.axis_size(axis))])

    def everywhere(array, axis):
        bit = 1
        while bit < lax.axis_size(axis):
            bit *= 2
        pieces = {0: array}
        while bit > 1:
            bit //= 2
            for k in sorted(pieces):
                pieces[k ^ bit] = swapped(pieces[k], axis, bit)
        return [pieces[k] for k in sorted(pieces)]

    def to_planes(array):
        pieces = []
        for k in range(coil_count):
            part = lax.dynamic_slice_in_dim(array, (coil_index ^ k) * own_planes, own_planes, 0)
            pieces.append(swapped(part, "coil", k) if k > 0 else part)
        return pieces

    measured = to_planes(kspace[0])
    sens_source, *measured = lax.optimization_barrier((sens_maps[0], *measured))
    sens = to_planes(sens_source)
    all_weights = everywhere(weights, "pencil")

    packed = jnp.concatenate([tile_slot, tile_block, send_list.reshape(-1)])
    places = lax.all_gather(packed, "pencil")
    lists = places[:, 2 * tile_count :].reshape(peers, peers, cap)
    holder = (jnp.arange(peers, dtype=jnp.int32) ^ lax.axis_index("pencil"))[:, None]
    own_places = jnp.take(places, holder[:, 0], axis=0)
    slots = own_places[:, :tile_count]
    block_of = (own_places[:, tile_count : 2 * tile_count] + blocks_dev * holder).reshape(-1)
    brick = (slots // cap * brick_dev + lists[slots // cap, holder, slots % cap]).reshape(-1)
    line = brick // runs
    run = brick % runs

    measured = jnp.stack(measured)
    measured = lax.all_gather(
        measured.reshape(channels, blocks_dev, size), "pencil", axis=1, tiled=True
    )
    measured = jnp.swapaxes(measured, 0, 1)

    cos_y, sin_y = wave(
        line - columns // 2, jnp.arange(columns, dtype=jnp.int32) - columns // 2, columns
    )
    row_ids = jnp.arange(rows, dtype=jnp.int32) + lax.axis_index("pencil") * rows - rows_total // 2
    cos_x, sin_x = wave(
        row_ids, jnp.arange(size, dtype=jnp.int32) - rows_total // 2, rows_total
    )
    turn = jnp.stack(quarter_turns(run, row_ids, runs))
    turn_back = jnp.stack(quarter_turns(row_ids, run, runs))

    def exchanged(partial, axis="pencil"):
        count = lax.axis_size(axis)
        return [partial] + [swapped(partial, axis, k) for k in range(1, count)]

    def summed_over(axes, dots):
        for axis in axes:
            dots = tree_sum(exchanged(dots, axis))
        return dots

    def added(samples):
        return tree_sum([part.astype(f32) for part in samples])

    def gathered(own):
        return lax.all_gather(own, "coil", axis=0, tiled=True).astype(f32)

    picture_shape = (own_planes, 2, rows, columns)

    if rows % 128 == 0 and columns % 128 == 0 and size % 128 == 0 and channels % 16 == 0:
        ey = jnp.concatenate([cos_y, sin_y], 0).astype(bf16)
        eb = jnp.concatenate(
            [jnp.concatenate([cos_y, sin_y], 1), jnp.concatenate([-sin_y, cos_y], 1)], 0
        )
        eb = table_parts(eb, 0)
        mx = jnp.concatenate(
            [jnp.concatenate([cos_x, -sin_x], 1), jnp.concatenate([sin_x, cos_x], 1)], 0
        )
        mx, mx_back = mx.astype(bf16), table_parts(mx, 1)
        places_spec = pl.BlockSpec(memory_space=pltpu.SMEM)
        plane_spec = pl.BlockSpec((1, 2, rows, columns), lambda p: (p, 0, 0, 0))
        all_coils = pl.BlockSpec(
            (coil_count, 1, 2, rows, columns), lambda p: (0, p, 0, 0, 0)
        )
        grid_scratch = pltpu.VMEM((tiles * channels, size), f32)
        sums_shape = (blocks, channels, size)
        params = pltpu.CompilerParams(vmem_limit_bytes=vmem_limit)

        def call(kernel, grid, inputs, specs, outs, out_specs, scratch, flops):
            read = sum(math.prod(i.shape) * i.dtype.itemsize for i in inputs)
            return pl.pallas_call(
                kernel,
                grid=grid,
                in_specs=specs,
                out_specs=out_specs,
                out_shape=outs,
                scratch_shapes=scratch,
                compiler_params=params,
                cost_estimate=pl.CostEstimate(
                    flops=flops, bytes_accessed=read, transcendentals=0
                ),
            )(*inputs)

        def shaped(shape, dtype=f32):
            return jax.ShapeDtypeStruct(shape, dtype)

        image_flops = 2 * images_count * 8 * tiles * rows * (columns + size)
        tile_flops = 4 * tiles * channels * size * size
        grid = (own_planes,)

        def measured_images():
            inputs = [block_of, measured, *all_weights, mx_back, eb, turn_back]
            return call(
                measured_kernel,
                grid,
                inputs,
                [places_spec] + [whole_block(i) for i in inputs[1:]],
                shaped((coil_count,) + picture_shape),
                all_coils,
                [grid_scratch],
                image_flops + tile_flops,
            )

        def start(images):
            chunk = 64
            spec = pl.BlockSpec((1, 2, chunk, columns), lambda p, r: (p, 0, r, 0))
            coils_spec = pl.BlockSpec(
                (coil_count, 1, 2, chunk, columns), lambda p, r: (0, p, 0, r, 0)
            )
            return call(
                start_kernel,
                (own_planes, rows // chunk),
                [images, *sens],
                [coils_spec] + [spec] * coil_count,
                [shaped(picture_shape), shaped(picture_shape, bf16), shaped((8, 128))],
                [spec, spec, whole_block(shaped((8, 128)))],
                [],
                8 * images_count * rows * columns,
            )

        def forward(picture):
            tail = [*all_weights, ey, mx, turn]
            return call(
                functools.partial(forward_kernel, coil_count),
                grid,
                [block_of, picture, *sens, *tail],
                [places_spec] + [plane_spec] * (1 + coil_count) + [whole_block(i) for i in tail],
                shaped(sums_shape, bf16),
                whole_block(shaped(sums_shape)),
                [grid_scratch, pltpu.VMEM(sums_shape, f32)],
                image_flops + tile_flops,
            )

        parts_scratch = pltpu.VMEM((blocks, 2 * channels, size), bf16)

        def back(kernel, samples, tables, vectors, outs, out_specs):
            inputs = [*samples, *all_weights]
            tables = [mx_back, eb, turn_back, *tables]
            return call(
                functools.partial(kernel, peers, coil_count),
                grid,
                [block_of, *inputs, *sens, *tables, *vectors],
                [places_spec]
                + [whole_block(i) for i in inputs]
                + [plane_spec] * coil_count
                + [whole_block(i) for i in tables]
                + [plane_spec] * len(vectors),
                outs,
                out_specs,
                [grid_scratch, parts_scratch],
                image_flops + tile_flops,
            )

        def first(samples, right_side):
            return back(
                first_kernel, samples, [], [right_side], shaped(picture_shape), plane_spec
            )

        def second(samples, totals, right_side, applied, residual):
            return back(
                second_kernel,
                samples,
                [totals],
                [right_side, applied, residual],
                [shaped(picture_shape, bf16), shaped((8, 128))],
                [plane_spec, whole_block(shaped((8, 128)))],
            )

    else:
        ein = functools.partial(jnp.einsum, precision=lax.Precision.HIGH)
        all_sens = jnp.stack(sens).astype(f32)
        map_real, map_imag = all_sens[:, :, 0], all_sens[:, :, 1]
        shape = (coil_count, own_planes)
        block_map = (block_of[:, None] == jnp.arange(blocks, dtype=jnp.int32)).astype(f32)
        tc, ts = turn[0][:, None, None], turn[1][:, None, None]
        wide_weights = jnp.concatenate(all_weights, 0).astype(f32)

        def forward(picture):
            coil_real = map_real * picture[None, :, 0] - map_imag * picture[None, :, 1]
            coil_imag = map_real * picture[None, :, 1] + map_imag * picture[None, :, 0]
            half_real = ein("ty,cpxy->tcpx", cos_y, coil_real) + ein(
                "ty,cpxy->tcpx", sin_y, coil_imag
            )
            half_imag = ein("ty,cpxy->tcpx", cos_y, coil_imag) - ein(
                "ty,cpxy->tcpx", sin_y, coil_real
            )
            real = half_real * tc + half_imag * ts
            imag = half_imag * tc - half_real * ts
            grid = jnp.stack(
                [
                    ein("tcpx,xi->tcpi", real, cos_x) + ein("tcpx,xi->tcpi", imag, sin_x),
                    ein("tcpx,xi->tcpi", imag, cos_x) - ein("tcpx,xi->tcpi", real, sin_x),
                ],
                3,
            ).reshape(tiles, channels, size)
            product = ein("tgi,tis->tgs", grid, wide_weights)
            return ein("tb,tgs->bgs", block_map, product).astype(bf16)

        def images_of(samples):
            spread = ein("tgs,tis->tgi", jnp.take(samples, block_of, axis=0), wide_weights)
            spread = spread.reshape(tiles, *shape, 2, size)
            back_real = ein("tcpi,xi->tcpx", spread[:, :, :, 0], cos_x) - ein(
                "tcpi,xi->tcpx", spread[:, :, :, 1], sin_x
            )
            back_imag = ein("tcpi,xi->tcpx", spread[:, :, :, 1], cos_x) + ein(
                "tcpi,xi->tcpx", spread[:, :, :, 0], sin_x
            )
            real = back_real * tc - back_imag * ts
            imag = back_imag * tc + back_real * ts
            return (
                ein("tcpx,ty->cpxy", real, cos_y) - ein("tcpx,ty->cpxy", imag, sin_y),
                ein("tcpx,ty->cpxy", imag, cos_y) + ein("tcpx,ty->cpxy", real, sin_y),
            )

        def combined(images):
            real, imag = images
            return jnp.stack(
                [
                    jnp.sum(map_real * real + map_imag * imag, 0),
                    jnp.sum(map_real * imag - map_imag * real, 0),
                ],
                1,
            )

        def stacked_dots(products):
            values = [jnp.sum(left * right) for left, right in products]
            values += [jnp.zeros((), f32)] * (8 - len(values))
            return jnp.broadcast_to(jnp.stack(values)[:, None], (8, 128))

        def measured_images():
            return images_of(measured.astype(f32))

        def start(images):
            right_side = combined(images)
            dots = stacked_dots([(right_side, right_side)])
            return right_side, right_side.astype(bf16), dots

        def first(samples, right_side):
            return combined(images_of(added(samples))) + damping * right_side

        def second(samples, totals, right_side, applied, residual):
            scale = totals[0, 0] / (totals[1, 0] + damping * totals[0, 0])
            again = combined(images_of(added(samples))) + damping * residual
            dots = stacked_dots(
                [
                    (residual, residual),
                    (residual, again),
                    (residual, applied),
                    (right_side, again),
                ]
            )
            return (residual - scale * again).astype(bf16), dots

    right_side, rounded, dots = start(measured_images())
    start_all = gathered(rounded)
    samples = exchanged(forward(right_side))
    dots = summed_over(["pencil"], dots)
    energy = jnp.sum(jnp.square(added(samples)))
    place = lax.broadcasted_iota(jnp.int32, dots.shape, 0)
    first_totals = summed_over(["coil"], jnp.where(place == 1, energy, dots))
    start_norm = first_totals[0, 0]
    start_curve = first_totals[1, 0] + damping * start_norm
    first_step = start_norm / start_curve
    applied = first(samples, right_side)
    residual = right_side - first_step * applied
    residual_all = gathered(residual.astype(bf16))
    samples = exchanged(forward(residual))
    rounded, dots = second(samples, first_totals, right_side, applied, residual)
    mixed = everywhere(rounded, "coil")
    totals = summed_over(["coil", "pencil"], dots)
    ratio = totals[0, 0] / start_norm
    curve = totals[1, 0] + ratio * (totals[2, 0] + totals[3, 0]) + ratio * ratio * start_curve
    second_step = totals[0, 0] / curve
    share = second_step / first_step
    picture = (first_step + second_step * ratio) * start_all + second_step * residual_all
    out = (1.0 - share + share * ratio) * residual_all - share * ratio * start_all
    for k, piece in enumerate(mixed):
        place = ((coil_index ^ k) * own_planes, 0, 0, 0)
        known = lax.dynamic_slice(out, place, piece.shape)
        out = lax.dynamic_update_slice(out, known + share * piece.astype(f32), place)
    return picture, out


def solution(mesh):
    in_specs = (
        P("coil", "scan", None, "pencil"),
        P("coil", "scan", None, "pencil", None),
        P("pencil", None, None),
        P("pencil"),
        P("pencil"),
        P("pencil", None, None),
    )
    out_specs = (P("scan", None, "pencil", None), P("scan", None, "pencil", None))
    return jax.shard_map(
        on_device, mesh=mesh, in_specs=in_specs, out_specs=out_specs, check_vma=False
    )
```

```python
import functools
import math

import jax
import jax.numpy as jnp
from jax import lax
from jax.experimental import pallas as pl
from jax.experimental.pallas import tpu as pltpu
from jax.sharding import PartitionSpec as P


damping = 0.5
f32, bf16 = jnp.float32, jnp.bfloat16
vmem_limit = 56 * 1024 * 1024


def wave(left, right, length):
    phases = left[:, None] * right[None, :] % length
    angles = phases.astype(f32) * (2.0 * math.pi / length)
    return jnp.cos(angles) / math.sqrt(length), jnp.sin(angles) / math.sqrt(length)


def quarter_turns(left, right, count):
    turns = left[:, None] * right[None, :] % count
    if count == 4:
        cosine = jnp.where(turns == 0, 1.0, 0.0) - jnp.where(turns == 2, 1.0, 0.0)
        sine = jnp.where(turns == 1, 1.0, 0.0) - jnp.where(turns == 3, 1.0, 0.0)
        return cosine.astype(f32), sine.astype(f32)
    angles = turns.astype(f32) * (2.0 * math.pi / count)
    return jnp.cos(angles), jnp.sin(angles)


def split(value):
    high = value.astype(bf16)
    return high, (value - high.astype(f32)).astype(bf16)


def table_parts(table, axis):
    high = lax.reduce_precision(table, 8, 7)
    low = (table - high).astype(bf16)
    high = high.astype(bf16)
    return jnp.concatenate([high, high, low], axis)


def data_parts(value):
    high, low = split(value)
    return jnp.concatenate([high, low, high], 1)


def nt(left, right):
    return lax.dot_general(left, right, (((1,), (1,)), ((), ())), preferred_element_type=f32)


def nn(left, right):
    return jnp.dot(left, right, preferred_element_type=f32)


def tree_sum(values):
    while len(values) > 1:
        values = [left + right for left, right in zip(values[::2], values[1::2])]
    return values[0]


def forward_image(step, real, imag, sens_ref, ey, mx, turn_ref, grid_ref):
    tiles = turn_ref.shape[1]
    rows = turn_ref.shape[2]
    channels = grid_ref.shape[0] // tiles
    sens_real = sens_ref[0, 0, 0].astype(f32)
    sens_imag = sens_ref[0, 0, 1].astype(f32)
    coil = jnp.concatenate(
        [sens_real * real - sens_imag * imag, sens_real * imag + sens_imag * real], 0
    )
    both = nt(ey[...], coil.astype(bf16))
    half_real = both[:tiles, :rows] + both[tiles:, rows:]
    half_imag = both[:tiles, rows:] - both[tiles:, :rows]
    turned = jnp.concatenate(
        [
            half_real * turn_ref[0] + half_imag * turn_ref[1],
            half_imag * turn_ref[0] - half_real * turn_ref[1],
        ],
        1,
    )
    grid = nn(turned.astype(bf16), mx[...])
    size = grid.shape[1] // 2
    grid_ref[pl.ds(2 * step, tiles, stride=channels), :] = grid[:, :size]
    grid_ref[pl.ds(2 * step + 1, tiles, stride=channels), :] = grid[:, size:]


def sample_tiles(block_ref, weights, grid_ref, sums_ref, out_ref):
    count = weights[0].shape[0]
    channels = sums_ref.shape[1]
    sums_ref[...] = jnp.zeros_like(sums_ref)

    for group, weights_ref in enumerate(weights):

        def one(place, carry):
            tile = group * count + place
            start = pl.multiple_of(tile * channels, channels)
            high, low = split(grid_ref[pl.ds(start, channels), :])
            product = nn(jnp.concatenate([high, low], 0), weights_ref[place])
            sums_ref[block_ref[tile]] += product[:channels] + product[channels:]
            return carry

        lax.fori_loop(0, count, one, 0, unroll=True)
    out_ref[...] = sums_ref[...].astype(bf16)


def spread_tiles(block_ref, weights, parts_ref, grid_ref):
    count = weights[0].shape[0]
    channels = grid_ref.shape[0] // (count * len(weights))

    for group, weights_ref in enumerate(weights):

        def one(place, carry):
            tile = group * count + place
            start = pl.multiple_of(tile * channels, channels)
            product = nt(parts_ref[block_ref[tile]], weights_ref[place])
            if product.shape[0] > channels:
                product = product[:channels] + product[channels:]
            grid_ref[pl.ds(start, channels), :] = product
            return carry

        lax.fori_loop(0, count, one, 0, unroll=True)


def adjoint_image(step, tiles, ey_back, mx_back, turn_ref, grid_ref):
    channels = grid_ref.shape[0] // tiles
    rows = turn_ref.shape[1]
    grid = jnp.concatenate(
        [
            grid_ref[pl.ds(2 * step, tiles, stride=channels), :],
            grid_ref[pl.ds(2 * step + 1, tiles, stride=channels), :],
        ],
        1,
    )
    back = nt(mx_back[...], data_parts(grid))
    turned = jnp.concatenate(
        [
            back[:rows] * turn_ref[0] - back[rows:] * turn_ref[1],
            back[rows:] * turn_ref[0] + back[:rows] * turn_ref[1],
        ],
        1,
    )
    image = nn(data_parts(turned), ey_back[...])
    columns = image.shape[1] // 2
    return image[:, :columns], image[:, columns:]


def add_dots(dots_ref, products):
    rows = lax.broadcasted_iota(jnp.int32, dots_ref.shape, 0)
    total = dots_ref[...]
    for place, (left, right) in enumerate(products):
        total += jnp.where(rows == place, jnp.sum(left * right), 0.0)
    dots_ref[...] = total


def measured_kernel(block, samples, *refs):
    *weights, mx, eb, turn, images, grid = refs
    plane = pl.program_id(0)
    coils = images.shape[0]

    @pl.when(plane == 0)
    def _():
        spread_tiles(block, weights, samples, grid)

    for coil in range(coils):
        real, imag = adjoint_image(
            coil * pl.num_programs(0) + plane, turn.shape[2], eb, mx, turn, grid
        )
        images[coil, 0, 0] = real
        images[coil, 0, 1] = imag


def combine(images, sens):
    total_real = total_imag = 0.0
    for (real, imag), sens_ref in zip(images, sens):
        sens_real = sens_ref[0, 0, 0].astype(f32)
        sens_imag = sens_ref[0, 0, 1].astype(f32)
        total_real += sens_real * real + sens_imag * imag
        total_imag += sens_real * imag - sens_imag * real
    return total_real, total_imag


def start_kernel(images, *refs):
    *sens, right_side, rounded, dots = refs
    total = combine([(images[c, 0, 0], images[c, 0, 1]) for c in range(len(sens))], sens)
    for part in range(2):
        right_side[0, part] = total[part]
        rounded[0, part] = total[part].astype(bf16)

    @pl.when((pl.program_id(0) == 0) & (pl.program_id(1) == 0))
    def _():
        dots[...] = jnp.zeros_like(dots)

    add_dots(dots, [(right_side[0], right_side[0])])


def forward_kernel(coils, block, picture, *refs):
    sens = refs[:coils]
    *weights, ey, mx, turn, samples, grid, sums = refs[coils:]
    plane = pl.program_id(0)
    for coil, sens_ref in enumerate(sens):
        forward_image(
            coil * pl.num_programs(0) + plane,
            picture[0, 0],
            picture[0, 1],
            sens_ref,
            ey,
            mx,
            turn,
            grid,
        )

    @pl.when(plane == pl.num_programs(0) - 1)
    def _():
        sample_tiles(block, weights, grid, sums, samples)


def spread_sum(block, samples, weights, grid, parts):
    summed = tree_sum([part[...].astype(f32) for part in samples])
    channels = summed.shape[1]
    high, low = split(summed)
    parts[:, :channels] = high
    parts[:, channels:] = low
    spread_tiles(block, weights, parts, grid)


def back_images(coils, plane, tiles, eb, mx, turn, grid):
    return [
        adjoint_image(coil * pl.num_programs(0) + plane, tiles, eb, mx, turn, grid)
        for coil in range(coils)
    ]


def first_kernel(peers, coils, block, *refs):
    samples, weights, sens = refs[:peers], refs[peers : 2 * peers], refs[2 * peers :][:coils]
    mx, eb, turn, right_side, applied, grid, parts = refs[2 * peers + coils :]
    plane = pl.program_id(0)

    @pl.when(plane == 0)
    def _():
        spread_sum(block, samples, weights, grid, parts)

    images = back_images(len(sens), plane, turn.shape[2], eb, mx, turn, grid)
    total = combine(images, sens)
    for part in range(2):
        applied[0, part] = total[part] + damping * right_side[0, part]


def first_step_of(totals):
    return totals[0:1, 0:1] / (totals[1:2, 0:1] + damping * totals[0:1, 0:1])


def second_kernel(peers, coils, block, *refs):
    samples, weights, sens = refs[:peers], refs[peers : 2 * peers], refs[2 * peers :][:coils]
    mx, eb, turn, totals, right_side, applied, residual = refs[2 * peers + coils :][:7]
    rounded, dots, grid, parts = refs[-4:]
    plane = pl.program_id(0)

    @pl.when(plane == 0)
    def _():
        dots[...] = jnp.zeros_like(dots)
        spread_sum(block, samples, weights, grid, parts)

    images = back_images(len(sens), plane, turn.shape[2], eb, mx, turn, grid)
    total = combine(images, sens)
    for part in range(2):
        vector = residual[0, part]
        again = total[part] + damping * vector
        rounded[0, part] = (vector - first_step_of(totals) * again).astype(bf16)
        add_dots(
            dots,
            [
                (vector, vector),
                (vector, again),
                (vector, applied[0, part]),
                (right_side[0, part], again),
            ],
        )


def whole_block(array):
    rank = len(array.shape)
    return pl.BlockSpec(array.shape, lambda *_: (0,) * rank)


def on_device(kspace, sens_maps, weights, tile_slot, tile_block, send_list):
    coil_count = lax.axis_size("coil")
    peers = lax.axis_size("pencil")
    planes = sens_maps.shape[1]
    own_planes = planes // coil_count
    rows = sens_maps.shape[3]
    columns = sens_maps.shape[4]
    rows_total = rows * peers
    size = weights.shape[1]
    tile_count = tile_slot.shape[0]
    tiles = tile_count * peers
    blocks_dev = kspace.shape[3] // size
    blocks = blocks_dev * peers
    cap = send_list.shape[2]
    runs = rows_total // size
    brick_dev = columns // peers * runs
    images_count = coil_count * own_planes
    channels = 2 * images_count

    coil_index = lax.axis_index("coil")

    def swapped(array, axis, k):
        return lax.ppermute(array, axis, [(i, i ^ k) for i in range(lax.axis_size(axis))])

    def everywhere(array, axis):
        bit = 1
        while bit < lax.axis_size(axis):
            bit *= 2
        pieces = {0: array}
        while bit > 1:
            bit //= 2
            for k in sorted(pieces):
                pieces[k ^ bit] = swapped(pieces[k], axis, bit)
        return [pieces[k] for k in sorted(pieces)]

    first_bits = [1 << bit for bit in range(coil_count.bit_length() - 1)]

    def completed(own, sent):
        pieces = {0: own}
        for bit, piece in zip(first_bits, sent):
            pieces[bit] = piece
        for bit in first_bits:
            for k in range(coil_count):
                if k not in pieces and (k ^ bit) in pieces:
                    pieces[k] = swapped(pieces[k ^ bit], "coil", bit)
        return [pieces[k] for k in range(coil_count)]

    def to_planes(array):
        pieces = []
        for k in range(coil_count):
            part = lax.dynamic_slice_in_dim(array, (coil_index ^ k) * own_planes, own_planes, 0)
            pieces.append(swapped(part, "coil", k) if k > 0 else part)
        return pieces

    sens = lax.all_to_all(sens_maps[0], "coil", split_axis=0, concat_axis=0, tiled=True)
    sens = sens.reshape(coil_count, own_planes, 2, rows, columns)
    measured = jnp.stack(to_planes(kspace[0]))
    by_coil = jnp.arange(coil_count, dtype=jnp.int32) ^ coil_index
    measured = jnp.take(measured, by_coil, axis=0)
    all_weights = everywhere(weights, "pencil")

    packed = jnp.concatenate([tile_slot, tile_block, send_list.reshape(-1)])
    places = jnp.stack(everywhere(packed, "pencil"))
    holder = (jnp.arange(peers, dtype=jnp.int32) ^ lax.axis_index("pencil"))[:, None]
    by_owner = jnp.take(places, holder[:, 0], axis=0)
    lists = by_owner[:, 2 * tile_count :].reshape(peers, peers, cap)
    slots = places[:, :tile_count]
    block_of = (places[:, tile_count : 2 * tile_count] + blocks_dev * holder).reshape(-1)
    brick = (slots // cap * brick_dev + lists[slots // cap, holder, slots % cap]).reshape(-1)
    line = brick // runs
    run = brick % runs

    measured = measured.reshape(channels, blocks_dev, size)
    measured = jnp.concatenate(everywhere(jnp.swapaxes(measured, 0, 1), "pencil"), 0)
    measured_block = (
        places[:, tile_count : 2 * tile_count]
        + blocks_dev * jnp.arange(peers, dtype=jnp.int32)[:, None]
    ).reshape(-1)

    cos_y, sin_y = wave(
        line - columns // 2, jnp.arange(columns, dtype=jnp.int32) - columns // 2, columns
    )
    row_ids = jnp.arange(rows, dtype=jnp.int32) + lax.axis_index("pencil") * rows - rows_total // 2
    cos_x, sin_x = wave(
        row_ids, jnp.arange(size, dtype=jnp.int32) - rows_total // 2, rows_total
    )
    turn = jnp.stack(quarter_turns(run, row_ids, runs))
    turn_back = jnp.stack(quarter_turns(row_ids, run, runs))

    def exchanged(partial, axis="pencil"):
        count = lax.axis_size(axis)
        return [partial] + [swapped(partial, axis, k) for k in range(1, count)]

    def summed_over(axes, dots):
        for axis in axes:
            dots = tree_sum(exchanged(dots, axis))
        return dots

    def added(samples):
        return tree_sum([part.astype(f32) for part in samples])

    picture_shape = (own_planes, 2, rows, columns)

    if rows % 128 == 0 and columns % 128 == 0 and size % 128 == 0 and channels % 16 == 0:
        ey = jnp.concatenate([cos_y, sin_y], 0).astype(bf16)
        eb = jnp.concatenate(
            [jnp.concatenate([cos_y, sin_y], 1), jnp.concatenate([-sin_y, cos_y], 1)], 0
        )
        eb = table_parts(eb, 0)
        mx = jnp.concatenate(
            [jnp.concatenate([cos_x, -sin_x], 1), jnp.concatenate([sin_x, cos_x], 1)], 0
        )
        mx, mx_back = mx.astype(bf16), table_parts(mx, 1)
        places_spec = pl.BlockSpec(memory_space=pltpu.SMEM)
        plane_spec = pl.BlockSpec((1, 2, rows, columns), lambda p: (p, 0, 0, 0))
        sens_specs = [
            pl.BlockSpec((1, 1, 2, rows, columns), functools.partial(lambda c, p: (c, p, 0, 0, 0), c))
            for c in range(coil_count)
        ]
        all_coils = pl.BlockSpec(
            (coil_count, 1, 2, rows, columns), lambda p: (0, p, 0, 0, 0)
        )
        grid_scratch = pltpu.VMEM((tiles * channels, size), f32)
        sums_shape = (blocks, channels, size)
        params = pltpu.CompilerParams(vmem_limit_bytes=vmem_limit)

        def call(kernel, grid, inputs, specs, outs, out_specs, scratch, flops):
            read = sum(math.prod(i.shape) * i.dtype.itemsize for i in inputs)
            return pl.pallas_call(
                kernel,
                grid=grid,
                in_specs=specs,
                out_specs=out_specs,
                out_shape=outs,
                scratch_shapes=scratch,
                compiler_params=params,
                cost_estimate=pl.CostEstimate(
                    flops=flops, bytes_accessed=read, transcendentals=0
                ),
            )(*inputs)

        def shaped(shape, dtype=f32):
            return jax.ShapeDtypeStruct(shape, dtype)

        image_flops = 2 * images_count * 8 * tiles * rows * (columns + size)
        tile_flops = 4 * tiles * channels * size * size
        grid = (own_planes,)

        def measured_images():
            inputs = [measured_block, measured, *all_weights, mx_back, eb, turn_back]
            return call(
                measured_kernel,
                grid,
                inputs,
                [places_spec] + [whole_block(i) for i in inputs[1:]],
                shaped((coil_count,) + picture_shape),
                all_coils,
                [grid_scratch],
                image_flops + tile_flops,
            )

        def start(images):
            chunk = 64
            spec = pl.BlockSpec((1, 2, chunk, columns), lambda p, r: (p, 0, r, 0))
            coils_spec = pl.BlockSpec(
                (coil_count, 1, 2, chunk, columns), lambda p, r: (0, p, 0, r, 0)
            )
            return call(
                start_kernel,
                (own_planes, rows // chunk),
                [images] + [sens] * coil_count,
                [coils_spec]
                + [
                    pl.BlockSpec(
                        (1, 1, 2, chunk, columns),
                        functools.partial(lambda c, p, r: (c, p, 0, r, 0), c),
                    )
                    for c in range(coil_count)
                ],
                [shaped(picture_shape), shaped(picture_shape, bf16), shaped((8, 128))],
                [spec, spec, whole_block(shaped((8, 128)))],
                [],
                8 * images_count * rows * columns,
            )

        def forward(picture):
            tail = [*all_weights, ey, mx, turn]
            return call(
                functools.partial(forward_kernel, coil_count),
                grid,
                [block_of, picture] + [sens] * coil_count + tail,
                [places_spec, plane_spec] + sens_specs + [whole_block(i) for i in tail],
                shaped(sums_shape, bf16),
                whole_block(shaped(sums_shape)),
                [grid_scratch, pltpu.VMEM(sums_shape, f32)],
                image_flops + tile_flops,
            )

        parts_scratch = pltpu.VMEM((blocks, 2 * channels, size), bf16)

        def back(kernel, samples, tables, vectors, outs, out_specs):
            inputs = [*samples, *all_weights]
            tables = [mx_back, eb, turn_back, *tables]
            return call(
                functools.partial(kernel, peers, coil_count),
                grid,
                [block_of, *inputs] + [sens] * coil_count + tables + vectors,
                [places_spec]
                + [whole_block(i) for i in inputs]
                + sens_specs
                + [whole_block(i) for i in tables]
                + [plane_spec] * len(vectors),
                outs,
                out_specs,
                [grid_scratch, parts_scratch],
                image_flops + tile_flops,
            )

        def first(samples, right_side):
            return back(
                first_kernel, samples, [], [right_side], shaped(picture_shape), plane_spec
            )

        def second(samples, totals, right_side, applied, residual):
            return back(
                second_kernel,
                samples,
                [totals],
                [right_side, applied, residual],
                [shaped(picture_shape, bf16), shaped((8, 128))],
                [plane_spec, whole_block(shaped((8, 128)))],
            )

    else:
        ein = functools.partial(jnp.einsum, precision=lax.Precision.HIGH)
        all_sens = sens.astype(f32)
        map_real, map_imag = all_sens[:, :, 0], all_sens[:, :, 1]
        shape = (coil_count, own_planes)
        block_map = (block_of[:, None] == jnp.arange(blocks, dtype=jnp.int32)).astype(f32)
        tc, ts = turn[0][:, None, None], turn[1][:, None, None]
        wide_weights = jnp.concatenate(all_weights, 0).astype(f32)

        def forward(picture):
            coil_real = map_real * picture[None, :, 0] - map_imag * picture[None, :, 1]
            coil_imag = map_real * picture[None, :, 1] + map_imag * picture[None, :, 0]
            half_real = ein("ty,cpxy->tcpx", cos_y, coil_real) + ein(
                "ty,cpxy->tcpx", sin_y, coil_imag
            )
            half_imag = ein("ty,cpxy->tcpx", cos_y, coil_imag) - ein(
                "ty,cpxy->tcpx", sin_y, coil_real
            )
            real = half_real * tc + half_imag * ts
            imag = half_imag * tc - half_real * ts
            grid = jnp.stack(
                [
                    ein("tcpx,xi->tcpi", real, cos_x) + ein("tcpx,xi->tcpi", imag, sin_x),
                    ein("tcpx,xi->tcpi", imag, cos_x) - ein("tcpx,xi->tcpi", real, sin_x),
                ],
                3,
            ).reshape(tiles, channels, size)
            product = ein("tgi,tis->tgs", grid, wide_weights)
            return ein("tb,tgs->bgs", block_map, product).astype(bf16)

        def images_of(samples, blocks_of=block_of):
            spread = ein("tgs,tis->tgi", jnp.take(samples, blocks_of, axis=0), wide_weights)
            spread = spread.reshape(tiles, *shape, 2, size)
            back_real = ein("tcpi,xi->tcpx", spread[:, :, :, 0], cos_x) - ein(
                "tcpi,xi->tcpx", spread[:, :, :, 1], sin_x
            )
            back_imag = ein("tcpi,xi->tcpx", spread[:, :, :, 1], cos_x) + ein(
                "tcpi,xi->tcpx", spread[:, :, :, 0], sin_x
            )
            real = back_real * tc - back_imag * ts
            imag = back_imag * tc + back_real * ts
            return (
                ein("tcpx,ty->cpxy", real, cos_y) - ein("tcpx,ty->cpxy", imag, sin_y),
                ein("tcpx,ty->cpxy", imag, cos_y) + ein("tcpx,ty->cpxy", real, sin_y),
            )

        def combined(images):
            real, imag = images
            return jnp.stack(
                [
                    jnp.sum(map_real * real + map_imag * imag, 0),
                    jnp.sum(map_real * imag - map_imag * real, 0),
                ],
                1,
            )

        def stacked_dots(products):
            values = [jnp.sum(left * right) for left, right in products]
            values += [jnp.zeros((), f32)] * (8 - len(values))
            return jnp.broadcast_to(jnp.stack(values)[:, None], (8, 128))

        def measured_images():
            return images_of(measured.astype(f32), measured_block)

        def start(images):
            right_side = combined(images)
            dots = stacked_dots([(right_side, right_side)])
            return right_side, right_side.astype(bf16), dots

        def first(samples, right_side):
            return combined(images_of(added(samples))) + damping * right_side

        def second(samples, totals, right_side, applied, residual):
            scale = totals[0, 0] / (totals[1, 0] + damping * totals[0, 0])
            again = combined(images_of(added(samples))) + damping * residual
            dots = stacked_dots(
                [
                    (residual, residual),
                    (residual, again),
                    (residual, applied),
                    (right_side, again),
                ]
            )
            return (residual - scale * again).astype(bf16), dots

    right_side, rounded, dots = start(measured_images())
    start_own = rounded
    start_sent = [swapped(start_own, "coil", k) for k in first_bits]
    samples = exchanged(forward(right_side))
    samples, start_sent = lax.optimization_barrier((samples, start_sent))
    dots = summed_over(["pencil"], dots)
    energy = jnp.sum(jnp.square(added(samples)))
    place = lax.broadcasted_iota(jnp.int32, dots.shape, 0)
    first_totals = summed_over(["coil"], jnp.where(place == 1, energy, dots))
    start_norm = first_totals[0, 0]
    start_curve = first_totals[1, 0] + damping * start_norm
    first_step = start_norm / start_curve
    applied, start_pieces = lax.optimization_barrier(
        (first(samples, right_side), completed(start_own, start_sent))
    )
    residual = right_side - first_step * applied
    residual_own = residual.astype(bf16)
    residual_sent = [swapped(residual_own, "coil", k) for k in first_bits]
    samples = exchanged(forward(residual))
    samples, residual_sent = lax.optimization_barrier((samples, residual_sent))
    rounded, dots = second(samples, first_totals, right_side, applied, residual)
    rounded, dots, residual_pieces = lax.optimization_barrier(
        (rounded, dots, completed(residual_own, residual_sent))
    )
    mixed = everywhere(rounded, "coil")
    totals = summed_over(["coil", "pencil"], dots)
    ratio = totals[0, 0] / start_norm
    curve = totals[1, 0] + ratio * (totals[2, 0] + totals[3, 0]) + ratio * ratio * start_curve
    second_step = totals[0, 0] / curve
    share = second_step / first_step

    picture = jnp.zeros((planes, 2, rows, columns), f32)
    out = jnp.zeros((planes, 2, rows, columns), f32)
    for k in range(coil_count):
        place = ((coil_index ^ k) * own_planes, 0, 0, 0)
        vector, known = start_pieces[k].astype(f32), residual_pieces[k].astype(f32)
        piece = (first_step + second_step * ratio) * vector + second_step * known
        picture = lax.dynamic_update_slice(picture, piece, place)
        piece = (1.0 - share + share * ratio) * known - share * ratio * vector
        piece += share * mixed[k].astype(f32)
        out = lax.dynamic_update_slice(out, piece, place)
    return picture, out


def solution(mesh):
    in_specs = (
        P("coil", "scan", None, "pencil"),
        P("coil", "scan", None, "pencil", None),
        P("pencil", None, None),
        P("pencil"),
        P("pencil"),
        P("pencil", None, None),
    )
    out_specs = (P("scan", None, "pencil", None), P("scan", None, "pencil", None))
    return jax.shard_map(
        on_device, mesh=mesh, in_specs=in_specs, out_specs=out_specs, check_vma=False
    )
```

```python
import functools
import math

import jax
import jax.numpy as jnp
from jax import lax
from jax.experimental import pallas as pl
from jax.experimental.pallas import tpu as pltpu
from jax.sharding import PartitionSpec as P


damping = 0.5
f32, bf16 = jnp.float32, jnp.bfloat16
vmem_limit = 56 * 1024 * 1024


def wave(left, right, length):
    phases = left[:, None] * right[None, :] % length
    angles = phases.astype(f32) * (2.0 * math.pi / length)
    return jnp.cos(angles) / math.sqrt(length), jnp.sin(angles) / math.sqrt(length)


def quarter_turns(left, right, count):
    turns = left[:, None] * right[None, :] % count
    if count == 4:
        cosine = jnp.where(turns == 0, 1.0, 0.0) - jnp.where(turns == 2, 1.0, 0.0)
        sine = jnp.where(turns == 1, 1.0, 0.0) - jnp.where(turns == 3, 1.0, 0.0)
        return cosine.astype(f32), sine.astype(f32)
    angles = turns.astype(f32) * (2.0 * math.pi / count)
    return jnp.cos(angles), jnp.sin(angles)


def split(value):
    high = value.astype(bf16)
    return high, (value - high.astype(f32)).astype(bf16)


def table_parts(table, axis):
    high = lax.reduce_precision(table, 8, 7)
    low = (table - high).astype(bf16)
    high = high.astype(bf16)
    return jnp.concatenate([high, high, low], axis)


def data_parts(value):
    high, low = split(value)
    return jnp.concatenate([high, low, high], 1)


def nt(left, right):
    return lax.dot_general(left, right, (((1,), (1,)), ((), ())), preferred_element_type=f32)


def nn(left, right):
    return jnp.dot(left, right, preferred_element_type=f32)


def tree_sum(values):
    while len(values) > 1:
        values = [left + right for left, right in zip(values[::2], values[1::2])]
    return values[0]


def forward_image(step, real, imag, sens_ref, ey, mx, turn_ref, grid_ref):
    tiles = turn_ref.shape[1]
    rows = turn_ref.shape[2]
    channels = grid_ref.shape[0] // tiles
    sens_real = sens_ref[0, 0, 0].astype(f32)
    sens_imag = sens_ref[0, 0, 1].astype(f32)
    coil = jnp.concatenate(
        [sens_real * real - sens_imag * imag, sens_real * imag + sens_imag * real], 0
    )
    both = nt(ey[...], coil.astype(bf16))
    half_real = both[:tiles, :rows] + both[tiles:, rows:]
    half_imag = both[:tiles, rows:] - both[tiles:, :rows]
    turned = jnp.concatenate(
        [
            half_real * turn_ref[0] + half_imag * turn_ref[1],
            half_imag * turn_ref[0] - half_real * turn_ref[1],
        ],
        1,
    )
    grid = nn(turned.astype(bf16), mx[...])
    size = grid.shape[1] // 2
    grid_ref[pl.ds(2 * step, tiles, stride=channels), :] = grid[:, :size]
    grid_ref[pl.ds(2 * step + 1, tiles, stride=channels), :] = grid[:, size:]


def sample_tiles(block_ref, weights, grid_ref, sums_ref, out_ref):
    count = weights[0].shape[0]
    channels = sums_ref.shape[1]
    sums_ref[...] = jnp.zeros_like(sums_ref)

    for group, weights_ref in enumerate(weights):

        def one(place, carry):
            tile = group * count + place
            start = pl.multiple_of(tile * channels, channels)
            value = grid_ref[pl.ds(start, channels), :]
            high = value.astype(bf16).astype(f32)
            both = jnp.concatenate([high, value - high], 0).astype(bf16)
            product = nn(both, weights_ref[place])
            sums_ref[block_ref[tile]] += product[:channels] + product[channels:]
            return carry

        lax.fori_loop(0, count, one, 0, unroll=True)
    out_ref[...] = sums_ref[...].reshape(out_ref.shape).astype(bf16)


def spread_tiles(block_ref, weights, parts_ref, grid_ref):
    count = weights[0].shape[0]
    channels = grid_ref.shape[0] // (count * len(weights))

    for group, weights_ref in enumerate(weights):

        def one(place, carry):
            tile = group * count + place
            start = pl.multiple_of(tile * channels, channels)
            product = nt(parts_ref[block_ref[tile]], weights_ref[place])
            if product.shape[0] > channels:
                product = product[:channels] + product[channels:]
            grid_ref[pl.ds(start, channels), :] = product
            return carry

        lax.fori_loop(0, count, one, 0, unroll=True)


def adjoint_image(step, tiles, ey_back, mx_back, turn_ref, grid_ref):
    channels = grid_ref.shape[0] // tiles
    rows = turn_ref.shape[1]
    grid = jnp.concatenate(
        [
            grid_ref[pl.ds(2 * step, tiles, stride=channels), :],
            grid_ref[pl.ds(2 * step + 1, tiles, stride=channels), :],
        ],
        1,
    )
    back = nt(mx_back[...], data_parts(grid))
    turned = jnp.concatenate(
        [
            back[:rows] * turn_ref[0] - back[rows:] * turn_ref[1],
            back[rows:] * turn_ref[0] + back[:rows] * turn_ref[1],
        ],
        1,
    )
    image = nn(data_parts(turned), ey_back[...])
    columns = image.shape[1] // 2
    return image[:, :columns], image[:, columns:]


def add_dots(dots_ref, products):
    rows = lax.broadcasted_iota(jnp.int32, dots_ref.shape, 0)
    total = dots_ref[...]
    for place, (left, right) in enumerate(products):
        total += jnp.where(rows == place, jnp.sum(left * right), 0.0)
    dots_ref[...] = total


def measured_kernel(block, samples, *refs):
    *weights, mx, eb, turn, images, grid = refs
    plane = pl.program_id(0)
    coils = images.shape[0]

    @pl.when(plane == 0)
    def _():
        spread_tiles(block, weights, samples, grid)

    for coil in range(coils):
        real, imag = adjoint_image(
            coil * pl.num_programs(0) + plane, turn.shape[2], eb, mx, turn, grid
        )
        images[coil, 0, 0] = real
        images[coil, 0, 1] = imag


def combine(images, sens):
    total_real = total_imag = 0.0
    for (real, imag), sens_ref in zip(images, sens):
        sens_real = sens_ref[0, 0, 0].astype(f32)
        sens_imag = sens_ref[0, 0, 1].astype(f32)
        total_real += sens_real * real + sens_imag * imag
        total_imag += sens_real * imag - sens_imag * real
    return total_real, total_imag


def start_kernel(images, *refs):
    *sens, right_side, rounded, dots = refs
    total = combine([(images[c, 0, 0], images[c, 0, 1]) for c in range(len(sens))], sens)
    for part in range(2):
        right_side[0, part] = total[part]
        rounded[0, part] = total[part].astype(bf16)

    @pl.when((pl.program_id(0) == 0) & (pl.program_id(1) == 0))
    def _():
        dots[...] = jnp.zeros_like(dots)

    add_dots(dots, [(right_side[0], right_side[0])])


def forward_kernel(coils, block, picture, *refs):
    sens = refs[:coils]
    *weights, ey, mx, turn, samples, grid, sums = refs[coils:]
    plane = pl.program_id(0)
    for coil, sens_ref in enumerate(sens):
        forward_image(
            coil * pl.num_programs(0) + plane,
            picture[0, 0],
            picture[0, 1],
            sens_ref,
            ey,
            mx,
            turn,
            grid,
        )

    @pl.when(plane == pl.num_programs(0) - 1)
    def _():
        sample_tiles(block, weights, grid, sums, samples)


def summed_parts(samples, parts):
    summed = tree_sum([part[...].astype(f32) for part in samples])
    blocks, channels, size = parts.shape[0], parts.shape[1] // 2, parts.shape[2]
    value = summed.reshape(blocks, channels, size)
    high = value.astype(bf16).astype(f32)
    parts[...] = jnp.concatenate([high, value - high], 1).astype(bf16)
    return summed


def back_images(coils, plane, tiles, eb, mx, turn, grid):
    return [
        adjoint_image(coil * pl.num_programs(0) + plane, tiles, eb, mx, turn, grid)
        for coil in range(coils)
    ]


def step_of(norm, energy):
    return jnp.where(norm > 0.0, norm / (energy + damping * norm), 1.0)


def first_kernel(peers, coils, block, *refs):
    samples, weights, sens = refs[:peers], refs[peers : 2 * peers], refs[2 * peers :][:coils]
    mx, eb, turn, *norms = refs[2 * peers + coils :][: 3 + peers]
    right_side, residual, rounded, facts, dots, total_samples, grid, parts = refs[-8:]
    plane = pl.program_id(0)

    @pl.when(plane == 0)
    def _():
        summed = summed_parts(samples, parts)
        total_samples[...] = summed
        rows = lax.broadcasted_iota(jnp.int32, facts.shape, 0)
        norm = tree_sum([part[...] for part in norms])
        facts[...] = jnp.where(rows == 1, jnp.sum(summed * summed), norm)
        dots[...] = jnp.zeros_like(dots)
        spread_tiles(block, weights, parts, grid)

    images = back_images(len(sens), plane, turn.shape[2], eb, mx, turn, grid)
    total = combine(images, sens)
    scale = step_of(facts[0:1, 0:1], facts[1:2, 0:1])
    for part in range(2):
        vector = right_side[0, part]
        value = vector - scale * (total[part] + damping * vector)
        residual[0, part] = value
        rounded[0, part] = value.astype(bf16)
        add_dots(dots, [(value, value), (value, vector)])


def second_kernel(peers, coils, block, *refs):
    samples, weights, sens = refs[:peers], refs[peers : 2 * peers], refs[2 * peers :][:coils]
    mx, eb, turn, facts, residual, rounded, grid, parts = refs[2 * peers + coils :]
    plane = pl.program_id(0)

    @pl.when(plane == 0)
    def _():
        summed_parts(samples, parts)
        spread_tiles(block, weights, parts, grid)

    images = back_images(len(sens), plane, turn.shape[2], eb, mx, turn, grid)
    total = combine(images, sens)
    scale = step_of(facts[0:1, 0:1], facts[1:2, 0:1])
    for part in range(2):
        vector = residual[0, part]
        again = total[part] + damping * vector
        rounded[0, part] = (vector - scale * again).astype(bf16)


def group_count_of(own_planes):
    return 1


def whole_block(array):
    rank = len(array.shape)
    return pl.BlockSpec(array.shape, lambda *_: (0,) * rank)


def on_device(kspace, sens_maps, weights, tile_slot, tile_block, send_list):
    coil_count = lax.axis_size("coil")
    peers = lax.axis_size("pencil")
    planes = sens_maps.shape[1]
    own_planes = planes // coil_count
    rows = sens_maps.shape[3]
    columns = sens_maps.shape[4]
    rows_total = rows * peers
    size = weights.shape[1]
    tile_count = tile_slot.shape[0]
    tiles = tile_count * peers
    blocks_dev = kspace.shape[3] // size
    blocks = blocks_dev * peers
    cap = send_list.shape[2]
    runs = rows_total // size
    brick_dev = columns // peers * runs
    images_count = coil_count * own_planes
    channels = 2 * images_count

    coil_index = lax.axis_index("coil")

    def swapped(array, axis, k):
        return lax.ppermute(array, axis, [(i, i ^ k) for i in range(lax.axis_size(axis))])

    def everywhere(array, axis):
        bit = 1
        while bit < lax.axis_size(axis):
            bit *= 2
        pieces = {0: array}
        while bit > 1:
            bit //= 2
            for k in sorted(pieces):
                pieces[k ^ bit] = swapped(pieces[k], axis, bit)
        return [pieces[k] for k in sorted(pieces)]

    first_bits = [1 << bit for bit in range(coil_count.bit_length() - 1)]

    def completed(own, sent):
        pieces = {0: own}
        for bit, piece in zip(first_bits, sent):
            pieces[bit] = piece
        for bit in first_bits:
            for k in range(coil_count):
                if k not in pieces and (k ^ bit) in pieces:
                    pieces[k] = swapped(pieces[k ^ bit], "coil", bit)
        return [pieces[k] for k in range(coil_count)]

    def to_planes(array):
        pieces = []
        for k in range(coil_count):
            part = lax.dynamic_slice_in_dim(array, (coil_index ^ k) * own_planes, own_planes, 0)
            pieces.append(swapped(part, "coil", k) if k > 0 else part)
        return pieces

    group_planes = own_planes // group_count_of(own_planes)
    groups = range(own_planes // group_planes)
    measured = to_planes(kspace[0])
    packed = jnp.concatenate([tile_slot, tile_block, send_list.reshape(-1)])
    sens_source, packed, measured = lax.optimization_barrier((sens_maps[0], packed, measured))
    sens_source = sens_source.reshape(coil_count, own_planes, 2, rows, columns)
    sens = [
        lax.all_to_all(
            sens_source[:, g * group_planes : (g + 1) * group_planes],
            "coil",
            split_axis=0,
            concat_axis=0,
            tiled=True,
        )
        for g in groups
    ]
    measured = jnp.stack(measured)
    by_coil = jnp.arange(coil_count, dtype=jnp.int32) ^ coil_index
    measured = jnp.take(measured, by_coil, axis=0)
    all_weights = everywhere(weights, "pencil")

    places = jnp.stack(everywhere(packed, "pencil"))
    holder = (jnp.arange(peers, dtype=jnp.int32) ^ lax.axis_index("pencil"))[:, None]
    by_owner = jnp.take(places, holder[:, 0], axis=0)
    lists = by_owner[:, 2 * tile_count :].reshape(peers, peers, cap)
    slots = places[:, :tile_count]
    block_of = (places[:, tile_count : 2 * tile_count] + blocks_dev * holder).reshape(-1)
    brick = (slots // cap * brick_dev + lists[slots // cap, holder, slots % cap]).reshape(-1)
    line = brick // runs
    run = brick % runs

    measured = measured.reshape(channels, blocks_dev, size)
    measured = jnp.concatenate(everywhere(jnp.swapaxes(measured, 0, 1), "pencil"), 0)
    measured_block = (
        places[:, tile_count : 2 * tile_count]
        + blocks_dev * jnp.arange(peers, dtype=jnp.int32)[:, None]
    ).reshape(-1)

    cos_y, sin_y = wave(
        line - columns // 2, jnp.arange(columns, dtype=jnp.int32) - columns // 2, columns
    )
    row_ids = jnp.arange(rows, dtype=jnp.int32) + lax.axis_index("pencil") * rows - rows_total // 2
    cos_x, sin_x = wave(
        row_ids, jnp.arange(size, dtype=jnp.int32) - rows_total // 2, rows_total
    )
    turn = jnp.stack(quarter_turns(run, row_ids, runs))
    turn_back = jnp.stack(quarter_turns(row_ids, run, runs))

    def exchanged(partial, axis="pencil"):
        count = lax.axis_size(axis)
        return [partial] + [swapped(partial, axis, k) for k in range(1, count)]

    group_shape = (group_planes, 2, rows, columns)
    group_images = coil_count * group_planes
    group_channels = 2 * group_images

    if (
        rows % 128 == 0
        and columns % 128 == 0
        and size % 128 == 0
        and channels % 16 == 0
        and group_channels % 8 == 0
    ):
        ey = jnp.concatenate([cos_y, sin_y], 0).astype(bf16)
        eb = jnp.concatenate(
            [jnp.concatenate([cos_y, sin_y], 1), jnp.concatenate([-sin_y, cos_y], 1)], 0
        )
        eb = table_parts(eb, 0)
        mx = jnp.concatenate(
            [jnp.concatenate([cos_x, -sin_x], 1), jnp.concatenate([sin_x, cos_x], 1)], 0
        )
        mx, mx_back = mx.astype(bf16), table_parts(mx, 1)
        places_spec = pl.BlockSpec(memory_space=pltpu.SMEM)
        plane_spec = pl.BlockSpec((1, 2, rows, columns), lambda p: (p, 0, 0, 0))
        sens_specs = [
            pl.BlockSpec((1, 1, 2, rows, columns), functools.partial(lambda c, p: (c, p, 0, 0, 0), c))
            for c in range(coil_count)
        ]
        grid_scratch = pltpu.VMEM((tiles * group_channels, size), f32)
        params = pltpu.CompilerParams(vmem_limit_bytes=vmem_limit)
        tail_tables = [mx_back, eb, turn_back]

        def shaped(shape, dtype=f32):
            return jax.ShapeDtypeStruct(shape, dtype)

        def call(kernel, grid, inputs, specs, outs, out_specs, scratch, images):
            flops = 2 * images * 8 * tiles * rows * (columns + size)
            return pl.pallas_call(
                kernel,
                grid=grid,
                in_specs=specs,
                out_specs=out_specs,
                out_shape=outs,
                scratch_shapes=scratch,
                compiler_params=params,
                cost_estimate=pl.CostEstimate(
                    flops=flops,
                    bytes_accessed=sum(math.prod(i.shape) * i.dtype.itemsize for i in inputs),
                    transcendentals=0,
                ),
            )(*inputs)

        def measured_images():
            inputs = [measured_block, measured, *all_weights, *tail_tables]
            shape = (coil_count, own_planes, 2, rows, columns)
            return call(
                measured_kernel,
                (own_planes,),
                inputs,
                [places_spec] + [whole_block(i) for i in inputs[1:]],
                shaped(shape),
                pl.BlockSpec((coil_count, 1, 2, rows, columns), lambda p: (0, p, 0, 0, 0)),
                [pltpu.VMEM((tiles * channels, size), f32)],
                images_count,
            )

        def start(images, g):
            chunk = 64
            spec = pl.BlockSpec((1, 2, chunk, columns), lambda p, r: (p, 0, r, 0))
            images_spec = pl.BlockSpec(
                (coil_count, 1, 2, chunk, columns),
                lambda p, r: (0, p + g * group_planes, 0, r, 0),
            )
            dots_shape = shaped((8, 128))
            return call(
                start_kernel,
                (group_planes, rows // chunk),
                [images] + [sens[g]] * coil_count,
                [images_spec]
                + [
                    pl.BlockSpec(
                        (1, 1, 2, chunk, columns),
                        functools.partial(lambda c, p, r: (c, p, 0, r, 0), c),
                    )
                    for c in range(coil_count)
                ],
                [shaped(group_shape), shaped(group_shape, bf16), dots_shape],
                [spec, spec, whole_block(dots_shape)],
                [],
                0,
            )

        def forward(picture, g):
            tail = [*all_weights, ey, mx, turn]
            out = shaped((blocks * group_channels, size), bf16)
            return call(
                functools.partial(forward_kernel, coil_count),
                (group_planes,),
                [block_of, picture] + [sens[g]] * coil_count + tail,
                [places_spec, plane_spec] + sens_specs + [whole_block(i) for i in tail],
                out,
                whole_block(out),
                [grid_scratch, pltpu.VMEM((blocks, group_channels, size), f32)],
                group_images,
            )

        def back(kernel, samples, tables, vectors, g, outs, out_specs):
            inputs = [*samples, *all_weights]
            tables = tail_tables + tables
            return call(
                functools.partial(kernel, peers, coil_count),
                (group_planes,),
                [block_of, *inputs] + [sens[g]] * coil_count + tables + vectors,
                [places_spec]
                + [whole_block(i) for i in inputs]
                + sens_specs
                + [whole_block(i) for i in tables]
                + [plane_spec] * len(vectors),
                outs,
                out_specs,
                [grid_scratch, pltpu.VMEM((blocks, 2 * group_channels, size), bf16)],
                group_images,
            )

        def first(samples, norms, right_side, g):
            small, large = shaped((8, 128)), shaped(samples[0].shape)
            return back(
                first_kernel,
                samples,
                norms,
                [right_side],
                g,
                [shaped(group_shape), shaped(group_shape, bf16), small, small, large],
                [plane_spec, plane_spec] + [whole_block(i) for i in (small, small, large)],
            )

        def second(samples, facts, residual, g):
            return back(
                second_kernel,
                samples,
                [facts],
                [residual],
                g,
                shaped(group_shape, bf16),
                plane_spec,
            )

    else:
        ein = functools.partial(jnp.einsum, precision=lax.Precision.HIGH)
        maps = [array.astype(f32) for array in sens]
        block_map = (block_of[:, None] == jnp.arange(blocks, dtype=jnp.int32)).astype(f32)
        tc, ts = turn[0][:, None, None], turn[1][:, None, None]
        wide_weights = jnp.concatenate(all_weights, 0).astype(f32)

        def forward(picture, g):
            map_real, map_imag = maps[g][:, :, 0], maps[g][:, :, 1]
            coil_real = map_real * picture[None, :, 0] - map_imag * picture[None, :, 1]
            coil_imag = map_real * picture[None, :, 1] + map_imag * picture[None, :, 0]
            half_real = ein("ty,cpxy->tcpx", cos_y, coil_real) + ein(
                "ty,cpxy->tcpx", sin_y, coil_imag
            )
            half_imag = ein("ty,cpxy->tcpx", cos_y, coil_imag) - ein(
                "ty,cpxy->tcpx", sin_y, coil_real
            )
            real = half_real * tc + half_imag * ts
            imag = half_imag * tc - half_real * ts
            grid = jnp.stack(
                [
                    ein("tcpx,xi->tcpi", real, cos_x) + ein("tcpx,xi->tcpi", imag, sin_x),
                    ein("tcpx,xi->tcpi", imag, cos_x) - ein("tcpx,xi->tcpi", real, sin_x),
                ],
                3,
            ).reshape(tiles, group_channels, size)
            product = ein("tgi,tis->tgs", grid, wide_weights)
            return ein("tb,tgs->bgs", block_map, product).astype(bf16).reshape(-1, size)

        def images_of(samples, blocks_of):
            spread = ein("tgs,tis->tgi", jnp.take(samples, blocks_of, axis=0), wide_weights)
            spread = spread.reshape(tiles, coil_count, -1, 2, size)
            back_real = ein("tcpi,xi->tcpx", spread[:, :, :, 0], cos_x) - ein(
                "tcpi,xi->tcpx", spread[:, :, :, 1], sin_x
            )
            back_imag = ein("tcpi,xi->tcpx", spread[:, :, :, 1], cos_x) + ein(
                "tcpi,xi->tcpx", spread[:, :, :, 0], sin_x
            )
            real = back_real * tc - back_imag * ts
            imag = back_imag * tc + back_real * ts
            return jnp.stack(
                [
                    ein("tcpx,ty->cpxy", real, cos_y) - ein("tcpx,ty->cpxy", imag, sin_y),
                    ein("tcpx,ty->cpxy", imag, cos_y) + ein("tcpx,ty->cpxy", real, sin_y),
                ],
                2,
            )

        def combined(images, g):
            map_real, map_imag = maps[g][:, :, 0], maps[g][:, :, 1]
            real, imag = images[:, :, 0], images[:, :, 1]
            return jnp.stack(
                [
                    jnp.sum(map_real * real + map_imag * imag, 0),
                    jnp.sum(map_real * imag - map_imag * real, 0),
                ],
                1,
            )

        def stacked_dots(values):
            values = values + [jnp.zeros((), f32)] * (8 - len(values))
            return jnp.broadcast_to(jnp.stack(values)[:, None], (8, 128))

        def applied_to(samples, vector, g):
            samples = added(samples).reshape(blocks, group_channels, size)
            return combined(images_of(samples, block_of), g) + damping * vector

        def measured_images():
            return images_of(measured.astype(f32), measured_block)

        def start(images, g):
            right_side = combined(images[:, g * group_planes : (g + 1) * group_planes], g)
            dots = stacked_dots([jnp.sum(right_side * right_side)])
            return right_side, right_side.astype(bf16), dots

        def first(samples, norms, right_side, g):
            norm = tree_sum(norms)[0, 0]
            total = added(samples)
            energy = jnp.sum(jnp.square(total))
            residual = right_side - step_of(norm, energy) * applied_to(samples, right_side, g)
            dots = [jnp.sum(residual * residual), jnp.sum(residual * right_side)]
            facts = stacked_dots([norm, energy])
            return residual, residual.astype(bf16), facts, stacked_dots(dots), total

        def second(samples, facts, residual, g):
            again = applied_to(samples, residual, g)
            return (residual - step_of(facts[0, 0], facts[1, 0]) * again).astype(bf16)

    def added(samples):
        return tree_sum([part.astype(f32) for part in samples])

    def sent_by_bits(own):
        return [swapped(own, "coil", k) for k in first_bits]

    images = measured_images()
    start_pieces, residual_pieces, mixed_own, mixed_sent, values = [], [], [], [], []
    for g in groups:
        right_side, start_own, norm = start(images, g)
        start_sent = sent_by_bits(start_own)
        samples = exchanged(forward(right_side, g))
        norms = exchanged(norm)
        samples, norms, start_sent = lax.optimization_barrier((samples, norms, start_sent))
        residual, residual_own, facts, dots, start_total = first(samples, norms, right_side, g)
        residual, residual_own, pieces = lax.optimization_barrier(
            (residual, residual_own, completed(start_own, start_sent))
        )
        start_pieces.append(pieces)
        residual_sent = sent_by_bits(residual_own)
        samples = exchanged(forward(residual, g))
        dots = exchanged(dots)
        samples, dots, residual_sent = lax.optimization_barrier((samples, dots, residual_sent))
        total = added(samples)
        square, cross = tree_sum(dots)[:2, 0]
        value = [facts[0, 0], facts[1, 0], square, cross]
        value += [jnp.sum(total * total), jnp.sum(total * start_total)]
        values.append(jnp.stack(value))
        rounded = second(samples, facts, residual, g)
        rounded, pieces = lax.optimization_barrier(
            (rounded, completed(residual_own, residual_sent))
        )
        residual_pieces.append(pieces)
        mixed_own.append(rounded)
        mixed_sent.append(sent_by_bits(rounded))

    values = jnp.stack(exchanged(jnp.stack(values), "coil"))
    values, mixed_sent[-1][0] = lax.optimization_barrier((values, mixed_sent[-1][0]))
    mixed_pieces = [completed(mixed_own[g], mixed_sent[g]) for g in groups]
    norm, energy, square, cross, again, mixed = [values[:, :, i] for i in range(6)]
    curve, mixed_curve = again + damping * square, mixed + damping * cross

    def over_all(value):
        return tree_sum([jnp.sum(value[k]) for k in range(coil_count)])

    sigma = step_of(norm, energy)
    start_norm = over_all(norm)
    first_step = start_norm / over_all(energy + damping * norm)
    part = first_step / sigma
    rest = 1.0 - part
    next_norm = over_all(part * part * square + 2.0 * part * rest * cross + rest * rest * norm)
    more = rest + next_norm / start_norm
    second_step = next_norm / over_all(
        part * part * curve
        + part * more * ((cross - square) / sigma + mixed_curve)
        + more * more * (energy + damping * norm)
    )
    share = second_step / sigma
    picture = jnp.zeros((planes, 2, rows, columns), f32)
    out = jnp.zeros((planes, 2, rows, columns), f32)
    for k in range(coil_count):
        for g in groups:
            place = ((coil_index ^ k) * own_planes + g * group_planes, 0, 0, 0)
            vector = start_pieces[g][k].astype(f32)
            known = residual_pieces[g][k].astype(f32)
            weight, ratio, length = part[k, g], more[k, g], share[k, g]
            piece = (first_step + second_step * ratio) * vector + second_step * weight * known
            picture = lax.dynamic_update_slice(picture, piece, place)
            piece = (weight - length * weight + length * ratio) * known
            piece += (rest[k, g] - length * ratio) * vector
            piece += length * weight * mixed_pieces[g][k].astype(f32)
            out = lax.dynamic_update_slice(out, piece, place)
    return picture, out


def solution(mesh):
    in_specs = (
        P("coil", "scan", None, "pencil"),
        P("coil", "scan", None, "pencil", None),
        P("pencil", None, None),
        P("pencil"),
        P("pencil"),
        P("pencil", None, None),
    )
    out_specs = (P("scan", None, "pencil", None), P("scan", None, "pencil", None))
    return jax.shard_map(
        on_device, mesh=mesh, in_specs=in_specs, out_specs=out_specs, check_vma=False
    )
```

```python
import functools
import math

import jax
import jax.numpy as jnp
from jax import lax
from jax.experimental import pallas as pl
from jax.experimental.pallas import tpu as pltpu
from jax.sharding import PartitionSpec as P


damping = 0.5
f32, bf16 = jnp.float32, jnp.bfloat16
vmem_limit = 56 * 1024 * 1024


def wave(left, right, length):
    phases = left[:, None] * right[None, :] % length
    angles = phases.astype(f32) * (2.0 * math.pi / length)
    return jnp.cos(angles) / math.sqrt(length), jnp.sin(angles) / math.sqrt(length)


def quarter_turns(left, right, count):
    turns = left[:, None] * right[None, :] % count
    if count == 4:
        cosine = jnp.where(turns == 0, 1.0, 0.0) - jnp.where(turns == 2, 1.0, 0.0)
        sine = jnp.where(turns == 1, 1.0, 0.0) - jnp.where(turns == 3, 1.0, 0.0)
        return cosine.astype(f32), sine.astype(f32)
    angles = turns.astype(f32) * (2.0 * math.pi / count)
    return jnp.cos(angles), jnp.sin(angles)


def split(value):
    high = value.astype(bf16)
    return high, (value - high.astype(f32)).astype(bf16)


def table_parts(table, axis):
    high = lax.reduce_precision(table, 8, 7)
    low = (table - high).astype(bf16)
    high = high.astype(bf16)
    return jnp.concatenate([high, high, low], axis)


def data_parts(value):
    high, low = split(value)
    return jnp.concatenate([high, low, high], 1)


def nt(left, right):
    return lax.dot_general(left, right, (((1,), (1,)), ((), ())), preferred_element_type=f32)


def nn(left, right):
    return jnp.dot(left, right, preferred_element_type=f32)


def tree_sum(values):
    while len(values) > 1:
        values = [left + right for left, right in zip(values[::2], values[1::2])]
    return values[0]


def forward_images(plane, planes, picture, sens, ey, mx, turn_ref, grid_ref):
    tiles = turn_ref.shape[1]
    rows = turn_ref.shape[2]
    channels = grid_ref.shape[0] // tiles
    real, imag = picture[0, 0], picture[0, 1]
    turned = []
    for sens_ref in sens:
        sens_real = sens_ref[0, 0, 0].astype(f32)
        sens_imag = sens_ref[0, 0, 1].astype(f32)
        coil = jnp.concatenate(
            [sens_real * real - sens_imag * imag, sens_real * imag + sens_imag * real], 0
        )
        both = nt(ey[...], coil.astype(bf16))
        half_real = both[:tiles, :rows] + both[tiles:, rows:]
        half_imag = both[:tiles, rows:] - both[tiles:, :rows]
        turned.append(
            jnp.concatenate(
                [
                    half_real * turn_ref[0] + half_imag * turn_ref[1],
                    half_imag * turn_ref[0] - half_real * turn_ref[1],
                ],
                1,
            ).astype(bf16)
        )
    grid = nn(jnp.concatenate(turned, 0), mx[...])
    size = grid.shape[1] // 2
    for coil in range(len(sens)):
        step = coil * planes + plane
        part = grid[coil * tiles : (coil + 1) * tiles]
        grid_ref[pl.ds(2 * step, tiles, stride=channels), :] = part[:, :size]
        grid_ref[pl.ds(2 * step + 1, tiles, stride=channels), :] = part[:, size:]


def sample_tiles(block_ref, weights, grid_ref, sums_ref, out_ref):
    count = weights[0].shape[0]
    channels = sums_ref.shape[1]
    sums_ref[...] = jnp.zeros_like(sums_ref)

    for group, weights_ref in enumerate(weights):

        def one(place, carry):
            tile = group * count + place
            start = pl.multiple_of(tile * channels, channels)
            value = grid_ref[pl.ds(start, channels), :]
            high = value.astype(bf16).astype(f32)
            both = jnp.concatenate([high, value - high], 0).astype(bf16)
            product = nn(both, weights_ref[place])
            sums_ref[block_ref[tile]] += product[:channels] + product[channels:]
            return carry

        lax.fori_loop(0, count, one, 0, unroll=True)
    out_ref[...] = sums_ref[...].reshape(out_ref.shape).astype(bf16)


def spread_tiles(block_ref, weights, parts_ref, grid_ref):
    count = weights[0].shape[0]
    channels = grid_ref.shape[0] // (count * len(weights))

    for group, weights_ref in enumerate(weights):

        def one(place, carry):
            tile = group * count + place
            start = pl.multiple_of(tile * channels, channels)
            product = nt(parts_ref[block_ref[tile]], weights_ref[place])
            if product.shape[0] > channels:
                product = product[:channels] + product[channels:]
            grid_ref[pl.ds(start, channels), :] = product
            return carry

        lax.fori_loop(0, count, one, 0, unroll=True)


def adjoint_images(coils, plane, planes, ey_back, mx_back, turn_ref, grid_ref):
    rows, tiles = turn_ref.shape[1], turn_ref.shape[2]
    channels = grid_ref.shape[0] // tiles
    grids = []
    for coil in range(coils):
        step = coil * planes + plane
        grid = jnp.concatenate(
            [
                grid_ref[pl.ds(2 * step, tiles, stride=channels), :],
                grid_ref[pl.ds(2 * step + 1, tiles, stride=channels), :],
            ],
            1,
        )
        grids.append(data_parts(grid))
    back = nt(mx_back[...], jnp.concatenate(grids, 0))
    turned = []
    for coil in range(coils):
        part = back[:, coil * tiles : (coil + 1) * tiles]
        both = jnp.concatenate(
            [
                part[:rows] * turn_ref[0] - part[rows:] * turn_ref[1],
                part[rows:] * turn_ref[0] + part[:rows] * turn_ref[1],
            ],
            1,
        )
        turned.append(data_parts(both))
    image = nn(jnp.concatenate(turned, 0), ey_back[...])
    columns = image.shape[1] // 2
    return [
        (image[c * rows : (c + 1) * rows, :columns], image[c * rows : (c + 1) * rows, columns:])
        for c in range(coils)
    ]


def add_dots(dots_ref, products):
    rows = lax.broadcasted_iota(jnp.int32, dots_ref.shape, 0)
    total = dots_ref[...]
    for place, (left, right) in enumerate(products):
        total += jnp.where(rows == place, jnp.sum(left * right), 0.0)
    dots_ref[...] = total


def measured_kernel(block, samples, *refs):
    *weights, mx, eb, turn, images, grid = refs
    plane = pl.program_id(0)
    coils = images.shape[0]

    @pl.when(plane == 0)
    def _():
        spread_tiles(block, weights, samples, grid)

    found = adjoint_images(coils, plane, pl.num_programs(0), eb, mx, turn, grid)
    for coil, (real, imag) in enumerate(found):
        images[coil, 0, 0] = real
        images[coil, 0, 1] = imag


def combine(images, sens):
    total_real = total_imag = 0.0
    for (real, imag), sens_ref in zip(images, sens):
        sens_real = sens_ref[0, 0, 0].astype(f32)
        sens_imag = sens_ref[0, 0, 1].astype(f32)
        total_real += sens_real * real + sens_imag * imag
        total_imag += sens_real * imag - sens_imag * real
    return total_real, total_imag


def start_kernel(images, *refs):
    *sens, right_side, rounded, dots = refs
    total = combine([(images[c, 0, 0], images[c, 0, 1]) for c in range(len(sens))], sens)
    for part in range(2):
        right_side[0, part] = total[part]
        rounded[0, part] = total[part].astype(bf16)

    @pl.when((pl.program_id(0) == 0) & (pl.program_id(1) == 0))
    def _():
        dots[...] = jnp.zeros_like(dots)

    add_dots(dots, [(right_side[0], right_side[0])])


def forward_kernel(coils, block, picture, *refs):
    sens = refs[:coils]
    *weights, ey, mx, turn, samples, grid, sums = refs[coils:]
    plane = pl.program_id(0)
    forward_images(plane, pl.num_programs(0), picture, sens, ey, mx, turn, grid)

    @pl.when(plane == pl.num_programs(0) - 1)
    def _():
        sample_tiles(block, weights, grid, sums, samples)


def summed_parts(samples, parts):
    summed = tree_sum([part[...].astype(f32) for part in samples])
    blocks, channels, size = parts.shape[0], parts.shape[1] // 2, parts.shape[2]
    value = summed.reshape(blocks, channels, size)
    high = value.astype(bf16).astype(f32)
    parts[...] = jnp.concatenate([high, value - high], 1).astype(bf16)
    return summed


def step_of(norm, energy):
    return jnp.where(norm > 0.0, norm / (energy + damping * norm), 1.0)


def first_kernel(peers, coils, block, *refs):
    samples, weights, sens = refs[:peers], refs[peers : 2 * peers], refs[2 * peers :][:coils]
    mx, eb, turn, *norms = refs[2 * peers + coils :][: 3 + peers]
    right_side, residual, rounded, facts, dots, total_samples, grid, parts = refs[-8:]
    plane = pl.program_id(0)

    @pl.when(plane == 0)
    def _():
        summed = summed_parts(samples, parts)
        total_samples[...] = summed
        rows = lax.broadcasted_iota(jnp.int32, facts.shape, 0)
        norm = tree_sum([part[...] for part in norms])
        facts[...] = jnp.where(rows == 1, jnp.sum(summed * summed), norm)
        dots[...] = jnp.zeros_like(dots)
        spread_tiles(block, weights, parts, grid)

    images = adjoint_images(coils, plane, pl.num_programs(0), eb, mx, turn, grid)
    total = combine(images, sens)
    scale = step_of(facts[0:1, 0:1], facts[1:2, 0:1])
    for part in range(2):
        vector = right_side[0, part]
        value = vector - scale * (total[part] + damping * vector)
        residual[0, part] = value
        rounded[0, part] = value.astype(bf16)
        add_dots(dots, [(value, value), (value, vector)])


def second_kernel(peers, coils, block, *refs):
    samples, weights, sens = refs[:peers], refs[peers : 2 * peers], refs[2 * peers :][:coils]
    mx, eb, turn, facts, residual, rounded, grid, parts = refs[2 * peers + coils :]
    plane = pl.program_id(0)

    @pl.when(plane == 0)
    def _():
        summed_parts(samples, parts)
        spread_tiles(block, weights, parts, grid)

    images = adjoint_images(coils, plane, pl.num_programs(0), eb, mx, turn, grid)
    total = combine(images, sens)
    scale = step_of(facts[0:1, 0:1], facts[1:2, 0:1])
    for part in range(2):
        vector = residual[0, part]
        again = total[part] + damping * vector
        rounded[0, part] = (vector - scale * again).astype(bf16)


def facts_kernel(peers, *refs):
    samples, dots = refs[:peers], refs[peers : 2 * peers]
    start_total, facts, out = refs[2 * peers :]
    summed = tree_sum([part[...].astype(f32) for part in samples])
    both = tree_sum([part[...] for part in dots])
    rows = lax.broadcasted_iota(jnp.int32, out.shape, 0)
    values = [facts[0:1], facts[1:2], both[0:1], both[1:2]]
    values += [jnp.sum(summed * summed), jnp.sum(summed * start_total[...])]
    total = jnp.zeros(out.shape, f32)
    for row, value in enumerate(values):
        total = jnp.where(rows == row, value, total)
    out[...] = total


def coefficients(norm, energy, square, cross, again, mixed):
    def over_all(values):
        return tree_sum([sum(of_coil) for of_coil in values])

    def each(function, *lists):
        return [[function(*items) for items in zip(*of_coil)] for of_coil in zip(*lists)]

    start_curve = each(lambda e, n: e + damping * n, energy, norm)
    curve = each(lambda e, n: e + damping * n, again, square)
    mixed_curve = each(lambda e, n: e + damping * n, mixed, cross)
    sigma = each(step_of, norm, energy)
    start_norm = over_all(norm)
    first_step = start_norm / over_all(start_curve)
    part = each(lambda s: first_step / s, sigma)
    next_norm = over_all(
        each(
            lambda w, n, c, s: w * w * s + 2.0 * w * (1.0 - w) * c + (1.0 - w) * (1.0 - w) * n,
            part,
            norm,
            cross,
            square,
        )
    )
    more = each(lambda w: 1.0 - w + next_norm / start_norm, part)
    second_step = next_norm / over_all(
        each(
            lambda w, m, q, c, s, z, qm, qs: w * w * q
            + w * m * ((c - s) / z + qm)
            + m * m * qs,
            part,
            more,
            curve,
            cross,
            square,
            sigma,
            mixed_curve,
            start_curve,
        )
    )
    share = each(lambda z: second_step / z, sigma)
    picture = each(lambda w, m: (first_step + second_step * m, second_step * w), part, more)
    residual = each(
        lambda w, m, h: (1.0 - w - h * m, w - h * w + h * m, h * w), part, more, share
    )
    return picture, residual


def assemble_kernel(coils, group_steps, combos, is_residual, order, *refs):
    infos, pieces, out = refs[:coils], refs[coils:-1], refs[-1]
    groups = infos[0].shape[0]
    numbers = [
        [[info[g, row : row + 1, 0:1] for g in range(groups)] for info in infos]
        for row in range(6)
    ]
    factors = coefficients(*numbers)[is_residual]
    count = 3 if is_residual else 2
    for place, (k, g) in enumerate(combos):

        @pl.when(pl.program_id(0) // group_steps == place)
        def _():
            total = 0.0
            for factor, piece in zip(factors[k][g], pieces[place * count :][:count]):
                total += factor.reshape(1, 1, 1, 1) * piece[...].astype(f32)
            out[...] = total


def group_count_of(own_planes):
    return 1


def whole_block(array):
    rank = len(array.shape)
    return pl.BlockSpec(array.shape, lambda *_: (0,) * rank)


def on_device(kspace, sens_maps, weights, tile_slot, tile_block, send_list):
    coil_count = lax.axis_size("coil")
    peers = lax.axis_size("pencil")
    planes = sens_maps.shape[1]
    own_planes = planes // coil_count
    rows = sens_maps.shape[3]
    columns = sens_maps.shape[4]
    rows_total = rows * peers
    size = weights.shape[1]
    tile_count = tile_slot.shape[0]
    tiles = tile_count * peers
    blocks_dev = kspace.shape[3] // size
    blocks = blocks_dev * peers
    cap = send_list.shape[2]
    runs = rows_total // size
    brick_dev = columns // peers * runs
    images_count = coil_count * own_planes
    channels = 2 * images_count

    coil_index = lax.axis_index("coil")

    def swapped(array, axis, k):
        return lax.ppermute(array, axis, [(i, i ^ k) for i in range(lax.axis_size(axis))])

    def everywhere(array, axis):
        bit = 1
        while bit < lax.axis_size(axis):
            bit *= 2
        pieces = {0: array}
        while bit > 1:
            bit //= 2
            for k in sorted(pieces):
                pieces[k ^ bit] = swapped(pieces[k], axis, bit)
        return [pieces[k] for k in sorted(pieces)]

    first_bits = [1 << bit for bit in range(coil_count.bit_length() - 1)]

    def completed(own, sent):
        pieces = {0: own}
        for bit, piece in zip(first_bits, sent):
            pieces[bit] = piece
        for bit in first_bits:
            for k in range(coil_count):
                if k not in pieces and (k ^ bit) in pieces:
                    pieces[k] = swapped(pieces[k ^ bit], "coil", bit)
        return [pieces[k] for k in range(coil_count)]

    def to_planes(array):
        pieces = []
        for k in range(coil_count):
            part = lax.dynamic_slice_in_dim(array, (coil_index ^ k) * own_planes, own_planes, 0)
            pieces.append(swapped(part, "coil", k) if k > 0 else part)
        return pieces

    group_planes = own_planes // group_count_of(own_planes)
    groups = range(own_planes // group_planes)
    measured = to_planes(kspace[0])
    packed = jnp.concatenate([tile_slot, tile_block, send_list.reshape(-1)])
    sens_source, packed, measured = lax.optimization_barrier((sens_maps[0], packed, measured))
    sens_source = sens_source.reshape(coil_count, own_planes, 2, rows, columns)
    sens = [
        lax.all_to_all(
            sens_source[:, g * group_planes : (g + 1) * group_planes],
            "coil",
            split_axis=0,
            concat_axis=0,
            tiled=True,
        )
        for g in groups
    ]
    measured = jnp.stack(measured)
    by_coil = jnp.arange(coil_count, dtype=jnp.int32) ^ coil_index
    measured = jnp.take(measured, by_coil, axis=0)
    all_weights = everywhere(weights, "pencil")

    places = jnp.stack(everywhere(packed, "pencil"))
    holder = (jnp.arange(peers, dtype=jnp.int32) ^ lax.axis_index("pencil"))[:, None]
    by_owner = jnp.take(places, holder[:, 0], axis=0)
    lists = by_owner[:, 2 * tile_count :].reshape(peers, peers, cap)
    slots = places[:, :tile_count]
    block_of = (places[:, tile_count : 2 * tile_count] + blocks_dev * holder).reshape(-1)
    brick = (slots // cap * brick_dev + lists[slots // cap, holder, slots % cap]).reshape(-1)
    line = brick // runs
    run = brick % runs

    measured = measured.reshape(channels, blocks_dev, size)
    measured = jnp.concatenate(everywhere(jnp.swapaxes(measured, 0, 1), "pencil"), 0)
    measured_block = (
        places[:, tile_count : 2 * tile_count]
        + blocks_dev * jnp.arange(peers, dtype=jnp.int32)[:, None]
    ).reshape(-1)

    cos_y, sin_y = wave(
        line - columns // 2, jnp.arange(columns, dtype=jnp.int32) - columns // 2, columns
    )
    row_ids = jnp.arange(rows, dtype=jnp.int32) + lax.axis_index("pencil") * rows - rows_total // 2
    cos_x, sin_x = wave(
        row_ids, jnp.arange(size, dtype=jnp.int32) - rows_total // 2, rows_total
    )
    turn = jnp.stack(quarter_turns(run, row_ids, runs))
    turn_back = jnp.stack(quarter_turns(row_ids, run, runs))

    def exchanged(partial, axis="pencil"):
        count = lax.axis_size(axis)
        return [partial] + [swapped(partial, axis, k) for k in range(1, count)]

    group_shape = (group_planes, 2, rows, columns)
    group_images = coil_count * group_planes
    group_channels = 2 * group_images

    if (
        rows % 128 == 0
        and columns % 128 == 0
        and size % 128 == 0
        and channels % 16 == 0
        and group_channels % 8 == 0
    ):
        ey = jnp.concatenate([cos_y, sin_y], 0).astype(bf16)
        eb = jnp.concatenate(
            [jnp.concatenate([cos_y, sin_y], 1), jnp.concatenate([-sin_y, cos_y], 1)], 0
        )
        eb = table_parts(eb, 0)
        mx = jnp.concatenate(
            [jnp.concatenate([cos_x, -sin_x], 1), jnp.concatenate([sin_x, cos_x], 1)], 0
        )
        mx, mx_back = mx.astype(bf16), table_parts(mx, 1)
        measured, ey, mx, turn, block_of = lax.optimization_barrier(
            (measured, ey, mx, turn, block_of)
        )
        places_spec = pl.BlockSpec(memory_space=pltpu.SMEM)
        plane_spec = pl.BlockSpec((1, 2, rows, columns), lambda p: (p, 0, 0, 0))
        sens_specs = [
            pl.BlockSpec((1, 1, 2, rows, columns), functools.partial(lambda c, p: (c, p, 0, 0, 0), c))
            for c in range(coil_count)
        ]
        grid_scratch = pltpu.VMEM((tiles * group_channels, size), f32)
        params = pltpu.CompilerParams(vmem_limit_bytes=vmem_limit)
        tail_tables = [mx_back, eb, turn_back]

        def shaped(shape, dtype=f32):
            return jax.ShapeDtypeStruct(shape, dtype)

        def call(kernel, grid, inputs, specs, outs, out_specs, scratch, images):
            flops = 2 * images * 8 * tiles * rows * (columns + size)
            return pl.pallas_call(
                kernel,
                grid=grid,
                in_specs=specs,
                out_specs=out_specs,
                out_shape=outs,
                scratch_shapes=scratch,
                compiler_params=params,
                cost_estimate=pl.CostEstimate(
                    flops=flops,
                    bytes_accessed=sum(math.prod(i.shape) * i.dtype.itemsize for i in inputs),
                    transcendentals=0,
                ),
            )(*inputs)

        def measured_images():
            inputs = [measured_block, measured, *all_weights, *tail_tables]
            shape = (coil_count, own_planes, 2, rows, columns)
            return call(
                measured_kernel,
                (own_planes,),
                inputs,
                [places_spec] + [whole_block(i) for i in inputs[1:]],
                shaped(shape),
                pl.BlockSpec((coil_count, 1, 2, rows, columns), lambda p: (0, p, 0, 0, 0)),
                [pltpu.VMEM((tiles * channels, size), f32)],
                images_count,
            )

        def start(images, g):
            chunk = 64
            spec = pl.BlockSpec((1, 2, chunk, columns), lambda p, r: (p, 0, r, 0))
            images_spec = pl.BlockSpec(
                (coil_count, 1, 2, chunk, columns),
                lambda p, r: (0, p + g * group_planes, 0, r, 0),
            )
            dots_shape = shaped((8, 128))
            return call(
                start_kernel,
                (group_planes, rows // chunk),
                [images] + [sens[g]] * coil_count,
                [images_spec]
                + [
                    pl.BlockSpec(
                        (1, 1, 2, chunk, columns),
                        functools.partial(lambda c, p, r: (c, p, 0, r, 0), c),
                    )
                    for c in range(coil_count)
                ],
                [shaped(group_shape), shaped(group_shape, bf16), dots_shape],
                [spec, spec, whole_block(dots_shape)],
                [],
                0,
            )

        def forward(picture, g):
            tail = [*all_weights, ey, mx, turn]
            out = shaped((blocks * group_channels, size), bf16)
            return call(
                functools.partial(forward_kernel, coil_count),
                (group_planes,),
                [block_of, picture] + [sens[g]] * coil_count + tail,
                [places_spec, plane_spec] + sens_specs + [whole_block(i) for i in tail],
                out,
                whole_block(out),
                [grid_scratch, pltpu.VMEM((blocks, group_channels, size), f32)],
                group_images,
            )

        def back(kernel, samples, tables, vectors, g, outs, out_specs):
            inputs = [*samples, *all_weights]
            tables = tail_tables + tables
            return call(
                functools.partial(kernel, peers, coil_count),
                (group_planes,),
                [block_of, *inputs] + [sens[g]] * coil_count + tables + vectors,
                [places_spec]
                + [whole_block(i) for i in inputs]
                + sens_specs
                + [whole_block(i) for i in tables]
                + [plane_spec] * len(vectors),
                outs,
                out_specs,
                [grid_scratch, pltpu.VMEM((blocks, 2 * group_channels, size), bf16)],
                group_images,
            )

        def first(samples, norms, right_side, g):
            small, large = shaped((8, 128)), shaped(samples[0].shape)
            return back(
                first_kernel,
                samples,
                norms,
                [right_side],
                g,
                [shaped(group_shape), shaped(group_shape, bf16), small, small, large],
                [plane_spec, plane_spec] + [whole_block(i) for i in (small, small, large)],
            )

        def facts_of(samples, dots, start_total, facts):
            inputs = [*samples, *dots, start_total, facts]
            return pl.pallas_call(
                functools.partial(facts_kernel, peers),
                in_specs=[pl.BlockSpec(memory_space=pltpu.VMEM)] * len(inputs),
                out_specs=pl.BlockSpec(memory_space=pltpu.VMEM),
                out_shape=shaped((8, 128)),
                compiler_params=params,
            )(*inputs)

        def assembled(infos, vectors, ks, out=None):
            combos = [(k, g) for k in ks for g in groups]
            order = jnp.stack(
                [
                    (coil_index ^ k) * own_planes + g * group_planes + p
                    for k, g in combos
                    for p in range(group_planes)
                ]
            ).astype(jnp.int32)
            inputs = [vector[g][k] for k, g in combos for vector in vectors]

            def spec(place):
                first_step = place // len(vectors) * group_planes
                return pl.BlockSpec(
                    (1, 2, rows, columns),
                    lambda i, o: (jnp.clip(i - first_step, 0, group_planes - 1), 0, 0, 0),
                )

            specs = [pl.BlockSpec(infos[0].shape, lambda i, o: (0, 0, 0))] * len(infos)
            specs += [spec(place) for place in range(len(inputs))]
            aliases = {}
            kernel = functools.partial(
                assemble_kernel, coil_count, group_planes, combos, len(vectors) == 3
            )
            if out is not None:
                aliases = {1 + len(infos) + len(inputs): 0}
                inner = kernel
                inputs = inputs + [out]
                specs.append(pl.BlockSpec(memory_space=pl.ANY))

                def kernel(*refs):
                    inner(*refs[:-2], refs[-1])

            return pl.pallas_call(
                kernel,
                grid_spec=pltpu.PrefetchScalarGridSpec(
                    num_scalar_prefetch=1,
                    grid=(len(combos) * group_planes,),
                    in_specs=specs,
                    out_specs=pl.BlockSpec((1, 2, rows, columns), lambda i, o: (o[i], 0, 0, 0)),
                ),
                out_shape=shaped((planes, 2, rows, columns)),
                input_output_aliases=aliases,
                compiler_params=params,
            )(order, *infos, *inputs)

        def second(samples, facts, residual, g):
            return back(
                second_kernel,
                samples,
                [facts],
                [residual],
                g,
                shaped(group_shape, bf16),
                plane_spec,
            )

    else:
        ein = functools.partial(jnp.einsum, precision=lax.Precision.HIGH)
        maps = [array.astype(f32) for array in sens]
        block_map = (block_of[:, None] == jnp.arange(blocks, dtype=jnp.int32)).astype(f32)
        tc, ts = turn[0][:, None, None], turn[1][:, None, None]
        wide_weights = jnp.concatenate(all_weights, 0).astype(f32)

        def forward(picture, g):
            map_real, map_imag = maps[g][:, :, 0], maps[g][:, :, 1]
            coil_real = map_real * picture[None, :, 0] - map_imag * picture[None, :, 1]
            coil_imag = map_real * picture[None, :, 1] + map_imag * picture[None, :, 0]
            half_real = ein("ty,cpxy->tcpx", cos_y, coil_real) + ein(
                "ty,cpxy->tcpx", sin_y, coil_imag
            )
            half_imag = ein("ty,cpxy->tcpx", cos_y, coil_imag) - ein(
                "ty,cpxy->tcpx", sin_y, coil_real
            )
            real = half_real * tc + half_imag * ts
            imag = half_imag * tc - half_real * ts
            grid = jnp.stack(
                [
                    ein("tcpx,xi->tcpi", real, cos_x) + ein("tcpx,xi->tcpi", imag, sin_x),
                    ein("tcpx,xi->tcpi", imag, cos_x) - ein("tcpx,xi->tcpi", real, sin_x),
                ],
                3,
            ).reshape(tiles, group_channels, size)
            product = ein("tgi,tis->tgs", grid, wide_weights)
            return ein("tb,tgs->bgs", block_map, product).astype(bf16).reshape(-1, size)

        def images_of(samples, blocks_of):
            spread = ein("tgs,tis->tgi", jnp.take(samples, blocks_of, axis=0), wide_weights)
            spread = spread.reshape(tiles, coil_count, -1, 2, size)
            back_real = ein("tcpi,xi->tcpx", spread[:, :, :, 0], cos_x) - ein(
                "tcpi,xi->tcpx", spread[:, :, :, 1], sin_x
            )
            back_imag = ein("tcpi,xi->tcpx", spread[:, :, :, 1], cos_x) + ein(
                "tcpi,xi->tcpx", spread[:, :, :, 0], sin_x
            )
            real = back_real * tc - back_imag * ts
            imag = back_imag * tc + back_real * ts
            return jnp.stack(
                [
                    ein("tcpx,ty->cpxy", real, cos_y) - ein("tcpx,ty->cpxy", imag, sin_y),
                    ein("tcpx,ty->cpxy", imag, cos_y) + ein("tcpx,ty->cpxy", real, sin_y),
                ],
                2,
            )

        def combined(images, g):
            map_real, map_imag = maps[g][:, :, 0], maps[g][:, :, 1]
            real, imag = images[:, :, 0], images[:, :, 1]
            return jnp.stack(
                [
                    jnp.sum(map_real * real + map_imag * imag, 0),
                    jnp.sum(map_real * imag - map_imag * real, 0),
                ],
                1,
            )

        def stacked_dots(values):
            values = values + [jnp.zeros((), f32)] * (8 - len(values))
            return jnp.broadcast_to(jnp.stack(values)[:, None], (8, 128))

        def applied_to(samples, vector, g):
            samples = added(samples).reshape(blocks, group_channels, size)
            return combined(images_of(samples, block_of), g) + damping * vector

        def measured_images():
            return images_of(measured.astype(f32), measured_block)

        def start(images, g):
            right_side = combined(images[:, g * group_planes : (g + 1) * group_planes], g)
            dots = stacked_dots([jnp.sum(right_side * right_side)])
            return right_side, right_side.astype(bf16), dots

        def first(samples, norms, right_side, g):
            norm = tree_sum(norms)[0, 0]
            total = added(samples)
            energy = jnp.sum(jnp.square(total))
            residual = right_side - step_of(norm, energy) * applied_to(samples, right_side, g)
            dots = [jnp.sum(residual * residual), jnp.sum(residual * right_side)]
            facts = stacked_dots([norm, energy])
            return residual, residual.astype(bf16), facts, stacked_dots(dots), total

        def facts_of(samples, dots, start_total, facts):
            total = added(samples)
            square, cross = tree_sum(dots)[:2, 0]
            values = [facts[0, 0], facts[1, 0], square, cross]
            values += [jnp.sum(total * total), jnp.sum(total * start_total)]
            return stacked_dots(values)

        def assembled(infos, vectors, ks, out=None):
            numbers = [
                [[info[g, row, 0] for g in groups] for info in infos] for row in range(6)
            ]
            factors = coefficients(*numbers)[len(vectors) == 3]
            if out is None:
                out = jnp.zeros((planes, 2, rows, columns), f32)
            for k in ks:
                for g in groups:
                    place = ((coil_index ^ k) * own_planes + g * group_planes, 0, 0, 0)
                    piece = sum(
                        factor * vector[g][k].astype(f32)
                        for factor, vector in zip(factors[k][g], vectors)
                    )
                    out = lax.dynamic_update_slice(out, piece, place)
            return out

        def second(samples, facts, residual, g):
            again = applied_to(samples, residual, g)
            return (residual - step_of(facts[0, 0], facts[1, 0]) * again).astype(bf16)

    def added(samples):
        return tree_sum([part.astype(f32) for part in samples])

    def sent_by_bits(own):
        return [swapped(own, "coil", k) for k in first_bits]

    images = measured_images()
    start_pieces, residual_pieces, mixed_pieces, infos = [], [], [], []
    for g in groups:
        right_side, start_own, norm = start(images, g)
        start_sent = sent_by_bits(start_own)
        samples = exchanged(forward(right_side, g))
        norms = exchanged(norm)
        samples, norms, start_sent = lax.optimization_barrier((samples, norms, start_sent))
        residual, residual_own, facts, dots, start_total = first(samples, norms, right_side, g)
        residual, residual_own, pieces = lax.optimization_barrier(
            (residual, residual_own, completed(start_own, start_sent))
        )
        start_pieces.append(pieces)
        residual_sent = sent_by_bits(residual_own)
        samples = exchanged(forward(residual, g))
        dots = exchanged(dots)
        samples, dots, residual_sent = lax.optimization_barrier((samples, dots, residual_sent))
        info = facts_of(samples, dots, start_total, facts)
        infos.append(info)
        rounded = second(samples, info, residual, g)
        last = g == groups[-1]
        others = exchanged(jnp.stack(infos), "coil") if last else []
        rounded, others, pieces = lax.optimization_barrier(
            (rounded, others, completed(residual_own, residual_sent))
        )
        residual_pieces.append(pieces)
        mixed_pieces.append(completed(rounded, sent_by_bits(rounded)))

    picture = assembled(others, [start_pieces, residual_pieces], range(coil_count))
    vectors = [start_pieces, residual_pieces, mixed_pieces]
    out = assembled(others, vectors, range(coil_count - 1))
    out = assembled(others, vectors, [coil_count - 1], out)
    return picture, out


def solution(mesh):
    in_specs = (
        P("coil", "scan", None, "pencil"),
        P("coil", "scan", None, "pencil", None),
        P("pencil", None, None),
        P("pencil"),
        P("pencil"),
        P("pencil", None, None),
    )
    out_specs = (P("scan", None, "pencil", None), P("scan", None, "pencil", None))
    return jax.shard_map(
        on_device, mesh=mesh, in_specs=in_specs, out_specs=out_specs, check_vma=False
    )
```

```python
import functools
import math

import jax
import jax.numpy as jnp
from jax import lax
from jax.experimental import pallas as pl
from jax.experimental.pallas import tpu as pltpu
from jax.sharding import PartitionSpec as P


damping = 0.5
f32, bf16 = jnp.float32, jnp.bfloat16
vmem_limit = 56 * 1024 * 1024


def wave(left, right, length):
    phases = left[:, None] * right[None, :] % length
    angles = phases.astype(f32) * (2.0 * math.pi / length)
    return jnp.cos(angles) / math.sqrt(length), jnp.sin(angles) / math.sqrt(length)


def quarter_turns(left, right, count):
    turns = left[:, None] * right[None, :] % count
    if count == 4:
        cosine = jnp.where(turns == 0, 1.0, 0.0) - jnp.where(turns == 2, 1.0, 0.0)
        sine = jnp.where(turns == 1, 1.0, 0.0) - jnp.where(turns == 3, 1.0, 0.0)
        return cosine.astype(f32), sine.astype(f32)
    angles = turns.astype(f32) * (2.0 * math.pi / count)
    return jnp.cos(angles), jnp.sin(angles)


def split(value):
    high = value.astype(bf16)
    return high, (value - high.astype(f32)).astype(bf16)


def table_parts(table, axis):
    high = lax.reduce_precision(table, 8, 7)
    low = (table - high).astype(bf16)
    high = high.astype(bf16)
    return jnp.concatenate([high, high, low], axis)


def data_parts(value):
    high, low = split(value)
    return jnp.concatenate([high, low, high], 1)


def nt(left, right):
    return lax.dot_general(left, right, (((1,), (1,)), ((), ())), preferred_element_type=f32)


def nn(left, right):
    return jnp.dot(left, right, preferred_element_type=f32)


def tree_sum(values):
    while len(values) > 1:
        values = [left + right for left, right in zip(values[::2], values[1::2])]
    return values[0]


def forward_images(plane, planes, picture, sens, ey, mx, turn_ref, grid_ref):
    tiles = turn_ref.shape[1]
    rows = turn_ref.shape[2]
    channels = grid_ref.shape[0] // tiles
    real, imag = picture[0, 0], picture[0, 1]
    turned = []
    for sens_ref in sens:
        sens_real = sens_ref[0, 0, 0].astype(f32)
        sens_imag = sens_ref[0, 0, 1].astype(f32)
        coil = jnp.concatenate(
            [sens_real * real - sens_imag * imag, sens_real * imag + sens_imag * real], 0
        )
        both = nt(ey[...], coil.astype(bf16))
        half_real = both[:tiles, :rows] + both[tiles:, rows:]
        half_imag = both[:tiles, rows:] - both[tiles:, :rows]
        turned.append(
            jnp.concatenate(
                [
                    half_real * turn_ref[0] + half_imag * turn_ref[1],
                    half_imag * turn_ref[0] - half_real * turn_ref[1],
                ],
                1,
            ).astype(bf16)
        )
    grid = nn(jnp.concatenate(turned, 0), mx[...])
    size = grid.shape[1] // 2
    for coil in range(len(sens)):
        step = coil * planes + plane
        part = grid[coil * tiles : (coil + 1) * tiles]
        grid_ref[pl.ds(2 * step, tiles, stride=channels), :] = part[:, :size]
        grid_ref[pl.ds(2 * step + 1, tiles, stride=channels), :] = part[:, size:]


def sample_tiles(block_ref, weights, grid_ref, sums_ref, out_ref):
    count = weights[0].shape[0]
    channels = sums_ref.shape[1]
    sums_ref[...] = jnp.zeros_like(sums_ref)

    for group, weights_ref in enumerate(weights):

        def one(place, carry):
            tile = group * count + place
            start = pl.multiple_of(tile * channels, channels)
            value = grid_ref[pl.ds(start, channels), :]
            high = value.astype(bf16).astype(f32)
            both = jnp.concatenate([high, value - high], 0).astype(bf16)
            product = nn(both, weights_ref[place])
            sums_ref[block_ref[tile]] += product[:channels] + product[channels:]
            return carry

        lax.fori_loop(0, count, one, 0, unroll=True)
    out_ref[...] = sums_ref[...].reshape(out_ref.shape).astype(bf16)


def spread_tiles(block_ref, weights, parts_ref, grid_ref):
    count = weights[0].shape[0]
    channels = grid_ref.shape[0] // (count * len(weights))

    for group, weights_ref in enumerate(weights):

        def one(place, carry):
            tile = group * count + place
            start = pl.multiple_of(tile * channels, channels)
            product = nt(parts_ref[block_ref[tile]], weights_ref[place])
            if product.shape[0] > channels:
                product = product[:channels] + product[channels:]
            grid_ref[pl.ds(start, channels), :] = product
            return carry

        lax.fori_loop(0, count, one, 0, unroll=True)


def adjoint_images(coils, plane, planes, ey_back, mx_back, turn_ref, grid_ref):
    rows, tiles = turn_ref.shape[1], turn_ref.shape[2]
    channels = grid_ref.shape[0] // tiles
    grids = []
    for coil in range(coils):
        step = coil * planes + plane
        grid = jnp.concatenate(
            [
                grid_ref[pl.ds(2 * step, tiles, stride=channels), :],
                grid_ref[pl.ds(2 * step + 1, tiles, stride=channels), :],
            ],
            1,
        )
        grids.append(data_parts(grid))
    back = nt(mx_back[...], jnp.concatenate(grids, 0))
    turned = []
    for coil in range(coils):
        part = back[:, coil * tiles : (coil + 1) * tiles]
        both = jnp.concatenate(
            [
                part[:rows] * turn_ref[0] - part[rows:] * turn_ref[1],
                part[rows:] * turn_ref[0] + part[:rows] * turn_ref[1],
            ],
            1,
        )
        turned.append(data_parts(both))
    image = nn(jnp.concatenate(turned, 0), ey_back[...])
    columns = image.shape[1] // 2
    return [
        (image[c * rows : (c + 1) * rows, :columns], image[c * rows : (c + 1) * rows, columns:])
        for c in range(coils)
    ]


def add_dots(dots_ref, products):
    rows = lax.broadcasted_iota(jnp.int32, dots_ref.shape, 0)
    total = dots_ref[...]
    for place, (left, right) in enumerate(products):
        total += jnp.where(rows == place, jnp.sum(left * right), 0.0)
    dots_ref[...] = total


def measured_kernel(block, samples, *refs):
    *weights, mx, eb, turn, images, grid = refs
    plane = pl.program_id(0)
    coils = images.shape[0]

    @pl.when(plane == 0)
    def _():
        spread_tiles(block, weights, samples, grid)

    found = adjoint_images(coils, plane, pl.num_programs(0), eb, mx, turn, grid)
    for coil, (real, imag) in enumerate(found):
        images[coil, 0, 0] = real
        images[coil, 0, 1] = imag


def combine(images, sens):
    total_real = total_imag = 0.0
    for (real, imag), sens_ref in zip(images, sens):
        sens_real = sens_ref[0, 0, 0].astype(f32)
        sens_imag = sens_ref[0, 0, 1].astype(f32)
        total_real += sens_real * real + sens_imag * imag
        total_imag += sens_real * imag - sens_imag * real
    return total_real, total_imag


def start_kernel(images, *refs):
    *sens, right_side, rounded, dots = refs
    total = combine([(images[c, 0, 0], images[c, 0, 1]) for c in range(len(sens))], sens)
    for part in range(2):
        right_side[0, part] = total[part]
        rounded[0, part] = total[part].astype(bf16)

    @pl.when((pl.program_id(0) == 0) & (pl.program_id(1) == 0))
    def _():
        dots[...] = jnp.zeros_like(dots)

    add_dots(dots, [(right_side[0], right_side[0])])


def forward_kernel(coils, block, picture, *refs):
    sens = refs[:coils]
    *weights, ey, mx, turn, samples, grid, sums = refs[coils:]
    plane = pl.program_id(0)
    forward_images(plane, pl.num_programs(0), picture, sens, ey, mx, turn, grid)

    @pl.when(plane == pl.num_programs(0) - 1)
    def _():
        sample_tiles(block, weights, grid, sums, samples)


def summed_parts(samples, parts):
    summed = tree_sum([part[...].astype(f32) for part in samples])
    blocks, channels, size = parts.shape[0], parts.shape[1] // 2, parts.shape[2]
    value = summed.reshape(blocks, channels, size)
    high = value.astype(bf16).astype(f32)
    parts[...] = jnp.concatenate([high, value - high], 1).astype(bf16)
    return summed


def step_of(norm, energy):
    return jnp.where(norm > 0.0, norm / (energy + damping * norm), 1.0)


def first_kernel(peers, coils, block, *refs):
    samples, weights, sens = refs[:peers], refs[peers : 2 * peers], refs[2 * peers :][:coils]
    mx, eb, turn, *norms = refs[2 * peers + coils :][: 3 + peers]
    right_side, residual, rounded, facts, dots, total_samples, grid, parts = refs[-8:]
    plane = pl.program_id(0)

    @pl.when(plane == 0)
    def _():
        summed = summed_parts(samples, parts)
        total_samples[...] = summed
        rows = lax.broadcasted_iota(jnp.int32, facts.shape, 0)
        norm = tree_sum([part[...] for part in norms])
        facts[...] = jnp.where(rows == 1, jnp.sum(summed * summed), norm)
        dots[...] = jnp.zeros_like(dots)
        spread_tiles(block, weights, parts, grid)

    images = adjoint_images(coils, plane, pl.num_programs(0), eb, mx, turn, grid)
    total = combine(images, sens)
    scale = step_of(facts[0:1, 0:1], facts[1:2, 0:1])
    for part in range(2):
        vector = right_side[0, part]
        value = vector - scale * (total[part] + damping * vector)
        residual[0, part] = value
        rounded[0, part] = value.astype(bf16)
        add_dots(dots, [(value, value), (value, vector)])


def second_kernel(peers, coils, block, *refs):
    samples, weights, sens = refs[:peers], refs[peers : 2 * peers], refs[2 * peers :][:coils]
    mx, eb, turn, facts, residual, rounded, grid, parts = refs[2 * peers + coils :]
    plane = pl.program_id(0)

    @pl.when(plane == 0)
    def _():
        summed_parts(samples, parts)
        spread_tiles(block, weights, parts, grid)

    images = adjoint_images(coils, plane, pl.num_programs(0), eb, mx, turn, grid)
    total = combine(images, sens)
    scale = step_of(facts[0:1, 0:1], facts[1:2, 0:1])
    for part in range(2):
        vector = residual[0, part]
        again = total[part] + damping * vector
        rounded[0, part] = (vector - scale * again).astype(bf16)


def facts_kernel(peers, *refs):
    samples = refs[:peers]
    dots, start_total, facts, out = refs[peers:]
    summed = tree_sum([part[...].astype(f32) for part in samples])
    rows = lax.broadcasted_iota(jnp.int32, out.shape, 0)
    values = [facts[0:1], facts[1:2], dots[0:1], dots[1:2]]
    values += [jnp.sum(summed * summed), jnp.sum(summed * start_total[...])]
    total = jnp.zeros(out.shape, f32)
    for row, value in enumerate(values):
        total = jnp.where(rows == row, value, total)
    out[...] = total


def coefficients(norm, energy, square, cross, again, mixed):
    def over_all(values):
        return tree_sum([sum(of_coil) for of_coil in values])

    def each(function, *lists):
        return [[function(*items) for items in zip(*of_coil)] for of_coil in zip(*lists)]

    start_curve = each(lambda e, n: e + damping * n, energy, norm)
    curve = each(lambda e, n: e + damping * n, again, square)
    mixed_curve = each(lambda e, n: e + damping * n, mixed, cross)
    sigma = each(step_of, norm, energy)
    start_norm = over_all(norm)
    first_step = start_norm / over_all(start_curve)
    part = each(lambda s: first_step / s, sigma)
    next_norm = over_all(
        each(
            lambda w, n, c, s: w * w * s + 2.0 * w * (1.0 - w) * c + (1.0 - w) * (1.0 - w) * n,
            part,
            norm,
            cross,
            square,
        )
    )
    more = each(lambda w: 1.0 - w + next_norm / start_norm, part)
    second_step = next_norm / over_all(
        each(
            lambda w, m, q, c, s, z, qm, qs: w * w * q
            + w * m * ((c - s) / z + qm)
            + m * m * qs,
            part,
            more,
            curve,
            cross,
            square,
            sigma,
            mixed_curve,
            start_curve,
        )
    )
    share = each(lambda z: second_step / z, sigma)
    picture = each(lambda w, m: (first_step + second_step * m, second_step * w), part, more)
    residual = each(
        lambda w, m, h: (1.0 - w - h * m, w - h * w + h * m, h * w), part, more, share
    )
    return picture, residual


def assemble_kernel(coils, group_steps, combos, is_residual, has_out, order, *refs):
    infos, pieces, (out, kept) = refs[:coils], refs[coils:-2], refs[-2:]
    groups = infos[0].shape[0]
    count = 3 if is_residual else 2

    @pl.when(pl.program_id(0) == 0)
    def _():
        numbers = [
            [[info[g, row : row + 1, 0:1] for g in range(groups)] for info in infos]
            for row in range(6)
        ]
        factors = coefficients(*numbers)[is_residual]
        rows = lax.broadcasted_iota(jnp.int32, kept.shape[1:], 0)
        for place, (k, g) in enumerate(combos):
            total = jnp.zeros(kept.shape[1:], f32)
            for row, factor in enumerate(factors[k][g]):
                total = jnp.where(rows == row, factor, total)
            kept[place] = total

    for place in range(len(combos)):

        @pl.when(pl.program_id(0) // group_steps == place)
        def _():
            total = 0.0
            for row, piece in enumerate(pieces[place * count :][:count]):
                factor = kept[place, row : row + 1, 0:1].reshape(1, 1, 1, 1)
                total += factor * piece[...].astype(f32)
            out[...] = total


def group_count_of(own_planes):
    return 1


def whole_block(array):
    rank = len(array.shape)
    return pl.BlockSpec(array.shape, lambda *_: (0,) * rank)


def on_device(kspace, sens_maps, weights, tile_slot, tile_block, send_list):
    coil_count = lax.axis_size("coil")
    peers = lax.axis_size("pencil")
    planes = sens_maps.shape[1]
    own_planes = planes // coil_count
    rows = sens_maps.shape[3]
    columns = sens_maps.shape[4]
    rows_total = rows * peers
    size = weights.shape[1]
    tile_count = tile_slot.shape[0]
    tiles = tile_count * peers
    blocks_dev = kspace.shape[3] // size
    blocks = blocks_dev * peers
    cap = send_list.shape[2]
    runs = rows_total // size
    brick_dev = columns // peers * runs
    images_count = coil_count * own_planes
    channels = 2 * images_count

    coil_index = lax.axis_index("coil")

    def swapped(array, axis, k):
        return lax.ppermute(array, axis, [(i, i ^ k) for i in range(lax.axis_size(axis))])

    def everywhere(array, axis):
        bit = 1
        while bit < lax.axis_size(axis):
            bit *= 2
        pieces = {0: array}
        while bit > 1:
            bit //= 2
            for k in sorted(pieces):
                pieces[k ^ bit] = swapped(pieces[k], axis, bit)
        return [pieces[k] for k in sorted(pieces)]

    first_bits = [1 << bit for bit in range(coil_count.bit_length() - 1)]

    def completed(own, sent):
        pieces = {0: own}
        for bit, piece in zip(first_bits, sent):
            pieces[bit] = piece
        for bit in first_bits:
            for k in range(coil_count):
                if k not in pieces and (k ^ bit) in pieces:
                    pieces[k] = swapped(pieces[k ^ bit], "coil", bit)
        return [pieces[k] for k in range(coil_count)]

    def to_planes(array):
        pieces = []
        for k in range(coil_count):
            part = lax.dynamic_slice_in_dim(array, (coil_index ^ k) * own_planes, own_planes, 0)
            pieces.append(swapped(part, "coil", k) if k > 0 else part)
        return pieces

    group_planes = own_planes // group_count_of(own_planes)
    groups = range(own_planes // group_planes)
    measured = to_planes(kspace[0])
    packed = jnp.concatenate([tile_slot, tile_block, send_list.reshape(-1)])
    sens_source, packed, measured = lax.optimization_barrier((sens_maps[0], packed, measured))
    sens_source = sens_source.reshape(coil_count, own_planes, 2, rows, columns)
    sens = [
        lax.all_to_all(
            sens_source[:, g * group_planes : (g + 1) * group_planes],
            "coil",
            split_axis=0,
            concat_axis=0,
            tiled=True,
        )
        for g in groups
    ]
    measured = jnp.stack(measured)
    by_coil = jnp.arange(coil_count, dtype=jnp.int32) ^ coil_index
    measured = jnp.take(measured, by_coil, axis=0)
    all_weights = everywhere(weights, "pencil")

    places = jnp.stack(everywhere(packed, "pencil"))
    holder = (jnp.arange(peers, dtype=jnp.int32) ^ lax.axis_index("pencil"))[:, None]
    by_owner = jnp.take(places, holder[:, 0], axis=0)
    lists = by_owner[:, 2 * tile_count :].reshape(peers, peers, cap)
    slots = places[:, :tile_count]
    block_of = (places[:, tile_count : 2 * tile_count] + blocks_dev * holder).reshape(-1)
    brick = (slots // cap * brick_dev + lists[slots // cap, holder, slots % cap]).reshape(-1)
    line = brick // runs
    run = brick % runs

    measured = measured.reshape(channels, blocks_dev, size)
    measured = jnp.concatenate(everywhere(jnp.swapaxes(measured, 0, 1), "pencil"), 0)
    measured_block = (
        places[:, tile_count : 2 * tile_count]
        + blocks_dev * jnp.arange(peers, dtype=jnp.int32)[:, None]
    ).reshape(-1)

    cos_y, sin_y = wave(
        line - columns // 2, jnp.arange(columns, dtype=jnp.int32) - columns // 2, columns
    )
    row_ids = jnp.arange(rows, dtype=jnp.int32) + lax.axis_index("pencil") * rows - rows_total // 2
    cos_x, sin_x = wave(
        row_ids, jnp.arange(size, dtype=jnp.int32) - rows_total // 2, rows_total
    )
    turn = jnp.stack(quarter_turns(run, row_ids, runs))
    turn_back = jnp.stack(quarter_turns(row_ids, run, runs))

    def exchanged(partial, axis="pencil"):
        count = lax.axis_size(axis)
        return [partial] + [swapped(partial, axis, k) for k in range(1, count)]

    group_shape = (group_planes, 2, rows, columns)
    group_images = coil_count * group_planes
    group_channels = 2 * group_images

    if (
        rows % 128 == 0
        and columns % 128 == 0
        and size % 128 == 0
        and channels % 16 == 0
        and group_channels % 8 == 0
    ):
        ey = jnp.concatenate([cos_y, sin_y], 0).astype(bf16)
        eb = jnp.concatenate(
            [jnp.concatenate([cos_y, sin_y], 1), jnp.concatenate([-sin_y, cos_y], 1)], 0
        )
        eb = table_parts(eb, 0)
        mx = jnp.concatenate(
            [jnp.concatenate([cos_x, -sin_x], 1), jnp.concatenate([sin_x, cos_x], 1)], 0
        )
        mx, mx_back = mx.astype(bf16), table_parts(mx, 1)
        measured, ey, mx, turn, block_of = lax.optimization_barrier(
            (measured, ey, mx, turn, block_of)
        )
        places_spec = pl.BlockSpec(memory_space=pltpu.SMEM)
        plane_spec = pl.BlockSpec((1, 2, rows, columns), lambda p: (p, 0, 0, 0))
        sens_specs = [
            pl.BlockSpec((1, 1, 2, rows, columns), functools.partial(lambda c, p: (c, p, 0, 0, 0), c))
            for c in range(coil_count)
        ]
        grid_scratch = pltpu.VMEM((tiles * group_channels, size), f32)
        params = pltpu.CompilerParams(vmem_limit_bytes=vmem_limit)
        tail_tables = [mx_back, eb, turn_back]

        def shaped(shape, dtype=f32):
            return jax.ShapeDtypeStruct(shape, dtype)

        def call(kernel, grid, inputs, specs, outs, out_specs, scratch, images):
            flops = 2 * images * 8 * tiles * rows * (columns + size)
            return pl.pallas_call(
                kernel,
                grid=grid,
                in_specs=specs,
                out_specs=out_specs,
                out_shape=outs,
                scratch_shapes=scratch,
                compiler_params=params,
                cost_estimate=pl.CostEstimate(
                    flops=flops,
                    bytes_accessed=sum(math.prod(i.shape) * i.dtype.itemsize for i in inputs),
                    transcendentals=0,
                ),
            )(*inputs)

        def measured_images():
            inputs = [measured_block, measured, *all_weights, *tail_tables]
            shape = (coil_count, own_planes, 2, rows, columns)
            return call(
                measured_kernel,
                (own_planes,),
                inputs,
                [places_spec] + [whole_block(i) for i in inputs[1:]],
                shaped(shape),
                pl.BlockSpec((coil_count, 1, 2, rows, columns), lambda p: (0, p, 0, 0, 0)),
                [pltpu.VMEM((tiles * channels, size), f32)],
                images_count,
            )

        def start(images, g):
            chunk = 64
            spec = pl.BlockSpec((1, 2, chunk, columns), lambda p, r: (p, 0, r, 0))
            images_spec = pl.BlockSpec(
                (coil_count, 1, 2, chunk, columns),
                lambda p, r: (0, p + g * group_planes, 0, r, 0),
            )
            dots_shape = shaped((8, 128))
            return call(
                start_kernel,
                (group_planes, rows // chunk),
                [images] + [sens[g]] * coil_count,
                [images_spec]
                + [
                    pl.BlockSpec(
                        (1, 1, 2, chunk, columns),
                        functools.partial(lambda c, p, r: (c, p, 0, r, 0), c),
                    )
                    for c in range(coil_count)
                ],
                [shaped(group_shape), shaped(group_shape, bf16), dots_shape],
                [spec, spec, whole_block(dots_shape)],
                [],
                0,
            )

        def forward(picture, g):
            tail = [*all_weights, ey, mx, turn]
            out = shaped((blocks * group_channels, size), bf16)
            return call(
                functools.partial(forward_kernel, coil_count),
                (group_planes,),
                [block_of, picture] + [sens[g]] * coil_count + tail,
                [places_spec, plane_spec] + sens_specs + [whole_block(i) for i in tail],
                out,
                whole_block(out),
                [grid_scratch, pltpu.VMEM((blocks, group_channels, size), f32)],
                group_images,
            )

        def back(kernel, samples, tables, vectors, g, outs, out_specs):
            inputs = [*samples, *all_weights]
            tables = tail_tables + tables
            return call(
                functools.partial(kernel, peers, coil_count),
                (group_planes,),
                [block_of, *inputs] + [sens[g]] * coil_count + tables + vectors,
                [places_spec]
                + [whole_block(i) for i in inputs]
                + sens_specs
                + [whole_block(i) for i in tables]
                + [plane_spec] * len(vectors),
                outs,
                out_specs,
                [grid_scratch, pltpu.VMEM((blocks, 2 * group_channels, size), bf16)],
                group_images,
            )

        def first(samples, norms, right_side, g):
            small, large = shaped((8, 128)), shaped(samples[0].shape)
            return back(
                first_kernel,
                samples,
                norms,
                [right_side],
                g,
                [shaped(group_shape), shaped(group_shape, bf16), small, small, large],
                [plane_spec, plane_spec] + [whole_block(i) for i in (small, small, large)],
            )

        def facts_of(samples, dots, start_total, facts):
            inputs = [*samples, dots, start_total, facts]
            return pl.pallas_call(
                functools.partial(facts_kernel, peers),
                in_specs=[pl.BlockSpec(memory_space=pltpu.VMEM)] * len(inputs),
                out_specs=pl.BlockSpec(memory_space=pltpu.VMEM),
                out_shape=shaped((8, 128)),
                compiler_params=params,
            )(*inputs)

        def assembled(infos, vectors, ks, out=None):
            combos = [(k, g) for k in ks for g in groups]
            order = jnp.stack(
                [
                    (coil_index ^ k) * own_planes + g * group_planes + p
                    for k, g in combos
                    for p in range(group_planes)
                ]
            ).astype(jnp.int32)
            inputs = [vector[g][k] for k, g in combos for vector in vectors]

            def spec(place):
                first_step = place // len(vectors) * group_planes
                return pl.BlockSpec(
                    (1, 2, rows, columns),
                    lambda i, o: (jnp.clip(i - first_step, 0, group_planes - 1), 0, 0, 0),
                )

            specs = [pl.BlockSpec(infos[0].shape, lambda i, o: (0, 0, 0))] * len(infos)
            specs += [spec(place) for place in range(len(inputs))]
            aliases = {}
            kernel = functools.partial(
                assemble_kernel,
                coil_count,
                group_planes,
                combos,
                len(vectors) == 3,
                out is not None,
            )
            if out is not None:
                aliases = {1 + len(infos) + len(inputs): 0}
                inputs = inputs + [out]
                specs.append(pl.BlockSpec(memory_space=pl.ANY))

            return pl.pallas_call(
                kernel,
                grid_spec=pltpu.PrefetchScalarGridSpec(
                    num_scalar_prefetch=1,
                    grid=(len(combos) * group_planes,),
                    in_specs=specs,
                    out_specs=pl.BlockSpec((1, 2, rows, columns), lambda i, o: (o[i], 0, 0, 0)),
                    scratch_shapes=[pltpu.VMEM((len(combos), 8, 128), f32)],
                ),
                out_shape=shaped((planes, 2, rows, columns)),
                input_output_aliases=aliases,
                compiler_params=params,
            )(order, *infos, *inputs)

        def second(samples, facts, residual, g):
            return back(
                second_kernel,
                samples,
                [facts],
                [residual],
                g,
                shaped(group_shape, bf16),
                plane_spec,
            )

    else:
        ein = functools.partial(jnp.einsum, precision=lax.Precision.HIGH)
        maps = [array.astype(f32) for array in sens]
        block_map = (block_of[:, None] == jnp.arange(blocks, dtype=jnp.int32)).astype(f32)
        tc, ts = turn[0][:, None, None], turn[1][:, None, None]
        wide_weights = jnp.concatenate(all_weights, 0).astype(f32)

        def forward(picture, g):
            map_real, map_imag = maps[g][:, :, 0], maps[g][:, :, 1]
            coil_real = map_real * picture[None, :, 0] - map_imag * picture[None, :, 1]
            coil_imag = map_real * picture[None, :, 1] + map_imag * picture[None, :, 0]
            half_real = ein("ty,cpxy->tcpx", cos_y, coil_real) + ein(
                "ty,cpxy->tcpx", sin_y, coil_imag
            )
            half_imag = ein("ty,cpxy->tcpx", cos_y, coil_imag) - ein(
                "ty,cpxy->tcpx", sin_y, coil_real
            )
            real = half_real * tc + half_imag * ts
            imag = half_imag * tc - half_real * ts
            grid = jnp.stack(
                [
                    ein("tcpx,xi->tcpi", real, cos_x) + ein("tcpx,xi->tcpi", imag, sin_x),
                    ein("tcpx,xi->tcpi", imag, cos_x) - ein("tcpx,xi->tcpi", real, sin_x),
                ],
                3,
            ).reshape(tiles, group_channels, size)
            product = ein("tgi,tis->tgs", grid, wide_weights)
            return ein("tb,tgs->bgs", block_map, product).astype(bf16).reshape(-1, size)

        def images_of(samples, blocks_of):
            spread = ein("tgs,tis->tgi", jnp.take(samples, blocks_of, axis=0), wide_weights)
            spread = spread.reshape(tiles, coil_count, -1, 2, size)
            back_real = ein("tcpi,xi->tcpx", spread[:, :, :, 0], cos_x) - ein(
                "tcpi,xi->tcpx", spread[:, :, :, 1], sin_x
            )
            back_imag = ein("tcpi,xi->tcpx", spread[:, :, :, 1], cos_x) + ein(
                "tcpi,xi->tcpx", spread[:, :, :, 0], sin_x
            )
            real = back_real * tc - back_imag * ts
            imag = back_imag * tc + back_real * ts
            return jnp.stack(
                [
                    ein("tcpx,ty->cpxy", real, cos_y) - ein("tcpx,ty->cpxy", imag, sin_y),
                    ein("tcpx,ty->cpxy", imag, cos_y) + ein("tcpx,ty->cpxy", real, sin_y),
                ],
                2,
            )

        def combined(images, g):
            map_real, map_imag = maps[g][:, :, 0], maps[g][:, :, 1]
            real, imag = images[:, :, 0], images[:, :, 1]
            return jnp.stack(
                [
                    jnp.sum(map_real * real + map_imag * imag, 0),
                    jnp.sum(map_real * imag - map_imag * real, 0),
                ],
                1,
            )

        def stacked_dots(values):
            values = values + [jnp.zeros((), f32)] * (8 - len(values))
            return jnp.broadcast_to(jnp.stack(values)[:, None], (8, 128))

        def applied_to(samples, vector, g):
            samples = added(samples).reshape(blocks, group_channels, size)
            return combined(images_of(samples, block_of), g) + damping * vector

        def measured_images():
            return images_of(measured.astype(f32), measured_block)

        def start(images, g):
            right_side = combined(images[:, g * group_planes : (g + 1) * group_planes], g)
            dots = stacked_dots([jnp.sum(right_side * right_side)])
            return right_side, right_side.astype(bf16), dots

        def first(samples, norms, right_side, g):
            norm = tree_sum(norms)[0, 0]
            total = added(samples)
            energy = jnp.sum(jnp.square(total))
            residual = right_side - step_of(norm, energy) * applied_to(samples, right_side, g)
            dots = [jnp.sum(residual * residual), jnp.sum(residual * right_side)]
            facts = stacked_dots([norm, energy])
            return residual, residual.astype(bf16), facts, stacked_dots(dots), total

        def facts_of(samples, dots, start_total, facts):
            total = added(samples)
            values = [facts[0, 0], facts[1, 0], dots[0, 0], dots[1, 0]]
            values += [jnp.sum(total * total), jnp.sum(total * start_total)]
            return stacked_dots(values)

        def assembled(infos, vectors, ks, out=None):
            numbers = [
                [[info[g, row, 0] for g in groups] for info in infos] for row in range(6)
            ]
            factors = coefficients(*numbers)[len(vectors) == 3]
            if out is None:
                out = jnp.zeros((planes, 2, rows, columns), f32)
            for k in ks:
                for g in groups:
                    place = ((coil_index ^ k) * own_planes + g * group_planes, 0, 0, 0)
                    piece = sum(
                        factor * vector[g][k].astype(f32)
                        for factor, vector in zip(factors[k][g], vectors)
                    )
                    out = lax.dynamic_update_slice(out, piece, place)
            return out

        def second(samples, facts, residual, g):
            again = applied_to(samples, residual, g)
            return (residual - step_of(facts[0, 0], facts[1, 0]) * again).astype(bf16)

    def added(samples):
        return tree_sum([part.astype(f32) for part in samples])

    def sent_by_bits(own):
        return [swapped(own, "coil", k) for k in first_bits]

    images = measured_images()
    start_pieces, residual_pieces, mixed_own, mixed_sent, infos = [], [], [], [], []
    for g in groups:
        right_side, start_own, norm = start(images, g)
        start_sent = sent_by_bits(start_own)
        samples = exchanged(forward(right_side, g))
        norms = exchanged(norm)
        residual, residual_own, facts, dots, start_total = first(samples, norms, right_side, g)
        residual, residual_own, start_sent = lax.optimization_barrier(
            (residual, residual_own, start_sent)
        )
        residual_sent = sent_by_bits(residual_own)
        samples = exchanged(forward(residual, g))
        samples, pieces = lax.optimization_barrier(
            (samples, completed(start_own, start_sent))
        )
        start_pieces.append(pieces)
        info = facts_of(samples, dots, start_total, facts)
        infos.append(info)
        rounded = second(samples, info, residual, g)
        last = g == groups[-1]
        others = exchanged(jnp.stack(infos), "coil") if last else []
        rounded, others, residual_sent = lax.optimization_barrier(
            (rounded, others, residual_sent)
        )
        residual_pieces.append(completed(residual_own, residual_sent))
        mixed_own.append(rounded)
        mixed_sent.append(sent_by_bits(rounded))

    others, mixed_sent[-1][0] = lax.optimization_barrier((jnp.stack(others), mixed_sent[-1][0]))
    rows_of = lax.broadcasted_iota(jnp.int32, others.shape, 2)
    shared = (rows_of == 2) | (rows_of == 3)
    others = jnp.where(shared, tree_sum(exchanged(others)), others)
    others = [others[k] for k in range(coil_count)]

    picture = assembled(others, [start_pieces, residual_pieces], range(coil_count))
    early = [
        [own, sent[0]] + [None] * (coil_count - 2)
        for own, sent in zip(mixed_own, mixed_sent)
    ]
    out = assembled(others, [start_pieces, residual_pieces, early], range(2))
    out, mixed_sent = lax.optimization_barrier((out, mixed_sent))
    mixed_pieces = [completed(own, sent) for own, sent in zip(mixed_own, mixed_sent)]
    vectors = [start_pieces, residual_pieces, mixed_pieces]
    late = coil_count - 1
    out = assembled(others, vectors, range(2, late), out)
    out = assembled(others, vectors, [late], out)
    return picture, out


def solution(mesh):
    in_specs = (
        P("coil", "scan", None, "pencil"),
        P("coil", "scan", None, "pencil", None),
        P("pencil", None, None),
        P("pencil"),
        P("pencil"),
        P("pencil", None, None),
    )
    out_specs = (P("scan", None, "pencil", None), P("scan", None, "pencil", None))
    return jax.shard_map(
        on_device, mesh=mesh, in_specs=in_specs, out_specs=out_specs, check_vma=False
    )
```

```python
import functools
import math

import jax
import jax.numpy as jnp
from jax import lax
from jax.experimental import pallas as pl
from jax.experimental.pallas import tpu as pltpu
from jax.sharding import PartitionSpec as P


damping = 0.5
f32, bf16 = jnp.float32, jnp.bfloat16
vmem_limit = 56 * 1024 * 1024


def wave(left, right, length):
    phases = left[:, None] * right[None, :] % length
    angles = phases.astype(f32) * (2.0 * math.pi / length)
    return jnp.cos(angles) / math.sqrt(length), jnp.sin(angles) / math.sqrt(length)


def quarter_turns(left, right, count):
    turns = left[:, None] * right[None, :] % count
    if count == 4:
        cosine = jnp.where(turns == 0, 1.0, 0.0) - jnp.where(turns == 2, 1.0, 0.0)
        sine = jnp.where(turns == 1, 1.0, 0.0) - jnp.where(turns == 3, 1.0, 0.0)
        return cosine.astype(f32), sine.astype(f32)
    angles = turns.astype(f32) * (2.0 * math.pi / count)
    return jnp.cos(angles), jnp.sin(angles)


def split(value):
    high = value.astype(bf16)
    return high, (value - high.astype(f32)).astype(bf16)


def table_parts(table, axis):
    high = lax.reduce_precision(table, 8, 7)
    low = (table - high).astype(bf16)
    high = high.astype(bf16)
    return jnp.concatenate([high, high, low], axis)


def data_parts(value):
    high, low = split(value)
    return jnp.concatenate([high, low, high], 1)


def nt(left, right):
    return lax.dot_general(left, right, (((1,), (1,)), ((), ())), preferred_element_type=f32)


def nn(left, right):
    return jnp.dot(left, right, preferred_element_type=f32)


def tree_sum(values):
    while len(values) > 1:
        values = [left + right for left, right in zip(values[::2], values[1::2])]
    return values[0]


def forward_images(plane, planes, picture, sens, ey, mx, turn_ref, grid_ref):
    tiles = turn_ref.shape[1]
    rows = turn_ref.shape[2]
    channels = grid_ref.shape[0] // tiles
    real, imag = picture[0, 0], picture[0, 1]
    turned = []
    for sens_ref in sens:
        sens_real = sens_ref[0, 0, 0].astype(f32)
        sens_imag = sens_ref[0, 0, 1].astype(f32)
        coil = jnp.concatenate(
            [sens_real * real - sens_imag * imag, sens_real * imag + sens_imag * real], 0
        )
        both = nt(ey[...], coil.astype(bf16))
        half_real = both[:tiles, :rows] + both[tiles:, rows:]
        half_imag = both[:tiles, rows:] - both[tiles:, :rows]
        turned.append(
            jnp.concatenate(
                [
                    half_real * turn_ref[0] + half_imag * turn_ref[1],
                    half_imag * turn_ref[0] - half_real * turn_ref[1],
                ],
                1,
            ).astype(bf16)
        )
    grid = nn(jnp.concatenate(turned, 0), mx[...])
    size = grid.shape[1] // 2
    for coil in range(len(sens)):
        step = coil * planes + plane
        part = grid[coil * tiles : (coil + 1) * tiles]
        grid_ref[pl.ds(2 * step, tiles, stride=channels), :] = part[:, :size]
        grid_ref[pl.ds(2 * step + 1, tiles, stride=channels), :] = part[:, size:]


def sample_tiles(block_ref, weights, grid_ref, sums_ref, out_ref):
    count = weights[0].shape[0]
    channels = sums_ref.shape[1]
    sums_ref[...] = jnp.zeros_like(sums_ref)

    for group, weights_ref in enumerate(weights):

        def one(place, carry):
            tile = group * count + place
            start = pl.multiple_of(tile * channels, channels)
            value = grid_ref[pl.ds(start, channels), :]
            high = value.astype(bf16).astype(f32)
            both = jnp.concatenate([high, value - high], 0).astype(bf16)
            product = nn(both, weights_ref[place])
            sums_ref[block_ref[tile]] += product[:channels] + product[channels:]
            return carry

        lax.fori_loop(0, count, one, 0, unroll=True)
    out_ref[...] = sums_ref[...].reshape(out_ref.shape).astype(bf16)


def spread_tiles(block_ref, weights, parts_ref, grid_ref):
    count = weights[0].shape[0]
    channels = grid_ref.shape[0] // (count * len(weights))

    for group, weights_ref in enumerate(weights):

        def one(place, carry):
            tile = group * count + place
            start = pl.multiple_of(tile * channels, channels)
            product = nt(parts_ref[block_ref[tile]], weights_ref[place])
            if product.shape[0] > channels:
                product = product[:channels] + product[channels:]
            grid_ref[pl.ds(start, channels), :] = product
            return carry

        lax.fori_loop(0, count, one, 0, unroll=True)


def adjoint_images(coils, plane, planes, ey_back, mx_back, turn_ref, grid_ref):
    rows, tiles = turn_ref.shape[1], turn_ref.shape[2]
    channels = grid_ref.shape[0] // tiles
    grids = []
    for coil in range(coils):
        step = coil * planes + plane
        grid = jnp.concatenate(
            [
                grid_ref[pl.ds(2 * step, tiles, stride=channels), :],
                grid_ref[pl.ds(2 * step + 1, tiles, stride=channels), :],
            ],
            1,
        )
        grids.append(data_parts(grid))
    back = nt(mx_back[...], jnp.concatenate(grids, 0))
    turned = []
    for coil in range(coils):
        part = back[:, coil * tiles : (coil + 1) * tiles]
        both = jnp.concatenate(
            [
                part[:rows] * turn_ref[0] - part[rows:] * turn_ref[1],
                part[rows:] * turn_ref[0] + part[:rows] * turn_ref[1],
            ],
            1,
        )
        turned.append(data_parts(both))
    image = nn(jnp.concatenate(turned, 0), ey_back[...])
    columns = image.shape[1] // 2
    return [
        (image[c * rows : (c + 1) * rows, :columns], image[c * rows : (c + 1) * rows, columns:])
        for c in range(coils)
    ]


def add_dots(dots_ref, products):
    rows = lax.broadcasted_iota(jnp.int32, dots_ref.shape, 0)
    total = dots_ref[...]
    for place, (left, right) in enumerate(products):
        total += jnp.where(rows == place, jnp.sum(left * right), 0.0)
    dots_ref[...] = total


def measured_kernel(block, samples, *refs):
    *weights, mx, eb, turn, images, grid = refs
    plane = pl.program_id(0)
    coils = images.shape[0]

    @pl.when(plane == 0)
    def _():
        spread_tiles(block, weights, samples, grid)

    found = adjoint_images(coils, plane, pl.num_programs(0), eb, mx, turn, grid)
    for coil, (real, imag) in enumerate(found):
        images[coil, 0, 0] = real
        images[coil, 0, 1] = imag


def combine(images, sens):
    total_real = total_imag = 0.0
    for (real, imag), sens_ref in zip(images, sens):
        sens_real = sens_ref[0, 0, 0].astype(f32)
        sens_imag = sens_ref[0, 0, 1].astype(f32)
        total_real += sens_real * real + sens_imag * imag
        total_imag += sens_real * imag - sens_imag * real
    return total_real, total_imag


def start_kernel(images, *refs):
    *sens, right_side, rounded, dots = refs
    total = combine([(images[c, 0, 0], images[c, 0, 1]) for c in range(len(sens))], sens)
    for part in range(2):
        right_side[0, part] = total[part]
        rounded[0, part] = total[part].astype(bf16)

    @pl.when((pl.program_id(0) == 0) & (pl.program_id(1) == 0))
    def _():
        dots[...] = jnp.zeros_like(dots)

    add_dots(dots, [(right_side[0], right_side[0])])


def forward_kernel(coils, block, picture, *refs):
    sens = refs[:coils]
    *weights, ey, mx, turn, samples, grid, sums = refs[coils:]
    plane = pl.program_id(0)
    forward_images(plane, pl.num_programs(0), picture, sens, ey, mx, turn, grid)

    @pl.when(plane == pl.num_programs(0) - 1)
    def _():
        sample_tiles(block, weights, grid, sums, samples)


def summed_parts(samples, parts):
    summed = tree_sum([part[...].astype(f32) for part in samples])
    blocks, channels, size = parts.shape[0], parts.shape[1] // 2, parts.shape[2]
    value = summed.reshape(blocks, channels, size)
    high = value.astype(bf16).astype(f32)
    parts[...] = jnp.concatenate([high, value - high], 1).astype(bf16)
    return summed


def step_of(norm, energy):
    return jnp.where(norm > 0.0, norm / (energy + damping * norm), 1.0)


def first_kernel(peers, coils, block, *refs):
    samples, weights, sens = refs[:peers], refs[peers : 2 * peers], refs[2 * peers :][:coils]
    mx, eb, turn, *norms = refs[2 * peers + coils :][: 3 + peers]
    right_side, residual, rounded, facts, dots, total_samples, grid, parts = refs[-8:]
    plane = pl.program_id(0)

    @pl.when(plane == 0)
    def _():
        summed = summed_parts(samples, parts)
        total_samples[...] = summed
        rows = lax.broadcasted_iota(jnp.int32, facts.shape, 0)
        norm = tree_sum([part[...] for part in norms])
        facts[...] = jnp.where(rows == 1, jnp.sum(summed * summed), norm)
        dots[...] = jnp.zeros_like(dots)
        spread_tiles(block, weights, parts, grid)

    images = adjoint_images(coils, plane, pl.num_programs(0), eb, mx, turn, grid)
    total = combine(images, sens)
    scale = step_of(facts[0:1, 0:1], facts[1:2, 0:1])
    for part in range(2):
        vector = right_side[0, part]
        value = vector - scale * (total[part] + damping * vector)
        residual[0, part] = value
        rounded[0, part] = value.astype(bf16)
        add_dots(dots, [(value, value), (value, vector)])


def second_kernel(peers, coils, block, *refs):
    samples, weights, sens = refs[:peers], refs[peers : 2 * peers], refs[2 * peers :][:coils]
    mx, eb, turn, facts, residual, rounded, grid, parts = refs[2 * peers + coils :]
    plane = pl.program_id(0)

    @pl.when(plane == 0)
    def _():
        summed_parts(samples, parts)
        spread_tiles(block, weights, parts, grid)

    images = adjoint_images(coils, plane, pl.num_programs(0), eb, mx, turn, grid)
    total = combine(images, sens)
    scale = step_of(facts[0:1, 0:1], facts[1:2, 0:1])
    for part in range(2):
        vector = residual[0, part]
        again = total[part] + damping * vector
        rounded[0, part] = (vector - scale * again).astype(rounded.dtype)


def facts_kernel(peers, *refs):
    samples, dots = refs[:peers], refs[peers : 2 * peers]
    start_total, facts, out = refs[2 * peers :]
    summed = tree_sum([part[...].astype(f32) for part in samples])
    both = tree_sum([part[...] for part in dots])
    rows = lax.broadcasted_iota(jnp.int32, out.shape, 0)
    values = [facts[0:1], facts[1:2], both[0:1], both[1:2]]
    values += [jnp.sum(summed * summed), jnp.sum(summed * start_total[...])]
    total = jnp.zeros(out.shape, f32)
    for row, value in enumerate(values):
        total = jnp.where(rows == row, value, total)
    out[...] = total


def coefficients(norm, energy, square, cross, again, mixed):
    def over_all(values):
        return tree_sum([sum(of_coil) for of_coil in values])

    def each(function, *lists):
        return [[function(*items) for items in zip(*of_coil)] for of_coil in zip(*lists)]

    start_curve = each(lambda e, n: e + damping * n, energy, norm)
    curve = each(lambda e, n: e + damping * n, again, square)
    mixed_curve = each(lambda e, n: e + damping * n, mixed, cross)
    sigma = each(step_of, norm, energy)
    start_norm = over_all(norm)
    first_step = start_norm / over_all(start_curve)
    part = each(lambda s: first_step / s, sigma)
    next_norm = over_all(
        each(
            lambda w, n, c, s: w * w * s + 2.0 * w * (1.0 - w) * c + (1.0 - w) * (1.0 - w) * n,
            part,
            norm,
            cross,
            square,
        )
    )
    more = each(lambda w: 1.0 - w + next_norm / start_norm, part)
    second_step = next_norm / over_all(
        each(
            lambda w, m, q, c, s, z, qm, qs: w * w * q
            + w * m * ((c - s) / z + qm)
            + m * m * qs,
            part,
            more,
            curve,
            cross,
            square,
            sigma,
            mixed_curve,
            start_curve,
        )
    )
    share = each(lambda z: second_step / z, sigma)
    picture = each(lambda w, m: (first_step + second_step * m, second_step * w), part, more)
    residual = each(
        lambda w, m, h: (1.0 - w - h * m, w - h * w + h * m, h * w), part, more, share
    )
    return picture, residual


def kept_coefficients(infos, kept, first, combos, is_residual):
    groups = infos[0].shape[0]
    numbers = [
        [[info[g, row : row + 1, 0:1] for g in range(groups)] for info in infos]
        for row in range(6)
    ]
    factors = coefficients(*numbers)[is_residual]
    rows = lax.broadcasted_iota(jnp.int32, kept.shape[1:], 0)
    for place, (k, g) in enumerate(combos):
        total = jnp.zeros(kept.shape[1:], f32)
        for row, factor in enumerate(factors[k][g]):
            total = jnp.where(rows == row, factor, total)
        kept[first + place] = total


def assemble_kernel(coils, group_steps, combos, counts, is_residual, order, *refs):
    infos, pieces, (out, kept) = refs[:coils], refs[coils:-2], refs[-2:]

    @pl.when(pl.program_id(0) == 0)
    def _():
        kept_coefficients(infos, kept, 0, combos, is_residual)

    def write(place, used):
        @pl.when(pl.program_id(0) // group_steps == place)
        def _():
            if len(used) == 1:
                out[...] = used[0][...].astype(f32)
            else:
                total = 0.0
                for row, piece in enumerate(used):
                    factor = kept[place, row : row + 1, 0:1].reshape(1, 1, 1, 1)
                    total += factor * piece[...].astype(f32)
                out[...] = total

    first = 0
    for place, count in enumerate(counts):
        write(place, pieces[first : first + count])
        first += count


def finish_kernel(coils, g, *refs):
    infos, (start, residual, mixed, picture, out, kept) = refs[:coils], refs[coils:]

    @pl.when((pl.program_id(0) == 0) & (pl.program_id(1) == 0))
    def _():
        kept_coefficients(infos, kept, 0, [(0, g)], False)
        kept_coefficients(infos, kept, 1, [(0, g)], True)

    def mixture(place, vectors):
        total = 0.0
        for row, vector in enumerate(vectors):
            factor = kept[place, row : row + 1, 0:1].reshape(1, 1, 1, 1)
            total += factor * vector[...]
        return total.astype(bf16)

    picture[...] = mixture(0, [start, residual])
    out[...] = mixture(1, [start, residual, mixed])


def group_count_of(own_planes):
    return 2 if own_planes % 2 == 0 else 1


def whole_block(array):
    rank = len(array.shape)
    return pl.BlockSpec(array.shape, lambda *_: (0,) * rank)


def on_device(kspace, sens_maps, weights, tile_slot, tile_block, send_list):
    coil_count = lax.axis_size("coil")
    peers = lax.axis_size("pencil")
    planes = sens_maps.shape[1]
    own_planes = planes // coil_count
    rows = sens_maps.shape[3]
    columns = sens_maps.shape[4]
    rows_total = rows * peers
    size = weights.shape[1]
    tile_count = tile_slot.shape[0]
    tiles = tile_count * peers
    blocks_dev = kspace.shape[3] // size
    blocks = blocks_dev * peers
    cap = send_list.shape[2]
    runs = rows_total // size
    brick_dev = columns // peers * runs
    images_count = coil_count * own_planes
    channels = 2 * images_count

    coil_index = lax.axis_index("coil")

    def swapped(array, axis, k):
        return lax.ppermute(array, axis, [(i, i ^ k) for i in range(lax.axis_size(axis))])

    def everywhere(array, axis):
        bit = 1
        while bit < lax.axis_size(axis):
            bit *= 2
        pieces = {0: array}
        while bit > 1:
            bit //= 2
            for k in sorted(pieces):
                pieces[k ^ bit] = swapped(pieces[k], axis, bit)
        return [pieces[k] for k in sorted(pieces)]

    first_bits = [1 << bit for bit in range(coil_count.bit_length() - 1)]

    def completed(own, sent):
        pieces = {0: own}
        for bit, piece in zip(first_bits, sent):
            pieces[bit] = piece
        for bit in first_bits:
            for k in range(coil_count):
                if k not in pieces and (k ^ bit) in pieces:
                    pieces[k] = swapped(pieces[k ^ bit], "coil", bit)
        return [pieces[k] for k in range(coil_count)]

    def to_planes(array):
        pieces = []
        for k in range(coil_count):
            part = lax.dynamic_slice_in_dim(array, (coil_index ^ k) * own_planes, own_planes, 0)
            pieces.append(swapped(part, "coil", k) if k > 0 else part)
        return pieces

    group_planes = own_planes // group_count_of(own_planes)
    groups = range(own_planes // group_planes)
    measured = to_planes(kspace[0])
    packed = jnp.concatenate([tile_slot, tile_block, send_list.reshape(-1)])
    sens_source, packed, measured = lax.optimization_barrier((sens_maps[0], packed, measured))
    sens_source = sens_source.reshape(coil_count, own_planes, 2, rows, columns)
    sens = []
    for g in groups:
        part = sens_source[:, g * group_planes : (g + 1) * group_planes]
        if g > 0:
            part, sens[-1] = lax.optimization_barrier((part, sens[-1]))
        sens.append(lax.all_to_all(part, "coil", split_axis=0, concat_axis=0, tiled=True))
    measured = jnp.stack(measured)
    by_coil = jnp.arange(coil_count, dtype=jnp.int32) ^ coil_index
    measured = jnp.take(measured, by_coil, axis=0)
    all_weights = everywhere(weights, "pencil")

    places = jnp.stack(everywhere(packed, "pencil"))
    holder = (jnp.arange(peers, dtype=jnp.int32) ^ lax.axis_index("pencil"))[:, None]
    by_owner = jnp.take(places, holder[:, 0], axis=0)
    lists = by_owner[:, 2 * tile_count :].reshape(peers, peers, cap)
    slots = places[:, :tile_count]
    block_of = (places[:, tile_count : 2 * tile_count] + blocks_dev * holder).reshape(-1)
    brick = (slots // cap * brick_dev + lists[slots // cap, holder, slots % cap]).reshape(-1)
    line = brick // runs
    run = brick % runs

    measured = measured.reshape(channels, blocks_dev, size)
    measured = jnp.concatenate(everywhere(jnp.swapaxes(measured, 0, 1), "pencil"), 0)
    measured_block = (
        places[:, tile_count : 2 * tile_count]
        + blocks_dev * jnp.arange(peers, dtype=jnp.int32)[:, None]
    ).reshape(-1)

    cos_y, sin_y = wave(
        line - columns // 2, jnp.arange(columns, dtype=jnp.int32) - columns // 2, columns
    )
    row_ids = jnp.arange(rows, dtype=jnp.int32) + lax.axis_index("pencil") * rows - rows_total // 2
    cos_x, sin_x = wave(
        row_ids, jnp.arange(size, dtype=jnp.int32) - rows_total // 2, rows_total
    )
    turn = jnp.stack(quarter_turns(run, row_ids, runs))
    turn_back = jnp.stack(quarter_turns(row_ids, run, runs))

    def exchanged(partial, axis="pencil"):
        count = lax.axis_size(axis)
        return [partial] + [swapped(partial, axis, k) for k in range(1, count)]

    group_shape = (group_planes, 2, rows, columns)
    group_images = coil_count * group_planes
    group_channels = 2 * group_images

    if (
        rows % 128 == 0
        and columns % 128 == 0
        and size % 128 == 0
        and channels % 16 == 0
        and group_channels % 8 == 0
    ):
        ey = jnp.concatenate([cos_y, sin_y], 0).astype(bf16)
        eb = jnp.concatenate(
            [jnp.concatenate([cos_y, sin_y], 1), jnp.concatenate([-sin_y, cos_y], 1)], 0
        )
        eb = table_parts(eb, 0)
        mx = jnp.concatenate(
            [jnp.concatenate([cos_x, -sin_x], 1), jnp.concatenate([sin_x, cos_x], 1)], 0
        )
        mx, mx_back = mx.astype(bf16), table_parts(mx, 1)
        measured, ey, mx, turn, block_of = lax.optimization_barrier(
            (measured, ey, mx, turn, block_of)
        )
        places_spec = pl.BlockSpec(memory_space=pltpu.SMEM)
        plane_spec = pl.BlockSpec((1, 2, rows, columns), lambda p: (p, 0, 0, 0))
        sens_specs = [
            pl.BlockSpec((1, 1, 2, rows, columns), functools.partial(lambda c, p: (c, p, 0, 0, 0), c))
            for c in range(coil_count)
        ]
        grid_scratch = pltpu.VMEM((tiles * group_channels, size), f32)
        params = pltpu.CompilerParams(vmem_limit_bytes=vmem_limit)
        tail_tables = [mx_back, eb, turn_back]

        def shaped(shape, dtype=f32):
            return jax.ShapeDtypeStruct(shape, dtype)

        def call(kernel, grid, inputs, specs, outs, out_specs, scratch, images):
            flops = 2 * images * 8 * tiles * rows * (columns + size)
            return pl.pallas_call(
                kernel,
                grid=grid,
                in_specs=specs,
                out_specs=out_specs,
                out_shape=outs,
                scratch_shapes=scratch,
                compiler_params=params,
                cost_estimate=pl.CostEstimate(
                    flops=flops,
                    bytes_accessed=sum(math.prod(i.shape) * i.dtype.itemsize for i in inputs),
                    transcendentals=0,
                ),
            )(*inputs)

        def measured_images():
            inputs = [measured_block, measured, *all_weights, *tail_tables]
            shape = (coil_count, own_planes, 2, rows, columns)
            return call(
                measured_kernel,
                (own_planes,),
                inputs,
                [places_spec] + [whole_block(i) for i in inputs[1:]],
                shaped(shape),
                pl.BlockSpec((coil_count, 1, 2, rows, columns), lambda p: (0, p, 0, 0, 0)),
                [pltpu.VMEM((tiles * channels, size), f32)],
                images_count,
            )

        def start(images, g):
            chunk = 64
            spec = pl.BlockSpec((1, 2, chunk, columns), lambda p, r: (p, 0, r, 0))
            images_spec = pl.BlockSpec(
                (coil_count, 1, 2, chunk, columns),
                lambda p, r: (0, p + g * group_planes, 0, r, 0),
            )
            dots_shape = shaped((8, 128))
            return call(
                start_kernel,
                (group_planes, rows // chunk),
                [images] + [sens[g]] * coil_count,
                [images_spec]
                + [
                    pl.BlockSpec(
                        (1, 1, 2, chunk, columns),
                        functools.partial(lambda c, p, r: (c, p, 0, r, 0), c),
                    )
                    for c in range(coil_count)
                ],
                [shaped(group_shape), shaped(group_shape, bf16), dots_shape],
                [spec, spec, whole_block(dots_shape)],
                [],
                0,
            )

        def forward(picture, g):
            tail = [*all_weights, ey, mx, turn]
            out = shaped((blocks * group_channels, size), bf16)
            return call(
                functools.partial(forward_kernel, coil_count),
                (group_planes,),
                [block_of, picture] + [sens[g]] * coil_count + tail,
                [places_spec, plane_spec] + sens_specs + [whole_block(i) for i in tail],
                out,
                whole_block(out),
                [grid_scratch, pltpu.VMEM((blocks, group_channels, size), f32)],
                group_images,
            )

        def back(kernel, samples, tables, vectors, g, outs, out_specs):
            inputs = [*samples, *all_weights]
            tables = tail_tables + tables
            return call(
                functools.partial(kernel, peers, coil_count),
                (group_planes,),
                [block_of, *inputs] + [sens[g]] * coil_count + tables + vectors,
                [places_spec]
                + [whole_block(i) for i in inputs]
                + sens_specs
                + [whole_block(i) for i in tables]
                + [plane_spec] * len(vectors),
                outs,
                out_specs,
                [grid_scratch, pltpu.VMEM((blocks, 2 * group_channels, size), bf16)],
                group_images,
            )

        def first(samples, norms, right_side, g):
            small, large = shaped((8, 128)), shaped(samples[0].shape)
            return back(
                first_kernel,
                samples,
                norms,
                [right_side],
                g,
                [shaped(group_shape), shaped(group_shape, bf16), small, small, large],
                [plane_spec, plane_spec] + [whole_block(i) for i in (small, small, large)],
            )

        def facts_of(samples, dots, start_total, facts):
            inputs = [*samples, *dots, start_total, facts]
            return pl.pallas_call(
                functools.partial(facts_kernel, peers),
                in_specs=[pl.BlockSpec(memory_space=pltpu.VMEM)] * len(inputs),
                out_specs=pl.BlockSpec(memory_space=pltpu.VMEM),
                out_shape=shaped((8, 128)),
                compiler_params=params,
            )(*inputs)

        def assembled(infos, vectors, ks, is_residual, out=None):
            combos = [(k, g) for k in ks for g in groups]
            counts = [len(vectors[g]) for k, g in combos]
            order = jnp.stack(
                [
                    (coil_index ^ k) * own_planes + g * group_planes + p
                    for k, g in combos
                    for p in range(group_planes)
                ]
            ).astype(jnp.int32)
            inputs, specs = [], [pl.BlockSpec(infos[0].shape, lambda i, o: (0, 0, 0))] * len(infos)
            for place, (k, g) in enumerate(combos):

                def plane_of(i, o, first=place * group_planes):
                    return jnp.clip(i - first, 0, group_planes - 1), 0, 0, 0

                for vector in vectors[g]:
                    inputs.append(vector[k])
                    specs.append(pl.BlockSpec((1, 2, rows, columns), plane_of))
            aliases = {}
            kernel = functools.partial(
                assemble_kernel, coil_count, group_planes, combos, counts, is_residual
            )
            if out is not None:
                aliases = {1 + len(infos) + len(inputs): 0}
                inputs.append(out)
                specs.append(pl.BlockSpec(memory_space=pl.ANY))
            return pl.pallas_call(
                kernel,
                grid_spec=pltpu.PrefetchScalarGridSpec(
                    num_scalar_prefetch=1,
                    grid=(len(combos) * group_planes,),
                    in_specs=specs,
                    out_specs=pl.BlockSpec((1, 2, rows, columns), lambda i, o: (o[i], 0, 0, 0)),
                    scratch_shapes=[pltpu.VMEM((len(combos), 8, 128), f32)],
                ),
                out_shape=shaped((planes, 2, rows, columns)),
                input_output_aliases=aliases,
                compiler_params=params,
            )(order, *infos, *inputs)

        def finished(infos, vectors, g):
            spec = pl.BlockSpec((1, 2, rows // 2, columns), lambda p, r: (p, 0, r, 0))
            small = pl.BlockSpec(infos[0].shape, lambda p, r: (0, 0, 0))
            return pl.pallas_call(
                functools.partial(finish_kernel, coil_count, g),
                grid=(group_planes, 2),
                in_specs=[small] * len(infos) + [spec] * 3,
                out_specs=[spec] * 2,
                out_shape=[shaped(group_shape, bf16)] * 2,
                scratch_shapes=[pltpu.VMEM((2, 8, 128), f32)],
                compiler_params=params,
            )(*infos, *vectors)

        def second(samples, facts, residual, g, dtype):
            return back(
                second_kernel,
                samples,
                [facts],
                [residual],
                g,
                shaped(group_shape, dtype),
                plane_spec,
            )

    else:
        ein = functools.partial(jnp.einsum, precision=lax.Precision.HIGH)
        maps = [array.astype(f32) for array in sens]
        block_map = (block_of[:, None] == jnp.arange(blocks, dtype=jnp.int32)).astype(f32)
        tc, ts = turn[0][:, None, None], turn[1][:, None, None]
        wide_weights = jnp.concatenate(all_weights, 0).astype(f32)

        def forward(picture, g):
            map_real, map_imag = maps[g][:, :, 0], maps[g][:, :, 1]
            coil_real = map_real * picture[None, :, 0] - map_imag * picture[None, :, 1]
            coil_imag = map_real * picture[None, :, 1] + map_imag * picture[None, :, 0]
            half_real = ein("ty,cpxy->tcpx", cos_y, coil_real) + ein(
                "ty,cpxy->tcpx", sin_y, coil_imag
            )
            half_imag = ein("ty,cpxy->tcpx", cos_y, coil_imag) - ein(
                "ty,cpxy->tcpx", sin_y, coil_real
            )
            real = half_real * tc + half_imag * ts
            imag = half_imag * tc - half_real * ts
            grid = jnp.stack(
                [
                    ein("tcpx,xi->tcpi", real, cos_x) + ein("tcpx,xi->tcpi", imag, sin_x),
                    ein("tcpx,xi->tcpi", imag, cos_x) - ein("tcpx,xi->tcpi", real, sin_x),
                ],
                3,
            ).reshape(tiles, group_channels, size)
            product = ein("tgi,tis->tgs", grid, wide_weights)
            return ein("tb,tgs->bgs", block_map, product).astype(bf16).reshape(-1, size)

        def images_of(samples, blocks_of):
            spread = ein("tgs,tis->tgi", jnp.take(samples, blocks_of, axis=0), wide_weights)
            spread = spread.reshape(tiles, coil_count, -1, 2, size)
            back_real = ein("tcpi,xi->tcpx", spread[:, :, :, 0], cos_x) - ein(
                "tcpi,xi->tcpx", spread[:, :, :, 1], sin_x
            )
            back_imag = ein("tcpi,xi->tcpx", spread[:, :, :, 1], cos_x) + ein(
                "tcpi,xi->tcpx", spread[:, :, :, 0], sin_x
            )
            real = back_real * tc - back_imag * ts
            imag = back_imag * tc + back_real * ts
            return jnp.stack(
                [
                    ein("tcpx,ty->cpxy", real, cos_y) - ein("tcpx,ty->cpxy", imag, sin_y),
                    ein("tcpx,ty->cpxy", imag, cos_y) + ein("tcpx,ty->cpxy", real, sin_y),
                ],
                2,
            )

        def combined(images, g):
            map_real, map_imag = maps[g][:, :, 0], maps[g][:, :, 1]
            real, imag = images[:, :, 0], images[:, :, 1]
            return jnp.stack(
                [
                    jnp.sum(map_real * real + map_imag * imag, 0),
                    jnp.sum(map_real * imag - map_imag * real, 0),
                ],
                1,
            )

        def stacked_dots(values):
            values = values + [jnp.zeros((), f32)] * (8 - len(values))
            return jnp.broadcast_to(jnp.stack(values)[:, None], (8, 128))

        def applied_to(samples, vector, g):
            samples = added(samples).reshape(blocks, group_channels, size)
            return combined(images_of(samples, block_of), g) + damping * vector

        def measured_images():
            return images_of(measured.astype(f32), measured_block)

        def start(images, g):
            right_side = combined(images[:, g * group_planes : (g + 1) * group_planes], g)
            dots = stacked_dots([jnp.sum(right_side * right_side)])
            return right_side, right_side.astype(bf16), dots

        def first(samples, norms, right_side, g):
            norm = tree_sum(norms)[0, 0]
            total = added(samples)
            energy = jnp.sum(jnp.square(total))
            residual = right_side - step_of(norm, energy) * applied_to(samples, right_side, g)
            dots = [jnp.sum(residual * residual), jnp.sum(residual * right_side)]
            facts = stacked_dots([norm, energy])
            return residual, residual.astype(bf16), facts, stacked_dots(dots), total

        def facts_of(samples, dots, start_total, facts):
            total = added(samples)
            square, cross = tree_sum(dots)[:2, 0]
            values = [facts[0, 0], facts[1, 0], square, cross]
            values += [jnp.sum(total * total), jnp.sum(total * start_total)]
            return stacked_dots(values)

        def factors_of(infos, is_residual):
            numbers = [
                [[info[g, row, 0] for g in groups] for info in infos] for row in range(6)
            ]
            return coefficients(*numbers)[is_residual]

        def mixture(factors, vectors):
            return sum(factor * vector.astype(f32) for factor, vector in zip(factors, vectors))

        def assembled(infos, vectors, ks, is_residual, out=None):
            factors = factors_of(infos, is_residual)
            if out is None:
                out = jnp.zeros((planes, 2, rows, columns), f32)
            for k in ks:
                for g in groups:
                    place = ((coil_index ^ k) * own_planes + g * group_planes, 0, 0, 0)
                    pieces = [vector[k] for vector in vectors[g]]
                    if len(pieces) == 1:
                        piece = pieces[0].astype(f32)
                    else:
                        piece = mixture(factors[k][g], pieces)
                    out = lax.dynamic_update_slice(out, piece, place)
            return out

        def finished(infos, vectors, g):
            return [
                mixture(factors_of(infos, i)[0][g], vectors).astype(bf16) for i in (False, True)
            ]

        def second(samples, facts, residual, g, dtype):
            again = applied_to(samples, residual, g)
            return (residual - step_of(facts[0, 0], facts[1, 0]) * again).astype(dtype)

    def added(samples):
        return tree_sum([part.astype(f32) for part in samples])

    def sent_by_bits(own):
        return [swapped(own, "coil", k) for k in first_bits]

    images = measured_images()
    last = len(groups) - 1
    starts, residuals, mixeds, start_owns, residual_owns, infos = [], [], [], [], [], []
    for g in groups:
        right_side, start_own, norm = start(images, g)
        samples = exchanged(forward(right_side, g))
        norms = exchanged(norm)
        residual, residual_own, facts, dots, start_total = first(samples, norms, right_side, g)
        if g == last and last > 0:
            owns = [start_owns[0], residual_owns[0]]
            *owns, _ = lax.optimization_barrier((*owns, sens[last]))
            sent = [sent_by_bits(own) for own in owns]
            residual, residual_own, sent = lax.optimization_barrier((residual, residual_own, sent))
            early = [completed(own, pieces) for own, pieces in zip(owns, sent)]
            mixed_sent = sent_by_bits(mixeds[0])
        dots = exchanged(dots)
        samples = exchanged(forward(residual, g))
        samples, dots = lax.optimization_barrier((samples, dots))
        info = facts_of(samples, dots, start_total, facts)
        mixed = second(samples, info, residual, g, bf16 if g < last else f32)
        infos.append(info)
        starts.append(right_side)
        residuals.append(residual)
        mixeds.append(mixed)
        start_owns.append(start_own)
        residual_owns.append(residual_own)

    others = exchanged(jnp.stack(infos), "coil")
    if last > 0:
        mixeds[last], others, early, mixed_sent = lax.optimization_barrier(
            (mixeds[last], others, early, mixed_sent)
        )
    final = finished(others, [starts[last], residuals[last], mixeds[last]], last)
    final_sent = [sent_by_bits(own) for own in final]
    first_vectors = []
    if last > 0:
        early.append(completed(mixeds[0], mixed_sent))
        first_vectors = [early]
    final_pieces = [completed(own, sent) for own, sent in zip(final, final_sent)]
    late = coil_count - 1
    near = [[own] + sent[:1] + [None] * (coil_count - 2) for own, sent in zip(final, final_sent)]
    vectors = [v[:2] for v in first_vectors]
    picture = assembled(others, vectors + [near[:1]], range(2), False)
    out = assembled(others, first_vectors + [near[1:]], range(2), True)
    vectors = vectors + [final_pieces[:1]]
    first_vectors = first_vectors + [final_pieces[1:]]
    picture = assembled(others, vectors, range(2, late), False, picture)
    out = assembled(others, first_vectors, range(2, late), True, out)
    picture = assembled(others, vectors, [late], False, picture)
    out = assembled(others, first_vectors, [late], True, out)
    return picture, out


def solution(mesh):
    in_specs = (
        P("coil", "scan", None, "pencil"),
        P("coil", "scan", None, "pencil", None),
        P("pencil", None, None),
        P("pencil"),
        P("pencil"),
        P("pencil", None, None),
    )
    out_specs = (P("scan", None, "pencil", None), P("scan", None, "pencil", None))
    return jax.shard_map(
        on_device, mesh=mesh, in_specs=in_specs, out_specs=out_specs, check_vma=False
    )
```

```python
import functools
import math

import jax
import jax.numpy as jnp
from jax import lax
from jax.experimental import pallas as pl
from jax.experimental.pallas import tpu as pltpu
from jax.sharding import PartitionSpec as P


damping = 0.5
f32, bf16 = jnp.float32, jnp.bfloat16
vmem_limit = 56 * 1024 * 1024


def wave(left, right, length):
    phases = left[:, None] * right[None, :] % length
    angles = phases.astype(f32) * (2.0 * math.pi / length)
    return jnp.cos(angles) / math.sqrt(length), jnp.sin(angles) / math.sqrt(length)


def quarter_turns(left, right, count):
    turns = left[:, None] * right[None, :] % count
    if count == 4:
        cosine = jnp.where(turns == 0, 1.0, 0.0) - jnp.where(turns == 2, 1.0, 0.0)
        sine = jnp.where(turns == 1, 1.0, 0.0) - jnp.where(turns == 3, 1.0, 0.0)
        return cosine.astype(f32), sine.astype(f32)
    angles = turns.astype(f32) * (2.0 * math.pi / count)
    return jnp.cos(angles), jnp.sin(angles)


def split(value):
    high = value.astype(bf16)
    return high, (value - high.astype(f32)).astype(bf16)


def table_parts(table, axis):
    high = lax.reduce_precision(table, 8, 7)
    low = (table - high).astype(bf16)
    high = high.astype(bf16)
    return jnp.concatenate([high, high, low], axis)


def data_parts(value):
    high, low = split(value)
    return jnp.concatenate([high, low, high], 1)


def nt(left, right):
    return lax.dot_general(left, right, (((1,), (1,)), ((), ())), preferred_element_type=f32)


def nn(left, right):
    return jnp.dot(left, right, preferred_element_type=f32)


def tree_sum(values):
    while len(values) > 1:
        values = [left + right for left, right in zip(values[::2], values[1::2])]
    return values[0]


def forward_images(plane, planes, picture, sens, ey, mx, turn_ref, grid_ref):
    tiles = turn_ref.shape[1]
    rows = turn_ref.shape[2]
    channels = grid_ref.shape[0] // tiles
    real, imag = picture[0, 0], picture[0, 1]
    turned = []
    for sens_ref in sens:
        sens_real = sens_ref[0, 0, 0].astype(f32)
        sens_imag = sens_ref[0, 0, 1].astype(f32)
        coil = jnp.concatenate(
            [sens_real * real - sens_imag * imag, sens_real * imag + sens_imag * real], 0
        )
        both = nt(ey[...], coil.astype(bf16))
        half_real = both[:tiles, :rows] + both[tiles:, rows:]
        half_imag = both[:tiles, rows:] - both[tiles:, :rows]
        turned.append(
            jnp.concatenate(
                [
                    half_real * turn_ref[0] + half_imag * turn_ref[1],
                    half_imag * turn_ref[0] - half_real * turn_ref[1],
                ],
                1,
            ).astype(bf16)
        )
    grid = nn(jnp.concatenate(turned, 0), mx[...])
    size = grid.shape[1] // 2
    for coil in range(len(sens)):
        step = coil * planes + plane
        part = grid[coil * tiles : (coil + 1) * tiles]
        grid_ref[pl.ds(2 * step, tiles, stride=channels), :] = part[:, :size]
        grid_ref[pl.ds(2 * step + 1, tiles, stride=channels), :] = part[:, size:]


def tile_products(lefts, rights):
    rows, size = lefts[0].shape
    empty = jnp.zeros((rows, size), bf16)
    left = jnp.concatenate(
        [
            jnp.concatenate([value, empty] if place % 2 == 0 else [empty, value], 1)
            for place, value in enumerate(lefts)
        ],
        0,
    )
    right = jnp.concatenate(
        [jnp.concatenate(rights[:2], 0), jnp.concatenate(rights[2:], 0)], 1
    )
    product = nn(left, right)
    return [
        product[place * rows : (place + 1) * rows, place // 2 * size : (place // 2 + 1) * size]
        for place in range(4)
    ]


def each_four(count, function):
    def one(index, carry):
        function([index * 4 + place for place in range(4)])
        return carry

    lax.fori_loop(0, count // 4, one, 0, unroll=True)


def sample_tiles(block_ref, weights, grid_ref, sums_ref, out_ref):
    count = weights[0].shape[0]
    channels = sums_ref.shape[1]
    sums_ref[...] = jnp.zeros_like(sums_ref)

    def left_of(tile):
        value = grid_ref[pl.ds(pl.multiple_of(tile * channels, channels), channels), :]
        high = value.astype(bf16).astype(f32)
        return jnp.concatenate([high, value - high], 0).astype(bf16)

    for group, weights_ref in enumerate(weights):

        def four(places):
            tiles = [group * count + place for place in places]
            products = tile_products(
                [left_of(tile) for tile in tiles], [weights_ref[place] for place in places]
            )
            for tile, product in zip(tiles, products):
                sums_ref[block_ref[tile]] += product[:channels] + product[channels:]

        each_four(count, four)
    out_ref[...] = sums_ref[...].reshape(out_ref.shape).astype(bf16)


def spread_tiles(block_ref, weights, parts_ref, grid_ref):
    count = weights[0].shape[0]
    channels = grid_ref.shape[0] // (count * len(weights))

    for group, weights_ref in enumerate(weights):

        def four(places):
            tiles = [group * count + place for place in places]
            products = tile_products(
                [parts_ref[block_ref[tile]] for tile in tiles],
                [weights_ref[place] for place in places],
            )
            for tile, product in zip(tiles, products):
                if product.shape[0] > channels:
                    product = product[:channels] + product[channels:]
                start = pl.multiple_of(tile * channels, channels)
                grid_ref[pl.ds(start, channels), :] = product

        each_four(count, four)


def adjoint_images(coils, plane, planes, ey_back, mx_back, turn_ref, grid_ref):
    rows, tiles = turn_ref.shape[1], turn_ref.shape[2]
    channels = grid_ref.shape[0] // tiles
    grids = []
    for coil in range(coils):
        step = coil * planes + plane
        grid = jnp.concatenate(
            [
                grid_ref[pl.ds(2 * step, tiles, stride=channels), :],
                grid_ref[pl.ds(2 * step + 1, tiles, stride=channels), :],
            ],
            1,
        )
        grids.append(data_parts(grid))
    back = nt(mx_back[...], jnp.concatenate(grids, 0))
    turned = []
    for coil in range(coils):
        part = back[:, coil * tiles : (coil + 1) * tiles]
        both = jnp.concatenate(
            [
                part[:rows] * turn_ref[0] - part[rows:] * turn_ref[1],
                part[rows:] * turn_ref[0] + part[:rows] * turn_ref[1],
            ],
            1,
        )
        turned.append(data_parts(both))
    image = nn(jnp.concatenate(turned, 0), ey_back[...])
    columns = image.shape[1] // 2
    return [
        (image[c * rows : (c + 1) * rows, :columns], image[c * rows : (c + 1) * rows, columns:])
        for c in range(coils)
    ]


def add_dots(dots_ref, products):
    rows = lax.broadcasted_iota(jnp.int32, dots_ref.shape, 0)
    total = dots_ref[...]
    for place, (left, right) in enumerate(products):
        total += jnp.where(rows == place, jnp.sum(left * right), 0.0)
    dots_ref[...] = total


def measured_kernel(block, samples, *refs):
    *weights, mx, eb, turn, images, grid = refs
    plane = pl.program_id(0)
    coils = images.shape[0]

    @pl.when(plane == 0)
    def _():
        spread_tiles(block, weights, samples, grid)

    found = adjoint_images(coils, plane, pl.num_programs(0), eb, mx, turn, grid)
    for coil, (real, imag) in enumerate(found):
        images[coil, 0, 0] = real
        images[coil, 0, 1] = imag


def combine(images, sens):
    total_real = total_imag = 0.0
    for (real, imag), sens_ref in zip(images, sens):
        sens_real = sens_ref[0, 0, 0].astype(f32)
        sens_imag = sens_ref[0, 0, 1].astype(f32)
        total_real += sens_real * real + sens_imag * imag
        total_imag += sens_real * imag - sens_imag * real
    return total_real, total_imag


def start_kernel(images, *refs):
    *sens, right_side, rounded, dots = refs
    total = combine([(images[c, 0, 0], images[c, 0, 1]) for c in range(len(sens))], sens)
    for part in range(2):
        right_side[0, part] = total[part]
        rounded[0, part] = total[part].astype(bf16)

    @pl.when((pl.program_id(0) == 0) & (pl.program_id(1) == 0))
    def _():
        dots[...] = jnp.zeros_like(dots)

    add_dots(dots, [(right_side[0], right_side[0])])


def forward_kernel(coils, block, picture, *refs):
    sens = refs[:coils]
    *weights, ey, mx, turn, samples, grid, sums = refs[coils:]
    plane = pl.program_id(0)
    forward_images(plane, pl.num_programs(0), picture, sens, ey, mx, turn, grid)

    @pl.when(plane == pl.num_programs(0) - 1)
    def _():
        sample_tiles(block, weights, grid, sums, samples)


def summed_parts(samples, parts):
    summed = tree_sum([part[...].astype(f32) for part in samples])
    blocks, channels, size = parts.shape[0], parts.shape[1] // 2, parts.shape[2]
    value = summed.reshape(blocks, channels, size)
    high = value.astype(bf16).astype(f32)
    parts[...] = jnp.concatenate([high, value - high], 1).astype(bf16)
    return summed


def step_of(norm, energy):
    return jnp.where(norm > 0.0, norm / (energy + damping * norm), 1.0)


def first_kernel(peers, coils, block, *refs):
    samples, weights, sens = refs[:peers], refs[peers : 2 * peers], refs[2 * peers :][:coils]
    mx, eb, turn, *norms = refs[2 * peers + coils :][: 3 + peers]
    right_side, residual, rounded, facts, dots, total_samples, grid, parts = refs[-8:]
    plane = pl.program_id(0)

    @pl.when(plane == 0)
    def _():
        summed = summed_parts(samples, parts)
        total_samples[...] = summed
        rows = lax.broadcasted_iota(jnp.int32, facts.shape, 0)
        norm = tree_sum([part[...] for part in norms])
        facts[...] = jnp.where(rows == 1, jnp.sum(summed * summed), norm)
        dots[...] = jnp.zeros_like(dots)
        spread_tiles(block, weights, parts, grid)

    images = adjoint_images(coils, plane, pl.num_programs(0), eb, mx, turn, grid)
    total = combine(images, sens)
    scale = step_of(facts[0:1, 0:1], facts[1:2, 0:1])
    for part in range(2):
        vector = right_side[0, part]
        value = vector - scale * (total[part] + damping * vector)
        residual[0, part] = value
        rounded[0, part] = value.astype(bf16)
        add_dots(dots, [(value, value), (value, vector)])


def second_kernel(peers, coils, block, *refs):
    samples, weights, sens = refs[:peers], refs[peers : 2 * peers], refs[2 * peers :][:coils]
    mx, eb, turn, facts, residual, rounded, grid, parts = refs[2 * peers + coils :]
    plane = pl.program_id(0)

    @pl.when(plane == 0)
    def _():
        summed_parts(samples, parts)
        spread_tiles(block, weights, parts, grid)

    images = adjoint_images(coils, plane, pl.num_programs(0), eb, mx, turn, grid)
    total = combine(images, sens)
    scale = step_of(facts[0:1, 0:1], facts[1:2, 0:1])
    for part in range(2):
        vector = residual[0, part]
        again = total[part] + damping * vector
        rounded[0, part] = (vector - scale * again).astype(bf16)


def facts_kernel(peers, *refs):
    samples, dots = refs[:peers], refs[peers : 2 * peers]
    start_total, facts, out = refs[2 * peers :]
    both = tree_sum([part[...] for part in dots])
    summed = tree_sum([part[...].astype(f32) for part in samples])
    rows = lax.broadcasted_iota(jnp.int32, out.shape, 0)
    values = [facts[0:1], facts[1:2], both[0:1], both[1:2]]
    values += [jnp.sum(summed * summed), jnp.sum(summed * start_total[...])]
    total = jnp.zeros(out.shape, f32)
    for row, value in enumerate(values):
        total = jnp.where(rows == row, value, total)
    out[...] = total


def coefficients(norm, energy, square, cross, again, mixed):
    def over_all(values):
        return tree_sum([sum(of_coil) for of_coil in values])

    def each(function, *lists):
        return [[function(*items) for items in zip(*of_coil)] for of_coil in zip(*lists)]

    start_curve = each(lambda e, n: e + damping * n, energy, norm)
    curve = each(lambda e, n: e + damping * n, again, square)
    mixed_curve = each(lambda e, n: e + damping * n, mixed, cross)
    sigma = each(step_of, norm, energy)
    start_norm = over_all(norm)
    first_step = start_norm / over_all(start_curve)
    part = each(lambda s: first_step / s, sigma)
    next_norm = over_all(
        each(
            lambda w, n, c, s: w * w * s + 2.0 * w * (1.0 - w) * c + (1.0 - w) * (1.0 - w) * n,
            part,
            norm,
            cross,
            square,
        )
    )
    more = each(lambda w: 1.0 - w + next_norm / start_norm, part)
    second_step = next_norm / over_all(
        each(
            lambda w, m, q, c, s, z, qm, qs: w * w * q
            + w * m * ((c - s) / z + qm)
            + m * m * qs,
            part,
            more,
            curve,
            cross,
            square,
            sigma,
            mixed_curve,
            start_curve,
        )
    )
    share = each(lambda z: second_step / z, sigma)
    picture = each(lambda w, m: (first_step + second_step * m, second_step * w), part, more)
    residual = each(
        lambda w, m, h: (1.0 - w - h * m, w - h * w + h * m, h * w), part, more, share
    )
    return picture, residual


def assemble_kernel(coils, group_steps, combos, is_residual, has_out, order, *refs):
    infos, pieces, (out, kept) = refs[:coils], refs[coils:-2], refs[-2:]
    groups = infos[0].shape[0]
    count = 3 if is_residual else 2

    @pl.when(pl.program_id(0) == 0)
    def _():
        numbers = [
            [[info[g, row : row + 1, 0:1] for g in range(groups)] for info in infos]
            for row in range(6)
        ]
        factors = coefficients(*numbers)[is_residual]
        rows = lax.broadcasted_iota(jnp.int32, kept.shape[1:], 0)
        for place, (k, g) in enumerate(combos):
            total = jnp.zeros(kept.shape[1:], f32)
            for row, factor in enumerate(factors[k][g]):
                total = jnp.where(rows == row, factor, total)
            kept[place] = total

    for place in range(len(combos)):

        @pl.when(pl.program_id(0) // group_steps == place)
        def _():
            total = 0.0
            for row, piece in enumerate(pieces[place * count :][:count]):
                factor = kept[place, row : row + 1, 0:1].reshape(1, 1, 1, 1)
                total += factor * piece[...].astype(f32)
            out[...] = total


def group_count_of(own_planes):
    return 1


def whole_block(array):
    rank = len(array.shape)
    return pl.BlockSpec(array.shape, lambda *_: (0,) * rank)


def on_device(kspace, sens_maps, weights, tile_slot, tile_block, send_list):
    coil_count = lax.axis_size("coil")
    peers = lax.axis_size("pencil")
    planes = sens_maps.shape[1]
    own_planes = planes // coil_count
    rows = sens_maps.shape[3]
    columns = sens_maps.shape[4]
    rows_total = rows * peers
    size = weights.shape[1]
    tile_count = tile_slot.shape[0]
    tiles = tile_count * peers
    blocks_dev = kspace.shape[3] // size
    blocks = blocks_dev * peers
    cap = send_list.shape[2]
    runs = rows_total // size
    brick_dev = columns // peers * runs
    images_count = coil_count * own_planes
    channels = 2 * images_count

    coil_index = lax.axis_index("coil")

    def swapped(array, axis, k):
        return lax.ppermute(array, axis, [(i, i ^ k) for i in range(lax.axis_size(axis))])

    def everywhere(array, axis):
        bit = 1
        while bit < lax.axis_size(axis):
            bit *= 2
        pieces = {0: array}
        while bit > 1:
            bit //= 2
            for k in sorted(pieces):
                pieces[k ^ bit] = swapped(pieces[k], axis, bit)
        return [pieces[k] for k in sorted(pieces)]

    first_bits = [1 << bit for bit in range(coil_count.bit_length() - 1)]

    def completed(own, sent):
        pieces = {0: own}
        for bit, piece in zip(first_bits, sent):
            pieces[bit] = piece
        for bit in first_bits:
            for k in range(coil_count):
                if k not in pieces and (k ^ bit) in pieces:
                    pieces[k] = swapped(pieces[k ^ bit], "coil", bit)
        return [pieces[k] for k in range(coil_count)]

    def to_planes(array):
        pieces = []
        for k in range(coil_count):
            part = lax.dynamic_slice_in_dim(array, (coil_index ^ k) * own_planes, own_planes, 0)
            pieces.append(swapped(part, "coil", k) if k > 0 else part)
        return pieces

    group_planes = own_planes // group_count_of(own_planes)
    groups = range(own_planes // group_planes)
    measured = to_planes(kspace[0])
    packed = jnp.concatenate([tile_slot, tile_block, send_list.reshape(-1)])
    sens_source, packed, measured = lax.optimization_barrier((sens_maps[0], packed, measured))
    sens_source = sens_source.reshape(coil_count, own_planes, 2, rows, columns)
    sens = [
        lax.all_to_all(
            sens_source[:, g * group_planes : (g + 1) * group_planes],
            "coil",
            split_axis=0,
            concat_axis=0,
            tiled=True,
        )
        for g in groups
    ]
    measured = jnp.stack(measured)
    by_coil = jnp.arange(coil_count, dtype=jnp.int32) ^ coil_index
    measured = jnp.take(measured, by_coil, axis=0)
    all_weights = everywhere(weights, "pencil")
    turned_weights = [jnp.swapaxes(array, 1, 2) for array in all_weights]

    places = jnp.stack(everywhere(packed, "pencil"))
    holder = (jnp.arange(peers, dtype=jnp.int32) ^ lax.axis_index("pencil"))[:, None]
    by_owner = jnp.take(places, holder[:, 0], axis=0)
    lists = by_owner[:, 2 * tile_count :].reshape(peers, peers, cap)
    slots = places[:, :tile_count]
    block_of = (places[:, tile_count : 2 * tile_count] + blocks_dev * holder).reshape(-1)
    brick = (slots // cap * brick_dev + lists[slots // cap, holder, slots % cap]).reshape(-1)
    line = brick // runs
    run = brick % runs

    measured = measured.reshape(channels, blocks_dev, size)
    measured = jnp.concatenate(everywhere(jnp.swapaxes(measured, 0, 1), "pencil"), 0)
    measured_block = (
        places[:, tile_count : 2 * tile_count]
        + blocks_dev * jnp.arange(peers, dtype=jnp.int32)[:, None]
    ).reshape(-1)

    cos_y, sin_y = wave(
        line - columns // 2, jnp.arange(columns, dtype=jnp.int32) - columns // 2, columns
    )
    row_ids = jnp.arange(rows, dtype=jnp.int32) + lax.axis_index("pencil") * rows - rows_total // 2
    cos_x, sin_x = wave(
        row_ids, jnp.arange(size, dtype=jnp.int32) - rows_total // 2, rows_total
    )
    turn = jnp.stack(quarter_turns(run, row_ids, runs))
    turn_back = jnp.stack(quarter_turns(row_ids, run, runs))

    def exchanged(partial, axis="pencil"):
        count = lax.axis_size(axis)
        return [partial] + [swapped(partial, axis, k) for k in range(1, count)]

    group_shape = (group_planes, 2, rows, columns)
    group_images = coil_count * group_planes
    group_channels = 2 * group_images

    if (
        rows % 128 == 0
        and columns % 128 == 0
        and size % 128 == 0
        and channels % 16 == 0
        and tile_count % 4 == 0
        and group_channels % 8 == 0
    ):
        ey = jnp.concatenate([cos_y, sin_y], 0).astype(bf16)
        eb = jnp.concatenate(
            [jnp.concatenate([cos_y, sin_y], 1), jnp.concatenate([-sin_y, cos_y], 1)], 0
        )
        eb = table_parts(eb, 0)
        mx = jnp.concatenate(
            [jnp.concatenate([cos_x, -sin_x], 1), jnp.concatenate([sin_x, cos_x], 1)], 0
        )
        mx, mx_back = mx.astype(bf16), table_parts(mx, 1)
        measured, ey, mx, turn, block_of = lax.optimization_barrier(
            (measured, ey, mx, turn, block_of)
        )
        places_spec = pl.BlockSpec(memory_space=pltpu.SMEM)
        plane_spec = pl.BlockSpec((1, 2, rows, columns), lambda p: (p, 0, 0, 0))
        sens_specs = [
            pl.BlockSpec((1, 1, 2, rows, columns), functools.partial(lambda c, p: (c, p, 0, 0, 0), c))
            for c in range(coil_count)
        ]
        grid_scratch = pltpu.VMEM((tiles * group_channels, size), f32)
        params = pltpu.CompilerParams(vmem_limit_bytes=vmem_limit)
        tail_tables = [mx_back, eb, turn_back]

        def shaped(shape, dtype=f32):
            return jax.ShapeDtypeStruct(shape, dtype)

        def call(kernel, grid, inputs, specs, outs, out_specs, scratch, images):
            flops = 2 * images * 8 * tiles * rows * (columns + size)
            return pl.pallas_call(
                kernel,
                grid=grid,
                in_specs=specs,
                out_specs=out_specs,
                out_shape=outs,
                scratch_shapes=scratch,
                compiler_params=params,
                cost_estimate=pl.CostEstimate(
                    flops=flops,
                    bytes_accessed=sum(math.prod(i.shape) * i.dtype.itemsize for i in inputs),
                    transcendentals=0,
                ),
            )(*inputs)

        def measured_images():
            inputs = [measured_block, measured, *turned_weights, *tail_tables]
            shape = (coil_count, own_planes, 2, rows, columns)
            return call(
                measured_kernel,
                (own_planes,),
                inputs,
                [places_spec] + [whole_block(i) for i in inputs[1:]],
                shaped(shape),
                pl.BlockSpec((coil_count, 1, 2, rows, columns), lambda p: (0, p, 0, 0, 0)),
                [pltpu.VMEM((tiles * channels, size), f32)],
                images_count,
            )

        def start(images, g):
            chunk = 64
            spec = pl.BlockSpec((1, 2, chunk, columns), lambda p, r: (p, 0, r, 0))
            images_spec = pl.BlockSpec(
                (coil_count, 1, 2, chunk, columns),
                lambda p, r: (0, p + g * group_planes, 0, r, 0),
            )
            dots_shape = shaped((8, 128))
            return call(
                start_kernel,
                (group_planes, rows // chunk),
                [images] + [sens[g]] * coil_count,
                [images_spec]
                + [
                    pl.BlockSpec(
                        (1, 1, 2, chunk, columns),
                        functools.partial(lambda c, p, r: (c, p, 0, r, 0), c),
                    )
                    for c in range(coil_count)
                ],
                [shaped(group_shape), shaped(group_shape, bf16), dots_shape],
                [spec, spec, whole_block(dots_shape)],
                [],
                0,
            )

        def forward(picture, g):
            tail = [*all_weights, ey, mx, turn]
            out = shaped((blocks * group_channels, size), bf16)
            return call(
                functools.partial(forward_kernel, coil_count),
                (group_planes,),
                [block_of, picture] + [sens[g]] * coil_count + tail,
                [places_spec, plane_spec] + sens_specs + [whole_block(i) for i in tail],
                out,
                whole_block(out),
                [grid_scratch, pltpu.VMEM((blocks, group_channels, size), f32)],
                group_images,
            )

        def back(kernel, samples, tables, vectors, g, outs, out_specs):
            inputs = [*samples, *turned_weights]
            tables = tail_tables + tables
            return call(
                functools.partial(kernel, peers, coil_count),
                (group_planes,),
                [block_of, *inputs] + [sens[g]] * coil_count + tables + vectors,
                [places_spec]
                + [whole_block(i) for i in inputs]
                + sens_specs
                + [whole_block(i) for i in tables]
                + [plane_spec] * len(vectors),
                outs,
                out_specs,
                [grid_scratch, pltpu.VMEM((blocks, 2 * group_channels, size), bf16)],
                group_images,
            )

        def first(samples, norms, right_side, g):
            small, large = shaped((8, 128)), shaped(samples[0].shape)
            return back(
                first_kernel,
                samples,
                norms,
                [right_side],
                g,
                [shaped(group_shape), shaped(group_shape, bf16), small, small, large],
                [plane_spec, plane_spec] + [whole_block(i) for i in (small, small, large)],
            )

        def facts_of(samples, dots, start_total, facts):
            inputs = [*samples, *dots, start_total, facts]
            return pl.pallas_call(
                functools.partial(facts_kernel, peers),
                in_specs=[pl.BlockSpec(memory_space=pltpu.VMEM)] * len(inputs),
                out_specs=pl.BlockSpec(memory_space=pltpu.VMEM),
                out_shape=shaped((8, 128)),
                compiler_params=params,
            )(*inputs)

        def assembled(infos, vectors, ks, out=None):
            combos = [(k, g) for k in ks for g in groups]
            order = jnp.stack(
                [
                    (coil_index ^ k) * own_planes + g * group_planes + p
                    for k, g in combos
                    for p in range(group_planes)
                ]
            ).astype(jnp.int32)
            inputs = [vector[g][k] for k, g in combos for vector in vectors]

            def spec(place):
                first_step = place // len(vectors) * group_planes
                return pl.BlockSpec(
                    (1, 2, rows, columns),
                    lambda i, o: (jnp.clip(i - first_step, 0, group_planes - 1), 0, 0, 0),
                )

            specs = [pl.BlockSpec(infos[0].shape, lambda i, o: (0, 0, 0))] * len(infos)
            specs += [spec(place) for place in range(len(inputs))]
            aliases = {}
            kernel = functools.partial(
                assemble_kernel,
                coil_count,
                group_planes,
                combos,
                len(vectors) == 3,
                out is not None,
            )
            if out is not None:
                aliases = {1 + len(infos) + len(inputs): 0}
                inputs = inputs + [out]
                specs.append(pl.BlockSpec(memory_space=pl.ANY))

            return pl.pallas_call(
                kernel,
                grid_spec=pltpu.PrefetchScalarGridSpec(
                    num_scalar_prefetch=1,
                    grid=(len(combos) * group_planes,),
                    in_specs=specs,
                    out_specs=pl.BlockSpec((1, 2, rows, columns), lambda i, o: (o[i], 0, 0, 0)),
                    scratch_shapes=[pltpu.VMEM((len(combos), 8, 128), f32)],
                ),
                out_shape=shaped((planes, 2, rows, columns)),
                input_output_aliases=aliases,
                compiler_params=params,
            )(order, *infos, *inputs)

        def second(samples, facts, residual, g):
            return back(
                second_kernel,
                samples,
                [facts],
                [residual],
                g,
                shaped(group_shape, bf16),
                plane_spec,
            )

    else:
        ein = functools.partial(jnp.einsum, precision=lax.Precision.HIGH)
        maps = [array.astype(f32) for array in sens]
        block_map = (block_of[:, None] == jnp.arange(blocks, dtype=jnp.int32)).astype(f32)
        tc, ts = turn[0][:, None, None], turn[1][:, None, None]
        wide_weights = jnp.concatenate(all_weights, 0).astype(f32)

        def forward(picture, g):
            map_real, map_imag = maps[g][:, :, 0], maps[g][:, :, 1]
            coil_real = map_real * picture[None, :, 0] - map_imag * picture[None, :, 1]
            coil_imag = map_real * picture[None, :, 1] + map_imag * picture[None, :, 0]
            half_real = ein("ty,cpxy->tcpx", cos_y, coil_real) + ein(
                "ty,cpxy->tcpx", sin_y, coil_imag
            )
            half_imag = ein("ty,cpxy->tcpx", cos_y, coil_imag) - ein(
                "ty,cpxy->tcpx", sin_y, coil_real
            )
            real = half_real * tc + half_imag * ts
            imag = half_imag * tc - half_real * ts
            grid = jnp.stack(
                [
                    ein("tcpx,xi->tcpi", real, cos_x) + ein("tcpx,xi->tcpi", imag, sin_x),
                    ein("tcpx,xi->tcpi", imag, cos_x) - ein("tcpx,xi->tcpi", real, sin_x),
                ],
                3,
            ).reshape(tiles, group_channels, size)
            product = ein("tgi,tis->tgs", grid, wide_weights)
            return ein("tb,tgs->bgs", block_map, product).astype(bf16).reshape(-1, size)

        def images_of(samples, blocks_of):
            spread = ein("tgs,tis->tgi", jnp.take(samples, blocks_of, axis=0), wide_weights)
            spread = spread.reshape(tiles, coil_count, -1, 2, size)
            back_real = ein("tcpi,xi->tcpx", spread[:, :, :, 0], cos_x) - ein(
                "tcpi,xi->tcpx", spread[:, :, :, 1], sin_x
            )
            back_imag = ein("tcpi,xi->tcpx", spread[:, :, :, 1], cos_x) + ein(
                "tcpi,xi->tcpx", spread[:, :, :, 0], sin_x
            )
            real = back_real * tc - back_imag * ts
            imag = back_imag * tc + back_real * ts
            return jnp.stack(
                [
                    ein("tcpx,ty->cpxy", real, cos_y) - ein("tcpx,ty->cpxy", imag, sin_y),
                    ein("tcpx,ty->cpxy", imag, cos_y) + ein("tcpx,ty->cpxy", real, sin_y),
                ],
                2,
            )

        def combined(images, g):
            map_real, map_imag = maps[g][:, :, 0], maps[g][:, :, 1]
            real, imag = images[:, :, 0], images[:, :, 1]
            return jnp.stack(
                [
                    jnp.sum(map_real * real + map_imag * imag, 0),
                    jnp.sum(map_real * imag - map_imag * real, 0),
                ],
                1,
            )

        def stacked_dots(values):
            values = values + [jnp.zeros((), f32)] * (8 - len(values))
            return jnp.broadcast_to(jnp.stack(values)[:, None], (8, 128))

        def applied_to(samples, vector, g):
            samples = added(samples).reshape(blocks, group_channels, size)
            return combined(images_of(samples, block_of), g) + damping * vector

        def measured_images():
            return images_of(measured.astype(f32), measured_block)

        def start(images, g):
            right_side = combined(images[:, g * group_planes : (g + 1) * group_planes], g)
            dots = stacked_dots([jnp.sum(right_side * right_side)])
            return right_side, right_side.astype(bf16), dots

        def first(samples, norms, right_side, g):
            norm = tree_sum(norms)[0, 0]
            total = added(samples)
            energy = jnp.sum(jnp.square(total))
            residual = right_side - step_of(norm, energy) * applied_to(samples, right_side, g)
            dots = [jnp.sum(residual * residual), jnp.sum(residual * right_side)]
            facts = stacked_dots([norm, energy])
            return residual, residual.astype(bf16), facts, stacked_dots(dots), total

        def facts_of(samples, dots, start_total, facts):
            total = added(samples)
            square, cross = tree_sum(dots)[:2, 0]
            values = [facts[0, 0], facts[1, 0], square, cross]
            values += [jnp.sum(total * total), jnp.sum(total * start_total)]
            return stacked_dots(values)

        def assembled(infos, vectors, ks, out=None):
            numbers = [
                [[info[g, row, 0] for g in groups] for info in infos] for row in range(6)
            ]
            factors = coefficients(*numbers)[len(vectors) == 3]
            if out is None:
                out = jnp.zeros((planes, 2, rows, columns), f32)
            for k in ks:
                for g in groups:
                    place = ((coil_index ^ k) * own_planes + g * group_planes, 0, 0, 0)
                    piece = sum(
                        factor * vector[g][k].astype(f32)
                        for factor, vector in zip(factors[k][g], vectors)
                    )
                    out = lax.dynamic_update_slice(out, piece, place)
            return out

        def second(samples, facts, residual, g):
            again = applied_to(samples, residual, g)
            return (residual - step_of(facts[0, 0], facts[1, 0]) * again).astype(bf16)

    def added(samples):
        return tree_sum([part.astype(f32) for part in samples])

    def sent_by_bits(own):
        return [swapped(own, "coil", k) for k in first_bits]

    images = measured_images()
    start_pieces, residual_pieces, mixed_own, mixed_sent, infos = [], [], [], [], []
    for g in groups:
        right_side, start_own, norm = start(images, g)
        start_sent = sent_by_bits(start_own)
        samples = exchanged(forward(right_side, g))
        norms = exchanged(norm)
        samples, norms, start_sent = lax.optimization_barrier((samples, norms, start_sent))
        residual, residual_own, facts, dots, start_total = first(samples, norms, right_side, g)
        residual, residual_own, pieces = lax.optimization_barrier(
            (residual, residual_own, completed(start_own, start_sent))
        )
        start_pieces.append(pieces)
        residual_sent = sent_by_bits(residual_own)
        dots = exchanged(dots)
        samples = exchanged(forward(residual, g))
        samples, dots, residual_sent = lax.optimization_barrier((samples, dots, residual_sent))
        info = facts_of(samples, dots, start_total, facts)
        infos.append(info)
        rounded = second(samples, info, residual, g)
        last = g == groups[-1]
        others = exchanged(jnp.stack(infos), "coil") if last else []
        rounded, others, pieces = lax.optimization_barrier(
            (rounded, others, completed(residual_own, residual_sent))
        )
        residual_pieces.append(pieces)
        mixed_own.append(rounded)
        mixed_sent.append(sent_by_bits(rounded))

    picture = assembled(others, [start_pieces, residual_pieces], range(coil_count))
    early = [
        [own, sent[0]] + [None] * (coil_count - 2)
        for own, sent in zip(mixed_own, mixed_sent)
    ]
    out = assembled(others, [start_pieces, residual_pieces, early], range(2))
    picture, out, mixed_sent = lax.optimization_barrier((picture, out, mixed_sent))
    mixed_pieces = [completed(own, sent) for own, sent in zip(mixed_own, mixed_sent)]
    vectors = [start_pieces, residual_pieces, mixed_pieces]
    late = coil_count - 1
    out = assembled(others, vectors, range(2, late), out)
    out = assembled(others, vectors, [late], out)
    return picture, out


def solution(mesh):
    in_specs = (
        P("coil", "scan", None, "pencil"),
        P("coil", "scan", None, "pencil", None),
        P("pencil", None, None),
        P("pencil"),
        P("pencil"),
        P("pencil", None, None),
    )
    out_specs = (P("scan", None, "pencil", None), P("scan", None, "pencil", None))
    return jax.shard_map(
        on_device, mesh=mesh, in_specs=in_specs, out_specs=out_specs, check_vma=False
    )
```

```python
import functools
import math

import jax
import jax.numpy as jnp
from jax import lax
from jax.experimental import pallas as pl
from jax.experimental.pallas import tpu as pltpu
from jax.sharding import PartitionSpec as P


damping = 0.5
f32, bf16 = jnp.float32, jnp.bfloat16
vmem_limit = 56 * 1024 * 1024


def wave(left, right, length):
    phases = left[:, None] * right[None, :] % length
    angles = phases.astype(f32) * (2.0 * math.pi / length)
    return jnp.cos(angles) / math.sqrt(length), jnp.sin(angles) / math.sqrt(length)


def quarter_turns(left, right, count):
    turns = left[:, None] * right[None, :] % count
    if count == 4:
        cosine = jnp.where(turns == 0, 1.0, 0.0) - jnp.where(turns == 2, 1.0, 0.0)
        sine = jnp.where(turns == 1, 1.0, 0.0) - jnp.where(turns == 3, 1.0, 0.0)
        return cosine.astype(f32), sine.astype(f32)
    angles = turns.astype(f32) * (2.0 * math.pi / count)
    return jnp.cos(angles), jnp.sin(angles)


def split(value):
    high = value.astype(bf16)
    return high, (value - high.astype(f32)).astype(bf16)


def table_parts(table, axis):
    high = lax.reduce_precision(table, 8, 7)
    low = (table - high).astype(bf16)
    high = high.astype(bf16)
    return jnp.concatenate([high, high, low], axis)


def data_parts(value):
    high, low = split(value)
    return jnp.concatenate([high, low, high], 1)


def nt(left, right):
    return lax.dot_general(left, right, (((1,), (1,)), ((), ())), preferred_element_type=f32)


def nn(left, right):
    return jnp.dot(left, right, preferred_element_type=f32)


def tree_sum(values):
    while len(values) > 1:
        values = [left + right for left, right in zip(values[::2], values[1::2])]
    return values[0]


def forward_images(plane, planes, picture, sens, ey, mx, turn_ref, grid_ref):
    tiles = turn_ref.shape[1]
    rows = turn_ref.shape[2]
    channels = grid_ref.shape[0] // tiles
    real, imag = picture[0, 0], picture[0, 1]
    turned = []
    for sens_ref in sens:
        sens_real = sens_ref[0, 0, 0].astype(f32)
        sens_imag = sens_ref[0, 0, 1].astype(f32)
        coil = jnp.concatenate(
            [sens_real * real - sens_imag * imag, sens_real * imag + sens_imag * real], 0
        )
        both = nt(ey[...], coil.astype(bf16))
        half_real = both[:tiles, :rows] + both[tiles:, rows:]
        half_imag = both[:tiles, rows:] - both[tiles:, :rows]
        turned.append(
            jnp.concatenate(
                [
                    half_real * turn_ref[0] + half_imag * turn_ref[1],
                    half_imag * turn_ref[0] - half_real * turn_ref[1],
                ],
                1,
            ).astype(bf16)
        )
    grid = nn(jnp.concatenate(turned, 0), mx[...])
    size = grid.shape[1] // 2
    for coil in range(len(sens)):
        step = coil * planes + plane
        part = grid[coil * tiles : (coil + 1) * tiles]
        grid_ref[pl.ds(2 * step, tiles, stride=channels), :] = part[:, :size]
        grid_ref[pl.ds(2 * step + 1, tiles, stride=channels), :] = part[:, size:]


def tile_products(lefts, rights):
    rows, size = lefts[0].shape
    empty = jnp.zeros((rows, size), bf16)
    left = jnp.concatenate(
        [
            jnp.concatenate([value, empty] if place % 2 == 0 else [empty, value], 1)
            for place, value in enumerate(lefts)
        ],
        0,
    )
    right = jnp.concatenate(
        [jnp.concatenate(rights[:2], 0), jnp.concatenate(rights[2:], 0)], 1
    )
    product = nn(left, right)
    return [
        product[place * rows : (place + 1) * rows, place // 2 * size : (place // 2 + 1) * size]
        for place in range(4)
    ]


def each_four(count, function):
    def one(index, carry):
        function([index * 4 + place for place in range(4)])
        return carry

    lax.fori_loop(0, count // 4, one, 0, unroll=True)


def weight_copies(weights, held, sems):
    return [
        pltpu.make_async_copy(ref, held.at[place], sems.at[place])
        for place, ref in enumerate(weights)
    ]


def start_copies(copies):
    for copy in copies:
        copy.start()


def sample_tiles(block_ref, copies, weights, grid_ref, sums_ref, out_ref):
    count = weights.shape[1]
    channels = sums_ref.shape[1]
    sums_ref[...] = jnp.zeros_like(sums_ref)

    def left_of(tile):
        value = grid_ref[pl.ds(pl.multiple_of(tile * channels, channels), channels), :]
        high = value.astype(bf16).astype(f32)
        return jnp.concatenate([high, value - high], 0).astype(bf16)

    for group, copy in enumerate(copies):
        copy.wait()

        def four(places):
            tiles = [group * count + place for place in places]
            products = tile_products(
                [left_of(tile) for tile in tiles], [weights[group, place] for place in places]
            )
            for tile, product in zip(tiles, products):
                sums_ref[block_ref[tile]] += product[:channels] + product[channels:]

        each_four(count, four)
    out_ref[...] = sums_ref[...].reshape(out_ref.shape).astype(bf16)


def spread_tiles(block_ref, copies, weights, parts_ref, grid_ref):
    count = weights.shape[1]
    channels = grid_ref.shape[0] // (count * len(copies))

    for group, copy in enumerate(copies):
        copy.wait()

        def four(places):
            tiles = [group * count + place for place in places]
            products = tile_products(
                [parts_ref[block_ref[tile]] for tile in tiles],
                [weights[group, place] for place in places],
            )
            for tile, product in zip(tiles, products):
                if product.shape[0] > channels:
                    product = product[:channels] + product[channels:]
                start = pl.multiple_of(tile * channels, channels)
                grid_ref[pl.ds(start, channels), :] = product

        each_four(count, four)


def adjoint_images(coils, plane, planes, ey_back, mx_back, turn_ref, grid_ref):
    rows, tiles = turn_ref.shape[1], turn_ref.shape[2]
    channels = grid_ref.shape[0] // tiles
    grids = []
    for coil in range(coils):
        step = coil * planes + plane
        grid = jnp.concatenate(
            [
                grid_ref[pl.ds(2 * step, tiles, stride=channels), :],
                grid_ref[pl.ds(2 * step + 1, tiles, stride=channels), :],
            ],
            1,
        )
        grids.append(data_parts(grid))
    back = nt(mx_back[...], jnp.concatenate(grids, 0))
    turned = []
    for coil in range(coils):
        part = back[:, coil * tiles : (coil + 1) * tiles]
        both = jnp.concatenate(
            [
                part[:rows] * turn_ref[0] - part[rows:] * turn_ref[1],
                part[rows:] * turn_ref[0] + part[:rows] * turn_ref[1],
            ],
            1,
        )
        turned.append(data_parts(both))
    image = nn(jnp.concatenate(turned, 0), ey_back[...])
    columns = image.shape[1] // 2
    return [
        (image[c * rows : (c + 1) * rows, :columns], image[c * rows : (c + 1) * rows, columns:])
        for c in range(coils)
    ]


def add_dots(dots_ref, products):
    rows = lax.broadcasted_iota(jnp.int32, dots_ref.shape, 0)
    total = dots_ref[...]
    for place, (left, right) in enumerate(products):
        total += jnp.where(rows == place, jnp.sum(left * right), 0.0)
    dots_ref[...] = total


def measured_kernel(block, samples, *refs):
    *weights, mx, eb, turn, images, grid, held, sems = refs
    plane = pl.program_id(0)
    coils = images.shape[0]

    @pl.when(plane == 0)
    def _():
        copies = weight_copies(weights, held, sems)
        start_copies(copies)
        spread_tiles(block, copies, held, samples, grid)

    found = adjoint_images(coils, plane, pl.num_programs(0), eb, mx, turn, grid)
    for coil, (real, imag) in enumerate(found):
        images[coil, 0, 0] = real
        images[coil, 0, 1] = imag


def combine(images, sens):
    total_real = total_imag = 0.0
    for (real, imag), sens_ref in zip(images, sens):
        sens_real = sens_ref[0, 0, 0].astype(f32)
        sens_imag = sens_ref[0, 0, 1].astype(f32)
        total_real += sens_real * real + sens_imag * imag
        total_imag += sens_real * imag - sens_imag * real
    return total_real, total_imag


def start_kernel(images, *refs):
    *sens, right_side, rounded, dots = refs
    total = combine([(images[c, 0, 0], images[c, 0, 1]) for c in range(len(sens))], sens)
    for part in range(2):
        right_side[0, part] = total[part]
        rounded[0, part] = total[part].astype(bf16)

    @pl.when((pl.program_id(0) == 0) & (pl.program_id(1) == 0))
    def _():
        dots[...] = jnp.zeros_like(dots)

    add_dots(dots, [(right_side[0], right_side[0])])


def forward_kernel(coils, block, picture, *refs):
    sens = refs[:coils]
    *weights, ey, mx, turn, samples, grid, sums, held, sems = refs[coils:]
    plane = pl.program_id(0)

    @pl.when(plane == 0)
    def _():
        start_copies(weight_copies(weights, held, sems))

    forward_images(plane, pl.num_programs(0), picture, sens, ey, mx, turn, grid)

    @pl.when(plane == pl.num_programs(0) - 1)
    def _():
        sample_tiles(block, weight_copies(weights, held, sems), held, grid, sums, samples)


def summed_parts(samples, parts):
    summed = tree_sum([part[...].astype(f32) for part in samples])
    blocks, channels, size = parts.shape[0], parts.shape[1] // 2, parts.shape[2]
    value = summed.reshape(blocks, channels, size)
    high = value.astype(bf16).astype(f32)
    parts[...] = jnp.concatenate([high, value - high], 1).astype(bf16)
    return summed


def step_of(norm, energy):
    return jnp.where(norm > 0.0, norm / (energy + damping * norm), 1.0)


def first_kernel(peers, coils, block, *refs):
    samples, weights, sens = refs[:peers], refs[peers : 2 * peers], refs[2 * peers :][:coils]
    mx, eb, turn, *norms = refs[2 * peers + coils :][: 3 + peers]
    right_side, residual, rounded, facts, dots, total_samples, grid, parts, held, sems = refs[-10:]
    plane = pl.program_id(0)

    @pl.when(plane == 0)
    def _():
        copies = weight_copies(weights, held, sems)
        start_copies(copies)
        summed = summed_parts(samples, parts)
        total_samples[...] = summed
        rows = lax.broadcasted_iota(jnp.int32, facts.shape, 0)
        norm = tree_sum([part[...] for part in norms])
        facts[...] = jnp.where(rows == 1, jnp.sum(summed * summed), norm)
        dots[...] = jnp.zeros_like(dots)
        spread_tiles(block, copies, held, parts, grid)

    images = adjoint_images(coils, plane, pl.num_programs(0), eb, mx, turn, grid)
    total = combine(images, sens)
    scale = step_of(facts[0:1, 0:1], facts[1:2, 0:1])
    for part in range(2):
        vector = right_side[0, part]
        value = vector - scale * (total[part] + damping * vector)
        residual[0, part] = value
        rounded[0, part] = value.astype(bf16)
        add_dots(dots, [(value, value), (value, vector)])


def second_kernel(peers, coils, block, *refs):
    samples, weights, sens = refs[:peers], refs[peers : 2 * peers], refs[2 * peers :][:coils]
    mx, eb, turn, facts, residual, rounded, grid, parts, held, sems = refs[2 * peers + coils :]
    plane = pl.program_id(0)

    @pl.when(plane == 0)
    def _():
        copies = weight_copies(weights, held, sems)
        start_copies(copies)
        summed_parts(samples, parts)
        spread_tiles(block, copies, held, parts, grid)

    images = adjoint_images(coils, plane, pl.num_programs(0), eb, mx, turn, grid)
    total = combine(images, sens)
    scale = step_of(facts[0:1, 0:1], facts[1:2, 0:1])
    for part in range(2):
        vector = residual[0, part]
        again = total[part] + damping * vector
        rounded[0, part] = (vector - scale * again).astype(bf16)


def facts_kernel(peers, *refs):
    samples, dots = refs[:peers], refs[peers : 2 * peers]
    start_total, facts, out = refs[2 * peers :]
    both = tree_sum([part[...] for part in dots])
    summed = tree_sum([part[...].astype(f32) for part in samples])
    rows = lax.broadcasted_iota(jnp.int32, out.shape, 0)
    values = [facts[0:1], facts[1:2], both[0:1], both[1:2]]
    values += [jnp.sum(summed * summed), jnp.sum(summed * start_total[...])]
    total = jnp.zeros(out.shape, f32)
    for row, value in enumerate(values):
        total = jnp.where(rows == row, value, total)
    out[...] = total


def coefficients(norm, energy, square, cross, again, mixed):
    def over_all(values):
        return tree_sum([sum(of_coil) for of_coil in values])

    def each(function, *lists):
        return [[function(*items) for items in zip(*of_coil)] for of_coil in zip(*lists)]

    start_curve = each(lambda e, n: e + damping * n, energy, norm)
    curve = each(lambda e, n: e + damping * n, again, square)
    mixed_curve = each(lambda e, n: e + damping * n, mixed, cross)
    sigma = each(step_of, norm, energy)
    start_norm = over_all(norm)
    first_step = start_norm / over_all(start_curve)
    part = each(lambda s: first_step / s, sigma)
    next_norm = over_all(
        each(
            lambda w, n, c, s: w * w * s + 2.0 * w * (1.0 - w) * c + (1.0 - w) * (1.0 - w) * n,
            part,
            norm,
            cross,
            square,
        )
    )
    more = each(lambda w: 1.0 - w + next_norm / start_norm, part)
    second_step = next_norm / over_all(
        each(
            lambda w, m, q, c, s, z, qm, qs: w * w * q
            + w * m * ((c - s) / z + qm)
            + m * m * qs,
            part,
            more,
            curve,
            cross,
            square,
            sigma,
            mixed_curve,
            start_curve,
        )
    )
    share = each(lambda z: second_step / z, sigma)
    picture = each(lambda w, m: (first_step + second_step * m, second_step * w), part, more)
    residual = each(
        lambda w, m, h: (1.0 - w - h * m, w - h * w + h * m, h * w), part, more, share
    )
    return picture, residual


def assemble_kernel(coils, group_steps, combos, is_residual, has_out, order, *refs):
    infos, pieces, (out, kept) = refs[:coils], refs[coils:-2], refs[-2:]
    groups = infos[0].shape[0]
    count = 3 if is_residual else 2

    @pl.when(pl.program_id(0) == 0)
    def _():
        numbers = [
            [[info[g, row : row + 1, 0:1] for g in range(groups)] for info in infos]
            for row in range(6)
        ]
        factors = coefficients(*numbers)[is_residual]
        rows = lax.broadcasted_iota(jnp.int32, kept.shape[1:], 0)
        for place, (k, g) in enumerate(combos):
            total = jnp.zeros(kept.shape[1:], f32)
            for row, factor in enumerate(factors[k][g]):
                total = jnp.where(rows == row, factor, total)
            kept[place] = total

    for place in range(len(combos)):

        @pl.when(pl.program_id(0) // group_steps == place)
        def _():
            total = 0.0
            for row, piece in enumerate(pieces[place * count :][:count]):
                factor = kept[place, row : row + 1, 0:1].reshape(1, 1, 1, 1)
                total += factor * piece[...].astype(f32)
            out[...] = total


def group_count_of(own_planes):
    return 1


def whole_block(array):
    rank = len(array.shape)
    return pl.BlockSpec(array.shape, lambda *_: (0,) * rank)


def on_device(kspace, sens_maps, weights, tile_slot, tile_block, send_list):
    coil_count = lax.axis_size("coil")
    peers = lax.axis_size("pencil")
    planes = sens_maps.shape[1]
    own_planes = planes // coil_count
    rows = sens_maps.shape[3]
    columns = sens_maps.shape[4]
    rows_total = rows * peers
    size = weights.shape[1]
    tile_count = tile_slot.shape[0]
    tiles = tile_count * peers
    blocks_dev = kspace.shape[3] // size
    blocks = blocks_dev * peers
    cap = send_list.shape[2]
    runs = rows_total // size
    brick_dev = columns // peers * runs
    images_count = coil_count * own_planes
    channels = 2 * images_count

    coil_index = lax.axis_index("coil")

    def swapped(array, axis, k):
        return lax.ppermute(array, axis, [(i, i ^ k) for i in range(lax.axis_size(axis))])

    def everywhere(array, axis):
        bit = 1
        while bit < lax.axis_size(axis):
            bit *= 2
        pieces = {0: array}
        while bit > 1:
            bit //= 2
            for k in sorted(pieces):
                pieces[k ^ bit] = swapped(pieces[k], axis, bit)
        return [pieces[k] for k in sorted(pieces)]

    first_bits = [1 << bit for bit in range(coil_count.bit_length() - 1)]

    def completed(own, sent):
        pieces = {0: own}
        for bit, piece in zip(first_bits, sent):
            pieces[bit] = piece
        for bit in first_bits:
            for k in range(coil_count):
                if k not in pieces and (k ^ bit) in pieces:
                    pieces[k] = swapped(pieces[k ^ bit], "coil", bit)
        return [pieces[k] for k in range(coil_count)]

    def to_planes(array):
        pieces = []
        for k in range(coil_count):
            part = lax.dynamic_slice_in_dim(array, (coil_index ^ k) * own_planes, own_planes, 0)
            pieces.append(swapped(part, "coil", k) if k > 0 else part)
        return pieces

    group_planes = own_planes // group_count_of(own_planes)
    groups = range(own_planes // group_planes)
    measured = to_planes(kspace[0])
    packed = jnp.concatenate([tile_slot, tile_block, send_list.reshape(-1)])
    sens_source, packed, measured = lax.optimization_barrier((sens_maps[0], packed, measured))
    sens_source = sens_source.reshape(coil_count, own_planes, 2, rows, columns)
    sens = [
        lax.all_to_all(
            sens_source[:, g * group_planes : (g + 1) * group_planes],
            "coil",
            split_axis=0,
            concat_axis=0,
            tiled=True,
        )
        for g in groups
    ]
    measured = jnp.stack(measured)
    by_coil = jnp.arange(coil_count, dtype=jnp.int32) ^ coil_index
    measured = jnp.take(measured, by_coil, axis=0)
    all_weights = everywhere(weights, "pencil")
    turned_weights = [jnp.swapaxes(array, 1, 2) for array in all_weights]

    places = jnp.stack(everywhere(packed, "pencil"))
    holder = (jnp.arange(peers, dtype=jnp.int32) ^ lax.axis_index("pencil"))[:, None]
    by_owner = jnp.take(places, holder[:, 0], axis=0)
    lists = by_owner[:, 2 * tile_count :].reshape(peers, peers, cap)
    slots = places[:, :tile_count]
    block_of = (places[:, tile_count : 2 * tile_count] + blocks_dev * holder).reshape(-1)
    brick = (slots // cap * brick_dev + lists[slots // cap, holder, slots % cap]).reshape(-1)
    line = brick // runs
    run = brick % runs

    measured = measured.reshape(channels, blocks_dev, size)
    measured = jnp.concatenate(everywhere(jnp.swapaxes(measured, 0, 1), "pencil"), 0)
    measured_block = (
        places[:, tile_count : 2 * tile_count]
        + blocks_dev * jnp.arange(peers, dtype=jnp.int32)[:, None]
    ).reshape(-1)

    cos_y, sin_y = wave(
        line - columns // 2, jnp.arange(columns, dtype=jnp.int32) - columns // 2, columns
    )
    row_ids = jnp.arange(rows, dtype=jnp.int32) + lax.axis_index("pencil") * rows - rows_total // 2
    cos_x, sin_x = wave(
        row_ids, jnp.arange(size, dtype=jnp.int32) - rows_total // 2, rows_total
    )
    turn = jnp.stack(quarter_turns(run, row_ids, runs))
    turn_back = jnp.stack(quarter_turns(row_ids, run, runs))

    def exchanged(partial, axis="pencil"):
        count = lax.axis_size(axis)
        return [partial] + [swapped(partial, axis, k) for k in range(1, count)]

    group_shape = (group_planes, 2, rows, columns)
    group_images = coil_count * group_planes
    group_channels = 2 * group_images

    if (
        rows % 128 == 0
        and columns % 128 == 0
        and size % 128 == 0
        and channels % 16 == 0
        and tile_count % 4 == 0
        and group_channels % 8 == 0
    ):
        ey = jnp.concatenate([cos_y, sin_y], 0).astype(bf16)
        eb = jnp.concatenate(
            [jnp.concatenate([cos_y, sin_y], 1), jnp.concatenate([-sin_y, cos_y], 1)], 0
        )
        eb = table_parts(eb, 0)
        mx = jnp.concatenate(
            [jnp.concatenate([cos_x, -sin_x], 1), jnp.concatenate([sin_x, cos_x], 1)], 0
        )
        mx, mx_back = mx.astype(bf16), table_parts(mx, 1)
        measured, ey, mx, turn, block_of, all_weights = lax.optimization_barrier(
            (measured, ey, mx, turn, block_of, all_weights)
        )
        places_spec = pl.BlockSpec(memory_space=pltpu.SMEM)
        plane_spec = pl.BlockSpec((1, 2, rows, columns), lambda p: (p, 0, 0, 0))
        sens_specs = [
            pl.BlockSpec((1, 1, 2, rows, columns), functools.partial(lambda c, p: (c, p, 0, 0, 0), c))
            for c in range(coil_count)
        ]
        grid_scratch = pltpu.VMEM((tiles * group_channels, size), f32)
        params = pltpu.CompilerParams(vmem_limit_bytes=vmem_limit)
        tail_tables = [mx_back, eb, turn_back]
        weights_specs = [pl.BlockSpec(memory_space=pl.ANY)] * peers
        held_weights = [
            pltpu.VMEM((peers,) + weights.shape, bf16),
            pltpu.SemaphoreType.DMA((peers,)),
        ]

        def shaped(shape, dtype=f32):
            return jax.ShapeDtypeStruct(shape, dtype)

        def call(kernel, grid, inputs, specs, outs, out_specs, scratch, images):
            flops = 2 * images * 8 * tiles * rows * (columns + size)
            return pl.pallas_call(
                kernel,
                grid=grid,
                in_specs=specs,
                out_specs=out_specs,
                out_shape=outs,
                scratch_shapes=scratch,
                compiler_params=params,
                cost_estimate=pl.CostEstimate(
                    flops=flops,
                    bytes_accessed=sum(math.prod(i.shape) * i.dtype.itemsize for i in inputs),
                    transcendentals=0,
                ),
            )(*inputs)

        def measured_images():
            inputs = [measured_block, measured, *turned_weights, *tail_tables]
            shape = (coil_count, own_planes, 2, rows, columns)
            return call(
                measured_kernel,
                (own_planes,),
                inputs,
                [places_spec, whole_block(measured)]
                + weights_specs
                + [whole_block(i) for i in tail_tables],
                shaped(shape),
                pl.BlockSpec((coil_count, 1, 2, rows, columns), lambda p: (0, p, 0, 0, 0)),
                [pltpu.VMEM((tiles * channels, size), f32)] + held_weights,
                images_count,
            )

        def start(images, g):
            chunk = 64
            spec = pl.BlockSpec((1, 2, chunk, columns), lambda p, r: (p, 0, r, 0))
            images_spec = pl.BlockSpec(
                (coil_count, 1, 2, chunk, columns),
                lambda p, r: (0, p + g * group_planes, 0, r, 0),
            )
            dots_shape = shaped((8, 128))
            return call(
                start_kernel,
                (group_planes, rows // chunk),
                [images] + [sens[g]] * coil_count,
                [images_spec]
                + [
                    pl.BlockSpec(
                        (1, 1, 2, chunk, columns),
                        functools.partial(lambda c, p, r: (c, p, 0, r, 0), c),
                    )
                    for c in range(coil_count)
                ],
                [shaped(group_shape), shaped(group_shape, bf16), dots_shape],
                [spec, spec, whole_block(dots_shape)],
                [],
                0,
            )

        def forward(picture, g):
            tail = [ey, mx, turn]
            out = shaped((blocks * group_channels, size), bf16)
            return call(
                functools.partial(forward_kernel, coil_count),
                (group_planes,),
                [block_of, picture] + [sens[g]] * coil_count + [*all_weights, *tail],
                [places_spec, plane_spec]
                + sens_specs
                + weights_specs
                + [whole_block(i) for i in tail],
                out,
                whole_block(out),
                [grid_scratch, pltpu.VMEM((blocks, group_channels, size), f32)] + held_weights,
                group_images,
            )

        def back(kernel, samples, tables, vectors, g, outs, out_specs):
            tables = tail_tables + tables
            return call(
                functools.partial(kernel, peers, coil_count),
                (group_planes,),
                [block_of, *samples, *turned_weights] + [sens[g]] * coil_count + tables + vectors,
                [places_spec]
                + [whole_block(i) for i in samples]
                + weights_specs
                + sens_specs
                + [whole_block(i) for i in tables]
                + [plane_spec] * len(vectors),
                outs,
                out_specs,
                [grid_scratch, pltpu.VMEM((blocks, 2 * group_channels, size), bf16)] + held_weights,
                group_images,
            )

        def first(samples, norms, right_side, g):
            small, large = shaped((8, 128)), shaped(samples[0].shape)
            return back(
                first_kernel,
                samples,
                norms,
                [right_side],
                g,
                [shaped(group_shape), shaped(group_shape, bf16), small, small, large],
                [plane_spec, plane_spec] + [whole_block(i) for i in (small, small, large)],
            )

        def facts_of(samples, dots, start_total, facts):
            inputs = [*samples, *dots, start_total, facts]
            return pl.pallas_call(
                functools.partial(facts_kernel, peers),
                in_specs=[pl.BlockSpec(memory_space=pltpu.VMEM)] * len(inputs),
                out_specs=pl.BlockSpec(memory_space=pltpu.VMEM),
                out_shape=shaped((8, 128)),
                compiler_params=params,
            )(*inputs)

        def assembled(infos, vectors, ks, out=None):
            combos = [(k, g) for k in ks for g in groups]
            order = jnp.stack(
                [
                    (coil_index ^ k) * own_planes + g * group_planes + p
                    for k, g in combos
                    for p in range(group_planes)
                ]
            ).astype(jnp.int32)
            inputs = [vector[g][k] for k, g in combos for vector in vectors]

            def spec(place):
                first_step = place // len(vectors) * group_planes
                return pl.BlockSpec(
                    (1, 2, rows, columns),
                    lambda i, o: (jnp.clip(i - first_step, 0, group_planes - 1), 0, 0, 0),
                )

            specs = [pl.BlockSpec(infos[0].shape, lambda i, o: (0, 0, 0))] * len(infos)
            specs += [spec(place) for place in range(len(inputs))]
            aliases = {}
            kernel = functools.partial(
                assemble_kernel,
                coil_count,
                group_planes,
                combos,
                len(vectors) == 3,
                out is not None,
            )
            if out is not None:
                aliases = {1 + len(infos) + len(inputs): 0}
                inputs = inputs + [out]
                specs.append(pl.BlockSpec(memory_space=pl.ANY))

            return pl.pallas_call(
                kernel,
                grid_spec=pltpu.PrefetchScalarGridSpec(
                    num_scalar_prefetch=1,
                    grid=(len(combos) * group_planes,),
                    in_specs=specs,
                    out_specs=pl.BlockSpec((1, 2, rows, columns), lambda i, o: (o[i], 0, 0, 0)),
                    scratch_shapes=[pltpu.VMEM((len(combos), 8, 128), f32)],
                ),
                out_shape=shaped((planes, 2, rows, columns)),
                input_output_aliases=aliases,
                compiler_params=params,
            )(order, *infos, *inputs)

        def second(samples, facts, residual, g):
            return back(
                second_kernel,
                samples,
                [facts],
                [residual],
                g,
                shaped(group_shape, bf16),
                plane_spec,
            )

    else:
        ein = functools.partial(jnp.einsum, precision=lax.Precision.HIGH)
        maps = [array.astype(f32) for array in sens]
        block_map = (block_of[:, None] == jnp.arange(blocks, dtype=jnp.int32)).astype(f32)
        tc, ts = turn[0][:, None, None], turn[1][:, None, None]
        wide_weights = jnp.concatenate(all_weights, 0).astype(f32)

        def forward(picture, g):
            map_real, map_imag = maps[g][:, :, 0], maps[g][:, :, 1]
            coil_real = map_real * picture[None, :, 0] - map_imag * picture[None, :, 1]
            coil_imag = map_real * picture[None, :, 1] + map_imag * picture[None, :, 0]
            half_real = ein("ty,cpxy->tcpx", cos_y, coil_real) + ein(
                "ty,cpxy->tcpx", sin_y, coil_imag
            )
            half_imag = ein("ty,cpxy->tcpx", cos_y, coil_imag) - ein(
                "ty,cpxy->tcpx", sin_y, coil_real
            )
            real = half_real * tc + half_imag * ts
            imag = half_imag * tc - half_real * ts
            grid = jnp.stack(
                [
                    ein("tcpx,xi->tcpi", real, cos_x) + ein("tcpx,xi->tcpi", imag, sin_x),
                    ein("tcpx,xi->tcpi", imag, cos_x) - ein("tcpx,xi->tcpi", real, sin_x),
                ],
                3,
            ).reshape(tiles, group_channels, size)
            product = ein("tgi,tis->tgs", grid, wide_weights)
            return ein("tb,tgs->bgs", block_map, product).astype(bf16).reshape(-1, size)

        def images_of(samples, blocks_of):
            spread = ein("tgs,tis->tgi", jnp.take(samples, blocks_of, axis=0), wide_weights)
            spread = spread.reshape(tiles, coil_count, -1, 2, size)
            back_real = ein("tcpi,xi->tcpx", spread[:, :, :, 0], cos_x) - ein(
                "tcpi,xi->tcpx", spread[:, :, :, 1], sin_x
            )
            back_imag = ein("tcpi,xi->tcpx", spread[:, :, :, 1], cos_x) + ein(
                "tcpi,xi->tcpx", spread[:, :, :, 0], sin_x
            )
            real = back_real * tc - back_imag * ts
            imag = back_imag * tc + back_real * ts
            return jnp.stack(
                [
                    ein("tcpx,ty->cpxy", real, cos_y) - ein("tcpx,ty->cpxy", imag, sin_y),
                    ein("tcpx,ty->cpxy", imag, cos_y) + ein("tcpx,ty->cpxy", real, sin_y),
                ],
                2,
            )

        def combined(images, g):
            map_real, map_imag = maps[g][:, :, 0], maps[g][:, :, 1]
            real, imag = images[:, :, 0], images[:, :, 1]
            return jnp.stack(
                [
                    jnp.sum(map_real * real + map_imag * imag, 0),
                    jnp.sum(map_real * imag - map_imag * real, 0),
                ],
                1,
            )

        def stacked_dots(values):
            values = values + [jnp.zeros((), f32)] * (8 - len(values))
            return jnp.broadcast_to(jnp.stack(values)[:, None], (8, 128))

        def applied_to(samples, vector, g):
            samples = added(samples).reshape(blocks, group_channels, size)
            return combined(images_of(samples, block_of), g) + damping * vector

        def measured_images():
            return images_of(measured.astype(f32), measured_block)

        def start(images, g):
            right_side = combined(images[:, g * group_planes : (g + 1) * group_planes], g)
            dots = stacked_dots([jnp.sum(right_side * right_side)])
            return right_side, right_side.astype(bf16), dots

        def first(samples, norms, right_side, g):
            norm = tree_sum(norms)[0, 0]
            total = added(samples)
            energy = jnp.sum(jnp.square(total))
            residual = right_side - step_of(norm, energy) * applied_to(samples, right_side, g)
            dots = [jnp.sum(residual * residual), jnp.sum(residual * right_side)]
            facts = stacked_dots([norm, energy])
            return residual, residual.astype(bf16), facts, stacked_dots(dots), total

        def facts_of(samples, dots, start_total, facts):
            total = added(samples)
            square, cross = tree_sum(dots)[:2, 0]
            values = [facts[0, 0], facts[1, 0], square, cross]
            values += [jnp.sum(total * total), jnp.sum(total * start_total)]
            return stacked_dots(values)

        def assembled(infos, vectors, ks, out=None):
            numbers = [
                [[info[g, row, 0] for g in groups] for info in infos] for row in range(6)
            ]
            factors = coefficients(*numbers)[len(vectors) == 3]
            if out is None:
                out = jnp.zeros((planes, 2, rows, columns), f32)
            for k in ks:
                for g in groups:
                    place = ((coil_index ^ k) * own_planes + g * group_planes, 0, 0, 0)
                    piece = sum(
                        factor * vector[g][k].astype(f32)
                        for factor, vector in zip(factors[k][g], vectors)
                    )
                    out = lax.dynamic_update_slice(out, piece, place)
            return out

        def second(samples, facts, residual, g):
            again = applied_to(samples, residual, g)
            return (residual - step_of(facts[0, 0], facts[1, 0]) * again).astype(bf16)

    def added(samples):
        return tree_sum([part.astype(f32) for part in samples])

    def sent_by_bits(own):
        return [swapped(own, "coil", k) for k in first_bits]

    images = measured_images()
    start_pieces, residual_pieces, mixed_own, mixed_sent, infos = [], [], [], [], []
    for g in groups:
        right_side, start_own, norm = start(images, g)
        start_sent = sent_by_bits(start_own)
        samples, norm = lax.optimization_barrier((forward(right_side, g), norm))
        samples = exchanged(samples)
        norms = exchanged(norm)
        samples, norms, start_sent = lax.optimization_barrier((samples, norms, start_sent))
        residual, residual_own, facts, dots, start_total = first(samples, norms, right_side, g)
        residual, residual_own, pieces = lax.optimization_barrier(
            (residual, residual_own, completed(start_own, start_sent))
        )
        start_pieces.append(pieces)
        residual_sent = sent_by_bits(residual_own)
        dots = exchanged(dots)
        samples = exchanged(forward(residual, g))
        samples, dots, residual_sent = lax.optimization_barrier((samples, dots, residual_sent))
        info = facts_of(samples, dots, start_total, facts)
        infos.append(info)
        rounded = second(samples, info, residual, g)
        last = g == groups[-1]
        others = exchanged(jnp.stack(infos), "coil") if last else []
        rounded, others, pieces = lax.optimization_barrier(
            (rounded, others, completed(residual_own, residual_sent))
        )
        residual_pieces.append(pieces)
        mixed_own.append(rounded)
        mixed_sent.append(sent_by_bits(rounded))

    picture = assembled(others, [start_pieces, residual_pieces], range(coil_count))
    early = [
        [own, sent[0]] + [None] * (coil_count - 2)
        for own, sent in zip(mixed_own, mixed_sent)
    ]
    out = assembled(others, [start_pieces, residual_pieces, early], range(2))
    picture, mixed_sent = lax.optimization_barrier((picture, mixed_sent))
    mixed_pieces = [completed(own, sent) for own, sent in zip(mixed_own, mixed_sent)]
    vectors = [start_pieces, residual_pieces, mixed_pieces]
    late = coil_count - 1
    out = assembled(others, vectors, range(2, late), out)
    out = assembled(others, vectors, [late], out)
    return picture, out


def solution(mesh):
    in_specs = (
        P("coil", "scan", None, "pencil"),
        P("coil", "scan", None, "pencil", None),
        P("pencil", None, None),
        P("pencil"),
        P("pencil"),
        P("pencil", None, None),
    )
    out_specs = (P("scan", None, "pencil", None), P("scan", None, "pencil", None))
    return jax.shard_map(
        on_device, mesh=mesh, in_specs=in_specs, out_specs=out_specs, check_vma=False
    )
```

```python
import functools
import math

import jax
import jax.numpy as jnp
from jax import lax
from jax.experimental import pallas as pl
from jax.experimental.pallas import tpu as pltpu
from jax.sharding import PartitionSpec as P


damping = 0.5
f32, bf16 = jnp.float32, jnp.bfloat16
vmem_limit = 56 * 1024 * 1024


def wave(left, right, length):
    phases = left[:, None] * right[None, :] % length
    angles = phases.astype(f32) * (2.0 * math.pi / length)
    return jnp.cos(angles) / math.sqrt(length), jnp.sin(angles) / math.sqrt(length)


def quarter_turns(left, right, count):
    turns = left[:, None] * right[None, :] % count
    if count == 4:
        cosine = jnp.where(turns == 0, 1.0, 0.0) - jnp.where(turns == 2, 1.0, 0.0)
        sine = jnp.where(turns == 1, 1.0, 0.0) - jnp.where(turns == 3, 1.0, 0.0)
        return cosine.astype(f32), sine.astype(f32)
    angles = turns.astype(f32) * (2.0 * math.pi / count)
    return jnp.cos(angles), jnp.sin(angles)


def split(value):
    high = value.astype(bf16)
    return high, (value - high.astype(f32)).astype(bf16)


def table_parts(table, axis):
    high = lax.reduce_precision(table, 8, 7)
    low = (table - high).astype(bf16)
    high = high.astype(bf16)
    return jnp.concatenate([high, high, low], axis)


def data_parts(value):
    high, low = split(value)
    return jnp.concatenate([high, low, high], 1)


def nt(left, right):
    return lax.dot_general(left, right, (((1,), (1,)), ((), ())), preferred_element_type=f32)


def nn(left, right):
    return jnp.dot(left, right, preferred_element_type=f32)


def tree_sum(values):
    while len(values) > 1:
        values = [left + right for left, right in zip(values[::2], values[1::2])]
    return values[0]


def forward_images(plane, planes, picture, sens, ey, mx, turn_ref, grid_ref):
    tiles = turn_ref.shape[1]
    rows = turn_ref.shape[2]
    channels = grid_ref.shape[0] // tiles
    real, imag = picture[0, 0], picture[0, 1]
    turned = []
    for sens_ref in sens:
        sens_real = sens_ref[0, 0, 0].astype(f32)
        sens_imag = sens_ref[0, 0, 1].astype(f32)
        coil = jnp.concatenate(
            [sens_real * real - sens_imag * imag, sens_real * imag + sens_imag * real], 0
        )
        both = nt(ey[...], coil.astype(bf16))
        half_real = both[:tiles, :rows] + both[tiles:, rows:]
        half_imag = both[:tiles, rows:] - both[tiles:, :rows]
        turned.append(
            jnp.concatenate(
                [
                    half_real * turn_ref[0] + half_imag * turn_ref[1],
                    half_imag * turn_ref[0] - half_real * turn_ref[1],
                ],
                1,
            ).astype(bf16)
        )
    grid = nn(jnp.concatenate(turned, 0), mx[...])
    size = grid.shape[1] // 2
    for coil in range(len(sens)):
        step = coil * planes + plane
        part = grid[coil * tiles : (coil + 1) * tiles]
        grid_ref[pl.ds(2 * step, tiles, stride=channels), :] = part[:, :size]
        grid_ref[pl.ds(2 * step + 1, tiles, stride=channels), :] = part[:, size:]


def tile_products(lefts, rights):
    rows, size = lefts[0].shape
    empty = jnp.zeros((rows, size), bf16)
    left = jnp.concatenate(
        [
            jnp.concatenate([value, empty] if place % 2 == 0 else [empty, value], 1)
            for place, value in enumerate(lefts)
        ],
        0,
    )
    right = jnp.concatenate(
        [jnp.concatenate(rights[:2], 0), jnp.concatenate(rights[2:], 0)], 1
    )
    product = nn(left, right)
    return [
        product[place * rows : (place + 1) * rows, place // 2 * size : (place // 2 + 1) * size]
        for place in range(4)
    ]


def each_four(count, function):
    def one(index, carry):
        function([index * 4 + place for place in range(4)])
        return carry

    lax.fori_loop(0, count // 4, one, 0, unroll=True)


def weight_copies(weights, held, sems):
    return [
        pltpu.make_async_copy(ref, held.at[place], sems.at[place])
        for place, ref in enumerate(weights)
    ]


def start_copies(copies):
    for copy in copies:
        copy.start()


def sample_tiles(block_ref, copies, weights, grid_ref, sums_ref, out_ref):
    count = weights.shape[1]
    channels = sums_ref.shape[1]
    sums_ref[...] = jnp.zeros_like(sums_ref)

    def left_of(tile):
        value = grid_ref[pl.ds(pl.multiple_of(tile * channels, channels), channels), :]
        high = value.astype(bf16).astype(f32)
        return jnp.concatenate([high, value - high], 0).astype(bf16)

    for group, copy in enumerate(copies):
        copy.wait()

        def four(places):
            tiles = [group * count + place for place in places]
            products = tile_products(
                [left_of(tile) for tile in tiles], [weights[group, place] for place in places]
            )
            for tile, product in zip(tiles, products):
                sums_ref[block_ref[tile]] += product[:channels] + product[channels:]

        each_four(count, four)
    out_ref[...] = sums_ref[...].reshape(out_ref.shape).astype(bf16)


def spread_tiles(block_ref, weights, parts_ref, grid_ref, turned_ref=None):
    count = weights[0].shape[0]
    channels = grid_ref.shape[0] // (count * len(weights))

    for group, weights_ref in enumerate(weights):

        def four(places):
            tiles = [group * count + place for place in places]
            rights = [weights_ref[place] for place in places]
            if turned_ref is not None:
                rights = [right.astype(f32).T.astype(bf16) for right in rights]
                for place, right in zip(places, rights):
                    turned_ref[group, place] = right
            products = tile_products([parts_ref[block_ref[tile]] for tile in tiles], rights)
            for tile, product in zip(tiles, products):
                if product.shape[0] > channels:
                    product = product[:channels] + product[channels:]
                start = pl.multiple_of(tile * channels, channels)
                grid_ref[pl.ds(start, channels), :] = product

        each_four(count, four)


def adjoint_images(coils, plane, planes, ey_back, mx_back, turn_ref, grid_ref):
    rows, tiles = turn_ref.shape[1], turn_ref.shape[2]
    channels = grid_ref.shape[0] // tiles
    grids = []
    for coil in range(coils):
        step = coil * planes + plane
        grid = jnp.concatenate(
            [
                grid_ref[pl.ds(2 * step, tiles, stride=channels), :],
                grid_ref[pl.ds(2 * step + 1, tiles, stride=channels), :],
            ],
            1,
        )
        grids.append(data_parts(grid))
    back = nt(mx_back[...], jnp.concatenate(grids, 0))
    turned = []
    for coil in range(coils):
        part = back[:, coil * tiles : (coil + 1) * tiles]
        both = jnp.concatenate(
            [
                part[:rows] * turn_ref[0] - part[rows:] * turn_ref[1],
                part[rows:] * turn_ref[0] + part[:rows] * turn_ref[1],
            ],
            1,
        )
        turned.append(data_parts(both))
    image = nn(jnp.concatenate(turned, 0), ey_back[...])
    columns = image.shape[1] // 2
    return [
        (image[c * rows : (c + 1) * rows, :columns], image[c * rows : (c + 1) * rows, columns:])
        for c in range(coils)
    ]


def add_dots(dots_ref, products):
    rows = lax.broadcasted_iota(jnp.int32, dots_ref.shape, 0)
    total = dots_ref[...]
    for place, (left, right) in enumerate(products):
        total += jnp.where(rows == place, jnp.sum(left * right), 0.0)
    dots_ref[...] = total


def measured_kernel(block, samples, *refs):
    *weights, mx, eb, turn, images, turned, grid = refs
    plane = pl.program_id(0)
    coils = images.shape[0]

    @pl.when(plane == 0)
    def _():
        spread_tiles(block, weights, samples, grid, turned)

    found = adjoint_images(coils, plane, pl.num_programs(0), eb, mx, turn, grid)
    for coil, (real, imag) in enumerate(found):
        images[coil, 0, 0] = real
        images[coil, 0, 1] = imag


def combine(images, sens):
    total_real = total_imag = 0.0
    for (real, imag), sens_ref in zip(images, sens):
        sens_real = sens_ref[0, 0, 0].astype(f32)
        sens_imag = sens_ref[0, 0, 1].astype(f32)
        total_real += sens_real * real + sens_imag * imag
        total_imag += sens_real * imag - sens_imag * real
    return total_real, total_imag


def start_kernel(images, *refs):
    *sens, right_side, rounded, dots = refs
    total = combine([(images[c, 0, 0], images[c, 0, 1]) for c in range(len(sens))], sens)
    for part in range(2):
        right_side[0, part] = total[part]
        rounded[0, part] = total[part].astype(bf16)

    @pl.when((pl.program_id(0) == 0) & (pl.program_id(1) == 0))
    def _():
        dots[...] = jnp.zeros_like(dots)

    add_dots(dots, [(right_side[0], right_side[0])])


def forward_kernel(coils, block, picture, *refs):
    sens = refs[:coils]
    *weights, ey, mx, turn, samples, grid, sums, held, sems = refs[coils:]
    plane = pl.program_id(0)

    @pl.when(plane == 0)
    def _():
        start_copies(weight_copies(weights, held, sems))

    forward_images(plane, pl.num_programs(0), picture, sens, ey, mx, turn, grid)

    @pl.when(plane == pl.num_programs(0) - 1)
    def _():
        sample_tiles(block, weight_copies(weights, held, sems), held, grid, sums, samples)


def summed_parts(samples, parts):
    summed = tree_sum([part[...].astype(f32) for part in samples])
    blocks, channels, size = parts.shape[0], parts.shape[1] // 2, parts.shape[2]
    value = summed.reshape(blocks, channels, size)
    high = value.astype(bf16).astype(f32)
    parts[...] = jnp.concatenate([high, value - high], 1).astype(bf16)
    return summed


def step_of(norm, energy):
    return jnp.where(norm > 0.0, norm / (energy + damping * norm), 1.0)


def first_kernel(peers, coils, block, *refs):
    samples, weights, sens = refs[:peers], refs[peers], refs[peers + 1 :][:coils]
    mx, eb, turn, *norms = refs[peers + 1 + coils :][: 3 + peers]
    right_side, residual, rounded, facts, dots, total_samples, grid, parts = refs[-8:]
    plane = pl.program_id(0)

    @pl.when(plane == 0)
    def _():
        summed = summed_parts(samples, parts)
        total_samples[...] = summed
        rows = lax.broadcasted_iota(jnp.int32, facts.shape, 0)
        norm = tree_sum([part[...] for part in norms])
        facts[...] = jnp.where(rows == 1, jnp.sum(summed * summed), norm)
        dots[...] = jnp.zeros_like(dots)
        spread_tiles(block, [weights.at[k] for k in range(peers)], parts, grid)

    images = adjoint_images(coils, plane, pl.num_programs(0), eb, mx, turn, grid)
    total = combine(images, sens)
    scale = step_of(facts[0:1, 0:1], facts[1:2, 0:1])
    for part in range(2):
        vector = right_side[0, part]
        value = vector - scale * (total[part] + damping * vector)
        residual[0, part] = value
        rounded[0, part] = value.astype(bf16)
        add_dots(dots, [(value, value), (value, vector)])


def second_kernel(peers, coils, block, *refs):
    samples, weights, sens = refs[:peers], refs[peers], refs[peers + 1 :][:coils]
    mx, eb, turn, facts, residual, rounded, grid, parts = refs[peers + 1 + coils :]
    plane = pl.program_id(0)

    @pl.when(plane == 0)
    def _():
        summed_parts(samples, parts)
        spread_tiles(block, [weights.at[k] for k in range(peers)], parts, grid)

    images = adjoint_images(coils, plane, pl.num_programs(0), eb, mx, turn, grid)
    total = combine(images, sens)
    scale = step_of(facts[0:1, 0:1], facts[1:2, 0:1])
    for part in range(2):
        vector = residual[0, part]
        again = total[part] + damping * vector
        rounded[0, part] = (vector - scale * again).astype(bf16)


def facts_kernel(peers, *refs):
    samples, dots = refs[:peers], refs[peers : 2 * peers]
    start_total, facts, out = refs[2 * peers :]
    both = tree_sum([part[...] for part in dots])
    summed = tree_sum([part[...].astype(f32) for part in samples])
    rows = lax.broadcasted_iota(jnp.int32, out.shape, 0)
    values = [facts[0:1], facts[1:2], both[0:1], both[1:2]]
    values += [jnp.sum(summed * summed), jnp.sum(summed * start_total[...])]
    total = jnp.zeros(out.shape, f32)
    for row, value in enumerate(values):
        total = jnp.where(rows == row, value, total)
    out[...] = total


def coefficients(norm, energy, square, cross, again, mixed):
    def over_all(values):
        return tree_sum([sum(of_coil) for of_coil in values])

    def each(function, *lists):
        return [[function(*items) for items in zip(*of_coil)] for of_coil in zip(*lists)]

    start_curve = each(lambda e, n: e + damping * n, energy, norm)
    curve = each(lambda e, n: e + damping * n, again, square)
    mixed_curve = each(lambda e, n: e + damping * n, mixed, cross)
    sigma = each(step_of, norm, energy)
    start_norm = over_all(norm)
    first_step = start_norm / over_all(start_curve)
    part = each(lambda s: first_step / s, sigma)
    next_norm = over_all(
        each(
            lambda w, n, c, s: w * w * s + 2.0 * w * (1.0 - w) * c + (1.0 - w) * (1.0 - w) * n,
            part,
            norm,
            cross,
            square,
        )
    )
    more = each(lambda w: 1.0 - w + next_norm / start_norm, part)
    second_step = next_norm / over_all(
        each(
            lambda w, m, q, c, s, z, qm, qs: w * w * q
            + w * m * ((c - s) / z + qm)
            + m * m * qs,
            part,
            more,
            curve,
            cross,
            square,
            sigma,
            mixed_curve,
            start_curve,
        )
    )
    share = each(lambda z: second_step / z, sigma)
    picture = each(lambda w, m: (first_step + second_step * m, second_step * w), part, more)
    residual = each(
        lambda w, m, h: (1.0 - w - h * m, w - h * w + h * m, h * w), part, more, share
    )
    return picture, residual


def assemble_kernel(coils, group_steps, combos, is_residual, order, *refs):
    infos, pieces, (out, kept) = refs[:coils], refs[coils:-2], refs[-2:]
    groups = infos[0].shape[0]
    count = 3 if is_residual else 2

    @pl.when(pl.program_id(0) == 0)
    def _():
        numbers = [
            [[info[g, row : row + 1, 0:1] for g in range(groups)] for info in infos]
            for row in range(6)
        ]
        factors = coefficients(*numbers)[is_residual]
        rows = lax.broadcasted_iota(jnp.int32, kept.shape[1:], 0)
        for place, (k, g) in enumerate(combos):
            total = jnp.zeros(kept.shape[1:], f32)
            for row, factor in enumerate(factors[k][g]):
                total = jnp.where(rows == row, factor, total)
            kept[place] = total

    for place in range(len(combos)):

        @pl.when(pl.program_id(0) // group_steps == place)
        def _():
            total = 0.0
            for row, piece in enumerate(pieces[place * count :][:count]):
                factor = kept[place, row : row + 1, 0:1].reshape(1, 1, 1, 1)
                total += factor * piece[...].astype(f32)
            out[...] = total


def group_count_of(own_planes):
    return 1


def whole_block(array):
    rank = len(array.shape)
    return pl.BlockSpec(array.shape, lambda *_: (0,) * rank)


def on_device(kspace, sens_maps, weights, tile_slot, tile_block, send_list):
    coil_count = lax.axis_size("coil")
    peers = lax.axis_size("pencil")
    planes = sens_maps.shape[1]
    own_planes = planes // coil_count
    rows = sens_maps.shape[3]
    columns = sens_maps.shape[4]
    rows_total = rows * peers
    size = weights.shape[1]
    tile_count = tile_slot.shape[0]
    tiles = tile_count * peers
    blocks_dev = kspace.shape[3] // size
    blocks = blocks_dev * peers
    cap = send_list.shape[2]
    runs = rows_total // size
    brick_dev = columns // peers * runs
    images_count = coil_count * own_planes
    channels = 2 * images_count

    coil_index = lax.axis_index("coil")

    def swapped(array, axis, k):
        return lax.ppermute(array, axis, [(i, i ^ k) for i in range(lax.axis_size(axis))])

    def everywhere(array, axis):
        bit = 1
        while bit < lax.axis_size(axis):
            bit *= 2
        pieces = {0: array}
        while bit > 1:
            bit //= 2
            for k in sorted(pieces):
                pieces[k ^ bit] = swapped(pieces[k], axis, bit)
        return [pieces[k] for k in sorted(pieces)]

    first_bits = [1 << bit for bit in range(coil_count.bit_length() - 1)]

    def completed(own, sent):
        pieces = {0: own}
        for bit, piece in zip(first_bits, sent):
            pieces[bit] = piece
        for bit in first_bits:
            for k in range(coil_count):
                if k not in pieces and (k ^ bit) in pieces:
                    pieces[k] = swapped(pieces[k ^ bit], "coil", bit)
        return [pieces[k] for k in range(coil_count)]

    def to_planes(array):
        pieces = []
        for k in range(coil_count):
            part = lax.dynamic_slice_in_dim(array, (coil_index ^ k) * own_planes, own_planes, 0)
            pieces.append(swapped(part, "coil", k) if k > 0 else part)
        return pieces

    group_planes = own_planes // group_count_of(own_planes)
    groups = range(own_planes // group_planes)
    measured = to_planes(kspace[0])
    packed = jnp.concatenate([tile_slot, tile_block, send_list.reshape(-1)])
    sens_source, packed, measured, own_weights = lax.optimization_barrier(
        (sens_maps[0], packed, measured, weights)
    )
    sens_source = sens_source.reshape(coil_count, own_planes, 2, rows, columns)
    sens = [
        lax.all_to_all(
            sens_source[:, g * group_planes : (g + 1) * group_planes],
            "coil",
            split_axis=0,
            concat_axis=0,
            tiled=True,
        )
        for g in groups
    ]
    measured = jnp.stack(measured)
    by_coil = jnp.arange(coil_count, dtype=jnp.int32) ^ coil_index
    measured = jnp.take(measured, by_coil, axis=0)
    all_weights = everywhere(own_weights, "pencil")

    places = jnp.stack(everywhere(packed, "pencil"))
    holder = (jnp.arange(peers, dtype=jnp.int32) ^ lax.axis_index("pencil"))[:, None]
    by_owner = jnp.take(places, holder[:, 0], axis=0)
    lists = by_owner[:, 2 * tile_count :].reshape(peers, peers, cap)
    slots = places[:, :tile_count]
    block_of = (places[:, tile_count : 2 * tile_count] + blocks_dev * holder).reshape(-1)
    brick = (slots // cap * brick_dev + lists[slots // cap, holder, slots % cap]).reshape(-1)
    line = brick // runs
    run = brick % runs

    measured = measured.reshape(channels, blocks_dev, size)
    measured = jnp.concatenate(everywhere(jnp.swapaxes(measured, 0, 1), "pencil"), 0)
    measured_block = (
        places[:, tile_count : 2 * tile_count]
        + blocks_dev * jnp.arange(peers, dtype=jnp.int32)[:, None]
    ).reshape(-1)

    cos_y, sin_y = wave(
        line - columns // 2, jnp.arange(columns, dtype=jnp.int32) - columns // 2, columns
    )
    row_ids = jnp.arange(rows, dtype=jnp.int32) + lax.axis_index("pencil") * rows - rows_total // 2
    cos_x, sin_x = wave(
        row_ids, jnp.arange(size, dtype=jnp.int32) - rows_total // 2, rows_total
    )
    turn = jnp.stack(quarter_turns(run, row_ids, runs))
    turn_back = jnp.stack(quarter_turns(row_ids, run, runs))

    def exchanged(partial, axis="pencil"):
        count = lax.axis_size(axis)
        return [partial] + [swapped(partial, axis, k) for k in range(1, count)]

    group_shape = (group_planes, 2, rows, columns)
    group_images = coil_count * group_planes
    group_channels = 2 * group_images

    if (
        rows % 128 == 0
        and columns % 128 == 0
        and size % 128 == 0
        and channels % 16 == 0
        and tile_count % 4 == 0
        and group_channels % 8 == 0
    ):
        ey = jnp.concatenate([cos_y, sin_y], 0).astype(bf16)
        eb = jnp.concatenate(
            [jnp.concatenate([cos_y, sin_y], 1), jnp.concatenate([-sin_y, cos_y], 1)], 0
        )
        eb = table_parts(eb, 0)
        mx = jnp.concatenate(
            [jnp.concatenate([cos_x, -sin_x], 1), jnp.concatenate([sin_x, cos_x], 1)], 0
        )
        mx, mx_back = mx.astype(bf16), table_parts(mx, 1)
        measured, ey, mx, turn, block_of, all_weights = lax.optimization_barrier(
            (measured, ey, mx, turn, block_of, all_weights)
        )
        places_spec = pl.BlockSpec(memory_space=pltpu.SMEM)
        plane_spec = pl.BlockSpec((1, 2, rows, columns), lambda p: (p, 0, 0, 0))
        sens_specs = [
            pl.BlockSpec((1, 1, 2, rows, columns), functools.partial(lambda c, p: (c, p, 0, 0, 0), c))
            for c in range(coil_count)
        ]
        grid_scratch = pltpu.VMEM((tiles * group_channels, size), f32)
        params = pltpu.CompilerParams(vmem_limit_bytes=vmem_limit)
        tail_tables = [mx_back, eb, turn_back]
        weights_specs = [pl.BlockSpec(memory_space=pl.ANY)] * peers
        held_weights = [
            pltpu.VMEM((peers,) + weights.shape, bf16),
            pltpu.SemaphoreType.DMA((peers,)),
        ]

        def shaped(shape, dtype=f32):
            return jax.ShapeDtypeStruct(shape, dtype)

        def call(kernel, grid, inputs, specs, outs, out_specs, scratch, images):
            flops = 2 * images * 8 * tiles * rows * (columns + size)
            return pl.pallas_call(
                kernel,
                grid=grid,
                in_specs=specs,
                out_specs=out_specs,
                out_shape=outs,
                scratch_shapes=scratch,
                compiler_params=params,
                cost_estimate=pl.CostEstimate(
                    flops=flops,
                    bytes_accessed=sum(math.prod(i.shape) * i.dtype.itemsize for i in inputs),
                    transcendentals=0,
                ),
            )(*inputs)

        def measured_images():
            inputs = [measured_block, measured, *all_weights, *tail_tables]
            turned_shape = shaped((peers,) + weights.shape, bf16)
            shape = (coil_count, own_planes, 2, rows, columns)
            return call(
                measured_kernel,
                (own_planes,),
                inputs,
                [places_spec] + [whole_block(i) for i in inputs[1:]],
                [shaped(shape), turned_shape],
                [
                    pl.BlockSpec((coil_count, 1, 2, rows, columns), lambda p: (0, p, 0, 0, 0)),
                    whole_block(turned_shape),
                ],
                [pltpu.VMEM((tiles * channels, size), f32)],
                images_count,
            )

        def start(images, g):
            chunk = 64
            spec = pl.BlockSpec((1, 2, chunk, columns), lambda p, r: (p, 0, r, 0))
            images_spec = pl.BlockSpec(
                (coil_count, 1, 2, chunk, columns),
                lambda p, r: (0, p + g * group_planes, 0, r, 0),
            )
            dots_shape = shaped((8, 128))
            return call(
                start_kernel,
                (group_planes, rows // chunk),
                [images] + [sens[g]] * coil_count,
                [images_spec]
                + [
                    pl.BlockSpec(
                        (1, 1, 2, chunk, columns),
                        functools.partial(lambda c, p, r: (c, p, 0, r, 0), c),
                    )
                    for c in range(coil_count)
                ],
                [shaped(group_shape), shaped(group_shape, bf16), dots_shape],
                [spec, spec, whole_block(dots_shape)],
                [],
                0,
            )

        def forward(picture, g):
            tail = [ey, mx, turn]
            out = shaped((blocks * group_channels, size), bf16)
            return call(
                functools.partial(forward_kernel, coil_count),
                (group_planes,),
                [block_of, picture] + [sens[g]] * coil_count + [*all_weights, *tail],
                [places_spec, plane_spec]
                + sens_specs
                + weights_specs
                + [whole_block(i) for i in tail],
                out,
                whole_block(out),
                [grid_scratch, pltpu.VMEM((blocks, group_channels, size), f32)] + held_weights,
                group_images,
            )

        def back(kernel, samples, tables, vectors, g, outs, out_specs):
            inputs = [*samples, turned_weights]
            tables = tail_tables + tables
            return call(
                functools.partial(kernel, peers, coil_count),
                (group_planes,),
                [block_of, *inputs] + [sens[g]] * coil_count + tables + vectors,
                [places_spec]
                + [whole_block(i) for i in inputs]
                + sens_specs
                + [whole_block(i) for i in tables]
                + [plane_spec] * len(vectors),
                outs,
                out_specs,
                [grid_scratch, pltpu.VMEM((blocks, 2 * group_channels, size), bf16)],
                group_images,
            )

        def first(samples, norms, right_side, g):
            small, large = shaped((8, 128)), shaped(samples[0].shape)
            return back(
                first_kernel,
                samples,
                norms,
                [right_side],
                g,
                [shaped(group_shape), shaped(group_shape, bf16), small, small, large],
                [plane_spec, plane_spec] + [whole_block(i) for i in (small, small, large)],
            )

        def facts_of(samples, dots, start_total, facts):
            inputs = [*samples, *dots, start_total, facts]
            return pl.pallas_call(
                functools.partial(facts_kernel, peers),
                in_specs=[pl.BlockSpec(memory_space=pltpu.VMEM)] * len(inputs),
                out_specs=pl.BlockSpec(memory_space=pltpu.VMEM),
                out_shape=shaped((8, 128)),
                compiler_params=params,
            )(*inputs)

        def assembled(infos, vectors, ks, out=None):
            combos = [(k, g) for k in ks for g in groups]
            order = jnp.stack(
                [
                    (coil_index ^ k) * own_planes + g * group_planes + p
                    for k, g in combos
                    for p in range(group_planes)
                ]
            ).astype(jnp.int32)
            chunks = rows // 64
            inputs = [vector[g][k] for k, g in combos for vector in vectors]

            def spec(place):
                first = place // len(vectors) * group_planes * chunks

                def part_of(i, o):
                    i = jnp.clip(i - first, 0, group_planes * chunks - 1)
                    return i // chunks, 0, i % chunks, 0

                return pl.BlockSpec((1, 2, 64, columns), part_of)

            specs = [pl.BlockSpec(infos[0].shape, lambda i, o: (0, 0, 0))] * len(infos)
            specs += [spec(place) for place in range(len(inputs))]
            aliases = {}
            if out is not None:
                aliases = {1 + len(infos) + len(inputs): 0}
                inputs = inputs + [out]
                specs.append(pl.BlockSpec(memory_space=pl.ANY))
            return pl.pallas_call(
                functools.partial(
                    assemble_kernel,
                    coil_count,
                    group_planes * chunks,
                    combos,
                    len(vectors) == 3,
                ),
                grid_spec=pltpu.PrefetchScalarGridSpec(
                    num_scalar_prefetch=1,
                    grid=(len(combos) * group_planes * chunks,),
                    in_specs=specs,
                    out_specs=pl.BlockSpec(
                        (1, 2, 64, columns), lambda i, o: (o[i // chunks], 0, i % chunks, 0)
                    ),
                    scratch_shapes=[pltpu.VMEM((len(combos), 8, 128), f32)],
                ),
                out_shape=shaped((planes, 2, rows, columns)),
                input_output_aliases=aliases,
                compiler_params=params,
            )(order, *infos, *inputs)

        def second(samples, facts, residual, g):
            return back(
                second_kernel,
                samples,
                [facts],
                [residual],
                g,
                shaped(group_shape, bf16),
                plane_spec,
            )

    else:
        ein = functools.partial(jnp.einsum, precision=lax.Precision.HIGH)
        maps = [array.astype(f32) for array in sens]
        block_map = (block_of[:, None] == jnp.arange(blocks, dtype=jnp.int32)).astype(f32)
        tc, ts = turn[0][:, None, None], turn[1][:, None, None]
        wide_weights = jnp.concatenate(all_weights, 0).astype(f32)

        def forward(picture, g):
            map_real, map_imag = maps[g][:, :, 0], maps[g][:, :, 1]
            coil_real = map_real * picture[None, :, 0] - map_imag * picture[None, :, 1]
            coil_imag = map_real * picture[None, :, 1] + map_imag * picture[None, :, 0]
            half_real = ein("ty,cpxy->tcpx", cos_y, coil_real) + ein(
                "ty,cpxy->tcpx", sin_y, coil_imag
            )
            half_imag = ein("ty,cpxy->tcpx", cos_y, coil_imag) - ein(
                "ty,cpxy->tcpx", sin_y, coil_real
            )
            real = half_real * tc + half_imag * ts
            imag = half_imag * tc - half_real * ts
            grid = jnp.stack(
                [
                    ein("tcpx,xi->tcpi", real, cos_x) + ein("tcpx,xi->tcpi", imag, sin_x),
                    ein("tcpx,xi->tcpi", imag, cos_x) - ein("tcpx,xi->tcpi", real, sin_x),
                ],
                3,
            ).reshape(tiles, group_channels, size)
            product = ein("tgi,tis->tgs", grid, wide_weights)
            return ein("tb,tgs->bgs", block_map, product).astype(bf16).reshape(-1, size)

        def images_of(samples, blocks_of):
            spread = ein("tgs,tis->tgi", jnp.take(samples, blocks_of, axis=0), wide_weights)
            spread = spread.reshape(tiles, coil_count, -1, 2, size)
            back_real = ein("tcpi,xi->tcpx", spread[:, :, :, 0], cos_x) - ein(
                "tcpi,xi->tcpx", spread[:, :, :, 1], sin_x
            )
            back_imag = ein("tcpi,xi->tcpx", spread[:, :, :, 1], cos_x) + ein(
                "tcpi,xi->tcpx", spread[:, :, :, 0], sin_x
            )
            real = back_real * tc - back_imag * ts
            imag = back_imag * tc + back_real * ts
            return jnp.stack(
                [
                    ein("tcpx,ty->cpxy", real, cos_y) - ein("tcpx,ty->cpxy", imag, sin_y),
                    ein("tcpx,ty->cpxy", imag, cos_y) + ein("tcpx,ty->cpxy", real, sin_y),
                ],
                2,
            )

        def combined(images, g):
            map_real, map_imag = maps[g][:, :, 0], maps[g][:, :, 1]
            real, imag = images[:, :, 0], images[:, :, 1]
            return jnp.stack(
                [
                    jnp.sum(map_real * real + map_imag * imag, 0),
                    jnp.sum(map_real * imag - map_imag * real, 0),
                ],
                1,
            )

        def stacked_dots(values):
            values = values + [jnp.zeros((), f32)] * (8 - len(values))
            return jnp.broadcast_to(jnp.stack(values)[:, None], (8, 128))

        def applied_to(samples, vector, g):
            samples = added(samples).reshape(blocks, group_channels, size)
            return combined(images_of(samples, block_of), g) + damping * vector

        def measured_images():
            return images_of(measured.astype(f32), measured_block), None

        def start(images, g):
            right_side = combined(images[:, g * group_planes : (g + 1) * group_planes], g)
            dots = stacked_dots([jnp.sum(right_side * right_side)])
            return right_side, right_side.astype(bf16), dots

        def first(samples, norms, right_side, g):
            norm = tree_sum(norms)[0, 0]
            total = added(samples)
            energy = jnp.sum(jnp.square(total))
            residual = right_side - step_of(norm, energy) * applied_to(samples, right_side, g)
            dots = [jnp.sum(residual * residual), jnp.sum(residual * right_side)]
            facts = stacked_dots([norm, energy])
            return residual, residual.astype(bf16), facts, stacked_dots(dots), total

        def facts_of(samples, dots, start_total, facts):
            total = added(samples)
            square, cross = tree_sum(dots)[:2, 0]
            values = [facts[0, 0], facts[1, 0], square, cross]
            values += [jnp.sum(total * total), jnp.sum(total * start_total)]
            return stacked_dots(values)

        def assembled(infos, vectors, ks, out=None):
            numbers = [
                [[info[g, row, 0] for g in groups] for info in infos] for row in range(6)
            ]
            factors = coefficients(*numbers)[len(vectors) == 3]
            if out is None:
                out = jnp.zeros((planes, 2, rows, columns), f32)
            for k in ks:
                for g in groups:
                    place = ((coil_index ^ k) * own_planes + g * group_planes, 0, 0, 0)
                    piece = sum(
                        factor * vector[g][k].astype(f32)
                        for factor, vector in zip(factors[k][g], vectors)
                    )
                    out = lax.dynamic_update_slice(out, piece, place)
            return out

        def second(samples, facts, residual, g):
            again = applied_to(samples, residual, g)
            return (residual - step_of(facts[0, 0], facts[1, 0]) * again).astype(bf16)

    def added(samples):
        return tree_sum([part.astype(f32) for part in samples])

    def sent_by_bits(own):
        return [swapped(own, "coil", k) for k in first_bits]

    images, turned_weights = measured_images()
    start_pieces, residual_pieces, mixed_own, mixed_sent, infos = [], [], [], [], []
    for g in groups:
        right_side, start_own, norm = start(images, g)
        start_sent = sent_by_bits(start_own)
        samples, norm = lax.optimization_barrier((forward(right_side, g), norm))
        samples = exchanged(samples)
        norms = exchanged(norm)
        samples, norms, start_sent = lax.optimization_barrier((samples, norms, start_sent))
        residual, residual_own, facts, dots, start_total = first(samples, norms, right_side, g)
        dots = exchanged(dots)
        residual, residual_own, dots, pieces = lax.optimization_barrier(
            (residual, residual_own, dots, completed(start_own, start_sent))
        )
        start_pieces.append(pieces)
        residual_sent = sent_by_bits(residual_own)
        samples = exchanged(forward(residual, g))
        samples, dots = lax.optimization_barrier((samples, dots))
        info = facts_of(samples, dots, start_total, facts)
        infos.append(info)
        others = exchanged(jnp.stack(infos), "coil") if g == groups[-1] else []
        samples, info, others, residual_sent = lax.optimization_barrier(
            (samples, info, others, residual_sent)
        )
        rounded = second(samples, info, residual, g)
        rounded, pieces = lax.optimization_barrier(
            (rounded, completed(residual_own, residual_sent))
        )
        residual_pieces.append(pieces)
        mixed_own.append(rounded)
        mixed_sent.append(sent_by_bits(rounded))

    picture = assembled(others, [start_pieces, residual_pieces], range(coil_count))
    early = [
        [own, sent[0]] + [None] * (coil_count - 2)
        for own, sent in zip(mixed_own, mixed_sent)
    ]
    out = assembled(others, [start_pieces, residual_pieces, early], range(2))
    picture, mixed_sent = lax.optimization_barrier((picture, mixed_sent))
    mixed_pieces = [completed(own, sent) for own, sent in zip(mixed_own, mixed_sent)]
    vectors = [start_pieces, residual_pieces, mixed_pieces]
    late = coil_count - 1
    out = assembled(others, vectors, range(2, late), out)
    out = assembled(others, vectors, [late], out)
    return picture, out


def solution(mesh):
    in_specs = (
        P("coil", "scan", None, "pencil"),
        P("coil", "scan", None, "pencil", None),
        P("pencil", None, None),
        P("pencil"),
        P("pencil"),
        P("pencil", None, None),
    )
    out_specs = (P("scan", None, "pencil", None), P("scan", None, "pencil", None))
    return jax.shard_map(
        on_device, mesh=mesh, in_specs=in_specs, out_specs=out_specs, check_vma=False
    )
```

```python
import functools
import math

import jax
import jax.numpy as jnp
from jax import lax
from jax.experimental import pallas as pl
from jax.experimental.pallas import tpu as pltpu
from jax.sharding import PartitionSpec as P


damping = 0.5
f32, bf16 = jnp.float32, jnp.bfloat16
vmem_limit = 56 * 1024 * 1024


def wave(left, right, length):
    phases = left[:, None] * right[None, :] % length
    angles = phases.astype(f32) * (2.0 * math.pi / length)
    return jnp.cos(angles) / math.sqrt(length), jnp.sin(angles) / math.sqrt(length)


def quarter_turns(left, right, count):
    turns = left[:, None] * right[None, :] % count
    if count == 4:
        cosine = jnp.where(turns == 0, 1.0, 0.0) - jnp.where(turns == 2, 1.0, 0.0)
        sine = jnp.where(turns == 1, 1.0, 0.0) - jnp.where(turns == 3, 1.0, 0.0)
        return cosine.astype(f32), sine.astype(f32)
    angles = turns.astype(f32) * (2.0 * math.pi / count)
    return jnp.cos(angles), jnp.sin(angles)


def split(value):
    high = value.astype(bf16)
    return high, (value - high.astype(f32)).astype(bf16)


def table_parts(table, axis):
    high = lax.reduce_precision(table, 8, 7)
    low = (table - high).astype(bf16)
    high = high.astype(bf16)
    return jnp.concatenate([high, high, low], axis)


def data_parts(value):
    high, low = split(value)
    return jnp.concatenate([high, low, high], 1)


def nt(left, right):
    return lax.dot_general(left, right, (((1,), (1,)), ((), ())), preferred_element_type=f32)


def nn(left, right):
    return jnp.dot(left, right, preferred_element_type=f32)


def tree_sum(values):
    while len(values) > 1:
        values = [left + right for left, right in zip(values[::2], values[1::2])]
    return values[0]


def forward_images(plane, planes, picture, sens, ey, mx, turn_ref, grid_ref):
    tiles = turn_ref.shape[1]
    rows = turn_ref.shape[2]
    channels = grid_ref.shape[0] // tiles
    real, imag = picture[0, 0], picture[0, 1]
    turned = []
    for sens_ref in sens:
        sens_real = sens_ref[0, 0, 0].astype(f32)
        sens_imag = sens_ref[0, 0, 1].astype(f32)
        coil = jnp.concatenate(
            [sens_real * real - sens_imag * imag, sens_real * imag + sens_imag * real], 0
        )
        both = nt(ey[...], coil.astype(bf16))
        half_real = both[:tiles, :rows] + both[tiles:, rows:]
        half_imag = both[:tiles, rows:] - both[tiles:, :rows]
        turned.append(
            jnp.concatenate(
                [
                    half_real * turn_ref[0] + half_imag * turn_ref[1],
                    half_imag * turn_ref[0] - half_real * turn_ref[1],
                ],
                1,
            ).astype(bf16)
        )
    grid = nn(jnp.concatenate(turned, 0), mx[...])
    size = grid.shape[1] // 2
    for coil in range(len(sens)):
        step = coil * planes + plane
        part = grid[coil * tiles : (coil + 1) * tiles]
        grid_ref[pl.ds(2 * step, tiles, stride=channels), :] = part[:, :size]
        grid_ref[pl.ds(2 * step + 1, tiles, stride=channels), :] = part[:, size:]


def tile_products(lefts, rights):
    rows, size = lefts[0].shape
    empty = jnp.zeros((rows, size), bf16)
    left = jnp.concatenate(
        [
            jnp.concatenate([value, empty] if place % 2 == 0 else [empty, value], 1)
            for place, value in enumerate(lefts)
        ],
        0,
    )
    right = jnp.concatenate(
        [jnp.concatenate(rights[:2], 0), jnp.concatenate(rights[2:], 0)], 1
    )
    product = nn(left, right)
    return [
        product[place * rows : (place + 1) * rows, place // 2 * size : (place // 2 + 1) * size]
        for place in range(4)
    ]


def each_four(count, function):
    def one(index, carry):
        function([index * 4 + place for place in range(4)])
        return carry

    lax.fori_loop(0, count // 4, one, 0, unroll=True)


def weight_copies(weights, held, sems):
    return [
        pltpu.make_async_copy(ref, held.at[place], sems.at[place])
        for place, ref in enumerate(weights)
    ]


def start_copies(copies):
    for copy in copies:
        copy.start()


def sample_tiles(block_ref, copies, weights, grid_ref, sums_ref, out_ref):
    count = weights.shape[1]
    channels = sums_ref.shape[1]
    sums_ref[...] = jnp.zeros_like(sums_ref)

    def left_of(tile):
        value = grid_ref[pl.ds(pl.multiple_of(tile * channels, channels), channels), :]
        high = value.astype(bf16).astype(f32)
        return jnp.concatenate([high, value - high], 0).astype(bf16)

    for group, copy in enumerate(copies):
        copy.wait()

        def four(places):
            tiles = [group * count + place for place in places]
            products = tile_products(
                [left_of(tile) for tile in tiles], [weights[group, place] for place in places]
            )
            for tile, product in zip(tiles, products):
                sums_ref[block_ref[tile]] += product[:channels] + product[channels:]

        each_four(count, four)
    out_ref[...] = sums_ref[...].reshape(out_ref.shape).astype(bf16)


def spread_tiles(block_ref, weights, parts_ref, grid_ref, turned_ref=None):
    count = weights[0].shape[0]
    channels = grid_ref.shape[0] // (count * len(weights))

    for group, weights_ref in enumerate(weights):

        def four(places):
            tiles = [group * count + place for place in places]
            rights = [weights_ref[place] for place in places]
            if turned_ref is not None:
                rights = [right.astype(f32).T.astype(bf16) for right in rights]
                for place, right in zip(places, rights):
                    turned_ref[group, place] = right
            products = tile_products([parts_ref[block_ref[tile]] for tile in tiles], rights)
            for tile, product in zip(tiles, products):
                if product.shape[0] > channels:
                    product = product[:channels] + product[channels:]
                start = pl.multiple_of(tile * channels, channels)
                grid_ref[pl.ds(start, channels), :] = product

        each_four(count, four)


def adjoint_images(coils, plane, planes, ey_back, mx_back, turn_ref, grid_ref):
    rows, tiles = turn_ref.shape[1], turn_ref.shape[2]
    channels = grid_ref.shape[0] // tiles
    grids = []
    for coil in range(coils):
        step = coil * planes + plane
        grid = jnp.concatenate(
            [
                grid_ref[pl.ds(2 * step, tiles, stride=channels), :],
                grid_ref[pl.ds(2 * step + 1, tiles, stride=channels), :],
            ],
            1,
        )
        grids.append(data_parts(grid))
    back = nt(mx_back[...], jnp.concatenate(grids, 0))
    turned = []
    for coil in range(coils):
        part = back[:, coil * tiles : (coil + 1) * tiles]
        both = jnp.concatenate(
            [
                part[:rows] * turn_ref[0] - part[rows:] * turn_ref[1],
                part[rows:] * turn_ref[0] + part[:rows] * turn_ref[1],
            ],
            1,
        )
        turned.append(data_parts(both))
    image = nn(jnp.concatenate(turned, 0), ey_back[...])
    columns = image.shape[1] // 2
    return [
        (image[c * rows : (c + 1) * rows, :columns], image[c * rows : (c + 1) * rows, columns:])
        for c in range(coils)
    ]


def add_dots(dots_ref, products):
    rows = lax.broadcasted_iota(jnp.int32, dots_ref.shape, 0)
    total = dots_ref[...]
    for place, (left, right) in enumerate(products):
        total += jnp.where(rows == place, jnp.sum(left * right), 0.0)
    dots_ref[...] = total


def measured_kernel(block, samples, *refs):
    *weights, mx, eb, turn, images, turned, grid = refs
    plane = pl.program_id(0)
    coils = images.shape[0]

    @pl.when(plane == 0)
    def _():
        spread_tiles(block, weights, samples, grid, turned)

    found = adjoint_images(coils, plane, pl.num_programs(0), eb, mx, turn, grid)
    for coil, (real, imag) in enumerate(found):
        images[coil, 0, 0] = real
        images[coil, 0, 1] = imag


def combine(images, sens):
    total_real = total_imag = 0.0
    for (real, imag), sens_ref in zip(images, sens):
        sens_real = sens_ref[0, 0, 0].astype(f32)
        sens_imag = sens_ref[0, 0, 1].astype(f32)
        total_real += sens_real * real + sens_imag * imag
        total_imag += sens_real * imag - sens_imag * real
    return total_real, total_imag


def start_kernel(images, *refs):
    *sens, right_side, rounded, dots = refs
    total = combine([(images[c, 0, 0], images[c, 0, 1]) for c in range(len(sens))], sens)
    for part in range(2):
        right_side[0, part] = total[part]
        rounded[0, part] = total[part].astype(bf16)

    @pl.when((pl.program_id(0) == 0) & (pl.program_id(1) == 0))
    def _():
        dots[...] = jnp.zeros_like(dots)

    add_dots(dots, [(right_side[0], right_side[0])])


def forward_kernel(coils, block, picture, *refs):
    sens = refs[:coils]
    *weights, ey, mx, turn, samples, grid, sums, held, sems = refs[coils:]
    plane = pl.program_id(0)

    @pl.when(plane == 0)
    def _():
        start_copies(weight_copies(weights, held, sems))

    forward_images(plane, pl.num_programs(0), picture, sens, ey, mx, turn, grid)

    @pl.when(plane == pl.num_programs(0) - 1)
    def _():
        sample_tiles(block, weight_copies(weights, held, sems), held, grid, sums, samples)


def summed_parts(samples, parts):
    summed = tree_sum([part[...].astype(f32) for part in samples])
    blocks, channels, size = parts.shape[0], parts.shape[1] // 2, parts.shape[2]
    value = summed.reshape(blocks, channels, size)
    high = value.astype(bf16).astype(f32)
    parts[...] = jnp.concatenate([high, value - high], 1).astype(bf16)
    return summed


def step_of(norm, energy):
    return jnp.where(norm > 0.0, norm / (energy + damping * norm), 1.0)


def first_kernel(peers, coils, block, *refs):
    samples, weights, sens = refs[:peers], refs[peers], refs[peers + 1 :][:coils]
    mx, eb, turn, *norms = refs[peers + 1 + coils :][: 3 + peers]
    right_side, residual, rounded, facts, dots, total_samples, grid, parts = refs[-8:]
    plane = pl.program_id(0)

    @pl.when(plane == 0)
    def _():
        summed = summed_parts(samples, parts)
        total_samples[...] = summed
        rows = lax.broadcasted_iota(jnp.int32, facts.shape, 0)
        norm = tree_sum([part[...] for part in norms])
        facts[...] = jnp.where(rows == 1, jnp.sum(summed * summed), norm)
        dots[...] = jnp.zeros_like(dots)
        spread_tiles(block, [weights.at[k] for k in range(peers)], parts, grid)

    images = adjoint_images(coils, plane, pl.num_programs(0), eb, mx, turn, grid)
    total = combine(images, sens)
    scale = step_of(facts[0:1, 0:1], facts[1:2, 0:1])
    for part in range(2):
        vector = right_side[0, part]
        value = vector - scale * (total[part] + damping * vector)
        residual[0, part] = value
        rounded[0, part] = value.astype(bf16)
        add_dots(dots, [(value, value), (value, vector)])


def second_kernel(peers, coils, block, *refs):
    samples, weights, sens = refs[:peers], refs[peers], refs[peers + 1 :][:coils]
    mx, eb, turn, facts, *infos = refs[peers + 1 + coils :][: 4 + coils]
    right_side, residual, rounded, grid, parts, kept = refs[-6:]
    plane = pl.program_id(0)

    @pl.when(plane == 0)
    def _():
        kept_coefficients(infos, kept, [0], True)
        summed_parts(samples, parts)
        spread_tiles(block, [weights.at[k] for k in range(peers)], parts, grid)

    images = adjoint_images(coils, plane, pl.num_programs(0), eb, mx, turn, grid)
    total = combine(images, sens)
    scale = step_of(facts[0:1, 0:1], facts[1:2, 0:1])
    for part in range(2):
        vector = residual[0, part]
        mixed = vector - scale * (total[part] + damping * vector)
        value = kept[0, 0:1, 0:1] * right_side[0, part] + kept[0, 1:2, 0:1] * vector
        rounded[0, part] = (value + kept[0, 2:3, 0:1] * mixed).astype(bf16)


def facts_kernel(peers, *refs):
    samples, dots = refs[:peers], refs[peers : 2 * peers]
    start_total, facts, out = refs[2 * peers :]
    both = tree_sum([part[...] for part in dots])
    summed = tree_sum([part[...].astype(f32) for part in samples])
    rows = lax.broadcasted_iota(jnp.int32, out.shape, 0)
    values = [facts[0:1], facts[1:2], both[0:1], both[1:2]]
    values += [jnp.sum(summed * summed), jnp.sum(summed * start_total[...])]
    total = jnp.zeros(out.shape, f32)
    for row, value in enumerate(values):
        total = jnp.where(rows == row, value, total)
    out[...] = total


def coefficients(norm, energy, square, cross, again, mixed):
    def over_all(values):
        return tree_sum([sum(of_coil) for of_coil in values])

    def each(function, *lists):
        return [[function(*items) for items in zip(*of_coil)] for of_coil in zip(*lists)]

    start_curve = each(lambda e, n: e + damping * n, energy, norm)
    curve = each(lambda e, n: e + damping * n, again, square)
    mixed_curve = each(lambda e, n: e + damping * n, mixed, cross)
    sigma = each(step_of, norm, energy)
    start_norm = over_all(norm)
    first_step = start_norm / over_all(start_curve)
    part = each(lambda s: first_step / s, sigma)
    next_norm = over_all(
        each(
            lambda w, n, c, s: w * w * s + 2.0 * w * (1.0 - w) * c + (1.0 - w) * (1.0 - w) * n,
            part,
            norm,
            cross,
            square,
        )
    )
    more = each(lambda w: 1.0 - w + next_norm / start_norm, part)
    second_step = next_norm / over_all(
        each(
            lambda w, m, q, c, s, z, qm, qs: w * w * q
            + w * m * ((c - s) / z + qm)
            + m * m * qs,
            part,
            more,
            curve,
            cross,
            square,
            sigma,
            mixed_curve,
            start_curve,
        )
    )
    share = each(lambda z: second_step / z, sigma)
    picture = each(lambda w, m: (first_step + second_step * m, second_step * w), part, more)
    residual = each(
        lambda w, m, h: (1.0 - w - h * m, w - h * w + h * m, h * w), part, more, share
    )
    return picture, residual


def kept_coefficients(infos, kept, ks, is_residual):
    numbers = [
        [[info[0, row : row + 1, 0:1]] for info in infos] for row in range(6)
    ]
    factors = coefficients(*numbers)[is_residual]
    rows = lax.broadcasted_iota(jnp.int32, kept.shape[1:], 0)
    for place, k in enumerate(ks):
        total = jnp.zeros(kept.shape[1:], f32)
        for row, factor in enumerate(factors[k][0]):
            total = jnp.where(rows == row, factor, total)
        kept[place] = total


def assemble_kernel(coils, ks, counts, order, *refs):
    infos, pieces, (out, kept) = refs[:coils], refs[coils:-2], refs[-2:]

    if max(counts) > 1:

        @pl.when(pl.program_id(0) == 0)
        def _():
            kept_coefficients(infos, kept, ks, False)

    def write(place, used):
        @pl.when(pl.program_id(0) == place)
        def _():
            if len(used) == 1:
                out[...] = used[0][...].astype(f32)
            else:
                total = 0.0
                for row, piece in enumerate(used):
                    factor = kept[place // len(counts), row : row + 1, 0:1]
                    total += factor.reshape(1, 1, 1, 1) * piece[...].astype(f32)
                out[...] = total

    first = 0
    for place in range(len(ks) * len(counts)):
        count = counts[place % len(counts)]
        write(place, pieces[first : first + count])
        first += count


def picture_kernel(coils, *refs):
    infos, (right_side, residual, out, kept) = refs[:coils], refs[coils:]

    @pl.when(pl.program_id(0) == 0)
    def _():
        kept_coefficients(infos, kept, [0], False)

    for part in range(2):
        value = kept[0, 0:1, 0:1] * right_side[0, part] + kept[0, 1:2, 0:1] * residual[0, part]
        out[0, part] = value.astype(bf16)


def whole_block(array):
    rank = len(array.shape)
    return pl.BlockSpec(array.shape, lambda *_: (0,) * rank)


def on_device(kspace, sens_maps, weights, tile_slot, tile_block, send_list):
    coil_count = lax.axis_size("coil")
    peers = lax.axis_size("pencil")
    planes = sens_maps.shape[1]
    own_planes = planes // coil_count
    rows = sens_maps.shape[3]
    columns = sens_maps.shape[4]
    rows_total = rows * peers
    size = weights.shape[1]
    tile_count = tile_slot.shape[0]
    tiles = tile_count * peers
    blocks_dev = kspace.shape[3] // size
    blocks = blocks_dev * peers
    cap = send_list.shape[2]
    runs = rows_total // size
    brick_dev = columns // peers * runs
    images_count = coil_count * own_planes
    channels = 2 * images_count

    coil_index = lax.axis_index("coil")

    def swapped(array, axis, k):
        return lax.ppermute(array, axis, [(i, i ^ k) for i in range(lax.axis_size(axis))])

    def everywhere(array, axis):
        bit = 1
        while bit < lax.axis_size(axis):
            bit *= 2
        pieces = {0: array}
        while bit > 1:
            bit //= 2
            for k in sorted(pieces):
                pieces[k ^ bit] = swapped(pieces[k], axis, bit)
        return [pieces[k] for k in sorted(pieces)]

    first_bits = [1 << bit for bit in range(coil_count.bit_length() - 1)]

    def completed(own, sent):
        pieces = {0: own}
        for bit, piece in zip(first_bits, sent):
            pieces[bit] = piece
        for bit in first_bits:
            for k in range(coil_count):
                if k not in pieces and (k ^ bit) in pieces:
                    pieces[k] = swapped(pieces[k ^ bit], "coil", bit)
        return [pieces[k] for k in range(coil_count)]

    def to_planes(array):
        pieces = []
        for k in range(coil_count):
            part = lax.dynamic_slice_in_dim(array, (coil_index ^ k) * own_planes, own_planes, 0)
            pieces.append(swapped(part, "coil", k) if k > 0 else part)
        return pieces

    group_planes = own_planes
    groups = range(own_planes // group_planes)
    measured = to_planes(kspace[0])
    packed = jnp.concatenate([tile_slot, tile_block, send_list.reshape(-1)])
    sens_source, packed, measured, own_weights = lax.optimization_barrier(
        (sens_maps[0], packed, measured, weights)
    )
    sens_source = sens_source.reshape(coil_count, own_planes, 2, rows, columns)
    sens = [
        lax.all_to_all(
            sens_source[:, g * group_planes : (g + 1) * group_planes],
            "coil",
            split_axis=0,
            concat_axis=0,
            tiled=True,
        )
        for g in groups
    ]
    measured = jnp.stack(measured)
    by_coil = jnp.arange(coil_count, dtype=jnp.int32) ^ coil_index
    measured = jnp.take(measured, by_coil, axis=0)
    all_weights = everywhere(own_weights, "pencil")

    places = jnp.stack(everywhere(packed, "pencil"))
    holder = (jnp.arange(peers, dtype=jnp.int32) ^ lax.axis_index("pencil"))[:, None]
    by_owner = jnp.take(places, holder[:, 0], axis=0)
    lists = by_owner[:, 2 * tile_count :].reshape(peers, peers, cap)
    slots = places[:, :tile_count]
    block_of = (places[:, tile_count : 2 * tile_count] + blocks_dev * holder).reshape(-1)
    brick = (slots // cap * brick_dev + lists[slots // cap, holder, slots % cap]).reshape(-1)
    line = brick // runs
    run = brick % runs

    measured = measured.reshape(channels, blocks_dev, size)
    measured = jnp.concatenate(everywhere(jnp.swapaxes(measured, 0, 1), "pencil"), 0)
    measured_block = (
        places[:, tile_count : 2 * tile_count]
        + blocks_dev * jnp.arange(peers, dtype=jnp.int32)[:, None]
    ).reshape(-1)

    cos_y, sin_y = wave(
        line - columns // 2, jnp.arange(columns, dtype=jnp.int32) - columns // 2, columns
    )
    row_ids = jnp.arange(rows, dtype=jnp.int32) + lax.axis_index("pencil") * rows - rows_total // 2
    cos_x, sin_x = wave(
        row_ids, jnp.arange(size, dtype=jnp.int32) - rows_total // 2, rows_total
    )
    turn = jnp.stack(quarter_turns(run, row_ids, runs))
    turn_back = jnp.stack(quarter_turns(row_ids, run, runs))

    def exchanged(partial, axis="pencil"):
        count = lax.axis_size(axis)
        return [partial] + [swapped(partial, axis, k) for k in range(1, count)]

    group_shape = (group_planes, 2, rows, columns)
    group_images = coil_count * group_planes
    group_channels = 2 * group_images

    if (
        rows % 128 == 0
        and columns % 128 == 0
        and size % 128 == 0
        and channels % 16 == 0
        and tile_count % 4 == 0
        and group_channels % 8 == 0
    ):
        ey = jnp.concatenate([cos_y, sin_y], 0).astype(bf16)
        eb = jnp.concatenate(
            [jnp.concatenate([cos_y, sin_y], 1), jnp.concatenate([-sin_y, cos_y], 1)], 0
        )
        eb = table_parts(eb, 0)
        mx = jnp.concatenate(
            [jnp.concatenate([cos_x, -sin_x], 1), jnp.concatenate([sin_x, cos_x], 1)], 0
        )
        mx, mx_back = mx.astype(bf16), table_parts(mx, 1)
        measured, ey, mx, turn, block_of, all_weights = lax.optimization_barrier(
            (measured, ey, mx, turn, block_of, all_weights)
        )
        places_spec = pl.BlockSpec(memory_space=pltpu.SMEM)
        plane_spec = pl.BlockSpec((1, 2, rows, columns), lambda p: (p, 0, 0, 0))
        sens_specs = [
            pl.BlockSpec((1, 1, 2, rows, columns), functools.partial(lambda c, p: (c, p, 0, 0, 0), c))
            for c in range(coil_count)
        ]
        grid_scratch = pltpu.VMEM((tiles * group_channels, size), f32)
        params = pltpu.CompilerParams(vmem_limit_bytes=vmem_limit)
        tail_tables = [mx_back, eb, turn_back]
        weights_specs = [pl.BlockSpec(memory_space=pl.ANY)] * peers
        held_weights = [
            pltpu.VMEM((peers,) + weights.shape, bf16),
            pltpu.SemaphoreType.DMA((peers,)),
        ]

        def shaped(shape, dtype=f32):
            return jax.ShapeDtypeStruct(shape, dtype)

        def call(kernel, grid, inputs, specs, outs, out_specs, scratch, images):
            flops = 2 * images * 8 * tiles * rows * (columns + size)
            return pl.pallas_call(
                kernel,
                grid=grid,
                in_specs=specs,
                out_specs=out_specs,
                out_shape=outs,
                scratch_shapes=scratch,
                compiler_params=params,
                cost_estimate=pl.CostEstimate(
                    flops=flops,
                    bytes_accessed=sum(math.prod(i.shape) * i.dtype.itemsize for i in inputs),
                    transcendentals=0,
                ),
            )(*inputs)

        def measured_images():
            inputs = [measured_block, measured, *all_weights, *tail_tables]
            turned_shape = shaped((peers,) + weights.shape, bf16)
            shape = (coil_count, own_planes, 2, rows, columns)
            return call(
                measured_kernel,
                (own_planes,),
                inputs,
                [places_spec] + [whole_block(i) for i in inputs[1:]],
                [shaped(shape), turned_shape],
                [
                    pl.BlockSpec((coil_count, 1, 2, rows, columns), lambda p: (0, p, 0, 0, 0)),
                    whole_block(turned_shape),
                ],
                [pltpu.VMEM((tiles * channels, size), f32)],
                images_count,
            )

        def start(images, g):
            chunk = 64
            spec = pl.BlockSpec((1, 2, chunk, columns), lambda p, r: (p, 0, r, 0))
            images_spec = pl.BlockSpec(
                (coil_count, 1, 2, chunk, columns),
                lambda p, r: (0, p + g * group_planes, 0, r, 0),
            )
            dots_shape = shaped((8, 128))
            return call(
                start_kernel,
                (group_planes, rows // chunk),
                [images] + [sens[g]] * coil_count,
                [images_spec]
                + [
                    pl.BlockSpec(
                        (1, 1, 2, chunk, columns),
                        functools.partial(lambda c, p, r: (c, p, 0, r, 0), c),
                    )
                    for c in range(coil_count)
                ],
                [shaped(group_shape), shaped(group_shape, bf16), dots_shape],
                [spec, spec, whole_block(dots_shape)],
                [],
                0,
            )

        def forward(picture, g):
            tail = [ey, mx, turn]
            out = shaped((blocks * group_channels, size), bf16)
            return call(
                functools.partial(forward_kernel, coil_count),
                (group_planes,),
                [block_of, picture] + [sens[g]] * coil_count + [*all_weights, *tail],
                [places_spec, plane_spec]
                + sens_specs
                + weights_specs
                + [whole_block(i) for i in tail],
                out,
                whole_block(out),
                [grid_scratch, pltpu.VMEM((blocks, group_channels, size), f32)] + held_weights,
                group_images,
            )

        def back(kernel, samples, tables, vectors, g, outs, out_specs, scratch=()):
            inputs = [*samples, turned_weights]
            tables = tail_tables + tables
            return call(
                functools.partial(kernel, peers, coil_count),
                (group_planes,),
                [block_of, *inputs] + [sens[g]] * coil_count + tables + vectors,
                [places_spec]
                + [whole_block(i) for i in inputs]
                + sens_specs
                + [whole_block(i) for i in tables]
                + [plane_spec] * len(vectors),
                outs,
                out_specs,
                [grid_scratch, pltpu.VMEM((blocks, 2 * group_channels, size), bf16), *scratch],
                group_images,
            )

        def first(samples, norms, right_side, g):
            small, large = shaped((8, 128)), shaped(samples[0].shape)
            return back(
                first_kernel,
                samples,
                norms,
                [right_side],
                g,
                [shaped(group_shape), shaped(group_shape, bf16), small, small, large],
                [plane_spec, plane_spec] + [whole_block(i) for i in (small, small, large)],
            )

        def facts_of(samples, dots, start_total, facts):
            inputs = [*samples, *dots, start_total, facts]
            return pl.pallas_call(
                functools.partial(facts_kernel, peers),
                in_specs=[pl.BlockSpec(memory_space=pltpu.VMEM)] * len(inputs),
                out_specs=pl.BlockSpec(memory_space=pltpu.VMEM),
                out_shape=shaped((8, 128)),
                compiler_params=params,
            )(*inputs)

        def assembled(infos, parts, ks, out=None):
            step = own_planes // len(parts)
            order = jnp.stack(
                [(coil_index ^ k) * len(parts) + h for k in ks for h in range(len(parts))]
            ).astype(jnp.int32)
            inputs, specs = [], [pl.BlockSpec(infos[0].shape, lambda i, o: (0, 0, 0))] * len(infos)
            for k in ks:
                for vectors, h in parts:
                    for vector in vectors:
                        inputs.append(vector[k])
                        specs.append(
                            pl.BlockSpec(
                                (step, 2, rows, columns),
                                functools.partial(lambda h, i, o: (h, 0, 0, 0), h),
                            )
                        )
            aliases = {}
            if out is not None:
                aliases = {1 + len(infos) + len(inputs): 0}
                inputs.append(out)
                specs.append(pl.BlockSpec(memory_space=pl.ANY))
            counts = [len(vectors) for vectors, h in parts]
            return pl.pallas_call(
                functools.partial(assemble_kernel, coil_count, list(ks), counts),
                grid_spec=pltpu.PrefetchScalarGridSpec(
                    num_scalar_prefetch=1,
                    grid=(len(ks) * len(parts),),
                    in_specs=specs,
                    out_specs=pl.BlockSpec(
                        (step, 2, rows, columns), lambda i, o: (o[i], 0, 0, 0)
                    ),
                    scratch_shapes=[pltpu.VMEM((len(ks), 8, 128), f32)],
                ),
                out_shape=shaped((planes, 2, rows, columns)),
                input_output_aliases=aliases,
                compiler_params=params,
            )(order, *infos, *inputs)

        def own_picture(infos, right_side, residual, first_plane):
            count = own_planes - first_plane
            spec = pl.BlockSpec((1, 2, rows, columns), lambda p: (p + first_plane, 0, 0, 0))
            small = pl.BlockSpec(infos[0].shape, lambda p: (0, 0, 0))
            return pl.pallas_call(
                functools.partial(picture_kernel, coil_count),
                grid=(count,),
                in_specs=[small] * len(infos) + [spec] * 2,
                out_specs=plane_spec,
                out_shape=shaped((count, 2, rows, columns), bf16),
                scratch_shapes=[pltpu.VMEM((1, 8, 128), f32)],
                compiler_params=params,
            )(*infos, right_side, residual)

        def second(samples, facts, infos, right_side, residual, g):
            return back(
                second_kernel,
                samples,
                [facts, *infos],
                [right_side, residual],
                g,
                shaped(group_shape, bf16),
                plane_spec,
                [pltpu.VMEM((1, 8, 128), f32)],
            )

    else:
        ein = functools.partial(jnp.einsum, precision=lax.Precision.HIGH)
        maps = [array.astype(f32) for array in sens]
        block_map = (block_of[:, None] == jnp.arange(blocks, dtype=jnp.int32)).astype(f32)
        tc, ts = turn[0][:, None, None], turn[1][:, None, None]
        wide_weights = jnp.concatenate(all_weights, 0).astype(f32)

        def forward(picture, g):
            map_real, map_imag = maps[g][:, :, 0], maps[g][:, :, 1]
            coil_real = map_real * picture[None, :, 0] - map_imag * picture[None, :, 1]
            coil_imag = map_real * picture[None, :, 1] + map_imag * picture[None, :, 0]
            half_real = ein("ty,cpxy->tcpx", cos_y, coil_real) + ein(
                "ty,cpxy->tcpx", sin_y, coil_imag
            )
            half_imag = ein("ty,cpxy->tcpx", cos_y, coil_imag) - ein(
                "ty,cpxy->tcpx", sin_y, coil_real
            )
            real = half_real * tc + half_imag * ts
            imag = half_imag * tc - half_real * ts
            grid = jnp.stack(
                [
                    ein("tcpx,xi->tcpi", real, cos_x) + ein("tcpx,xi->tcpi", imag, sin_x),
                    ein("tcpx,xi->tcpi", imag, cos_x) - ein("tcpx,xi->tcpi", real, sin_x),
                ],
                3,
            ).reshape(tiles, group_channels, size)
            product = ein("tgi,tis->tgs", grid, wide_weights)
            return ein("tb,tgs->bgs", block_map, product).astype(bf16).reshape(-1, size)

        def images_of(samples, blocks_of):
            spread = ein("tgs,tis->tgi", jnp.take(samples, blocks_of, axis=0), wide_weights)
            spread = spread.reshape(tiles, coil_count, -1, 2, size)
            back_real = ein("tcpi,xi->tcpx", spread[:, :, :, 0], cos_x) - ein(
                "tcpi,xi->tcpx", spread[:, :, :, 1], sin_x
            )
            back_imag = ein("tcpi,xi->tcpx", spread[:, :, :, 1], cos_x) + ein(
                "tcpi,xi->tcpx", spread[:, :, :, 0], sin_x
            )
            real = back_real * tc - back_imag * ts
            imag = back_imag * tc + back_real * ts
            return jnp.stack(
                [
                    ein("tcpx,ty->cpxy", real, cos_y) - ein("tcpx,ty->cpxy", imag, sin_y),
                    ein("tcpx,ty->cpxy", imag, cos_y) + ein("tcpx,ty->cpxy", real, sin_y),
                ],
                2,
            )

        def combined(images, g):
            map_real, map_imag = maps[g][:, :, 0], maps[g][:, :, 1]
            real, imag = images[:, :, 0], images[:, :, 1]
            return jnp.stack(
                [
                    jnp.sum(map_real * real + map_imag * imag, 0),
                    jnp.sum(map_real * imag - map_imag * real, 0),
                ],
                1,
            )

        def stacked_dots(values):
            values = values + [jnp.zeros((), f32)] * (8 - len(values))
            return jnp.broadcast_to(jnp.stack(values)[:, None], (8, 128))

        def applied_to(samples, vector, g):
            samples = added(samples).reshape(blocks, group_channels, size)
            return combined(images_of(samples, block_of), g) + damping * vector

        def measured_images():
            return images_of(measured.astype(f32), measured_block), None

        def start(images, g):
            right_side = combined(images[:, g * group_planes : (g + 1) * group_planes], g)
            dots = stacked_dots([jnp.sum(right_side * right_side)])
            return right_side, right_side.astype(bf16), dots

        def first(samples, norms, right_side, g):
            norm = tree_sum(norms)[0, 0]
            total = added(samples)
            energy = jnp.sum(jnp.square(total))
            residual = right_side - step_of(norm, energy) * applied_to(samples, right_side, g)
            dots = [jnp.sum(residual * residual), jnp.sum(residual * right_side)]
            facts = stacked_dots([norm, energy])
            return residual, residual.astype(bf16), facts, stacked_dots(dots), total

        def facts_of(samples, dots, start_total, facts):
            total = added(samples)
            square, cross = tree_sum(dots)[:2, 0]
            values = [facts[0, 0], facts[1, 0], square, cross]
            values += [jnp.sum(total * total), jnp.sum(total * start_total)]
            return stacked_dots(values)

        def factors_of(infos, is_residual):
            numbers = [[[info[0, row, 0]] for info in infos] for row in range(6)]
            return [factors[0] for factors in coefficients(*numbers)[is_residual]]

        def mixture(factors, vectors):
            return sum(factor * vector.astype(f32) for factor, vector in zip(factors, vectors))

        def assembled(infos, parts, ks, out=None):
            factors = factors_of(infos, False)
            step = own_planes // len(parts)
            if out is None:
                out = jnp.zeros((planes, 2, rows, columns), f32)
            for k in ks:
                for h, (vectors, at) in enumerate(parts):
                    place = ((coil_index ^ k) * own_planes + h * step, 0, 0, 0)
                    pieces = [vector[k][at * step : (at + 1) * step] for vector in vectors]
                    if len(pieces) == 1:
                        piece = pieces[0].astype(f32)
                    else:
                        piece = mixture(factors[k], pieces)
                    out = lax.dynamic_update_slice(out, piece, place)
            return out

        def own_picture(infos, right_side, residual, first_plane):
            vectors = [right_side[first_plane:], residual[first_plane:]]
            return mixture(factors_of(infos, False)[0], vectors).astype(bf16)

        def second(samples, facts, infos, right_side, residual, g):
            mixed = residual - step_of(facts[0, 0], facts[1, 0]) * applied_to(samples, residual, g)
            return mixture(factors_of(infos, True)[0], [right_side, residual, mixed]).astype(bf16)

    def added(samples):
        return tree_sum([part.astype(f32) for part in samples])

    def sent_by_bits(own):
        return [swapped(own, "coil", k) for k in first_bits]

    images, turned_weights = measured_images()
    halves = 2 if own_planes % 2 == 0 else 1
    early = own_planes // 2 if halves == 2 else 0

    def first_planes(own):
        return own[:early]

    right_side, start_own, norm = start(images, 0)
    start_sent = sent_by_bits(first_planes(start_own)) if early else []
    samples, norm = lax.optimization_barrier((forward(right_side, 0), norm))
    samples = exchanged(samples)
    norms = exchanged(norm)
    samples, norms, start_sent = lax.optimization_barrier((samples, norms, start_sent))
    residual, residual_own, facts, dots, start_total = first(samples, norms, right_side, 0)
    dots = exchanged(dots)
    start_pieces = completed(first_planes(start_own), start_sent) if early else []
    residual, residual_own, dots, start_pieces = lax.optimization_barrier(
        (residual, residual_own, dots, start_pieces)
    )
    residual_sent = sent_by_bits(first_planes(residual_own)) if early else []
    samples = exchanged(forward(residual, 0))
    samples, dots = lax.optimization_barrier((samples, dots))
    info = facts_of(samples, dots, start_total, facts)
    others = exchanged(info[None], "coil")
    picture_own = own_picture(others, right_side, residual, early)
    samples, others, picture_own, residual_sent = lax.optimization_barrier(
        (samples, others, picture_own, residual_sent)
    )
    residual_pieces = completed(first_planes(residual_own), residual_sent) if early else []
    picture_sent = sent_by_bits(picture_own)
    final_own = second(samples, info, others, right_side, residual, 0)
    final_own, picture_sent, residual_pieces = lax.optimization_barrier(
        (final_own, picture_sent, residual_pieces)
    )
    final_sent = sent_by_bits(final_own)
    picture_pieces = completed(picture_own, picture_sent)
    parts = [([start_pieces, residual_pieces], 0)] * (halves - 1) + [([picture_pieces], 0)]
    picture = assembled(others, parts, range(coil_count))
    near = [final_own, final_sent[0]] + [None] * (coil_count - 2)
    out = assembled(others, [([near], h) for h in range(halves)], range(2))
    picture, final_sent = lax.optimization_barrier((picture, final_sent))
    final_pieces = completed(final_own, final_sent)
    parts = [([final_pieces], h) for h in range(halves)]
    late = coil_count - 1
    out = assembled(others, parts, range(2, late), out)
    out = assembled(others, parts, [late], out)
    return picture, out


def solution(mesh):
    in_specs = (
        P("coil", "scan", None, "pencil"),
        P("coil", "scan", None, "pencil", None),
        P("pencil", None, None),
        P("pencil"),
        P("pencil"),
        P("pencil", None, None),
    )
    out_specs = (P("scan", None, "pencil", None), P("scan", None, "pencil", None))
    return jax.shard_map(
        on_device, mesh=mesh, in_specs=in_specs, out_specs=out_specs, check_vma=False
    )
```

```python
import functools
import math

import jax
import jax.numpy as jnp
from jax import lax
from jax.experimental import pallas as pl
from jax.experimental.pallas import tpu as pltpu
from jax.sharding import PartitionSpec as P


damping = 0.5
f32, bf16 = jnp.float32, jnp.bfloat16
vmem_limit = 56 * 1024 * 1024


def wave(left, right, length):
    phases = left[:, None] * right[None, :] % length
    angles = phases.astype(f32) * (2.0 * math.pi / length)
    return jnp.cos(angles) / math.sqrt(length), jnp.sin(angles) / math.sqrt(length)


def quarter_turns(left, right, count):
    turns = left[:, None] * right[None, :] % count
    if count == 4:
        cosine = jnp.where(turns == 0, 1.0, 0.0) - jnp.where(turns == 2, 1.0, 0.0)
        sine = jnp.where(turns == 1, 1.0, 0.0) - jnp.where(turns == 3, 1.0, 0.0)
        return cosine.astype(f32), sine.astype(f32)
    angles = turns.astype(f32) * (2.0 * math.pi / count)
    return jnp.cos(angles), jnp.sin(angles)


def split(value):
    high = value.astype(bf16)
    return high, (value - high.astype(f32)).astype(bf16)


def table_parts(table, axis):
    high = lax.reduce_precision(table, 8, 7)
    low = (table - high).astype(bf16)
    high = high.astype(bf16)
    return jnp.concatenate([high, high, low], axis)


def data_parts(value):
    high, low = split(value)
    return jnp.concatenate([high, low, high], 1)


def nt(left, right):
    return lax.dot_general(left, right, (((1,), (1,)), ((), ())), preferred_element_type=f32)


def nn(left, right):
    return jnp.dot(left, right, preferred_element_type=f32)


def tree_sum(values):
    while len(values) > 1:
        values = [left + right for left, right in zip(values[::2], values[1::2])]
    return values[0]


def forward_images(plane, planes, picture, sens, ey, mx, turn_ref, grid_ref):
    tiles = turn_ref.shape[1]
    rows = turn_ref.shape[2]
    channels = grid_ref.shape[0] // tiles
    real, imag = picture[0, 0], picture[0, 1]
    turned = []
    for sens_ref in sens:
        sens_real = sens_ref[0, 0, 0].astype(f32)
        sens_imag = sens_ref[0, 0, 1].astype(f32)
        coil = jnp.concatenate(
            [sens_real * real - sens_imag * imag, sens_real * imag + sens_imag * real], 0
        )
        both = nt(ey[...], coil.astype(bf16))
        half_real = both[:tiles, :rows] + both[tiles:, rows:]
        half_imag = both[:tiles, rows:] - both[tiles:, :rows]
        turned.append(
            jnp.concatenate(
                [
                    half_real * turn_ref[0] + half_imag * turn_ref[1],
                    half_imag * turn_ref[0] - half_real * turn_ref[1],
                ],
                1,
            ).astype(bf16)
        )
    grid = nn(jnp.concatenate(turned, 0), mx[...])
    size = grid.shape[1] // 2
    for coil in range(len(sens)):
        step = coil * planes + plane
        part = grid[coil * tiles : (coil + 1) * tiles]
        grid_ref[pl.ds(2 * step, tiles, stride=channels), :] = part[:, :size]
        grid_ref[pl.ds(2 * step + 1, tiles, stride=channels), :] = part[:, size:]


def tile_products(lefts, rights):
    rows, size = lefts[0].shape
    empty = jnp.zeros((rows, size), bf16)
    left = jnp.concatenate(
        [
            jnp.concatenate([value, empty] if place % 2 == 0 else [empty, value], 1)
            for place, value in enumerate(lefts)
        ],
        0,
    )
    right = jnp.concatenate(
        [jnp.concatenate(rights[:2], 0), jnp.concatenate(rights[2:], 0)], 1
    )
    product = nn(left, right)
    return [
        product[place * rows : (place + 1) * rows, place // 2 * size : (place // 2 + 1) * size]
        for place in range(4)
    ]


def each_four(count, function):
    def one(index, carry):
        function([index * 4 + place for place in range(4)])
        return carry

    lax.fori_loop(0, count // 4, one, 0, unroll=True)


def weight_copies(weights, held, sems):
    return [
        pltpu.make_async_copy(ref, held.at[place], sems.at[place])
        for place, ref in enumerate(weights)
    ]


def start_copies(copies):
    for copy in copies:
        copy.start()


def sample_tiles(block_ref, copies, weights, grid_ref, sums_ref, out_ref):
    count = weights.shape[1]
    channels = sums_ref.shape[1]
    sums_ref[...] = jnp.zeros_like(sums_ref)

    def left_of(tile):
        value = grid_ref[pl.ds(pl.multiple_of(tile * channels, channels), channels), :]
        high = value.astype(bf16).astype(f32)
        return jnp.concatenate([high, value - high], 0).astype(bf16)

    for group, copy in enumerate(copies):
        copy.wait()

        def four(places):
            tiles = [group * count + place for place in places]
            products = tile_products(
                [left_of(tile) for tile in tiles], [weights[group, place] for place in places]
            )
            for tile, product in zip(tiles, products):
                sums_ref[block_ref[tile]] += product[:channels] + product[channels:]

        each_four(count, four)
    out_ref[...] = sums_ref[...].reshape(out_ref.shape).astype(bf16)


def spread_tiles(block_ref, weights, parts_ref, grid_ref, turned_ref=None):
    count = weights[0].shape[0]
    channels = grid_ref.shape[0] // (count * len(weights))

    for group, weights_ref in enumerate(weights):

        def four(places):
            tiles = [group * count + place for place in places]
            rights = [weights_ref[place] for place in places]
            if turned_ref is not None:
                rights = [right.astype(f32).T.astype(bf16) for right in rights]
                for place, right in zip(places, rights):
                    turned_ref[group, place] = right
            products = tile_products([parts_ref[block_ref[tile]] for tile in tiles], rights)
            for tile, product in zip(tiles, products):
                if product.shape[0] > channels:
                    product = product[:channels] + product[channels:]
                start = pl.multiple_of(tile * channels, channels)
                grid_ref[pl.ds(start, channels), :] = product

        each_four(count, four)


def adjoint_images(coils, plane, planes, ey_back, mx_back, turn_ref, grid_ref):
    rows, tiles = turn_ref.shape[1], turn_ref.shape[2]
    channels = grid_ref.shape[0] // tiles
    grids = []
    for coil in range(coils):
        step = coil * planes + plane
        grid = jnp.concatenate(
            [
                grid_ref[pl.ds(2 * step, tiles, stride=channels), :],
                grid_ref[pl.ds(2 * step + 1, tiles, stride=channels), :],
            ],
            1,
        )
        grids.append(data_parts(grid))
    back = nt(mx_back[...], jnp.concatenate(grids, 0))
    turned = []
    for coil in range(coils):
        part = back[:, coil * tiles : (coil + 1) * tiles]
        both = jnp.concatenate(
            [
                part[:rows] * turn_ref[0] - part[rows:] * turn_ref[1],
                part[rows:] * turn_ref[0] + part[:rows] * turn_ref[1],
            ],
            1,
        )
        turned.append(data_parts(both))
    image = nn(jnp.concatenate(turned, 0), ey_back[...])
    columns = image.shape[1] // 2
    return [
        (image[c * rows : (c + 1) * rows, :columns], image[c * rows : (c + 1) * rows, columns:])
        for c in range(coils)
    ]


def add_dots(dots_ref, products):
    rows = lax.broadcasted_iota(jnp.int32, dots_ref.shape, 0)
    total = dots_ref[...]
    for place, (left, right) in enumerate(products):
        total += jnp.where(rows == place, jnp.sum(left * right), 0.0)
    dots_ref[...] = total


def measured_kernel(block, samples, *refs):
    *weights, mx, eb, turn, images, turned, grid = refs
    plane = pl.program_id(0)
    coils = images.shape[0]

    @pl.when(plane == 0)
    def _():
        spread_tiles(block, weights, samples, grid, turned)

    found = adjoint_images(coils, plane, pl.num_programs(0), eb, mx, turn, grid)
    for coil, (real, imag) in enumerate(found):
        images[coil, 0, 0] = real
        images[coil, 0, 1] = imag


def combine(images, sens):
    total_real = total_imag = 0.0
    for (real, imag), sens_ref in zip(images, sens):
        sens_real = sens_ref[0, 0, 0].astype(f32)
        sens_imag = sens_ref[0, 0, 1].astype(f32)
        total_real += sens_real * real + sens_imag * imag
        total_imag += sens_real * imag - sens_imag * real
    return total_real, total_imag


def start_kernel(images, *refs):
    *sens, right_side, rounded, dots = refs
    total = combine([(images[c, 0, 0], images[c, 0, 1]) for c in range(len(sens))], sens)
    for part in range(2):
        right_side[0, part] = total[part]
        rounded[0, part] = total[part].astype(bf16)

    @pl.when((pl.program_id(0) == 0) & (pl.program_id(1) == 0))
    def _():
        dots[...] = jnp.zeros_like(dots)

    add_dots(dots, [(right_side[0], right_side[0])])


def forward_kernel(coils, block, picture, *refs):
    sens = refs[:coils]
    *weights, ey, mx, turn, samples, grid, sums, held, sems = refs[coils:]
    plane = pl.program_id(0)

    @pl.when(plane == 0)
    def _():
        start_copies(weight_copies(weights, held, sems))

    forward_images(plane, pl.num_programs(0), picture, sens, ey, mx, turn, grid)

    @pl.when(plane == pl.num_programs(0) - 1)
    def _():
        sample_tiles(block, weight_copies(weights, held, sems), held, grid, sums, samples)


def summed_parts(samples, parts):
    summed = tree_sum([part[...].astype(f32) for part in samples])
    blocks, channels, size = parts.shape[0], parts.shape[1] // 2, parts.shape[2]
    value = summed.reshape(blocks, channels, size)
    high = value.astype(bf16).astype(f32)
    parts[...] = jnp.concatenate([high, value - high], 1).astype(bf16)
    return summed


def step_of(norm, energy):
    return jnp.where(norm > 0.0, norm / (energy + damping * norm), 1.0)


def first_kernel(peers, coils, block, *refs):
    samples, weights, sens = refs[:peers], refs[peers], refs[peers + 1 :][:coils]
    mx, eb, turn, *norms = refs[peers + 1 + coils :][: 3 + peers]
    right_side, residual, rounded, facts, dots, total_samples, grid, parts = refs[-8:]
    plane = pl.program_id(0)

    @pl.when(plane == 0)
    def _():
        summed = summed_parts(samples, parts)
        total_samples[...] = summed
        rows = lax.broadcasted_iota(jnp.int32, facts.shape, 0)
        norm = tree_sum([part[...] for part in norms])
        facts[...] = jnp.where(rows == 1, jnp.sum(summed * summed), norm)
        dots[...] = jnp.zeros_like(dots)
        spread_tiles(block, [weights.at[k] for k in range(peers)], parts, grid)

    images = adjoint_images(coils, plane, pl.num_programs(0), eb, mx, turn, grid)
    total = combine(images, sens)
    scale = step_of(facts[0:1, 0:1], facts[1:2, 0:1])
    for part in range(2):
        vector = right_side[0, part]
        value = vector - scale * (total[part] + damping * vector)
        residual[0, part] = value
        rounded[0, part] = value.astype(bf16)
        add_dots(dots, [(value, value), (value, vector)])


def second_kernel(peers, coils, block, *refs):
    samples, weights, sens = refs[:peers], refs[peers], refs[peers + 1 :][:coils]
    mx, eb, turn, facts, *infos = refs[peers + 1 + coils :][: 4 + coils]
    right_side, residual, rounded, grid, parts, kept = refs[-6:]
    plane = pl.program_id(0)

    @pl.when(plane == 0)
    def _():
        kept_coefficients(infos, kept, [0], True)
        summed_parts(samples, parts)
        spread_tiles(block, [weights.at[k] for k in range(peers)], parts, grid)

    images = adjoint_images(coils, plane, pl.num_programs(0), eb, mx, turn, grid)
    total = combine(images, sens)
    scale = step_of(facts[0:1, 0:1], facts[1:2, 0:1])
    for part in range(2):
        vector = residual[0, part]
        mixed = vector - scale * (total[part] + damping * vector)
        value = kept[0, 0:1, 0:1] * right_side[0, part] + kept[0, 1:2, 0:1] * vector
        rounded[0, part] = (value + kept[0, 2:3, 0:1] * mixed).astype(bf16)


def facts_kernel(peers, *refs):
    samples, dots = refs[:peers], refs[peers : 2 * peers]
    start_total, facts, out = refs[2 * peers :]
    both = tree_sum([part[...] for part in dots])
    summed = tree_sum([part[...].astype(f32) for part in samples])
    rows = lax.broadcasted_iota(jnp.int32, out.shape, 0)
    values = [facts[0:1], facts[1:2], both[0:1], both[1:2]]
    values += [jnp.sum(summed * summed), jnp.sum(summed * start_total[...])]
    total = jnp.zeros(out.shape, f32)
    for row, value in enumerate(values):
        total = jnp.where(rows == row, value, total)
    out[...] = total


def coefficients(norm, energy, square, cross, again, mixed):
    def over_all(values):
        return tree_sum([sum(of_coil) for of_coil in values])

    def each(function, *lists):
        return [[function(*items) for items in zip(*of_coil)] for of_coil in zip(*lists)]

    start_curve = each(lambda e, n: e + damping * n, energy, norm)
    curve = each(lambda e, n: e + damping * n, again, square)
    mixed_curve = each(lambda e, n: e + damping * n, mixed, cross)
    sigma = each(step_of, norm, energy)
    start_norm = over_all(norm)
    first_step = start_norm / over_all(start_curve)
    part = each(lambda s: first_step / s, sigma)
    next_norm = over_all(
        each(
            lambda w, n, c, s: w * w * s + 2.0 * w * (1.0 - w) * c + (1.0 - w) * (1.0 - w) * n,
            part,
            norm,
            cross,
            square,
        )
    )
    more = each(lambda w: 1.0 - w + next_norm / start_norm, part)
    second_step = next_norm / over_all(
        each(
            lambda w, m, q, c, s, z, qm, qs: w * w * q
            + w * m * ((c - s) / z + qm)
            + m * m * qs,
            part,
            more,
            curve,
            cross,
            square,
            sigma,
            mixed_curve,
            start_curve,
        )
    )
    share = each(lambda z: second_step / z, sigma)
    picture = each(lambda w, m: (first_step + second_step * m, second_step * w), part, more)
    residual = each(
        lambda w, m, h: (1.0 - w - h * m, w - h * w + h * m, h * w), part, more, share
    )
    return picture, residual


def kept_coefficients(infos, kept, ks, is_residual):
    numbers = [
        [[info[0, row : row + 1, 0:1]] for info in infos] for row in range(6)
    ]
    factors = coefficients(*numbers)[is_residual]
    rows = lax.broadcasted_iota(jnp.int32, kept.shape[1:], 0)
    for place, k in enumerate(ks):
        total = jnp.zeros(kept.shape[1:], f32)
        for row, factor in enumerate(factors[k][0]):
            total = jnp.where(rows == row, factor, total)
        kept[place] = total


def assemble_kernel(coils, ks, counts, order, *refs):
    infos, pieces, (out, kept) = refs[:coils], refs[coils:-2], refs[-2:]

    if max(counts) > 1:

        @pl.when(pl.program_id(0) == 0)
        def _():
            kept_coefficients(infos, kept, ks, False)

    def write(place, used):
        @pl.when(pl.program_id(0) == place)
        def _():
            if len(used) == 1:
                out[...] = used[0][...].astype(f32)
            else:
                total = 0.0
                for row, piece in enumerate(used):
                    factor = kept[place // len(counts), row : row + 1, 0:1]
                    total += factor.reshape(1, 1, 1, 1) * piece[...].astype(f32)
                out[...] = total

    first = 0
    for place in range(len(ks) * len(counts)):
        count = counts[place % len(counts)]
        write(place, pieces[first : first + count])
        first += count


def whole_block(array):
    rank = len(array.shape)
    return pl.BlockSpec(array.shape, lambda *_: (0,) * rank)


def on_device(kspace, sens_maps, weights, tile_slot, tile_block, send_list):
    coil_count = lax.axis_size("coil")
    peers = lax.axis_size("pencil")
    planes = sens_maps.shape[1]
    own_planes = planes // coil_count
    rows = sens_maps.shape[3]
    columns = sens_maps.shape[4]
    rows_total = rows * peers
    size = weights.shape[1]
    tile_count = tile_slot.shape[0]
    tiles = tile_count * peers
    blocks_dev = kspace.shape[3] // size
    blocks = blocks_dev * peers
    cap = send_list.shape[2]
    runs = rows_total // size
    brick_dev = columns // peers * runs
    images_count = coil_count * own_planes
    channels = 2 * images_count

    coil_index = lax.axis_index("coil")

    def swapped(array, axis, k):
        return lax.ppermute(array, axis, [(i, i ^ k) for i in range(lax.axis_size(axis))])

    def everywhere(array, axis):
        bit = 1
        while bit < lax.axis_size(axis):
            bit *= 2
        pieces = {0: array}
        while bit > 1:
            bit //= 2
            for k in sorted(pieces):
                pieces[k ^ bit] = swapped(pieces[k], axis, bit)
        return [pieces[k] for k in sorted(pieces)]

    first_bits = [1 << bit for bit in range(coil_count.bit_length() - 1)]

    def completed(own, sent):
        pieces = {0: own}
        for bit, piece in zip(first_bits, sent):
            pieces[bit] = piece
        for bit in first_bits:
            for k in range(coil_count):
                if k not in pieces and (k ^ bit) in pieces:
                    pieces[k] = swapped(pieces[k ^ bit], "coil", bit)
        return [pieces[k] for k in range(coil_count)]

    def to_planes(array):
        pieces = []
        for k in range(coil_count):
            part = lax.dynamic_slice_in_dim(array, (coil_index ^ k) * own_planes, own_planes, 0)
            pieces.append(swapped(part, "coil", k) if k > 0 else part)
        return pieces

    group_planes = own_planes
    groups = range(own_planes // group_planes)
    measured = to_planes(kspace[0])
    packed = jnp.concatenate([tile_slot, tile_block, send_list.reshape(-1)])
    sens_source, packed, measured, own_weights = lax.optimization_barrier(
        (sens_maps[0], packed, measured, weights)
    )
    sens_source = sens_source.reshape(coil_count, own_planes, 2, rows, columns)
    sens = [
        lax.all_to_all(
            sens_source[:, g * group_planes : (g + 1) * group_planes],
            "coil",
            split_axis=0,
            concat_axis=0,
            tiled=True,
        )
        for g in groups
    ]
    measured = jnp.stack(measured)
    by_coil = jnp.arange(coil_count, dtype=jnp.int32) ^ coil_index
    measured = jnp.take(measured, by_coil, axis=0)
    all_weights = everywhere(own_weights, "pencil")

    places = jnp.stack(everywhere(packed, "pencil"))
    holder = (jnp.arange(peers, dtype=jnp.int32) ^ lax.axis_index("pencil"))[:, None]
    by_owner = jnp.take(places, holder[:, 0], axis=0)
    lists = by_owner[:, 2 * tile_count :].reshape(peers, peers, cap)
    slots = places[:, :tile_count]
    block_of = (places[:, tile_count : 2 * tile_count] + blocks_dev * holder).reshape(-1)
    brick = (slots // cap * brick_dev + lists[slots // cap, holder, slots % cap]).reshape(-1)
    line = brick // runs
    run = brick % runs

    measured = measured.reshape(channels, blocks_dev, size)
    measured = jnp.concatenate(everywhere(jnp.swapaxes(measured, 0, 1), "pencil"), 0)
    measured_block = (
        places[:, tile_count : 2 * tile_count]
        + blocks_dev * jnp.arange(peers, dtype=jnp.int32)[:, None]
    ).reshape(-1)

    cos_y, sin_y = wave(
        line - columns // 2, jnp.arange(columns, dtype=jnp.int32) - columns // 2, columns
    )
    row_ids = jnp.arange(rows, dtype=jnp.int32) + lax.axis_index("pencil") * rows - rows_total // 2
    cos_x, sin_x = wave(
        row_ids, jnp.arange(size, dtype=jnp.int32) - rows_total // 2, rows_total
    )
    turn = jnp.stack(quarter_turns(run, row_ids, runs))
    turn_back = jnp.stack(quarter_turns(row_ids, run, runs))

    def exchanged(partial, axis="pencil"):
        count = lax.axis_size(axis)
        return [partial] + [swapped(partial, axis, k) for k in range(1, count)]

    group_shape = (group_planes, 2, rows, columns)
    group_images = coil_count * group_planes
    group_channels = 2 * group_images

    if (
        rows % 128 == 0
        and columns % 128 == 0
        and size % 128 == 0
        and channels % 16 == 0
        and tile_count % 4 == 0
        and group_channels % 8 == 0
    ):
        ey = jnp.concatenate([cos_y, sin_y], 0).astype(bf16)
        eb = jnp.concatenate(
            [jnp.concatenate([cos_y, sin_y], 1), jnp.concatenate([-sin_y, cos_y], 1)], 0
        )
        eb = table_parts(eb, 0)
        mx = jnp.concatenate(
            [jnp.concatenate([cos_x, -sin_x], 1), jnp.concatenate([sin_x, cos_x], 1)], 0
        )
        mx, mx_back = mx.astype(bf16), table_parts(mx, 1)
        measured, ey, mx, turn, block_of, all_weights = lax.optimization_barrier(
            (measured, ey, mx, turn, block_of, all_weights)
        )
        places_spec = pl.BlockSpec(memory_space=pltpu.SMEM)
        plane_spec = pl.BlockSpec((1, 2, rows, columns), lambda p: (p, 0, 0, 0))
        sens_specs = [
            pl.BlockSpec((1, 1, 2, rows, columns), functools.partial(lambda c, p: (c, p, 0, 0, 0), c))
            for c in range(coil_count)
        ]
        grid_scratch = pltpu.VMEM((tiles * group_channels, size), f32)
        params = pltpu.CompilerParams(vmem_limit_bytes=vmem_limit)
        tail_tables = [mx_back, eb, turn_back]
        weights_specs = [pl.BlockSpec(memory_space=pl.ANY)] * peers
        held_weights = [
            pltpu.VMEM((peers,) + weights.shape, bf16),
            pltpu.SemaphoreType.DMA((peers,)),
        ]

        def shaped(shape, dtype=f32):
            return jax.ShapeDtypeStruct(shape, dtype)

        def call(kernel, grid, inputs, specs, outs, out_specs, scratch, images):
            flops = 2 * images * 8 * tiles * rows * (columns + size)
            return pl.pallas_call(
                kernel,
                grid=grid,
                in_specs=specs,
                out_specs=out_specs,
                out_shape=outs,
                scratch_shapes=scratch,
                compiler_params=params,
                cost_estimate=pl.CostEstimate(
                    flops=flops,
                    bytes_accessed=sum(math.prod(i.shape) * i.dtype.itemsize for i in inputs),
                    transcendentals=0,
                ),
            )(*inputs)

        def measured_images():
            inputs = [measured_block, measured, *all_weights, *tail_tables]
            turned_shape = shaped((peers,) + weights.shape, bf16)
            shape = (coil_count, own_planes, 2, rows, columns)
            return call(
                measured_kernel,
                (own_planes,),
                inputs,
                [places_spec] + [whole_block(i) for i in inputs[1:]],
                [shaped(shape), turned_shape],
                [
                    pl.BlockSpec((coil_count, 1, 2, rows, columns), lambda p: (0, p, 0, 0, 0)),
                    whole_block(turned_shape),
                ],
                [pltpu.VMEM((tiles * channels, size), f32)],
                images_count,
            )

        def start(images, g):
            chunk = 64
            spec = pl.BlockSpec((1, 2, chunk, columns), lambda p, r: (p, 0, r, 0))
            images_spec = pl.BlockSpec(
                (coil_count, 1, 2, chunk, columns),
                lambda p, r: (0, p + g * group_planes, 0, r, 0),
            )
            dots_shape = shaped((8, 128))
            return call(
                start_kernel,
                (group_planes, rows // chunk),
                [images] + [sens[g]] * coil_count,
                [images_spec]
                + [
                    pl.BlockSpec(
                        (1, 1, 2, chunk, columns),
                        functools.partial(lambda c, p, r: (c, p, 0, r, 0), c),
                    )
                    for c in range(coil_count)
                ],
                [shaped(group_shape), shaped(group_shape, bf16), dots_shape],
                [spec, spec, whole_block(dots_shape)],
                [],
                0,
            )

        def forward(picture, g):
            tail = [ey, mx, turn]
            out = shaped((blocks * group_channels, size), bf16)
            return call(
                functools.partial(forward_kernel, coil_count),
                (group_planes,),
                [block_of, picture] + [sens[g]] * coil_count + [*all_weights, *tail],
                [places_spec, plane_spec]
                + sens_specs
                + weights_specs
                + [whole_block(i) for i in tail],
                out,
                whole_block(out),
                [grid_scratch, pltpu.VMEM((blocks, group_channels, size), f32)] + held_weights,
                group_images,
            )

        def back(kernel, samples, tables, vectors, g, outs, out_specs, scratch=()):
            inputs = [*samples, turned_weights]
            tables = tail_tables + tables
            return call(
                functools.partial(kernel, peers, coil_count),
                (group_planes,),
                [block_of, *inputs] + [sens[g]] * coil_count + tables + vectors,
                [places_spec]
                + [whole_block(i) for i in inputs]
                + sens_specs
                + [whole_block(i) for i in tables]
                + [plane_spec] * len(vectors),
                outs,
                out_specs,
                [grid_scratch, pltpu.VMEM((blocks, 2 * group_channels, size), bf16), *scratch],
                group_images,
            )

        def first(samples, norms, right_side, g):
            small, large = shaped((8, 128)), shaped(samples[0].shape)
            return back(
                first_kernel,
                samples,
                norms,
                [right_side],
                g,
                [shaped(group_shape), shaped(group_shape, bf16), small, small, large],
                [plane_spec, plane_spec] + [whole_block(i) for i in (small, small, large)],
            )

        def facts_of(samples, dots, start_total, facts):
            inputs = [*samples, *dots, start_total, facts]
            return pl.pallas_call(
                functools.partial(facts_kernel, peers),
                in_specs=[pl.BlockSpec(memory_space=pltpu.VMEM)] * len(inputs),
                out_specs=pl.BlockSpec(memory_space=pltpu.VMEM),
                out_shape=shaped((8, 128)),
                compiler_params=params,
            )(*inputs)

        def assembled(infos, parts, ks, out=None):
            step = own_planes // len(parts)
            order = jnp.stack(
                [(coil_index ^ k) * len(parts) + h for k in ks for h in range(len(parts))]
            ).astype(jnp.int32)
            inputs, specs = [], [pl.BlockSpec(infos[0].shape, lambda i, o: (0, 0, 0))] * len(infos)
            for k in ks:
                for vectors, h in parts:
                    for vector in vectors:
                        inputs.append(vector[k])
                        specs.append(
                            pl.BlockSpec(
                                (step, 2, rows, columns),
                                functools.partial(lambda h, i, o: (h, 0, 0, 0), h),
                            )
                        )
            aliases = {}
            if out is not None:
                aliases = {1 + len(infos) + len(inputs): 0}
                inputs.append(out)
                specs.append(pl.BlockSpec(memory_space=pl.ANY))
            counts = [len(vectors) for vectors, h in parts]
            return pl.pallas_call(
                functools.partial(assemble_kernel, coil_count, list(ks), counts),
                grid_spec=pltpu.PrefetchScalarGridSpec(
                    num_scalar_prefetch=1,
                    grid=(len(ks) * len(parts),),
                    in_specs=specs,
                    out_specs=pl.BlockSpec(
                        (step, 2, rows, columns), lambda i, o: (o[i], 0, 0, 0)
                    ),
                    scratch_shapes=[pltpu.VMEM((len(ks), 8, 128), f32)],
                ),
                out_shape=shaped((planes, 2, rows, columns)),
                input_output_aliases=aliases,
                compiler_params=params,
            )(order, *infos, *inputs)

        def second(samples, facts, infos, right_side, residual, g):
            return back(
                second_kernel,
                samples,
                [facts, *infos],
                [right_side, residual],
                g,
                shaped(group_shape, bf16),
                plane_spec,
                [pltpu.VMEM((1, 8, 128), f32)],
            )

    else:
        ein = functools.partial(jnp.einsum, precision=lax.Precision.HIGH)
        maps = [array.astype(f32) for array in sens]
        block_map = (block_of[:, None] == jnp.arange(blocks, dtype=jnp.int32)).astype(f32)
        tc, ts = turn[0][:, None, None], turn[1][:, None, None]
        wide_weights = jnp.concatenate(all_weights, 0).astype(f32)

        def forward(picture, g):
            map_real, map_imag = maps[g][:, :, 0], maps[g][:, :, 1]
            coil_real = map_real * picture[None, :, 0] - map_imag * picture[None, :, 1]
            coil_imag = map_real * picture[None, :, 1] + map_imag * picture[None, :, 0]
            half_real = ein("ty,cpxy->tcpx", cos_y, coil_real) + ein(
                "ty,cpxy->tcpx", sin_y, coil_imag
            )
            half_imag = ein("ty,cpxy->tcpx", cos_y, coil_imag) - ein(
                "ty,cpxy->tcpx", sin_y, coil_real
            )
            real = half_real * tc + half_imag * ts
            imag = half_imag * tc - half_real * ts
            grid = jnp.stack(
                [
                    ein("tcpx,xi->tcpi", real, cos_x) + ein("tcpx,xi->tcpi", imag, sin_x),
                    ein("tcpx,xi->tcpi", imag, cos_x) - ein("tcpx,xi->tcpi", real, sin_x),
                ],
                3,
            ).reshape(tiles, group_channels, size)
            product = ein("tgi,tis->tgs", grid, wide_weights)
            return ein("tb,tgs->bgs", block_map, product).astype(bf16).reshape(-1, size)

        def images_of(samples, blocks_of):
            spread = ein("tgs,tis->tgi", jnp.take(samples, blocks_of, axis=0), wide_weights)
            spread = spread.reshape(tiles, coil_count, -1, 2, size)
            back_real = ein("tcpi,xi->tcpx", spread[:, :, :, 0], cos_x) - ein(
                "tcpi,xi->tcpx", spread[:, :, :, 1], sin_x
            )
            back_imag = ein("tcpi,xi->tcpx", spread[:, :, :, 1], cos_x) + ein(
                "tcpi,xi->tcpx", spread[:, :, :, 0], sin_x
            )
            real = back_real * tc - back_imag * ts
            imag = back_imag * tc + back_real * ts
            return jnp.stack(
                [
                    ein("tcpx,ty->cpxy", real, cos_y) - ein("tcpx,ty->cpxy", imag, sin_y),
                    ein("tcpx,ty->cpxy", imag, cos_y) + ein("tcpx,ty->cpxy", real, sin_y),
                ],
                2,
            )

        def combined(images, g):
            map_real, map_imag = maps[g][:, :, 0], maps[g][:, :, 1]
            real, imag = images[:, :, 0], images[:, :, 1]
            return jnp.stack(
                [
                    jnp.sum(map_real * real + map_imag * imag, 0),
                    jnp.sum(map_real * imag - map_imag * real, 0),
                ],
                1,
            )

        def stacked_dots(values):
            values = values + [jnp.zeros((), f32)] * (8 - len(values))
            return jnp.broadcast_to(jnp.stack(values)[:, None], (8, 128))

        def applied_to(samples, vector, g):
            samples = added(samples).reshape(blocks, group_channels, size)
            return combined(images_of(samples, block_of), g) + damping * vector

        def measured_images():
            return images_of(measured.astype(f32), measured_block), None

        def start(images, g):
            right_side = combined(images[:, g * group_planes : (g + 1) * group_planes], g)
            dots = stacked_dots([jnp.sum(right_side * right_side)])
            return right_side, right_side.astype(bf16), dots

        def first(samples, norms, right_side, g):
            norm = tree_sum(norms)[0, 0]
            total = added(samples)
            energy = jnp.sum(jnp.square(total))
            residual = right_side - step_of(norm, energy) * applied_to(samples, right_side, g)
            dots = [jnp.sum(residual * residual), jnp.sum(residual * right_side)]
            facts = stacked_dots([norm, energy])
            return residual, residual.astype(bf16), facts, stacked_dots(dots), total

        def facts_of(samples, dots, start_total, facts):
            total = added(samples)
            square, cross = tree_sum(dots)[:2, 0]
            values = [facts[0, 0], facts[1, 0], square, cross]
            values += [jnp.sum(total * total), jnp.sum(total * start_total)]
            return stacked_dots(values)

        def factors_of(infos, is_residual):
            numbers = [[[info[0, row, 0]] for info in infos] for row in range(6)]
            return [factors[0] for factors in coefficients(*numbers)[is_residual]]

        def mixture(factors, vectors):
            return sum(factor * vector.astype(f32) for factor, vector in zip(factors, vectors))

        def assembled(infos, parts, ks, out=None):
            factors = factors_of(infos, False)
            step = own_planes // len(parts)
            if out is None:
                out = jnp.zeros((planes, 2, rows, columns), f32)
            for k in ks:
                for h, (vectors, at) in enumerate(parts):
                    place = ((coil_index ^ k) * own_planes + h * step, 0, 0, 0)
                    pieces = [vector[k][at * step : (at + 1) * step] for vector in vectors]
                    if len(pieces) == 1:
                        piece = pieces[0].astype(f32)
                    else:
                        piece = mixture(factors[k], pieces)
                    out = lax.dynamic_update_slice(out, piece, place)
            return out

        def second(samples, facts, infos, right_side, residual, g):
            mixed = residual - step_of(facts[0, 0], facts[1, 0]) * applied_to(samples, residual, g)
            return mixture(factors_of(infos, True)[0], [right_side, residual, mixed]).astype(bf16)

    def added(samples):
        return tree_sum([part.astype(f32) for part in samples])

    def sent_by_bits(own):
        return [swapped(own, "coil", k) for k in first_bits]

    images, turned_weights = measured_images()
    right_side, start_own, norm = start(images, 0)
    start_sent = sent_by_bits(start_own)
    samples, norm = lax.optimization_barrier((forward(right_side, 0), norm))
    samples = exchanged(samples)
    norms = exchanged(norm)
    samples, norms, start_sent = lax.optimization_barrier((samples, norms, start_sent))
    residual, residual_own, facts, dots, start_total = first(samples, norms, right_side, 0)
    dots = exchanged(dots)
    residual, residual_own, dots, start_pieces = lax.optimization_barrier(
        (residual, residual_own, dots, completed(start_own, start_sent))
    )
    residual_sent = sent_by_bits(residual_own)
    samples = exchanged(forward(residual, 0))
    samples, dots = lax.optimization_barrier((samples, dots))
    info = facts_of(samples, dots, start_total, facts)
    others = exchanged(info[None], "coil")
    samples, others, residual_sent = lax.optimization_barrier((samples, others, residual_sent))
    final_own = second(samples, info, others, right_side, residual, 0)
    final_own, residual_pieces = lax.optimization_barrier(
        (final_own, completed(residual_own, residual_sent))
    )
    final_sent = sent_by_bits(final_own)

    picture = assembled(others, [([start_pieces, residual_pieces], 0)], range(coil_count))
    near = [final_own, final_sent[0]] + [None] * (coil_count - 2)
    out = assembled(others, [([near], 0)], range(2))
    picture, final_sent = lax.optimization_barrier((picture, final_sent))
    parts = [([completed(final_own, final_sent)], 0)]
    late = coil_count - 1
    out = assembled(others, parts, range(2, late), out)
    out = assembled(others, parts, [late], out)
    return picture, out


def solution(mesh):
    in_specs = (
        P("coil", "scan", None, "pencil"),
        P("coil", "scan", None, "pencil", None),
        P("pencil", None, None),
        P("pencil"),
        P("pencil"),
        P("pencil", None, None),
    )
    out_specs = (P("scan", None, "pencil", None), P("scan", None, "pencil", None))
    return jax.shard_map(
        on_device, mesh=mesh, in_specs=in_specs, out_specs=out_specs, check_vma=False
    )
```

```python
import functools
import math

import jax
import jax.numpy as jnp
from jax import lax
from jax.experimental import pallas as pl
from jax.experimental.pallas import tpu as pltpu
from jax.sharding import PartitionSpec as P


damping = 0.5
f32, bf16 = jnp.float32, jnp.bfloat16
vmem_limit = 56 * 1024 * 1024


def wave(left, right, length):
    phases = left[:, None] * right[None, :] % length
    angles = phases.astype(f32) * (2.0 * math.pi / length)
    return jnp.cos(angles) / math.sqrt(length), jnp.sin(angles) / math.sqrt(length)


def quarter_turns(left, right, count):
    turns = left[:, None] * right[None, :] % count
    if count == 4:
        cosine = jnp.where(turns == 0, 1.0, 0.0) - jnp.where(turns == 2, 1.0, 0.0)
        sine = jnp.where(turns == 1, 1.0, 0.0) - jnp.where(turns == 3, 1.0, 0.0)
        return cosine.astype(f32), sine.astype(f32)
    angles = turns.astype(f32) * (2.0 * math.pi / count)
    return jnp.cos(angles), jnp.sin(angles)


def split(value):
    high = value.astype(bf16)
    return high, (value - high.astype(f32)).astype(bf16)


def table_parts(table, axis):
    high = lax.reduce_precision(table, 8, 7)
    low = (table - high).astype(bf16)
    high = high.astype(bf16)
    return jnp.concatenate([high, high, low], axis)


def data_parts(value):
    high, low = split(value)
    return jnp.concatenate([high, low, high], 1)


def nt(left, right):
    return lax.dot_general(left, right, (((1,), (1,)), ((), ())), preferred_element_type=f32)


def nn(left, right):
    return jnp.dot(left, right, preferred_element_type=f32)


def tree_sum(values):
    while len(values) > 1:
        values = [left + right for left, right in zip(values[::2], values[1::2])]
    return values[0]


def forward_images(plane, planes, picture, sens, ey, mx, turn_ref, grid_ref):
    tiles = turn_ref.shape[1]
    rows = turn_ref.shape[2]
    channels = grid_ref.shape[0] // tiles
    real, imag = picture[0, 0], picture[0, 1]
    turned = []
    for sens_ref in sens:
        sens_real = sens_ref[0, 0, 0].astype(f32)
        sens_imag = sens_ref[0, 0, 1].astype(f32)
        coil = jnp.concatenate(
            [sens_real * real - sens_imag * imag, sens_real * imag + sens_imag * real], 0
        )
        both = nt(ey[...], coil.astype(bf16))
        half_real = both[:tiles, :rows] + both[tiles:, rows:]
        half_imag = both[:tiles, rows:] - both[tiles:, :rows]
        turned.append(
            jnp.concatenate(
                [
                    half_real * turn_ref[0] + half_imag * turn_ref[1],
                    half_imag * turn_ref[0] - half_real * turn_ref[1],
                ],
                1,
            ).astype(bf16)
        )
    grid = nn(jnp.concatenate(turned, 0), mx[...])
    size = grid.shape[1] // 2
    for coil in range(len(sens)):
        step = coil * planes + plane
        part = grid[coil * tiles : (coil + 1) * tiles]
        grid_ref[pl.ds(2 * step, tiles, stride=channels), :] = part[:, :size]
        grid_ref[pl.ds(2 * step + 1, tiles, stride=channels), :] = part[:, size:]


def tile_products(lefts, rights):
    rows, size = lefts[0].shape
    empty = jnp.zeros((rows, size), bf16)
    left = jnp.concatenate(
        [
            jnp.concatenate([value, empty] if place % 2 == 0 else [empty, value], 1)
            for place, value in enumerate(lefts)
        ],
        0,
    )
    right = jnp.concatenate(
        [jnp.concatenate(rights[:2], 0), jnp.concatenate(rights[2:], 0)], 1
    )
    product = nn(left, right)
    return [
        product[place * rows : (place + 1) * rows, place // 2 * size : (place // 2 + 1) * size]
        for place in range(4)
    ]


def each_four(count, function):
    def one(index, carry):
        function([index * 4 + place for place in range(4)])
        return carry

    lax.fori_loop(0, count // 4, one, 0, unroll=True)


def weight_copies(weights, held, sems):
    return [
        pltpu.make_async_copy(ref, held.at[place], sems.at[place])
        for place, ref in enumerate(weights)
    ]


def start_copies(copies):
    for copy in copies:
        copy.start()


def sample_tiles(block_ref, copies, weights, grid_ref, sums_ref, out_ref):
    count = weights.shape[1]
    channels = sums_ref.shape[1]
    sums_ref[...] = jnp.zeros_like(sums_ref)

    def left_of(tile):
        value = grid_ref[pl.ds(pl.multiple_of(tile * channels, channels), channels), :]
        high = value.astype(bf16).astype(f32)
        return jnp.concatenate([high, value - high], 0).astype(bf16)

    for group, copy in enumerate(copies):
        copy.wait()

        def four(places):
            tiles = [group * count + place for place in places]
            products = tile_products(
                [left_of(tile) for tile in tiles], [weights[group, place] for place in places]
            )
            for tile, product in zip(tiles, products):
                sums_ref[block_ref[tile]] += product[:channels] + product[channels:]

        each_four(count, four)
    out_ref[...] = sums_ref[...].reshape(out_ref.shape).astype(bf16)


def spread_tiles(block_ref, weights, parts_ref, grid_ref, turned_ref=None):
    count = weights[0].shape[0]
    channels = grid_ref.shape[0] // (count * len(weights))

    for group, weights_ref in enumerate(weights):

        def four(places):
            tiles = [group * count + place for place in places]
            rights = [weights_ref[place] for place in places]
            if turned_ref is not None:
                rights = [right.astype(f32).T.astype(bf16) for right in rights]
                for place, right in zip(places, rights):
                    turned_ref[group, place] = right
            products = tile_products([parts_ref[block_ref[tile]] for tile in tiles], rights)
            for tile, product in zip(tiles, products):
                if product.shape[0] > channels:
                    product = product[:channels] + product[channels:]
                start = pl.multiple_of(tile * channels, channels)
                grid_ref[pl.ds(start, channels), :] = product

        each_four(count, four)


def adjoint_images(coils, plane, planes, ey_back, mx_back, turn_ref, grid_ref):
    rows, tiles = turn_ref.shape[1], turn_ref.shape[2]
    channels = grid_ref.shape[0] // tiles
    grids = []
    for coil in range(coils):
        step = coil * planes + plane
        grid = jnp.concatenate(
            [
                grid_ref[pl.ds(2 * step, tiles, stride=channels), :],
                grid_ref[pl.ds(2 * step + 1, tiles, stride=channels), :],
            ],
            1,
        )
        grids.append(data_parts(grid))
    back = nt(mx_back[...], jnp.concatenate(grids, 0))
    turned = []
    for coil in range(coils):
        part = back[:, coil * tiles : (coil + 1) * tiles]
        both = jnp.concatenate(
            [
                part[:rows] * turn_ref[0] - part[rows:] * turn_ref[1],
                part[rows:] * turn_ref[0] + part[:rows] * turn_ref[1],
            ],
            1,
        )
        turned.append(data_parts(both))
    image = nn(jnp.concatenate(turned, 0), ey_back[...])
    columns = image.shape[1] // 2
    return [
        (image[c * rows : (c + 1) * rows, :columns], image[c * rows : (c + 1) * rows, columns:])
        for c in range(coils)
    ]


def add_dots(dots_ref, products):
    rows = lax.broadcasted_iota(jnp.int32, dots_ref.shape, 0)
    total = dots_ref[...]
    for place, (left, right) in enumerate(products):
        total += jnp.where(rows == place, jnp.sum(left * right), 0.0)
    dots_ref[...] = total


def measured_kernel(block, samples, *refs):
    *weights, mx, eb, turn, images, turned, grid = refs
    plane = pl.program_id(0)
    coils = images.shape[0]

    @pl.when(plane == 0)
    def _():
        spread_tiles(block, weights, samples, grid, turned)

    found = adjoint_images(coils, plane, pl.num_programs(0), eb, mx, turn, grid)
    for coil, (real, imag) in enumerate(found):
        images[coil, 0, 0] = real
        images[coil, 0, 1] = imag


def combine(images, sens):
    total_real = total_imag = 0.0
    for (real, imag), sens_ref in zip(images, sens):
        sens_real = sens_ref[0, 0, 0].astype(f32)
        sens_imag = sens_ref[0, 0, 1].astype(f32)
        total_real += sens_real * real + sens_imag * imag
        total_imag += sens_real * imag - sens_imag * real
    return total_real, total_imag


def start_kernel(images, *refs):
    *sens, right_side, rounded, dots = refs
    total = combine([(images[c, 0, 0], images[c, 0, 1]) for c in range(len(sens))], sens)
    for part in range(2):
        right_side[0, part] = total[part]
        rounded[0, part] = total[part].astype(bf16)

    @pl.when((pl.program_id(0) == 0) & (pl.program_id(1) == 0))
    def _():
        dots[...] = jnp.zeros_like(dots)

    add_dots(dots, [(right_side[0], right_side[0])])


def forward_kernel(coils, block, picture, *refs):
    sens = refs[:coils]
    *weights, ey, mx, turn, samples, grid, sums, held, sems = refs[coils:]
    plane = pl.program_id(0)

    @pl.when(plane == 0)
    def _():
        start_copies(weight_copies(weights, held, sems))

    forward_images(plane, pl.num_programs(0), picture, sens, ey, mx, turn, grid)

    @pl.when(plane == pl.num_programs(0) - 1)
    def _():
        sample_tiles(block, weight_copies(weights, held, sems), held, grid, sums, samples)


def summed_parts(samples, parts):
    summed = tree_sum([part[...].astype(f32) for part in samples])
    blocks, channels, size = parts.shape[0], parts.shape[1] // 2, parts.shape[2]
    value = summed.reshape(blocks, channels, size)
    high = value.astype(bf16).astype(f32)
    parts[...] = jnp.concatenate([high, value - high], 1).astype(bf16)
    return summed


def step_of(norm, energy):
    return jnp.where(norm > 0.0, norm / (energy + damping * norm), 1.0)


def first_kernel(peers, coils, block, *refs):
    samples, weights, sens = refs[:peers], refs[peers], refs[peers + 1 :][:coils]
    mx, eb, turn, *norms = refs[peers + 1 + coils :][: 3 + peers]
    right_side, residual, rounded, facts, dots, total_samples, grid, parts = refs[-8:]
    plane = pl.program_id(0)

    @pl.when(plane == 0)
    def _():
        summed = summed_parts(samples, parts)
        total_samples[...] = summed
        rows = lax.broadcasted_iota(jnp.int32, facts.shape, 0)
        norm = tree_sum([part[...] for part in norms])
        facts[...] = jnp.where(rows == 1, jnp.sum(summed * summed), norm)
        dots[...] = jnp.zeros_like(dots)
        spread_tiles(block, [weights.at[k] for k in range(peers)], parts, grid)

    images = adjoint_images(coils, plane, pl.num_programs(0), eb, mx, turn, grid)
    total = combine(images, sens)
    scale = step_of(facts[0:1, 0:1], facts[1:2, 0:1])
    for part in range(2):
        vector = right_side[0, part]
        value = vector - scale * (total[part] + damping * vector)
        residual[0, part] = value
        rounded[0, part] = value.astype(bf16)
        add_dots(dots, [(value, value), (value, vector)])


def second_kernel(peers, coils, block, *refs):
    samples, weights, sens = refs[:peers], refs[peers], refs[peers + 1 :][:coils]
    mx, eb, turn, facts, *infos = refs[peers + 1 + coils :][: 4 + coils]
    right_side, residual, rounded, grid, parts, kept = refs[-6:]
    plane = pl.program_id(0)

    @pl.when(plane == 0)
    def _():
        kept_coefficients(infos, kept, [0], True)
        summed_parts(samples, parts)
        spread_tiles(block, [weights.at[k] for k in range(peers)], parts, grid)

    images = adjoint_images(coils, plane, pl.num_programs(0), eb, mx, turn, grid)
    total = combine(images, sens)
    scale = step_of(facts[0:1, 0:1], facts[1:2, 0:1])
    for part in range(2):
        vector = residual[0, part]
        mixed = vector - scale * (total[part] + damping * vector)
        value = kept[0, 0:1, 0:1] * right_side[0, part] + kept[0, 1:2, 0:1] * vector
        rounded[0, part] = (value + kept[0, 2:3, 0:1] * mixed).astype(bf16)


def facts_kernel(peers, *refs):
    samples, dots = refs[:peers], refs[peers : 2 * peers]
    start_total, facts, out = refs[2 * peers :]
    both = tree_sum([part[...] for part in dots])
    summed = tree_sum([part[...].astype(f32) for part in samples])
    rows = lax.broadcasted_iota(jnp.int32, out.shape, 0)
    values = [facts[0:1], facts[1:2], both[0:1], both[1:2]]
    values += [jnp.sum(summed * summed), jnp.sum(summed * start_total[...])]
    total = jnp.zeros(out.shape, f32)
    for row, value in enumerate(values):
        total = jnp.where(rows == row, value, total)
    out[...] = total


def coefficients(norm, energy, square, cross, again, mixed):
    def over_all(values):
        return tree_sum([sum(of_coil) for of_coil in values])

    def each(function, *lists):
        return [[function(*items) for items in zip(*of_coil)] for of_coil in zip(*lists)]

    start_curve = each(lambda e, n: e + damping * n, energy, norm)
    curve = each(lambda e, n: e + damping * n, again, square)
    mixed_curve = each(lambda e, n: e + damping * n, mixed, cross)
    sigma = each(step_of, norm, energy)
    start_norm = over_all(norm)
    first_step = start_norm / over_all(start_curve)
    part = each(lambda s: first_step / s, sigma)
    next_norm = over_all(
        each(
            lambda w, n, c, s: w * w * s + 2.0 * w * (1.0 - w) * c + (1.0 - w) * (1.0 - w) * n,
            part,
            norm,
            cross,
            square,
        )
    )
    more = each(lambda w: 1.0 - w + next_norm / start_norm, part)
    second_step = next_norm / over_all(
        each(
            lambda w, m, q, c, s, z, qm, qs: w * w * q
            + w * m * ((c - s) / z + qm)
            + m * m * qs,
            part,
            more,
            curve,
            cross,
            square,
            sigma,
            mixed_curve,
            start_curve,
        )
    )
    share = each(lambda z: second_step / z, sigma)
    picture = each(lambda w, m: (first_step + second_step * m, second_step * w), part, more)
    residual = each(
        lambda w, m, h: (1.0 - w - h * m, w - h * w + h * m, h * w), part, more, share
    )
    return picture, residual


def kept_coefficients(infos, kept, ks, is_residual):
    numbers = [
        [[info[0, row : row + 1, 0:1]] for info in infos] for row in range(6)
    ]
    factors = coefficients(*numbers)[is_residual]
    rows = lax.broadcasted_iota(jnp.int32, kept.shape[1:], 0)
    for place, k in enumerate(ks):
        total = jnp.zeros(kept.shape[1:], f32)
        for row, factor in enumerate(factors[k][0]):
            total = jnp.where(rows == row, factor, total)
        kept[place] = total


def assemble_kernel(coils, ks, counts, order, *refs):
    infos, pieces, (out, kept) = refs[:coils], refs[coils:-2], refs[-2:]

    if max(counts) > 1:

        @pl.when(pl.program_id(0) == 0)
        def _():
            kept_coefficients(infos, kept, ks, False)

    def write(place, used):
        @pl.when(pl.program_id(0) == place)
        def _():
            if len(used) == 1:
                out[...] = used[0][...].astype(f32)
            else:
                total = 0.0
                for row, piece in enumerate(used):
                    factor = kept[place // len(counts), row : row + 1, 0:1]
                    total += factor.reshape(1, 1, 1, 1) * piece[...].astype(f32)
                out[...] = total

    first = 0
    for place in range(len(ks) * len(counts)):
        count = counts[place % len(counts)]
        write(place, pieces[first : first + count])
        first += count


def whole_block(array):
    rank = len(array.shape)
    return pl.BlockSpec(array.shape, lambda *_: (0,) * rank)


def on_device(kspace, sens_maps, weights, tile_slot, tile_block, send_list):
    coil_count = lax.axis_size("coil")
    peers = lax.axis_size("pencil")
    planes = sens_maps.shape[1]
    own_planes = planes // coil_count
    rows = sens_maps.shape[3]
    columns = sens_maps.shape[4]
    rows_total = rows * peers
    size = weights.shape[1]
    tile_count = tile_slot.shape[0]
    tiles = tile_count * peers
    blocks_dev = kspace.shape[3] // size
    blocks = blocks_dev * peers
    cap = send_list.shape[2]
    runs = rows_total // size
    brick_dev = columns // peers * runs
    images_count = coil_count * own_planes
    channels = 2 * images_count

    coil_index = lax.axis_index("coil")

    def swapped(array, axis, k):
        return lax.ppermute(array, axis, [(i, i ^ k) for i in range(lax.axis_size(axis))])

    def everywhere(array, axis):
        bit = 1
        while bit < lax.axis_size(axis):
            bit *= 2
        pieces = {0: array}
        while bit > 1:
            bit //= 2
            for k in sorted(pieces):
                pieces[k ^ bit] = swapped(pieces[k], axis, bit)
        return [pieces[k] for k in sorted(pieces)]

    first_bits = [1 << bit for bit in range(coil_count.bit_length() - 1)]

    def completed(own, sent):
        pieces = {0: own}
        for bit, piece in zip(first_bits, sent):
            pieces[bit] = piece
        for bit in first_bits:
            for k in range(coil_count):
                if k not in pieces and (k ^ bit) in pieces:
                    pieces[k] = swapped(pieces[k ^ bit], "coil", bit)
        return [pieces[k] for k in range(coil_count)]

    def to_planes(array):
        pieces = []
        for k in range(coil_count):
            part = lax.dynamic_slice_in_dim(array, (coil_index ^ k) * own_planes, own_planes, 0)
            pieces.append(swapped(part, "coil", k) if k > 0 else part)
        return pieces

    group_planes = own_planes
    groups = range(own_planes // group_planes)
    measured = to_planes(kspace[0])
    packed = jnp.concatenate([tile_slot, tile_block, send_list.reshape(-1)])
    sens_source, packed, measured, own_weights = lax.optimization_barrier(
        (sens_maps[0], packed, measured, weights)
    )
    sens_source = sens_source.reshape(coil_count, own_planes, 2, rows, columns)
    sens = [
        lax.all_to_all(
            sens_source[:, g * group_planes : (g + 1) * group_planes],
            "coil",
            split_axis=0,
            concat_axis=0,
            tiled=True,
        )
        for g in groups
    ]
    measured = jnp.stack(measured)
    by_coil = jnp.arange(coil_count, dtype=jnp.int32) ^ coil_index
    measured = jnp.take(measured, by_coil, axis=0)
    all_weights = everywhere(own_weights, "pencil")

    places = jnp.stack(everywhere(packed, "pencil"))
    holder = (jnp.arange(peers, dtype=jnp.int32) ^ lax.axis_index("pencil"))[:, None]
    by_owner = jnp.take(places, holder[:, 0], axis=0)
    lists = by_owner[:, 2 * tile_count :].reshape(peers, peers, cap)
    slots = places[:, :tile_count]
    block_of = (places[:, tile_count : 2 * tile_count] + blocks_dev * holder).reshape(-1)
    brick = (slots // cap * brick_dev + lists[slots // cap, holder, slots % cap]).reshape(-1)
    line = brick // runs
    run = brick % runs

    measured = measured.reshape(channels, blocks_dev, size)
    measured = jnp.concatenate(everywhere(jnp.swapaxes(measured, 0, 1), "pencil"), 0)
    measured_block = (
        places[:, tile_count : 2 * tile_count]
        + blocks_dev * jnp.arange(peers, dtype=jnp.int32)[:, None]
    ).reshape(-1)

    cos_y, sin_y = wave(
        line - columns // 2, jnp.arange(columns, dtype=jnp.int32) - columns // 2, columns
    )
    row_ids = jnp.arange(rows, dtype=jnp.int32) + lax.axis_index("pencil") * rows - rows_total // 2
    cos_x, sin_x = wave(
        row_ids, jnp.arange(size, dtype=jnp.int32) - rows_total // 2, rows_total
    )
    turn = jnp.stack(quarter_turns(run, row_ids, runs))
    turn_back = jnp.stack(quarter_turns(row_ids, run, runs))

    def exchanged(partial, axis="pencil"):
        count = lax.axis_size(axis)
        return [partial] + [swapped(partial, axis, k) for k in range(1, count)]

    group_shape = (group_planes, 2, rows, columns)
    group_images = coil_count * group_planes
    group_channels = 2 * group_images

    if (
        rows % 128 == 0
        and columns % 128 == 0
        and size % 128 == 0
        and channels % 16 == 0
        and tile_count % 4 == 0
        and group_channels % 8 == 0
    ):
        ey = jnp.concatenate([cos_y, sin_y], 0).astype(bf16)
        eb = jnp.concatenate(
            [jnp.concatenate([cos_y, sin_y], 1), jnp.concatenate([-sin_y, cos_y], 1)], 0
        )
        eb = table_parts(eb, 0)
        mx = jnp.concatenate(
            [jnp.concatenate([cos_x, -sin_x], 1), jnp.concatenate([sin_x, cos_x], 1)], 0
        )
        mx, mx_back = mx.astype(bf16), table_parts(mx, 1)
        measured, ey, mx, turn, block_of, all_weights = lax.optimization_barrier(
            (measured, ey, mx, turn, block_of, all_weights)
        )
        places_spec = pl.BlockSpec(memory_space=pltpu.SMEM)
        plane_spec = pl.BlockSpec((1, 2, rows, columns), lambda p: (p, 0, 0, 0))
        sens_specs = [
            pl.BlockSpec((1, 1, 2, rows, columns), functools.partial(lambda c, p: (c, p, 0, 0, 0), c))
            for c in range(coil_count)
        ]
        grid_scratch = pltpu.VMEM((tiles * group_channels, size), f32)
        params = pltpu.CompilerParams(vmem_limit_bytes=vmem_limit)
        tail_tables = [mx_back, eb, turn_back]
        weights_specs = [pl.BlockSpec(memory_space=pl.ANY)] * peers
        held_weights = [
            pltpu.VMEM((peers,) + weights.shape, bf16),
            pltpu.SemaphoreType.DMA((peers,)),
        ]

        def shaped(shape, dtype=f32):
            return jax.ShapeDtypeStruct(shape, dtype)

        def call(kernel, grid, inputs, specs, outs, out_specs, scratch, images):
            flops = 2 * images * 8 * tiles * rows * (columns + size)
            return pl.pallas_call(
                kernel,
                grid=grid,
                in_specs=specs,
                out_specs=out_specs,
                out_shape=outs,
                scratch_shapes=scratch,
                compiler_params=params,
                cost_estimate=pl.CostEstimate(
                    flops=flops,
                    bytes_accessed=sum(math.prod(i.shape) * i.dtype.itemsize for i in inputs),
                    transcendentals=0,
                ),
            )(*inputs)

        def measured_images():
            inputs = [measured_block, measured, *all_weights, *tail_tables]
            turned_shape = shaped((peers,) + weights.shape, bf16)
            shape = (coil_count, own_planes, 2, rows, columns)
            return call(
                measured_kernel,
                (own_planes,),
                inputs,
                [places_spec] + [whole_block(i) for i in inputs[1:]],
                [shaped(shape), turned_shape],
                [
                    pl.BlockSpec((coil_count, 1, 2, rows, columns), lambda p: (0, p, 0, 0, 0)),
                    whole_block(turned_shape),
                ],
                [pltpu.VMEM((tiles * channels, size), f32)],
                images_count,
            )

        def start(images, g):
            chunk = rows
            spec = pl.BlockSpec((1, 2, chunk, columns), lambda p, r: (p, 0, r, 0))
            images_spec = pl.BlockSpec(
                (coil_count, 1, 2, chunk, columns),
                lambda p, r: (0, p + g * group_planes, 0, r, 0),
            )
            dots_shape = shaped((8, 128))
            return call(
                start_kernel,
                (group_planes, rows // chunk),
                [images] + [sens[g]] * coil_count,
                [images_spec]
                + [
                    pl.BlockSpec(
                        (1, 1, 2, chunk, columns),
                        functools.partial(lambda c, p, r: (c, p, 0, r, 0), c),
                    )
                    for c in range(coil_count)
                ],
                [shaped(group_shape), shaped(group_shape, bf16), dots_shape],
                [spec, spec, whole_block(dots_shape)],
                [],
                0,
            )

        def forward(picture, g):
            tail = [ey, mx, turn]
            out = shaped((blocks * group_channels, size), bf16)
            return call(
                functools.partial(forward_kernel, coil_count),
                (group_planes,),
                [block_of, picture] + [sens[g]] * coil_count + [*all_weights, *tail],
                [places_spec, plane_spec]
                + sens_specs
                + weights_specs
                + [whole_block(i) for i in tail],
                out,
                whole_block(out),
                [grid_scratch, pltpu.VMEM((blocks, group_channels, size), f32)] + held_weights,
                group_images,
            )

        def back(kernel, samples, tables, vectors, g, outs, out_specs, scratch=()):
            inputs = [*samples, turned_weights]
            tables = tail_tables + tables
            return call(
                functools.partial(kernel, peers, coil_count),
                (group_planes,),
                [block_of, *inputs] + [sens[g]] * coil_count + tables + vectors,
                [places_spec]
                + [whole_block(i) for i in inputs]
                + sens_specs
                + [whole_block(i) for i in tables]
                + [plane_spec] * len(vectors),
                outs,
                out_specs,
                [grid_scratch, pltpu.VMEM((blocks, 2 * group_channels, size), bf16), *scratch],
                group_images,
            )

        def first(samples, norms, right_side, g):
            small, large = shaped((8, 128)), shaped(samples[0].shape)
            return back(
                first_kernel,
                samples,
                norms,
                [right_side],
                g,
                [shaped(group_shape), shaped(group_shape, bf16), small, small, large],
                [plane_spec, plane_spec] + [whole_block(i) for i in (small, small, large)],
            )

        def facts_of(samples, dots, start_total, facts):
            inputs = [*samples, *dots, start_total, facts]
            return pl.pallas_call(
                functools.partial(facts_kernel, peers),
                in_specs=[pl.BlockSpec(memory_space=pltpu.VMEM)] * len(inputs),
                out_specs=pl.BlockSpec(memory_space=pltpu.VMEM),
                out_shape=shaped((8, 128)),
                compiler_params=params,
            )(*inputs)

        def assembled(infos, parts, ks, out=None):
            step = own_planes // len(parts)
            order = jnp.stack(
                [(coil_index ^ k) * len(parts) + h for k in ks for h in range(len(parts))]
            ).astype(jnp.int32)
            inputs, specs = [], [pl.BlockSpec(infos[0].shape, lambda i, o: (0, 0, 0))] * len(infos)
            for k in ks:
                for vectors, h in parts:
                    for vector in vectors:
                        inputs.append(vector[k])
                        specs.append(
                            pl.BlockSpec(
                                (step, 2, rows, columns),
                                functools.partial(lambda h, i, o: (h, 0, 0, 0), h),
                            )
                        )
            aliases = {}
            if out is not None:
                aliases = {1 + len(infos) + len(inputs): 0}
                inputs.append(out)
                specs.append(pl.BlockSpec(memory_space=pl.ANY))
            counts = [len(vectors) for vectors, h in parts]
            return pl.pallas_call(
                functools.partial(assemble_kernel, coil_count, list(ks), counts),
                grid_spec=pltpu.PrefetchScalarGridSpec(
                    num_scalar_prefetch=1,
                    grid=(len(ks) * len(parts),),
                    in_specs=specs,
                    out_specs=pl.BlockSpec(
                        (step, 2, rows, columns), lambda i, o: (o[i], 0, 0, 0)
                    ),
                    scratch_shapes=[pltpu.VMEM((len(ks), 8, 128), f32)],
                ),
                out_shape=shaped((planes, 2, rows, columns)),
                input_output_aliases=aliases,
                compiler_params=params,
            )(order, *infos, *inputs)

        def second(samples, facts, infos, right_side, residual, g):
            return back(
                second_kernel,
                samples,
                [facts, *infos],
                [right_side, residual],
                g,
                shaped(group_shape, bf16),
                plane_spec,
                [pltpu.VMEM((1, 8, 128), f32)],
            )

    else:
        ein = functools.partial(jnp.einsum, precision=lax.Precision.HIGH)
        maps = [array.astype(f32) for array in sens]
        block_map = (block_of[:, None] == jnp.arange(blocks, dtype=jnp.int32)).astype(f32)
        tc, ts = turn[0][:, None, None], turn[1][:, None, None]
        wide_weights = jnp.concatenate(all_weights, 0).astype(f32)

        def forward(picture, g):
            map_real, map_imag = maps[g][:, :, 0], maps[g][:, :, 1]
            coil_real = map_real * picture[None, :, 0] - map_imag * picture[None, :, 1]
            coil_imag = map_real * picture[None, :, 1] + map_imag * picture[None, :, 0]
            half_real = ein("ty,cpxy->tcpx", cos_y, coil_real) + ein(
                "ty,cpxy->tcpx", sin_y, coil_imag
            )
            half_imag = ein("ty,cpxy->tcpx", cos_y, coil_imag) - ein(
                "ty,cpxy->tcpx", sin_y, coil_real
            )
            real = half_real * tc + half_imag * ts
            imag = half_imag * tc - half_real * ts
            grid = jnp.stack(
                [
                    ein("tcpx,xi->tcpi", real, cos_x) + ein("tcpx,xi->tcpi", imag, sin_x),
                    ein("tcpx,xi->tcpi", imag, cos_x) - ein("tcpx,xi->tcpi", real, sin_x),
                ],
                3,
            ).reshape(tiles, group_channels, size)
            product = ein("tgi,tis->tgs", grid, wide_weights)
            return ein("tb,tgs->bgs", block_map, product).astype(bf16).reshape(-1, size)

        def images_of(samples, blocks_of):
            spread = ein("tgs,tis->tgi", jnp.take(samples, blocks_of, axis=0), wide_weights)
            spread = spread.reshape(tiles, coil_count, -1, 2, size)
            back_real = ein("tcpi,xi->tcpx", spread[:, :, :, 0], cos_x) - ein(
                "tcpi,xi->tcpx", spread[:, :, :, 1], sin_x
            )
            back_imag = ein("tcpi,xi->tcpx", spread[:, :, :, 1], cos_x) + ein(
                "tcpi,xi->tcpx", spread[:, :, :, 0], sin_x
            )
            real = back_real * tc - back_imag * ts
            imag = back_imag * tc + back_real * ts
            return jnp.stack(
                [
                    ein("tcpx,ty->cpxy", real, cos_y) - ein("tcpx,ty->cpxy", imag, sin_y),
                    ein("tcpx,ty->cpxy", imag, cos_y) + ein("tcpx,ty->cpxy", real, sin_y),
                ],
                2,
            )

        def combined(images, g):
            map_real, map_imag = maps[g][:, :, 0], maps[g][:, :, 1]
            real, imag = images[:, :, 0], images[:, :, 1]
            return jnp.stack(
                [
                    jnp.sum(map_real * real + map_imag * imag, 0),
                    jnp.sum(map_real * imag - map_imag * real, 0),
                ],
                1,
            )

        def stacked_dots(values):
            values = values + [jnp.zeros((), f32)] * (8 - len(values))
            return jnp.broadcast_to(jnp.stack(values)[:, None], (8, 128))

        def applied_to(samples, vector, g):
            samples = added(samples).reshape(blocks, group_channels, size)
            return combined(images_of(samples, block_of), g) + damping * vector

        def measured_images():
            return images_of(measured.astype(f32), measured_block), None

        def start(images, g):
            right_side = combined(images[:, g * group_planes : (g + 1) * group_planes], g)
            dots = stacked_dots([jnp.sum(right_side * right_side)])
            return right_side, right_side.astype(bf16), dots

        def first(samples, norms, right_side, g):
            norm = tree_sum(norms)[0, 0]
            total = added(samples)
            energy = jnp.sum(jnp.square(total))
            residual = right_side - step_of(norm, energy) * applied_to(samples, right_side, g)
            dots = [jnp.sum(residual * residual), jnp.sum(residual * right_side)]
            facts = stacked_dots([norm, energy])
            return residual, residual.astype(bf16), facts, stacked_dots(dots), total

        def facts_of(samples, dots, start_total, facts):
            total = added(samples)
            square, cross = tree_sum(dots)[:2, 0]
            values = [facts[0, 0], facts[1, 0], square, cross]
            values += [jnp.sum(total * total), jnp.sum(total * start_total)]
            return stacked_dots(values)

        def factors_of(infos, is_residual):
            numbers = [[[info[0, row, 0]] for info in infos] for row in range(6)]
            return [factors[0] for factors in coefficients(*numbers)[is_residual]]

        def mixture(factors, vectors):
            return sum(factor * vector.astype(f32) for factor, vector in zip(factors, vectors))

        def assembled(infos, parts, ks, out=None):
            factors = factors_of(infos, False)
            step = own_planes // len(parts)
            if out is None:
                out = jnp.zeros((planes, 2, rows, columns), f32)
            for k in ks:
                for h, (vectors, at) in enumerate(parts):
                    place = ((coil_index ^ k) * own_planes + h * step, 0, 0, 0)
                    pieces = [vector[k][at * step : (at + 1) * step] for vector in vectors]
                    if len(pieces) == 1:
                        piece = pieces[0].astype(f32)
                    else:
                        piece = mixture(factors[k], pieces)
                    out = lax.dynamic_update_slice(out, piece, place)
            return out

        def second(samples, facts, infos, right_side, residual, g):
            mixed = residual - step_of(facts[0, 0], facts[1, 0]) * applied_to(samples, residual, g)
            return mixture(factors_of(infos, True)[0], [right_side, residual, mixed]).astype(bf16)

    def added(samples):
        return tree_sum([part.astype(f32) for part in samples])

    def sent_by_bits(own):
        return [swapped(own, "coil", k) for k in first_bits]

    images, turned_weights = measured_images()
    right_side, start_own, norm = start(images, 0)
    start_sent = sent_by_bits(start_own)
    samples, norm = lax.optimization_barrier((forward(right_side, 0), norm))
    samples = exchanged(samples)
    norms = exchanged(norm)
    samples, norms, start_sent = lax.optimization_barrier((samples, norms, start_sent))
    residual, residual_own, facts, dots, start_total = first(samples, norms, right_side, 0)
    dots = exchanged(dots)
    residual, residual_own, dots, start_pieces = lax.optimization_barrier(
        (residual, residual_own, dots, completed(start_own, start_sent))
    )
    residual_sent = sent_by_bits(residual_own)
    samples = exchanged(forward(residual, 0))
    samples, dots = lax.optimization_barrier((samples, dots))
    info = facts_of(samples, dots, start_total, facts)
    others = exchanged(info[None], "coil")
    samples, others, residual_sent = lax.optimization_barrier((samples, others, residual_sent))
    final_own = second(samples, info, others, right_side, residual, 0)
    final_own, residual_pieces = lax.optimization_barrier(
        (final_own, completed(residual_own, residual_sent))
    )
    final_sent = sent_by_bits(final_own)

    picture = assembled(others, [([start_pieces, residual_pieces], 0)], range(coil_count))
    near = [final_own, final_sent[0]] + [None] * (coil_count - 2)
    out = assembled(others, [([near], 0)], range(2))
    picture, final_sent = lax.optimization_barrier((picture, final_sent))
    parts = [([completed(final_own, final_sent)], 0)]
    late = coil_count - 1
    out = assembled(others, parts, range(2, late), out)
    out = assembled(others, parts, [late], out)
    return picture, out


def solution(mesh):
    in_specs = (
        P("coil", "scan", None, "pencil"),
        P("coil", "scan", None, "pencil", None),
        P("pencil", None, None),
        P("pencil"),
        P("pencil"),
        P("pencil", None, None),
    )
    out_specs = (P("scan", None, "pencil", None), P("scan", None, "pencil", None))
    return jax.shard_map(
        on_device, mesh=mesh, in_specs=in_specs, out_specs=out_specs, check_vma=False
    )
```
